32 devices in a mesh: section: 2 (over x), dp: 16 (over z, y, core).
Axes of the slice: x: 2, y: 2, z: 4, core: 2. Of those that a mesh axis runs over, the one named last changes fastest.
Arguments:
- tokens: bfloat16 [2, 4096, 1152], P(None, 'dp'), may hold values from -6 to 6
- kept_index: int32 [2, 2048], P(None, 'dp'), may hold values from 0 to 255, as said below
- big_image: int32 [2, 16], P(None, 'dp'), may hold values from 0 to 1
- timesteps: int32 [2, 64], P(None, 'dp'), may hold values from 0 to 999
- labels: int32 [2, 64], P(None, 'dp'), may hold values from 0 to 999
- cotangent: bfloat16 [2, 4096, 1152], P(None, 'dp'), may hold values from -6 to 6
- mask_token: bfloat16 [1152], replicated, may hold values from -6 to 6
- time_weight: bfloat16 [256, 1152], replicated, may hold values from -0.375 to 0.375
- class_table: bfloat16 [1000, 1152], replicated, may hold values from -6 to 6
- ada_weight: bfloat16 [2, 1152, 6912], P('section', 'dp'), may hold values from -0.1875 to 0.1875
- ada_bias: bfloat16 [2, 6912], P('section', 'dp'), may hold values from -3 to 3
- qkv_weight: bfloat16 [2, 1152, 3456], P('section', 'dp'), may hold values from -0.1875 to 0.1875
- proj_weight: bfloat16 [2, 1152, 1152], P('section', 'dp'), may hold values from -2 to 2
- up_weight: bfloat16 [2, 1152, 4608], P('section', 'dp'), may hold values from -0.1875 to 0.1875
- down_weight: bfloat16 [2, 4608, 1152], P('section', 'dp'), may hold values from -0.09375 to 0.09375
Outputs:
- decoded: bfloat16 [2, 4096, 1152], P(None, 'dp', 'section')
- token_grad: bfloat16 [2, 4096, 1152], P(None, 'dp', 'section')
- mask_grad: float32 [1152], replicated
- time_grad: float32 [256, 1152], replicated
- table_grad: float32 [1000, 1152], replicated
- ada_grad: float32 [2, 1152, 6912], P('section', 'dp')
- ada_bias_grad: float32 [2, 6912], P('section', 'dp')
- qkv_grad: float32 [2, 1152, 3456], P('section', 'dp')
- proj_grad: float32 [2, 1152, 1152], P('section', 'dp')
- up_grad: float32 [2, 1152, 4608], P('section', 'dp')
- down_grad: float32 [2, 4608, 1152], P('section', 'dp')
The draws below stay inside these ranges and needn't reach their ends.
Inputs may be any that keep to these rules, and one draw needn't show every extreme that they name: `kept_index`: each device's block of 128 entries of a micro-batch lists kept positions among that device's 256 positions, ascending; each of the 4 quarters of 64 positions keeps exactly half of its positions. `big_image`: where it is 1, only the first of the device's 4 image entries is used.
All inputs are finite; a program needn't handle non-finite values.
Results may differ from the reference program's by a relative error of at most 0.035.
The reference program's roundings to bfloat16 on the way count: a program that leaves them out, or rounds other values in their place, can miss the bound.
Values may be sent and summed in bfloat16 or wider, within the bound.
A program may use at most 1 GiB of HBM per device.

```python
import math
import jax
import jax.numpy as jnp
from jax import lax

D = 1152
HEADS = 16
HD = 72
FF = 4608
FREQ = 256
NCLS = 1000
SLOT = 256
SMALL_PER = 4
MICRO = 2
KEPT = 128
TOKENS = 4096
KEPT_ALL = 2048
IMAGE_SLOTS = 64
N_DP = 16


def draw_kept_index(key, part):
    key = jax.random.fold_in(key, 11)
    quarter = SLOT // SMALL_PER
    quarter_count = MICRO * TOKENS // quarter
    key_list = jax.random.split(key, quarter_count)

    def pick_half(one_key):
        order = jax.random.permutation(one_key, quarter)
        return jnp.sort(order[:quarter // 2])
    chosen = jax.vmap(pick_half)(key_list)
    offsets = jnp.arange(quarter_count, dtype=jnp.int32) % SMALL_PER * quarter
    return (chosen + offsets[:, None]).astype(jnp.int32).reshape(MICRO, KEPT_ALL)


def plant(drawn, own_key, smallest, largest):
    extent = drawn.shape
    place = [jax.random.randint(jax.random.fold_in(own_key, axis), (), 0, extent[axis]) for axis in range(len(extent))]
    drawn = drawn.at[tuple(place)].set(smallest)
    longest = extent.index(max(extent))
    place[longest] = (place[longest] + 1) % extent[longest]
    return drawn.at[tuple(place)].set(largest)


def shard_levels(own_key, shape, cuts, smallest, largest):
    loudness, own = 1.0, jax.random.fold_in(own_key, 6)
    for dim, blocks in cuts:
        heights = jnp.exp(jax.random.uniform(jax.random.fold_in(own, dim), (blocks,), jnp.float32, smallest / len(cuts), largest / len(cuts)))
        loudness = loudness * jnp.repeat(heights, shape[dim] // blocks).reshape([-1 if axis == dim else 1 for axis in range(len(shape))])
    return loudness


def gaussian(stream_key, dims, deviation, bound, shards=(), held_as=jnp.bfloat16):
    values = jax.random.normal(stream_key, dims, jnp.float32) * deviation
    if len(shards) > 0:
        values = shard_levels(stream_key, dims, shards, -0.22, 0.18) * values
    return jnp.clip(values, min=-bound, max=bound).astype(held_as)


def setup_inputs(seed: int = 0) -> dict:
    keys = jax.random.split(jax.random.key(seed), 16)
    return {
        "tokens": gaussian(keys[0], (MICRO, TOKENS, D), 1.0, 6.0, ((1, 16),)),
        "kept_index": draw_kept_index(jax.random.fold_in(keys[15], 71), 0),
        "big_image": plant(jax.random.randint(keys[2], (MICRO, N_DP), 0, 2), jax.random.fold_in(keys[2], 1), 0, 1).astype(jnp.int32),
        "timesteps": plant(jax.random.randint(keys[3], (MICRO, IMAGE_SLOTS), 0, 1000), jax.random.fold_in(keys[3], 1), 0, 999).astype(jnp.int32),
        "labels": plant(jax.random.randint(keys[4], (MICRO, IMAGE_SLOTS), 0, NCLS), jax.random.fold_in(keys[4], 1), 0, NCLS - 1).astype(jnp.int32),
        "cotangent": gaussian(keys[5], (MICRO, TOKENS, D), 1.0, 6.0, ((1, 16),)),
        "mask_token": gaussian(keys[6], (D,), 1.0, 6.0),
        "time_weight": gaussian(keys[7], (FREQ, D), FREQ ** -0.5, 0.375),
        "class_table": gaussian(keys[8], (NCLS, D), 1.0, 6.0),
        "ada_weight": gaussian(keys[9], (2, D, 6 * D), D ** -0.5, 0.1875, ((0, 2), (1, 16))),
        "ada_bias": gaussian(keys[10], (2, 6 * D), 0.5, 3.0, ((0, 2), (1, 16))),
        "qkv_weight": gaussian(keys[11], (2, D, 3 * D), D ** -0.5, 0.1875, ((0, 2), (1, 16))),
        "proj_weight": gaussian(keys[12], (2, D, D), (max(D // 128, 1)) ** -0.5, 2.0, ((0, 2), (1, 16))),
        "up_weight": gaussian(keys[13], (2, D, FF), D ** -0.5, 0.1875, ((0, 2), (1, 16))),
        "down_weight": gaussian(keys[14], (2, FF, D), FF ** -0.5, 0.09375, ((0, 2), (1, 16))),
    }


@jax.custom_vjp
def low(v):
    return lax.optimization_barrier(v.astype(jnp.bfloat16)).astype(jnp.float32)

@jax.custom_vjp
def low_back(v):
    return v

def low_keep(v):
    return (low(v), None)

def low_pass(kept, grad):
    return (grad,)

def back_keep(v):
    return (v, None)

def back_low(kept, grad):
    return (low(grad),)
low.defvjp(low_keep, low_pass)
low_back.defvjp(back_keep, back_low)

def matmul(left_side, right_side):
    return jnp.dot(left_side, right_side, precision=lax.Precision.HIGHEST)

def pre_norm(token_row_matrix, shift_rows, scale_rows):
    centred = token_row_matrix - lax.optimization_barrier(jnp.mean(token_row_matrix, axis=-1, keepdims=True))
    variance = lax.optimization_barrier(jnp.mean(centred * centred, axis=-1, keepdims=True))
    return centred * lax.rsqrt(variance + 1e-06) * (1.0 + scale_rows) + shift_rows

def softmax_rows(scores):
    highest = lax.optimization_barrier(jnp.max(scores, axis=-1, keepdims=True))
    exp_scores = jnp.exp(scores - highest)
    return exp_scores / lax.optimization_barrier(jnp.sum(exp_scores, axis=-1, keepdims=True))

def transformer_block(token_row_matrix, segment_index, condition_vector, modulation_weight_whole, bias_whole, query_key_value_whole, projection_whole, up_weight_whole, down_weight_whole):
    row_count = token_row_matrix.shape[0]
    lifted = low(jax.nn.silu(condition_vector))
    modulation = matmul(lifted, modulation_weight_whole) + bias_whole
    pieces = jnp.split(jnp.take(modulation, segment_index, axis=0), 6, axis=-1)
    first_in = low(pre_norm(token_row_matrix, pieces[0], pieces[1]))
    qkv_rows = low_back(low(matmul(first_in, query_key_value_whole)))
    query_part = qkv_rows[:, :D].reshape(row_count, HEADS, HD)
    key_part = qkv_rows[:, D:2 * D].reshape(row_count, HEADS, HD)
    value_part = qkv_rows[:, 2 * D:].reshape(row_count, HEADS, HD)
    raw_scores = jnp.einsum('qhd,khd->hqk', query_part, key_part, precision=lax.Precision.HIGHEST) * HD ** (-0.5)
    allowed = segment_index[:, None] == segment_index[None, :]
    scores = low_back(jnp.where(allowed[None], raw_scores, -1e+30))
    prob_rows = softmax_rows(scores)
    attended = jnp.einsum('hqk,khd->qhd', low(prob_rows), value_part, precision=lax.Precision.HIGHEST)
    attended = low_back(low(attended.reshape(row_count, D)))
    middle_rows = token_row_matrix + pieces[2] * low_back(matmul(attended, projection_whole))
    second_in = low(pre_norm(middle_rows, pieces[3], pieces[4]))
    hidden = low_back(matmul(second_in, up_weight_whole))
    active = low(jax.nn.gelu(hidden, approximate=True))
    return middle_rows + pieces[5] * low_back(matmul(active, down_weight_whole))

def conditioning(time_ids, label_ids, time_full, table_full):
    halfway = FREQ // 2
    frequencies = jnp.exp(-math.log(10000.0) * jnp.arange(halfway, dtype=jnp.float32) / halfway)
    angles = time_ids.astype(jnp.float32)[:, None] * frequencies[None, :]
    embedding = jnp.concatenate([jnp.cos(angles), jnp.sin(angles)], axis=-1)
    return matmul(low(embedding), time_full) + jnp.take(table_full, label_ids, axis=0)

def reference(tokens, kept_index, big_image, timesteps, labels, cotangent, mask_token, time_weight, class_table, ada_weight, ada_bias, qkv_weight, proj_weight, up_weight, down_weight):
    params = tuple((item.astype(jnp.float32) for item in (mask_token, time_weight, class_table, ada_weight, ada_bias, qkv_weight, proj_weight, up_weight, down_weight)))
    slot_count = MICRO * N_DP
    inputs = (tokens.reshape(slot_count, SLOT, D), kept_index.reshape(slot_count, KEPT).astype(jnp.int32), big_image.reshape(slot_count).astype(jnp.int32), timesteps.reshape(slot_count, SMALL_PER), labels.reshape(slot_count, SMALL_PER).astype(jnp.int32), cotangent.reshape(slot_count, SLOT, D))
    positions = jnp.arange(SLOT, dtype=jnp.int32)

    def one_slot(running, slot_inputs):
        token_slot, retained_row, big_flag, time_ids, label_ids, cot_slot = slot_inputs
        segment_whole = jnp.where(big_flag > 0, 0, positions // (SLOT // SMALL_PER)).astype(jnp.int32)
        segment_retained = jnp.take(segment_whole, retained_row, axis=0)

        def forward(token_values_float, mask_full, time_full, table_full, modulation_weight_stack, bias_stack, query_key_value_stack, projection_stack, up_weight_stack, down_weight_stack):
            condition_vector = conditioning(time_ids, label_ids, time_full, table_full)
            encoder_output = transformer_block(jnp.take(token_values_float, retained_row, axis=0), segment_retained, condition_vector, modulation_weight_stack[0], bias_stack[0], query_key_value_stack[0], projection_stack[0], up_weight_stack[0], down_weight_stack[0])
            encoder_output = low_back(low(encoder_output))
            kept_flags = jnp.zeros((SLOT,), jnp.float32).at[retained_row].set(1.0)
            decoder_input = jnp.zeros((SLOT, D), jnp.float32).at[retained_row].set(encoder_output) + (1.0 - kept_flags)[:, None] * mask_full[None, :]
            return transformer_block(decoder_input, segment_whole, condition_vector, modulation_weight_stack[1], bias_stack[1], query_key_value_stack[1], projection_stack[1], up_weight_stack[1], down_weight_stack[1])
        output, pull_back = jax.vjp(forward, token_slot.astype(jnp.float32), *params)
        gradients = pull_back(cot_slot.astype(jnp.float32))
        updated = tuple((before + after for before, after in zip(running, gradients[1:])))
        return (updated, (output.astype(jnp.bfloat16), gradients[0].astype(jnp.bfloat16)))
    start = tuple((jnp.zeros_like(item) for item in params))
    totals, (outputs, token_grads) = lax.scan(one_slot, start, inputs)
    return (outputs.reshape(MICRO, TOKENS, D), token_grads.reshape(MICRO, TOKENS, D), totals[0], totals[1], totals[2], totals[3], totals[4], totals[5], totals[6], totals[7], totals[8])
```

```python
import functools
import math

import jax
import jax.numpy as jnp
from jax import lax
from jax.experimental import pallas as pl
from jax.experimental.pallas import tpu as pltpu
from jax.sharding import PartitionSpec as P

HEADS = 16
HD = 72
SMALL_PER = 4
ATT_ROWS = 256
EPS = 1e-6
MASKED = -1e30
MESH = pl.DeviceIdType.MESH
F32 = jnp.float32
BF16 = jnp.bfloat16


def remote(src, dst, send_sem, recv_sem, target):
    return pltpu.make_async_remote_copy(
        src_ref=src,
        dst_ref=dst,
        send_sem=send_sem,
        recv_sem=recv_sem,
        device_id=target,
        device_id_type=MESH,
    )


def when(condition, run):
    pl.when(condition)(run)


def position():
    me = lax.axis_index("dp")
    return me // 4, (me // 2) % 2, me % 2


def at(line, pair, core):
    return {"dp": (line * 2 + pair) * 2 + core}


def greet(length, a, b, c):
    has_up, has_down = a < length - 1, a > 0
    barrier = pltpu.get_barrier_semaphore()

    def tell(target):
        pl.semaphore_signal(barrier, inc=1, device_id=target, device_id_type=MESH)

    tell(at(a, 1 - b, c))
    tell(at(a, b, 1 - c))
    when(has_up, lambda: tell(at(a + 1, b, c)))
    when(has_down, lambda: tell(at(a - 1, b, c)))
    pl.semaphore_wait(barrier, 2 + has_up.astype(jnp.int32) + has_down.astype(jnp.int32))
    return has_up, has_down


def piece(ref, lead, plan_entry):
    _, low, size, _ = plan_entry
    if size == 0:
        return ref.at[lead + (low,)]
    return ref.at[lead + (slice(None), pl.ds(low, size))]


def gather_kernel(length, plan, count, *refs):
    sources = refs[:count]
    outs = refs[count : 2 * count]
    up_s, up_r, down_s, down_r, pair_s, pair_r, core_s, core_r, own_sem = refs[2 * count :]
    a, b, c = position()
    has_up, has_down = greet(length, a, b, c)
    chunks = range(len(plan))
    line_first = [plan[i][3] == "line" for i in chunks]

    def slot(i, aa, bb, cc):
        return piece(outs[plan[i][0]], (aa, bb, cc), plan[i])

    def own(i):
        return piece(sources[plan[i][0]], (), plan[i])

    def rows_of(i):
        return (b,) if line_first[i] else (b, 1 - b)

    def up(i, k, bb, src=None):
        s = slot(i, a - k, bb, c)
        return remote(s if src is None else src, s, up_s.at[i, k, bb], up_r.at[i, k, bb], at(a + 1, b, c))

    def up_arrival(i, k, bb):
        s = slot(i, a - 1 - k, bb, c)
        return remote(s, s, up_s.at[i, k, bb], up_r.at[i, k, bb], at(a + 1, b, c))

    def down(i, k, bb, src=None):
        s = slot(i, a + k, bb, c)
        return remote(s if src is None else src, s, down_s.at[i, k, bb], down_r.at[i, k, bb], at(a - 1, b, c))

    def down_arrival(i, k, bb):
        s = slot(i, a + 1 + k, bb, c)
        return remote(s, s, down_s.at[i, k, bb], down_r.at[i, k, bb], at(a - 1, b, c))

    def across(i, aa, src=None):
        s = slot(i, aa, b, c)
        return remote(s if src is None else src, s, pair_s.at[i, aa], pair_r.at[i, aa], at(a, 1 - b, c))

    def across_arrival(i, aa):
        s = slot(i, aa, 1 - b, c)
        return remote(s, s, pair_s.at[i, aa], pair_r.at[i, aa], at(a, 1 - b, c))

    def to_core(i, aa, bb, src=None):
        s = slot(i, aa, bb, c)
        return remote(s if src is None else src, s, core_s.at[i, aa, bb], core_r.at[i, aa, bb], at(a, b, 1 - c))

    def core_arrival(i, aa, bb):
        s = slot(i, aa, bb, 1 - c)
        return remote(s, s, core_s.at[i, aa, bb], core_r.at[i, aa, bb], at(a, b, 1 - c))

    def after_across(i, aa):
        across_arrival(i, aa).wait_recv()
        to_core(i, aa, 1 - b).start()

    for i in chunks:
        src = own(i)
        pltpu.make_async_copy(src, slot(i, a, b, c), own_sem.at[i]).start()
        across(i, a, src).start()
        when(has_up, lambda: up(i, 0, b, src).start())
        when(has_down, lambda: down(i, 0, b, src).start())
        to_core(i, a, b, src).start()
    for i in chunks:
        if not line_first[i]:
            across_arrival(i, a).wait_recv()
            when(has_up, lambda: up(i, 0, 1 - b).start())
            when(has_down, lambda: down(i, 0, 1 - b).start())
            to_core(i, a, 1 - b).start()
    for k in range(1, length):
        for i in chunks:
            for bb in rows_of(i):

                def from_below():
                    up_arrival(i, k - 1, bb).wait_recv()
                    when(has_up, lambda: up(i, k, bb).start())
                    if line_first[i]:
                        across(i, a - k).start()
                    to_core(i, a - k, bb).start()

                def from_above():
                    down_arrival(i, k - 1, bb).wait_recv()
                    when(has_down, lambda: down(i, k, bb).start())
                    if line_first[i]:
                        across(i, a + k).start()
                    to_core(i, a + k, bb).start()

                when(a - k >= 0, from_below)
                when(a + k <= length - 1, from_above)
            if line_first[i]:
                if k == 1:
                    after_across(i, a)
                else:
                    when(a - k + 1 >= 0, lambda: after_across(i, a - k + 1))
                    when(a + k - 1 <= length - 1, lambda: after_across(i, a + k - 1))
    for i in chunks:
        if line_first[i]:
            k = length - 1
            when(a - k >= 0, lambda: after_across(i, a - k))
            when(a + k <= length - 1, lambda: after_across(i, a + k))
    for i in chunks:
        pltpu.make_async_copy(own(i), slot(i, a, b, c), own_sem.at[i]).wait()
        for aa in range(length):
            for bb in range(2):
                core_arrival(i, aa, bb).wait_recv()
                to_core(i, aa, bb).wait_send()
            if line_first[i]:
                across(i, aa).wait_send()
        if not line_first[i]:
            across(i, a).wait_send()
        for k in range(length - 1):
            for bb in rows_of(i):
                when(jnp.logical_and(has_up, a - k >= 0), lambda: up(i, k, bb).wait_send())
                when(
                    jnp.logical_and(has_down, a + k <= length - 1),
                    lambda: down(i, k, bb).wait_send(),
                )


def gather_all(shards, plan, length):
    count, n = len(shards), len(plan)
    dma = pltpu.SemaphoreType.DMA
    anywhere = [pl.BlockSpec(memory_space=pl.ANY)] * count
    return pl.pallas_call(
        functools.partial(gather_kernel, length, plan, count),
        out_shape=tuple(jax.ShapeDtypeStruct((length, 2, 2) + s.shape, s.dtype) for s in shards),
        in_specs=anywhere,
        out_specs=anywhere,
        scratch_shapes=[dma((n, length, 2))] * 4
        + [dma((n, length))] * 2
        + [dma((n, length, 2))] * 2
        + [dma((n,))],
        compiler_params=pltpu.CompilerParams(collective_id=0, has_side_effects=True),
        name="gather_weights",
    )(*shards)


def scatter_kernel(length, plan, count, slots, *refs):
    grads = refs[:count]
    outs = refs[count : 2 * count]
    (held, core_in, pair_in, up_in, down_in) = refs[2 * count : 2 * count + 5]
    (
        core_s, core_r, load_sem, pair_s, pair_r, up_s, up_r, down_s, down_r, out_sem, credit,
    ) = refs[2 * count + 5 :]
    a, b, c = position()
    greet(length, a, b, c)
    n = len(plan)
    pair_first = [plan[i][3] == "pair" for i in range(n)]
    base, total = [], 0
    for i in range(n):
        base.append(total)
        total += (length - 1) * (1 if pair_first[i] else 2)

    def chunk_of(i, cc):
        w, low, size, _ = plan[i]
        if size == 0:
            return grads[w].at[:, :, cc, low]
        return grads[w].at[:, :, cc, :, pl.ds(low, size)]

    def to_core(i):
        return remote(chunk_of(i, 1 - c), core_in.at[i % slots], core_s.at[i], core_r.at[i], at(a, b, 1 - c))

    def load(i):
        return pltpu.make_async_copy(chunk_of(i, c), held.at[i], load_sem.at[i])

    def across(i):
        if pair_first[i]:
            return remote(held.at[i, :, 1 - b], pair_in.at[i], pair_s.at[i], pair_r.at[i], at(a, 1 - b, c))
        return remote(
            held.at[i, a, 1 - b], pair_in.at[i, 0], pair_s.at[i], pair_r.at[i], at(a, 1 - b, c)
        )

    def rows_of(i):
        return (b,) if pair_first[i] else (b, 1 - b)

    def flow_index(i, dest, bb):
        if pair_first[i]:
            return base[i] + dest
        return base[i] + dest * 2 + bb

    def up(i, line, dest, bb):
        x = flow_index(i, dest - 1, bb)
        return remote(held.at[i, dest, bb], up_in.at[x], up_s.at[x], up_r.at[x], at(line + 1, b, c))

    def down(i, line, dest, bb):
        x = flow_index(i, dest, bb)
        return remote(held.at[i, dest, bb], down_in.at[x], down_s.at[x], down_r.at[x], at(line - 1, b, c))

    def add(dst, src):
        dst[...] = dst[...] + src[...]

    def first_add(i):
        to_core(i).wait_recv()
        load(i).wait()

        def body(s, carry):
            add(held.at[i, s // 2, s % 2], core_in.at[i % slots, s // 2, s % 2])
            return carry

        lax.fori_loop(0, 2 * length, body, 0)
        if i + slots < n:
            pl.semaphore_signal(credit, inc=1, device_id=at(a, b, 1 - c), device_id_type=MESH)
        if pair_first[i]:
            across(i).start()

    def second_add(i):
        if not pair_first[i]:
            return
        across(i).wait_recv()

        def body(s, carry):
            add(held.at[i, s, b], pair_in.at[i, s])
            return carry

        lax.fori_loop(0, length, body, 0)

    def line_step(i, j):
        def going_up():
            for dest in range(length - 1, j - 1, -1):
                for bb in rows_of(i):
                    if j > 0:
                        up(i, j - 1, dest, bb).wait_recv()
                        add(held.at[i, dest, bb], up_in.at[flow_index(i, dest - 1, bb)])
                    if dest > j:
                        up(i, j, dest, bb).start()

        def going_down():
            here = length - 1 - j
            for dest in range(0, here + 1):
                for bb in rows_of(i):
                    if j > 0:
                        down(i, here + 1, dest, bb).wait_recv()
                        add(held.at[i, dest, bb], down_in.at[flow_index(i, dest, bb)])
                    if dest < here:
                        down(i, here, dest, bb).start()

        when(a == j, going_up)
        when(a == length - 1 - j, going_down)

    def result(i):
        w, low, size, _ = plan[i]
        dst = outs[w].at[low] if size == 0 else outs[w].at[:, pl.ds(low, size)]
        return pltpu.make_async_copy(held.at[i, a, b], dst, out_sem.at[i])

    def finish(i):
        if pair_first[i]:
            result(i).start()
        else:
            across(i).start()

    def finish_late(i):
        if not pair_first[i]:
            across(i).wait_recv()
            add(held.at[i, a, b], pair_in.at[i, 0])
            result(i).start()

    for i in range(n):
        load(i).start()
        if i < slots:
            to_core(i).start()
    for t in range(n + length + 3):
        if t < n:
            first_add(t)
            if t + slots < n:
                pl.semaphore_wait(credit, 1)
                to_core(t + slots).start()
        if 0 <= t - 1 < n:
            second_add(t - 1)
        for j in range(length):
            if 0 <= t - 2 - j < n:
                line_step(t - 2 - j, j)
        if 0 <= t - 1 - length < n:
            finish(t - 1 - length)
        if 0 <= t - 2 - length < n:
            finish_late(t - 2 - length)
    for i in range(n):
        to_core(i).wait_send()
        across(i).wait_send()
        result(i).wait()
        for bb in rows_of(i):
            for here in range(length):

                def sent():
                    for dest in range(here + 1, length):
                        up(i, here, dest, bb).wait_send()
                    for dest in range(0, here):
                        down(i, here, dest, bb).wait_send()

                when(a == here, sent)


def scatter_all(grads, plan, length):
    count, n = len(grads), len(plan)
    slots = 3
    rows = grads[0].shape[3]
    width = plan[0][2]
    dtype = grads[0].dtype
    flows = sum((length - 1) * (1 if p[3] == "pair" else 2) for p in plan)
    dma = pltpu.SemaphoreType.DMA
    anywhere = [pl.BlockSpec(memory_space=pl.ANY)] * count
    slab = (rows, width)
    return pl.pallas_call(
        functools.partial(scatter_kernel, length, plan, count, slots),
        out_shape=tuple(jax.ShapeDtypeStruct(g.shape[3:], dtype) for g in grads),
        in_specs=anywhere,
        out_specs=anywhere,
        scratch_shapes=[
            pltpu.VMEM((n, length, 2) + slab, dtype),
            pltpu.VMEM((slots, length, 2) + slab, dtype),
            pltpu.VMEM((n, length) + slab, dtype),
            pltpu.VMEM((flows,) + slab, dtype),
            pltpu.VMEM((flows,) + slab, dtype),
            dma((n,)), dma((n,)), dma((n,)), dma((n,)), dma((n,)),
            dma((flows,)), dma((flows,)), dma((flows,)), dma((flows,)), dma((n,)),
            pltpu.SemaphoreType.REGULAR,
        ],
        compiler_params=pltpu.CompilerParams(
            collective_id=1, has_side_effects=True, vmem_limit_bytes=60 * 1024 * 1024
        ),
        name="scatter_grads",
    )(*grads)


def head_window(h):
    low, high = h * HD, h * HD + HD
    start = low // 128 * 128
    return low, high, start, -(-high // 128) * 128


def contract(x, y, dims):
    return lax.dot_general(x, y, ((dims[0], dims[1]), ((), ())), preferred_element_type=F32)


def head_operands(qkv_ref, h):
    width = qkv_ref.shape[1] // 3
    low, high, start, stop = head_window(h)
    lane = lax.broadcasted_iota(jnp.int32, (1, stop - start), 1) + start
    inside = jnp.logical_and(lane >= low, lane < high)
    parts = [qkv_ref[:, j * width + start : j * width + stop] for j in range(3)]
    return inside, slice(start, stop), parts


def only(inside, x):
    return jnp.where(inside, x, jnp.zeros_like(x))


def softmax_of(query, key, allowed):
    scores = jnp.where(allowed, contract(query, key, ((1,), (1,))) * HD**-0.5, MASKED)
    weights = jnp.exp(scores - jnp.max(scores, axis=-1, keepdims=True))
    return weights * (1.0 / jnp.sum(weights, axis=-1, keepdims=True))


def attend_kernel(qkv_ref, row_ref, column_ref, out_ref, total):
    allowed = row_ref[...] == column_ref[0]
    total[...] = jnp.zeros_like(total)
    for h in range(HEADS):
        inside, window, (query, key, value) = head_operands(qkv_ref, h)
        probs = softmax_of(only(inside, query), key, allowed).astype(BF16)
        mixed = contract(probs, value, ((1,), (0,)))
        total[:, window] += only(inside, mixed)
    out_ref[...] = total[...].astype(BF16)


def attend_back_kernel(qkv_ref, grad_ref, row_ref, column_ref, out_ref, total):
    allowed = row_ref[...] == column_ref[0]
    width = grad_ref.shape[1]
    total[...] = jnp.zeros_like(total)
    for h in range(HEADS):
        inside, window, (query, key, value) = head_operands(qkv_ref, h)
        query, key = only(inside, query), only(inside, key)
        grad = only(inside, grad_ref[:, window])
        probs = softmax_of(query, key, allowed)
        grad_probs = contract(grad, value, ((1,), (1,)))
        centre = jnp.sum(probs * grad_probs, axis=-1, keepdims=True)
        grad_scores = (probs * (grad_probs - centre)).astype(BF16)
        start, stop = window.start, window.stop
        total[:, start:stop] += contract(grad_scores, key, ((1,), (0,))) * HD**-0.5
        total[:, width + start : width + stop] += contract(grad_scores, query, ((0,), (0,))) * HD**-0.5
        total[:, 2 * width + start : 2 * width + stop] += contract(probs.astype(BF16), grad, ((0,), (0,)))
    out_ref[...] = total[...].astype(BF16)


def attention_call(kernel, operands, segments, out_width, matmuls):
    rows = operands[0].shape[0]
    blocks = rows // ATT_ROWS
    row_ids = segments.reshape(rows, 1)
    column_ids = segments.reshape(blocks, 1, ATT_ROWS)
    wide = lambda n: pl.BlockSpec((ATT_ROWS, n), lambda i: (i, 0))
    return pl.pallas_call(
        kernel,
        grid=(blocks,),
        out_shape=jax.ShapeDtypeStruct((rows, out_width), BF16),
        in_specs=[wide(x.shape[1]) for x in operands]
        + [wide(1), pl.BlockSpec((1, 1, ATT_ROWS), lambda i: (i, 0, 0))],
        out_specs=wide(out_width),
        scratch_shapes=[pltpu.VMEM((ATT_ROWS, out_width), F32)],
        compiler_params=pltpu.CompilerParams(vmem_limit_bytes=32 * 1024 * 1024),
        cost_estimate=pl.CostEstimate(
            flops=matmuls * blocks * HEADS * 2 * ATT_ROWS**3,
            bytes_accessed=2 * rows * (out_width + sum(x.shape[1] for x in operands)),
            transcendentals=blocks * HEADS * ATT_ROWS**2,
        ),
    )(*operands, row_ids, column_ids)


def dot(x, y):
    return jnp.dot(x, y, preferred_element_type=F32)


def dot_back(x, y):
    return lax.dot_general(x, y, (((1,), (1,)), ((), ())), preferred_element_type=F32)


def dot_rows(x, y):
    return lax.dot_general(x, y, (((0,), (0,)), ((), ())), preferred_element_type=F32)


def flat(x):
    return x.reshape(-1, x.shape[-1])


def normal(x):
    centred = x - jnp.mean(x, axis=-1, keepdims=True)
    scale = lax.rsqrt(jnp.mean(centred * centred, axis=-1, keepdims=True) + EPS)
    return centred * scale, scale


def pieces_of(modulation):
    return [p[:, None, :] for p in jnp.split(modulation, 6, axis=-1)]


def block_forward(x, segments, modulation, weights):
    qkv_weight, proj_weight, up_weight, down_weight = weights
    shape, width = x.shape, x.shape[-1]
    shift1, scale1, gate1, shift2, scale2, gate2 = pieces_of(modulation)
    first_in = flat((normal(x)[0] * (1.0 + scale1) + shift1).astype(BF16))
    qkv = dot(first_in, qkv_weight).astype(BF16)
    attended = attention_call(attend_kernel, (qkv,), segments, width, 2)
    branch = dot(attended, proj_weight).reshape(shape)
    middle = x + gate1 * branch
    second_in = flat((normal(middle)[0] * (1.0 + scale2) + shift2).astype(BF16))
    hidden = dot(second_in, up_weight)
    active = jax.nn.gelu(hidden, approximate=True).astype(BF16)
    mlp = dot(active, down_weight).reshape(shape)
    output = middle + gate2 * mlp
    return output, (first_in, qkv, attended, branch, middle, second_in, hidden, active, mlp)


def norm_back(grad, x, scale):
    hat, inverse = normal(x)
    inner = grad * (1.0 + scale)
    along = jnp.mean(inner * hat, axis=-1, keepdims=True)
    grad_x = inverse * (inner - jnp.mean(inner, axis=-1, keepdims=True) - hat * along)
    return grad_x, jnp.sum(grad, axis=1), jnp.sum(grad * hat, axis=1)


def block_backward(x, segments, modulation, weights, kept, grad_out):
    qkv_weight, proj_weight, up_weight, down_weight = weights
    first_in, qkv, attended, branch, middle, second_in, hidden, active, mlp = kept
    shape, width = x.shape, x.shape[-1]
    shift1, scale1, gate1, shift2, scale2, gate2 = pieces_of(modulation)
    grad_mlp = flat((gate2 * grad_out).astype(BF16))
    grad_gate2 = jnp.sum(grad_out * mlp, axis=1)
    _, pull = jax.vjp(lambda h: jax.nn.gelu(h, approximate=True), hidden)
    grad_hidden = pull(dot_back(grad_mlp, down_weight))[0].astype(BF16)
    down_grad = dot_rows(active, grad_mlp).astype(BF16)
    grad_second = dot_back(grad_hidden, up_weight).reshape(shape)
    up_grad = dot_rows(second_in, grad_hidden).astype(BF16)
    grad_middle, grad_shift2, grad_scale2 = norm_back(grad_second, middle, scale2)
    grad_middle = grad_middle + grad_out
    grad_gate1 = jnp.sum(grad_middle * branch, axis=1)
    grad_branch = flat((gate1 * grad_middle).astype(BF16))
    grad_attended = dot_back(grad_branch, proj_weight).astype(BF16)
    proj_grad = dot_rows(attended, grad_branch).astype(BF16)
    grad_qkv = attention_call(attend_back_kernel, (qkv, grad_attended), segments, 3 * width, 5)
    grad_first = dot_back(grad_qkv, qkv_weight).reshape(shape)
    qkv_grad = dot_rows(first_in, grad_qkv).astype(BF16)
    grad_x, grad_shift1, grad_scale1 = norm_back(grad_first, x, scale1)
    grad_modulation = jnp.concatenate(
        [grad_shift1, grad_scale1, grad_gate1, grad_shift2, grad_scale2, grad_gate2], axis=-1
    )
    return grad_x + grad_middle, grad_modulation, (qkv_grad, proj_grad, up_grad, down_grad)


def plan_of(widths, lead, unit, other, last, names):
    plan = []
    for w, width in enumerate(widths):
        for low in range(0, width, unit):
            plan.append([w, low, unit, names[0]])
    for j in range(lead):
        plan.append([len(widths), j, 0, names[0]])
    chosen = range(len(plan) - other, len(plan)) if last else range(other)
    for j in chosen:
        plan[j][3] = names[1]
    return tuple(tuple(p) for p in plan)


def swap_sections(x):
    return lax.ppermute(x, "section", [(0, 1), (1, 0)])


def on_device(
    tokens, kept_index, big_image, timesteps, labels, cotangent, mask_token, time_weight, class_table,
    ada_weight, ada_bias, qkv_weight, proj_weight, up_weight, down_weight,
):
    section = lax.axis_index("section")
    me = lax.axis_index("dp")
    devices = lax.axis_size("dp")
    micro, slot, width = tokens.shape
    kept_count = kept_index.shape[1]
    own_width = ada_weight.shape[1]
    images = micro * SMALL_PER
    quarters = micro * SMALL_PER
    ada = ada_weight[0]

    ids = jnp.stack([timesteps, labels])
    ids = lax.all_gather(ids, "dp", axis=0)
    times = ids[:, 0].reshape(devices * images)
    classes = ids[:, 1].reshape(devices * images)
    half = time_weight.shape[0] // 2
    frequencies = jnp.exp(-math.log(10000.0) * jnp.arange(half, dtype=F32) / half)
    angles = times.astype(F32)[:, None] * frequencies[None, :]
    embedding = jnp.concatenate([jnp.cos(angles), jnp.sin(angles)], axis=-1).astype(BF16)
    onehot = (classes[:, None] == jnp.arange(class_table.shape[0])[None, :]).astype(BF16)
    cond = dot(embedding, time_weight) + dot(onehot, class_table)
    cond = lax.dynamic_slice_in_dim(cond, me * own_width, own_width, axis=1)
    lifted = jax.nn.silu(cond).astype(BF16)
    bias_width = ada_bias.shape[1]
    bias = lax.dynamic_update_slice_in_dim(
        jnp.zeros((1, 6 * width), F32), ada_bias.astype(F32), me * bias_width, axis=1
    )
    partial = (dot(lifted, ada) + bias).astype(BF16).reshape(devices, images, 6 * width)
    modulation = lax.psum_scatter(partial, "dp", scatter_dimension=0, tiled=False).astype(F32)

    shards = (qkv_weight[0], proj_weight[0], up_weight[0])
    lead = down_weight.shape[1] // qkv_weight.shape[1]
    down_shard = down_weight[0].reshape(lead, own_width, width)
    length = devices // 4
    widths = [s.shape[1] for s in shards]
    if length == 4:
        plan = plan_of(widths, lead, width, 2, True, ("line", "pair"))
        whole = gather_all(shards + (down_shard,), plan, length)
    else:
        whole = tuple(lax.all_gather(s, "dp", axis=0) for s in shards + (down_shard,))
    weights = tuple(w.reshape(-1, w.shape[-1]) for w in whole)

    big = big_image[:, :1] > 0
    modulation = modulation.reshape(micro, SMALL_PER, 6 * width)
    modulation = jnp.where(big[:, :, None], modulation[:, :1], modulation).reshape(quarters, 6 * width)
    quarter_ids = jnp.arange(quarters, dtype=jnp.int32).reshape(micro, SMALL_PER)
    segment_of = jnp.where(big, quarter_ids[:, :1], quarter_ids).reshape(quarters)
    positions = jnp.arange(slot, dtype=jnp.int32)
    placement = (positions[None, :, None] == kept_index[:, None, :]).astype(BF16)
    enc_segments = jnp.repeat(segment_of, kept_count // SMALL_PER)
    dec_segments = jnp.repeat(segment_of, slot // SMALL_PER)

    def to_kept(rows):
        return jnp.einsum("msk,msd->mkd", placement, rows, preferred_element_type=F32)

    def to_slots(rows):
        return jnp.einsum("msk,mkd->msd", placement, rows, preferred_element_type=F32)

    enc_rows = (quarters, kept_count // SMALL_PER, width)
    dec_rows = (quarters, slot // SMALL_PER, width)

    def encode():
        x = to_kept(tokens).reshape(enc_rows)
        out, kept = block_forward(x, enc_segments, modulation, weights)
        return out.astype(BF16), (x, kept)

    idle = lambda f: jax.tree.map(lambda s: jnp.zeros(s.shape, s.dtype), jax.eval_shape(f))
    encoded, enc_kept = lax.cond(section == 0, encode, lambda: idle(encode))
    received = swap_sections(encoded).reshape(micro, kept_count, width)

    def decode():
        flags = jnp.sum(placement.astype(F32), axis=2)[:, :, None]
        x = to_slots(received) + (1.0 - flags) * mask_token.astype(F32)[None, None, :]
        x = x.reshape(dec_rows)
        out, kept = block_forward(x, dec_segments, modulation, weights)
        grad = cotangent.astype(F32).reshape(dec_rows)
        grad_x, grad_mod, grads = block_backward(x, dec_segments, modulation, weights, kept, grad)
        grad_x = grad_x.reshape(micro, slot, width)
        mask_part = jnp.sum((1.0 - flags) * grad_x, axis=(0, 1))
        back = to_kept(grad_x.astype(BF16)).astype(BF16)
        return out.astype(BF16).reshape(micro, slot, width), mask_part, back, grad_mod, grads

    decoded, mask_part, back, grad_mod, grads = lax.cond(section == 1, decode, lambda: idle(decode))
    received = swap_sections(back)

    def encode_back():
        x, kept = enc_kept
        grad = received.astype(F32).reshape(enc_rows)
        grad_x, grad_mod, grads = block_backward(x, enc_segments, modulation, weights, kept, grad)
        grad_x = grad_x.astype(BF16).reshape(micro, kept_count, width)
        return to_slots(grad_x).astype(BF16), grad_mod, grads

    token_grad, grad_mod, grads = lax.cond(
        section == 0, encode_back, lambda: (jnp.zeros_like(decoded), grad_mod, grads)
    )

    half_width = width // 2
    outgoing = jnp.where(section == 0, token_grad[:, :, half_width:], decoded[:, :, :half_width])
    incoming = swap_sections(outgoing)
    decoded_half = jnp.where(section == 0, incoming, decoded[:, :, half_width:])
    token_half = jnp.where(section == 0, token_grad[:, :, :half_width], incoming)

    grad_mod = grad_mod.reshape(micro, SMALL_PER, 6 * width)
    first_only = (jnp.arange(SMALL_PER) == 0)[None, :, None]
    grad_mod = jnp.where(
        big[:, :, None], jnp.where(first_only, jnp.sum(grad_mod, axis=1, keepdims=True), 0.0), grad_mod
    )
    grad_mod = grad_mod.reshape(images, 6 * width).astype(BF16)
    every_mod = lax.all_gather(grad_mod, "dp", axis=0, tiled=True)
    ada_grad = dot_rows(lifted, every_mod)
    bias_grad = jnp.sum(
        lax.dynamic_slice_in_dim(every_mod, me * bias_width, bias_width, axis=1).astype(F32), axis=0
    )
    grad_lifted = dot_back(every_mod, ada)
    _, pull = jax.vjp(jax.nn.silu, cond)
    grad_cond = pull(grad_lifted)[0].astype(BF16)
    every_cond = lax.all_gather(grad_cond.T, ("section", "dp"), axis=0)
    every_cond = every_cond.reshape(2, width, devices * images)
    inputs = jnp.concatenate([embedding, onehot], axis=1)
    shared = lax.dot_general(
        jnp.concatenate([inputs, inputs], axis=0),
        jnp.concatenate([every_cond[0], every_cond[1]], axis=1),
        (((0,), (1,)), ((), ())),
        preferred_element_type=F32,
    )
    time_grad, table_grad = shared[: time_weight.shape[0]], shared[time_weight.shape[0] :]
    mask_grad = lax.psum(mask_part, ("section", "dp"))

    split = tuple(g.reshape((devices,) + s.shape) for g, s in zip(grads, shards + (down_shard,)))
    if length == 4:
        plan = plan_of(widths, lead, width, 2, False, ("pair", "line"))
        split = tuple(g.reshape((length, 2, 2) + g.shape[1:]) for g in split)
        mine = scatter_all(split, plan, length)
    else:
        mine = tuple(lax.psum_scatter(g, "dp", scatter_dimension=0) for g in split)
    qkv_grad, proj_grad, up_grad, down_grad = (g.astype(F32) for g in mine)
    return (
        decoded_half,
        token_half,
        mask_grad,
        time_grad,
        table_grad,
        ada_grad[None],
        bias_grad[None],
        qkv_grad[None],
        proj_grad[None],
        up_grad[None],
        down_grad.reshape(down_weight.shape),
    )


def solution(mesh):
    rows = P(None, "dp", None)
    ids = P(None, "dp")
    weight = P("section", "dp", None)
    halves = P(None, "dp", "section")
    in_specs = (rows, ids, ids, ids, ids, rows, P(), P(), P(), weight, P("section", "dp")) + (weight,) * 4
    out_specs = (halves, halves, P(), P(), P(), weight, P("section", "dp")) + (weight,) * 4
    return jax.shard_map(
        on_device, mesh=mesh, in_specs=in_specs, out_specs=out_specs, check_vma=False
    )
```

```python
import functools
import math

import jax
import jax.numpy as jnp
from jax import lax
from jax.experimental import pallas as pl
from jax.experimental.pallas import tpu as pltpu
from jax.sharding import PartitionSpec as P

HEADS = 16
HD = 72
SMALL_PER = 4
ATT_ROWS = 256
EPS = 1e-6
MASKED = -1e30
MESH = pl.DeviceIdType.MESH
F32 = jnp.float32
BF16 = jnp.bfloat16


def remote(src, dst, send_sem, recv_sem, target):
    return pltpu.make_async_remote_copy(
        src_ref=src,
        dst_ref=dst,
        send_sem=send_sem,
        recv_sem=recv_sem,
        device_id=target,
        device_id_type=MESH,
    )


def when(condition, run):
    pl.when(condition)(run)


def position():
    me = lax.axis_index("dp")
    return me // 4, (me // 2) % 2, me % 2


def at(line, pair, core):
    return {"dp": (line * 2 + pair) * 2 + core}


def greet(length, a, b, c):
    has_up, has_down = a < length - 1, a > 0
    barrier = pltpu.get_barrier_semaphore()

    def tell(target):
        pl.semaphore_signal(barrier, inc=1, device_id=target, device_id_type=MESH)

    tell(at(a, 1 - b, c))
    tell(at(a, b, 1 - c))
    when(has_up, lambda: tell(at(a + 1, b, c)))
    when(has_down, lambda: tell(at(a - 1, b, c)))
    pl.semaphore_wait(barrier, 2 + has_up.astype(jnp.int32) + has_down.astype(jnp.int32))
    return has_up, has_down


def piece(ref, lead, plan_entry):
    _, low, size, _ = plan_entry
    if size == 0:
        return ref.at[lead + (low,)]
    return ref.at[lead + (slice(None), pl.ds(low, size))]


def gather_kernel(length, plan, count, *refs):
    sources = refs[:count]
    outs = refs[count : 2 * count]
    up_s, up_r, down_s, down_r, pair_s, pair_r, core_s, core_r, own_sem = refs[2 * count :]
    a, b, c = position()
    has_up, has_down = greet(length, a, b, c)
    chunks = range(len(plan))
    line_first = [plan[i][3] == "line" for i in chunks]

    def slot(i, aa, bb, cc):
        return piece(outs[plan[i][0]], (aa, bb, cc), plan[i])

    def own(i):
        return piece(sources[plan[i][0]], (), plan[i])

    def rows_of(i):
        return (b,) if line_first[i] else (b, 1 - b)

    def up(i, k, bb, src=None):
        s = slot(i, a - k, bb, c)
        return remote(s if src is None else src, s, up_s.at[i, k, bb], up_r.at[i, k, bb], at(a + 1, b, c))

    def up_arrival(i, k, bb):
        s = slot(i, a - 1 - k, bb, c)
        return remote(s, s, up_s.at[i, k, bb], up_r.at[i, k, bb], at(a + 1, b, c))

    def down(i, k, bb, src=None):
        s = slot(i, a + k, bb, c)
        return remote(s if src is None else src, s, down_s.at[i, k, bb], down_r.at[i, k, bb], at(a - 1, b, c))

    def down_arrival(i, k, bb):
        s = slot(i, a + 1 + k, bb, c)
        return remote(s, s, down_s.at[i, k, bb], down_r.at[i, k, bb], at(a - 1, b, c))

    def across(i, aa, src=None):
        s = slot(i, aa, b, c)
        return remote(s if src is None else src, s, pair_s.at[i, aa], pair_r.at[i, aa], at(a, 1 - b, c))

    def across_arrival(i, aa):
        s = slot(i, aa, 1 - b, c)
        return remote(s, s, pair_s.at[i, aa], pair_r.at[i, aa], at(a, 1 - b, c))

    def to_core(i, aa, bb, src=None):
        s = slot(i, aa, bb, c)
        return remote(s if src is None else src, s, core_s.at[i, aa, bb], core_r.at[i, aa, bb], at(a, b, 1 - c))

    def core_arrival(i, aa, bb):
        s = slot(i, aa, bb, 1 - c)
        return remote(s, s, core_s.at[i, aa, bb], core_r.at[i, aa, bb], at(a, b, 1 - c))

    def after_across(i, aa):
        across_arrival(i, aa).wait_recv()
        to_core(i, aa, 1 - b).start()

    for i in chunks:
        src = own(i)
        pltpu.make_async_copy(src, slot(i, a, b, c), own_sem.at[i]).start()
        across(i, a, src).start()
        when(has_up, lambda: up(i, 0, b, src).start())
        when(has_down, lambda: down(i, 0, b, src).start())
        to_core(i, a, b, src).start()
    for i in chunks:
        if not line_first[i]:
            across_arrival(i, a).wait_recv()
            when(has_up, lambda: up(i, 0, 1 - b).start())
            when(has_down, lambda: down(i, 0, 1 - b).start())
            to_core(i, a, 1 - b).start()
    for k in range(1, length):
        for i in chunks:
            for bb in rows_of(i):

                def from_below():
                    up_arrival(i, k - 1, bb).wait_recv()
                    when(has_up, lambda: up(i, k, bb).start())
                    if line_first[i]:
                        across(i, a - k).start()
                    to_core(i, a - k, bb).start()

                def from_above():
                    down_arrival(i, k - 1, bb).wait_recv()
                    when(has_down, lambda: down(i, k, bb).start())
                    if line_first[i]:
                        across(i, a + k).start()
                    to_core(i, a + k, bb).start()

                when(a - k >= 0, from_below)
                when(a + k <= length - 1, from_above)
            if line_first[i]:
                if k == 1:
                    after_across(i, a)
                else:
                    when(a - k + 1 >= 0, lambda: after_across(i, a - k + 1))
                    when(a + k - 1 <= length - 1, lambda: after_across(i, a + k - 1))
    for i in chunks:
        if line_first[i]:
            k = length - 1
            when(a - k >= 0, lambda: after_across(i, a - k))
            when(a + k <= length - 1, lambda: after_across(i, a + k))
    for i in chunks:
        pltpu.make_async_copy(own(i), slot(i, a, b, c), own_sem.at[i]).wait()
        for aa in range(length):
            for bb in range(2):
                core_arrival(i, aa, bb).wait_recv()
                to_core(i, aa, bb).wait_send()
            if line_first[i]:
                across(i, aa).wait_send()
        if not line_first[i]:
            across(i, a).wait_send()
        for k in range(length - 1):
            for bb in rows_of(i):
                when(jnp.logical_and(has_up, a - k >= 0), lambda: up(i, k, bb).wait_send())
                when(
                    jnp.logical_and(has_down, a + k <= length - 1),
                    lambda: down(i, k, bb).wait_send(),
                )


def gather_all(shards, plan, length):
    count, n = len(shards), len(plan)
    dma = pltpu.SemaphoreType.DMA
    anywhere = [pl.BlockSpec(memory_space=pl.ANY)] * count
    return pl.pallas_call(
        functools.partial(gather_kernel, length, plan, count),
        out_shape=tuple(jax.ShapeDtypeStruct((length, 2, 2) + s.shape, s.dtype) for s in shards),
        in_specs=anywhere,
        out_specs=anywhere,
        scratch_shapes=[dma((n, length, 2))] * 4
        + [dma((n, length))] * 2
        + [dma((n, length, 2))] * 2
        + [dma((n,))],
        compiler_params=pltpu.CompilerParams(collective_id=0, has_side_effects=True),
        name="gather_weights",
    )(*shards)


def scatter_kernel(length, plan, slots, pair_slots, *refs):
    lefts, rights = refs[:4], refs[4:8]
    outs = refs[8:12]
    (
        raw, right, left_t, held, sent, core_in, pair_in, pair_late, up_in, down_in,
    ) = refs[12:22]
    (
        raw_sem, right_sem, core_s, core_r, pair_s, pair_r, up_s, up_r, down_s, down_r, out_sem,
        core_credit, pair_credit,
    ) = refs[22:]
    a, b, c = position()
    greet(length, a, b, c)
    n = len(plan)
    rows, width = held.shape[3:]
    total_rows = raw.shape[1]
    pair_first = [p[3] == "pair" for p in plan]
    order = [sum(pair_first[:i]) if pair_first[i] else i - sum(pair_first[:i]) for i in range(n)]
    base, total = [], 0
    for i in range(n):
        base.append(total)
        total += (length - 1) * (1 if pair_first[i] else 2)
    groups = 2 * length

    def blocks_of(w):
        return lefts[w].shape[1] // width

    raw_jobs = []
    right_jobs = []
    for i, (w, low, size, _) in enumerate(plan):
        if i == 0 or plan[i - 1][0] != w:
            raw_jobs += [(w, k) for k in range(blocks_of(w))]
        if size != 0 or plan[i - 1][0] != w:
            right_jobs.append(i)

    def raw_load(x):
        w, k = raw_jobs[x]
        src = lefts[w].at[:, pl.ds(k * width, width)]
        return pltpu.make_async_copy(src, raw.at[x % 2], raw_sem.at[x])

    def right_load(x):
        w, low, size, _ = plan[right_jobs[x]]
        src = rights[w].at[:, pl.ds(low if size else 0, width)]
        return pltpu.make_async_copy(src, right.at[x % 2], right_sem.at[x])

    progress = {"raw": 0, "right": -1}

    def turn(w):
        count = blocks_of(w)
        for k in range(count):
            x = progress["raw"]
            progress["raw"] += 1
            raw_load(x).wait()
            slot = x % 2

            def body(r, carry):
                start = pl.multiple_of(r * 128, 128)
                block = raw[slot, pl.ds(start, 128), :].astype(F32).T
                if count == 1:
                    split = block.reshape(groups, 2, rows, 128)
                    for q in range(2):
                        part = split[:, q].reshape(groups * rows, 128)
                        left_t[q, :, pl.ds(start, 128)] = part.astype(BF16)
                else:
                    near = groups // count
                    split = block.reshape(near, 2, count, rows, 128)
                    for q in range(2):
                        for j in range(count):
                            part = split[:, q, j].reshape(near * rows, 128)
                            left_t[
                                q * count + j, pl.ds(k * near * rows, near * rows), pl.ds(start, 128)
                            ] = part.astype(BF16)
                return carry

            lax.fori_loop(0, total_rows // 128, body, 0)
            if x + 2 < len(raw_jobs):
                raw_load(x + 2).start()

    def product(i, q, put):
        w, low, size, _ = plan[i]
        count = blocks_of(w)
        row_set = q if count == 1 else q * count + low
        slot = progress["right"] % 2
        tile = width // 3

        def body(k, carry):
            columns = pl.ds(pl.multiple_of(k * tile, 128), tile)
            result = jnp.dot(left_t[row_set], right[slot, :, columns], preferred_element_type=F32)
            for s in range(groups):
                put(s, columns, result[s * rows : (s + 1) * rows].astype(BF16))
            return carry

        lax.fori_loop(0, 3, body, 0)

    def to_core(i):
        return remote(sent.at[i % slots], core_in.at[i % slots], core_s.at[i], core_r.at[i], at(a, b, 1 - c))

    def across(i):
        target = at(a, 1 - b, c)
        if pair_first[i]:
            return remote(
                held.at[i, :, 1 - b], pair_in.at[order[i] % pair_slots], pair_s.at[i], pair_r.at[i], target
            )
        return remote(held.at[i, a, 1 - b], pair_late.at[order[i]], pair_s.at[i], pair_r.at[i], target)

    def rows_of(i):
        return (b,) if pair_first[i] else (b, 1 - b)

    def flow_index(i, dest, bb):
        if pair_first[i]:
            return base[i] + dest
        return base[i] + dest * 2 + bb

    def up(i, line, dest, bb):
        x = flow_index(i, dest - 1, bb)
        return remote(held.at[i, dest, bb], up_in.at[x], up_s.at[x], up_r.at[x], at(line + 1, b, c))

    def down(i, line, dest, bb):
        x = flow_index(i, dest, bb)
        return remote(held.at[i, dest, bb], down_in.at[x], down_s.at[x], down_r.at[x], at(line - 1, b, c))

    def add(dst, src):
        dst[...] = dst[...] + src[...]

    def credit(sem, target):
        pl.semaphore_signal(sem, inc=1, device_id=target, device_id_type=MESH)

    def produce(i):
        w = plan[i][0]
        if i == 0 or plan[i - 1][0] != w:
            turn(w)
        if progress["right"] + 1 < len(right_jobs) and right_jobs[progress["right"] + 1] == i:
            progress["right"] += 1
            right_load(progress["right"]).wait()
            if progress["right"] + 1 < len(right_jobs):
                right_load(progress["right"] + 1).start()
        if i >= slots:
            to_core(i - slots).wait_send()

        def put_sent(s, columns, value):
            sent[i % slots, s // 2, s % 2, :, columns] = value

        def put_held(s, columns, value):
            held[i, s // 2, s % 2, :, columns] = value

        product(i, 1 - c, put_sent)
        if i >= slots:
            pl.semaphore_wait(core_credit, 1)
        to_core(i).start()
        product(i, c, put_held)

    def first_add(i):
        to_core(i).wait_recv()

        def body(s, carry):
            add(held.at[i, s // 2, s % 2], core_in.at[i % slots, s // 2, s % 2])
            return carry

        lax.fori_loop(0, groups, body, 0)
        if i + slots < n:
            credit(core_credit, at(a, b, 1 - c))
        if pair_first[i]:
            if order[i] >= pair_slots:
                pl.semaphore_wait(pair_credit, 1)
            across(i).start()

    def second_add(i):
        if not pair_first[i]:
            return
        across(i).wait_recv()

        def body(s, carry):
            add(held.at[i, s, b], pair_in.at[order[i] % pair_slots, s])
            return carry

        lax.fori_loop(0, length, body, 0)
        if order[i] + pair_slots < sum(pair_first):
            credit(pair_credit, at(a, 1 - b, c))

    def line_step(i, j):
        def going_up():
            for dest in range(length - 1, j - 1, -1):
                for bb in rows_of(i):
                    if j > 0:
                        up(i, j - 1, dest, bb).wait_recv()
                        add(held.at[i, dest, bb], up_in.at[flow_index(i, dest - 1, bb)])
                    if dest > j:
                        up(i, j, dest, bb).start()

        def going_down():
            here = length - 1 - j
            for dest in range(0, here + 1):
                for bb in rows_of(i):
                    if j > 0:
                        down(i, here + 1, dest, bb).wait_recv()
                        add(held.at[i, dest, bb], down_in.at[flow_index(i, dest, bb)])
                    if dest < here:
                        down(i, here, dest, bb).start()

        when(a == j, going_up)
        when(a == length - 1 - j, going_down)

    def result(i):
        w, low, size, _ = plan[i]
        dst = outs[w].at[low] if size == 0 else outs[w].at[:, pl.ds(low, size)]
        return pltpu.make_async_copy(held.at[i, a, b], dst, out_sem.at[i])

    def finish(i):
        if pair_first[i]:
            result(i).start()
        else:
            across(i).start()

    def finish_late(i):
        if not pair_first[i]:
            across(i).wait_recv()
            add(held.at[i, a, b], pair_late.at[order[i]])
            result(i).start()

    raw_load(0).start()
    right_load(0).start()
    raw_load(1).start()
    produce(0)
    for t in range(n + length + 3):
        if t + 1 < n:
            produce(t + 1)
        if t < n:
            first_add(t)
        if 0 <= t - 1 < n:
            second_add(t - 1)
        for j in range(length):
            if 0 <= t - 2 - j < n:
                line_step(t - 2 - j, j)
        if 0 <= t - 1 - length < n:
            finish(t - 1 - length)
        if 0 <= t - 2 - length < n:
            finish_late(t - 2 - length)
    for i in range(n):
        if i >= n - slots:
            to_core(i).wait_send()
        across(i).wait_send()
        result(i).wait()
        for bb in rows_of(i):
            for here in range(length):

                def gone():
                    for dest in range(here + 1, length):
                        up(i, here, dest, bb).wait_send()
                    for dest in range(0, here):
                        down(i, here, dest, bb).wait_send()

                when(a == here, gone)


def scatter_all(lefts, rights, shard_shapes, plan, length):
    n = len(plan)
    slots, pair_slots = 2, 4
    total_rows = lefts[0].shape[0]
    rows, width = shard_shapes[0][0], plan[0][2]
    late = sum(p[3] != "pair" for p in plan)
    flows = (length - 1) * (n + late)
    lead = shard_shapes[-1][0]
    dma = pltpu.SemaphoreType.DMA
    anywhere = pl.BlockSpec(memory_space=pl.ANY)
    slab = (rows, width)
    return pl.pallas_call(
        functools.partial(scatter_kernel, length, plan, slots, pair_slots),
        out_shape=tuple(jax.ShapeDtypeStruct(s, BF16) for s in shard_shapes),
        in_specs=[anywhere] * 8,
        out_specs=[anywhere] * 4,
        scratch_shapes=[
            pltpu.VMEM((2, total_rows, width), BF16),
            pltpu.VMEM((2, total_rows, width), BF16),
            pltpu.VMEM((2 * lead, 2 * length * rows, total_rows), BF16),
            pltpu.VMEM((n, length, 2) + slab, BF16),
            pltpu.VMEM((slots, length, 2) + slab, BF16),
            pltpu.VMEM((slots, length, 2) + slab, BF16),
            pltpu.VMEM((pair_slots, length) + slab, BF16),
            pltpu.VMEM((late,) + slab, BF16),
            pltpu.VMEM((flows,) + slab, BF16),
            pltpu.VMEM((flows,) + slab, BF16),
            dma((lead + 3,)), dma((n,)), dma((n,)), dma((n,)), dma((n,)), dma((n,)),
            dma((flows,)), dma((flows,)), dma((flows,)), dma((flows,)), dma((n,)),
            pltpu.SemaphoreType.REGULAR, pltpu.SemaphoreType.REGULAR,
        ],
        compiler_params=pltpu.CompilerParams(
            collective_id=1, has_side_effects=True, vmem_limit_bytes=62 * 1024 * 1024
        ),
        name="scatter_grads",
    )(*lefts, *rights)


def small_gather_kernel(length, sum_sections, own_ref, out_ref, other, *sems):
    line_s, line_r, pair_s, pair_r, core_s, core_r, side_s, side_r = sems
    a, b, c = position()
    partner = {"section": 1 - lax.axis_index("section")}
    barrier = pltpu.get_barrier_semaphore()

    def tell(target):
        pl.semaphore_signal(barrier, inc=1, device_id=target, device_id_type=MESH)

    tell(at(a, 1 - b, c))
    tell(at(a, b, 1 - c))
    for k in range(1, length):
        tell(at(lax.rem(a + k, length), b, c))
    if sum_sections:
        tell(partner)
    pl.semaphore_wait(barrier, length + 1 + int(sum_sections))
    value = own_ref[...]
    if sum_sections:
        side = remote(own_ref, other, side_s, side_r, partner)
        side.start()
        side.wait()
        value = value + other[...]
    out_ref[a, b, c] = value
    mine = out_ref.at[a, b, c]
    copies = []
    for k in range(1, length):
        to = lax.rem(a + k, length)
        copy = remote(mine, mine, line_s.at[k - 1], line_r.at[k - 1], at(to, b, c))
        copy.start()
        copies.append(copy)
    for k in range(1, length):
        source = lax.rem(a + length - k, length)
        slab = out_ref.at[source, b, c]
        remote(slab, slab, line_s.at[k - 1], line_r.at[k - 1], at(a, 1 - b, c)).wait_recv()
        copies[k - 1].wait_send()
    for go, come, s, r, to in (
        (out_ref.at[:, b, c], out_ref.at[:, 1 - b, c], pair_s, pair_r, at(a, 1 - b, c)),
        (out_ref.at[:, :, c], out_ref.at[:, :, 1 - c], core_s, core_r, at(a, b, 1 - c)),
    ):
        copy = remote(go, go, s, r, to)
        copy.start()
        remote(come, come, s, r, to).wait_recv()
        copy.wait_send()


def small_gather(own, length, sum_sections, collective_id):
    dma = pltpu.SemaphoreType.DMA
    vmem = pl.BlockSpec(memory_space=pltpu.VMEM)
    shape = (length, 2, 2) + own.shape
    return pl.pallas_call(
        functools.partial(small_gather_kernel, length, sum_sections),
        out_shape=jax.ShapeDtypeStruct(shape, own.dtype),
        in_specs=[vmem],
        out_specs=vmem,
        scratch_shapes=[
            pltpu.VMEM(own.shape, own.dtype), dma((length - 1,)), dma((length - 1,)), dma, dma, dma, dma, dma, dma,
        ],
        compiler_params=pltpu.CompilerParams(collective_id=collective_id, has_side_effects=True),
        name="small_gather",
    )(own).reshape((4 * length,) + own.shape)


def head_window(h):
    low, high = h * HD, h * HD + HD
    start = low // 128 * 128
    return low, high, start, -(-high // 128) * 128


def contract(x, y, dims):
    return lax.dot_general(x, y, ((dims[0], dims[1]), ((), ())), preferred_element_type=F32)


def head_operands(qkv_ref, h):
    width = qkv_ref.shape[1] // 3
    low, high, start, stop = head_window(h)
    lane = lax.broadcasted_iota(jnp.int32, (1, stop - start), 1) + start
    inside = jnp.logical_and(lane >= low, lane < high)
    parts = [qkv_ref[:, j * width + start : j * width + stop] for j in range(3)]
    return inside, slice(start, stop), parts


def only(inside, x):
    return jnp.where(inside, x, jnp.zeros_like(x))


def softmax_of(query, key, allowed):
    scores = jnp.where(allowed, contract(query, key, ((1,), (1,))) * HD**-0.5, MASKED)
    weights = jnp.exp(scores - jnp.max(scores, axis=-1, keepdims=True))
    return weights * (1.0 / jnp.sum(weights, axis=-1, keepdims=True))


def attend_kernel(qkv_ref, row_ref, column_ref, out_ref, total):
    allowed = row_ref[...] == column_ref[0]
    total[...] = jnp.zeros_like(total)
    for h in range(HEADS):
        inside, window, (query, key, value) = head_operands(qkv_ref, h)
        probs = softmax_of(only(inside, query), key, allowed).astype(BF16)
        mixed = contract(probs, value, ((1,), (0,)))
        total[:, window] += only(inside, mixed)
    out_ref[...] = total[...].astype(BF16)


def attend_back_kernel(qkv_ref, grad_ref, row_ref, column_ref, out_ref, total):
    allowed = row_ref[...] == column_ref[0]
    width = grad_ref.shape[1]
    total[...] = jnp.zeros_like(total)
    for h in range(HEADS):
        inside, window, (query, key, value) = head_operands(qkv_ref, h)
        query, key = only(inside, query), only(inside, key)
        grad = only(inside, grad_ref[:, window])
        probs = softmax_of(query, key, allowed)
        grad_probs = contract(grad, value, ((1,), (1,)))
        centre = jnp.sum(probs * grad_probs, axis=-1, keepdims=True)
        grad_scores = (probs * (grad_probs - centre)).astype(BF16)
        start, stop = window.start, window.stop
        total[:, start:stop] += contract(grad_scores, key, ((1,), (0,))) * HD**-0.5
        total[:, width + start : width + stop] += contract(grad_scores, query, ((0,), (0,))) * HD**-0.5
        total[:, 2 * width + start : 2 * width + stop] += contract(probs.astype(BF16), grad, ((0,), (0,)))
    out_ref[...] = total[...].astype(BF16)


def attention_call(kernel, operands, segments, out_width, matmuls):
    rows = operands[0].shape[0]
    blocks = rows // ATT_ROWS
    row_ids = segments.reshape(rows, 1)
    column_ids = segments.reshape(blocks, 1, ATT_ROWS)
    wide = lambda n: pl.BlockSpec((ATT_ROWS, n), lambda i: (i, 0))
    return pl.pallas_call(
        kernel,
        grid=(blocks,),
        out_shape=jax.ShapeDtypeStruct((rows, out_width), BF16),
        in_specs=[wide(x.shape[1]) for x in operands]
        + [wide(1), pl.BlockSpec((1, 1, ATT_ROWS), lambda i: (i, 0, 0))],
        out_specs=wide(out_width),
        scratch_shapes=[pltpu.VMEM((ATT_ROWS, out_width), F32)],
        compiler_params=pltpu.CompilerParams(vmem_limit_bytes=32 * 1024 * 1024),
        cost_estimate=pl.CostEstimate(
            flops=matmuls * blocks * HEADS * 2 * ATT_ROWS**3,
            bytes_accessed=2 * rows * (out_width + sum(x.shape[1] for x in operands)),
            transcendentals=blocks * HEADS * ATT_ROWS**2,
        ),
    )(*operands, row_ids, column_ids)


def dot(x, y):
    return jnp.dot(x, y, preferred_element_type=F32)


def dot_back(x, y):
    return lax.dot_general(x, y, (((1,), (1,)), ((), ())), preferred_element_type=F32)


def dot_rows(x, y):
    return lax.dot_general(x, y, (((0,), (0,)), ((), ())), preferred_element_type=F32)


def flat(x):
    return x.reshape(-1, x.shape[-1])


def normal(x):
    centred = x - jnp.mean(x, axis=-1, keepdims=True)
    scale = lax.rsqrt(jnp.mean(centred * centred, axis=-1, keepdims=True) + EPS)
    return centred * scale, scale


def pieces_of(modulation):
    return [p[:, None, :] for p in jnp.split(modulation, 6, axis=-1)]


def block_forward(x, segments, modulation, weights):
    qkv_weight, proj_weight, up_weight, down_weight = weights
    shape, width = x.shape, x.shape[-1]
    shift1, scale1, gate1, shift2, scale2, gate2 = pieces_of(modulation)
    first_in = flat((normal(x)[0] * (1.0 + scale1) + shift1).astype(BF16))
    qkv = dot(first_in, qkv_weight).astype(BF16)
    attended = attention_call(attend_kernel, (qkv,), segments, width, 2)
    branch = dot(attended, proj_weight).reshape(shape)
    middle = x + gate1 * branch
    second_in = flat((normal(middle)[0] * (1.0 + scale2) + shift2).astype(BF16))
    hidden = dot(second_in, up_weight)
    active = jax.nn.gelu(hidden, approximate=True).astype(BF16)
    mlp = dot(active, down_weight).reshape(shape)
    output = middle + gate2 * mlp
    return output, (first_in, qkv, attended, branch, middle, second_in, hidden, active, mlp)


def norm_back(grad, x, scale):
    hat, inverse = normal(x)
    inner = grad * (1.0 + scale)
    along = jnp.mean(inner * hat, axis=-1, keepdims=True)
    grad_x = inverse * (inner - jnp.mean(inner, axis=-1, keepdims=True) - hat * along)
    return grad_x, jnp.sum(grad, axis=1), jnp.sum(grad * hat, axis=1)


def block_backward(x, segments, modulation, weights, kept, grad_out):
    qkv_weight, proj_weight, up_weight, down_weight = weights
    first_in, qkv, attended, branch, middle, second_in, hidden, active, mlp = kept
    shape, width = x.shape, x.shape[-1]
    shift1, scale1, gate1, shift2, scale2, gate2 = pieces_of(modulation)
    grad_mlp = flat((gate2 * grad_out).astype(BF16))
    grad_gate2 = jnp.sum(grad_out * mlp, axis=1)
    _, pull = jax.vjp(lambda h: jax.nn.gelu(h, approximate=True), hidden)
    grad_hidden = pull(dot_back(grad_mlp, down_weight))[0].astype(BF16)
    grad_second = dot_back(grad_hidden, up_weight).reshape(shape)
    grad_middle, grad_shift2, grad_scale2 = norm_back(grad_second, middle, scale2)
    grad_middle = grad_middle + grad_out
    grad_gate1 = jnp.sum(grad_middle * branch, axis=1)
    grad_branch = flat((gate1 * grad_middle).astype(BF16))
    grad_attended = dot_back(grad_branch, proj_weight).astype(BF16)
    grad_qkv = attention_call(attend_back_kernel, (qkv, grad_attended), segments, 3 * width, 5)
    grad_first = dot_back(grad_qkv, qkv_weight).reshape(shape)
    grad_x, grad_shift1, grad_scale1 = norm_back(grad_first, x, scale1)
    grad_modulation = jnp.concatenate(
        [grad_shift1, grad_scale1, grad_gate1, grad_shift2, grad_scale2, grad_gate2], axis=-1
    )
    operands = ((first_in, attended, second_in, active), (grad_qkv, grad_branch, grad_hidden, grad_mlp))
    return grad_x + grad_middle, grad_modulation, operands


def plan_of(widths, lead, unit, other, last, names):
    plan = []
    for w, width in enumerate(widths):
        for low in range(0, width, unit):
            plan.append([w, low, unit, names[0]])
    for j in range(lead):
        plan.append([len(widths), j, 0, names[0]])
    chosen = range(len(plan) - other, len(plan)) if last else range(other)
    for j in chosen:
        plan[j][3] = names[1]
    return tuple(tuple(p) for p in plan)


def swap_sections(x):
    return lax.ppermute(x, "section", [(0, 1), (1, 0)])


def on_device(
    tokens, kept_index, big_image, timesteps, labels, cotangent, mask_token, time_weight, class_table,
    ada_weight, ada_bias, qkv_weight, proj_weight, up_weight, down_weight,
):
    section = lax.axis_index("section")
    me = lax.axis_index("dp")
    devices = lax.axis_size("dp")
    micro, slot, width = tokens.shape
    kept_count = kept_index.shape[1]
    own_width = ada_weight.shape[1]
    images = micro * SMALL_PER
    quarters = micro * SMALL_PER
    ada = ada_weight[0]

    length = devices // 4
    ids = jnp.concatenate([timesteps.reshape(1, images), labels.reshape(1, images)])
    if length == 4:
        ids = small_gather(jnp.pad(ids, ((0, 6), (0, 128 - images))), length, False, 2)
    else:
        ids = lax.all_gather(ids, "dp", axis=0)
    times = ids[:, 0, :images].reshape(devices * images)
    classes = ids[:, 1, :images].reshape(devices * images)
    half = time_weight.shape[0] // 2
    frequencies = jnp.exp(-math.log(10000.0) * jnp.arange(half, dtype=F32) / half)
    angles = times.astype(F32)[:, None] * frequencies[None, :]
    embedding = jnp.concatenate([jnp.cos(angles), jnp.sin(angles)], axis=-1).astype(BF16)
    onehot = (classes[:, None] == jnp.arange(class_table.shape[0])[None, :]).astype(BF16)
    cond = dot(embedding, time_weight) + dot(onehot, class_table)
    cond = lax.dynamic_slice_in_dim(cond, me * own_width, own_width, axis=1)
    lifted = jax.nn.silu(cond).astype(BF16)
    bias_width = ada_bias.shape[1]
    bias = lax.dynamic_update_slice_in_dim(
        jnp.zeros((1, 6 * width), F32), ada_bias.astype(F32), me * bias_width, axis=1
    )
    partial = (dot(lifted, ada) + bias).astype(BF16).reshape(devices, images, 6 * width)
    modulation = lax.psum_scatter(partial, "dp", scatter_dimension=0, tiled=False).astype(F32)

    shards = (qkv_weight[0], proj_weight[0], up_weight[0])
    lead = down_weight.shape[1] // qkv_weight.shape[1]
    down_shard = down_weight[0].reshape(lead, own_width, width)
    widths = [s.shape[1] for s in shards]
    if length == 4:
        plan = plan_of(widths, lead, width, 2, True, ("line", "pair"))
        whole = gather_all(shards + (down_shard,), plan, length)
    else:
        whole = tuple(lax.all_gather(s, "dp", axis=0) for s in shards + (down_shard,))
    weights = tuple(w.reshape(-1, w.shape[-1]) for w in whole)

    big = big_image[:, :1] > 0
    modulation = modulation.reshape(micro, SMALL_PER, 6 * width)
    modulation = jnp.where(big[:, :, None], modulation[:, :1], modulation).reshape(quarters, 6 * width)
    quarter_ids = jnp.arange(quarters, dtype=jnp.int32).reshape(micro, SMALL_PER)
    segment_of = jnp.where(big, quarter_ids[:, :1], quarter_ids).reshape(quarters)
    positions = jnp.arange(slot, dtype=jnp.int32)
    placement = (positions[None, :, None] == kept_index[:, None, :]).astype(BF16)
    enc_segments = jnp.repeat(segment_of, kept_count // SMALL_PER)
    dec_segments = jnp.repeat(segment_of, slot // SMALL_PER)

    def to_kept(rows):
        return jnp.einsum("msk,msd->mkd", placement, rows, preferred_element_type=F32)

    def to_slots(rows):
        return jnp.einsum("msk,mkd->msd", placement, rows, preferred_element_type=F32)

    enc_rows = (quarters, kept_count // SMALL_PER, width)
    dec_rows = (quarters, slot // SMALL_PER, width)

    def encode():
        x = to_kept(tokens).reshape(enc_rows)
        out, kept = block_forward(x, enc_segments, modulation, weights)
        return out.astype(BF16), (x, kept)

    idle = lambda f: jax.tree.map(lambda s: jnp.zeros(s.shape, s.dtype), jax.eval_shape(f))
    encoded, enc_kept = lax.cond(section == 0, encode, lambda: idle(encode))
    received = swap_sections(encoded).reshape(micro, kept_count, width)

    def decode():
        flags = jnp.sum(placement.astype(F32), axis=2)[:, :, None]
        x = to_slots(received) + (1.0 - flags) * mask_token.astype(F32)[None, None, :]
        x = x.reshape(dec_rows)
        out, kept = block_forward(x, dec_segments, modulation, weights)
        grad = cotangent.astype(F32).reshape(dec_rows)
        grad_x, grad_mod, grads = block_backward(x, dec_segments, modulation, weights, kept, grad)
        grad_x = grad_x.reshape(micro, slot, width)
        mask_part = jnp.sum((1.0 - flags) * grad_x, axis=(0, 1))
        back = to_kept(grad_x.astype(BF16)).astype(BF16)
        return out.astype(BF16).reshape(micro, slot, width), mask_part, back, grad_mod, grads

    decoded, mask_part, back, grad_mod, grads = lax.cond(section == 1, decode, lambda: idle(decode))
    received = swap_sections(back)

    def encode_back():
        x, kept = enc_kept
        grad = received.astype(F32).reshape(enc_rows)
        grad_x, grad_mod, grads = block_backward(x, enc_segments, modulation, weights, kept, grad)
        grad_x = grad_x.astype(BF16).reshape(micro, kept_count, width)
        grads = jax.tree.map(lambda g: jnp.pad(g, ((0, micro * (slot - kept_count)), (0, 0))), grads)
        return to_slots(grad_x).astype(BF16), grad_mod, grads

    token_grad, grad_mod, grads = lax.cond(
        section == 0, encode_back, lambda: (jnp.zeros_like(decoded), grad_mod, grads)
    )

    half_width = width // 2
    outgoing = jnp.where(section == 0, token_grad[:, :, half_width:], decoded[:, :, :half_width])
    incoming = swap_sections(outgoing)
    decoded_half = jnp.where(section == 0, incoming, decoded[:, :, half_width:])
    token_half = jnp.where(section == 0, token_grad[:, :, :half_width], incoming)

    grad_mod = grad_mod.reshape(micro, SMALL_PER, 6 * width)
    first_only = (jnp.arange(SMALL_PER) == 0)[None, :, None]
    grad_mod = jnp.where(
        big[:, :, None], jnp.where(first_only, jnp.sum(grad_mod, axis=1, keepdims=True), 0.0), grad_mod
    )
    grad_mod = grad_mod.reshape(images, 6 * width).astype(BF16)
    every_mod = lax.all_gather(grad_mod, "dp", axis=0, tiled=True)
    ada_grad = dot_rows(lifted, every_mod)
    bias_grad = jnp.sum(
        lax.dynamic_slice_in_dim(every_mod, me * bias_width, bias_width, axis=1).astype(F32), axis=0
    )
    grad_lifted = dot_back(every_mod, ada)
    _, pull = jax.vjp(jax.nn.silu, cond)
    grad_cond = pull(grad_lifted)[0]
    mask_rows = mask_part.reshape(-1, devices * images) if length == 4 else None
    if length == 4:
        payload = jnp.concatenate([grad_cond.T, mask_rows])
        extra = -payload.shape[0] % 8
        payload = small_gather(jnp.pad(payload, ((0, extra), (0, 0))), length, True, 3)
        every_cond = payload[:, :own_width].reshape(width, devices * images)
        mask_grad = jnp.sum(payload[:, own_width : own_width + mask_rows.shape[0]], axis=0).reshape(width)
    else:
        every_cond = lax.psum(lax.all_gather(grad_cond.T, "dp", axis=0, tiled=True), "section")
        mask_grad = lax.psum(mask_part, ("section", "dp"))
    inputs = jnp.concatenate([embedding, onehot], axis=1)
    shared = lax.dot_general(
        inputs, every_cond.astype(BF16), (((0,), (1,)), ((), ())), preferred_element_type=F32
    )
    time_grad, table_grad = shared[: time_weight.shape[0]], shared[time_weight.shape[0] :]

    shapes = tuple(x.shape for x in shards + (down_shard,))
    lefts, rights = grads
    if length == 4:
        names = ("pair", "line")
        plan = plan_of(widths, lead, width, 2, False, names)
        mine = scatter_all(lefts, rights, shapes, plan, length)
    else:
        split = (dot_rows(x, y).astype(BF16).reshape((devices,) + s) for x, y, s in zip(lefts, rights, shapes))
        mine = tuple(lax.psum_scatter(g, "dp", scatter_dimension=0) for g in split)
    qkv_grad, proj_grad, up_grad, down_grad = (g.astype(F32) for g in mine)
    return (
        decoded_half,
        token_half,
        mask_grad,
        time_grad,
        table_grad,
        ada_grad[None],
        bias_grad[None],
        qkv_grad[None],
        proj_grad[None],
        up_grad[None],
        down_grad.reshape(down_weight.shape),
    )


def solution(mesh):
    rows = P(None, "dp", None)
    ids = P(None, "dp")
    weight = P("section", "dp", None)
    halves = P(None, "dp", "section")
    in_specs = (rows, ids, ids, ids, ids, rows, P(), P(), P(), weight, P("section", "dp")) + (weight,) * 4
    out_specs = (halves, halves, P(), P(), P(), weight, P("section", "dp")) + (weight,) * 4
    return jax.shard_map(
        on_device, mesh=mesh, in_specs=in_specs, out_specs=out_specs, check_vma=False
    )
```

```python
import functools
import math

import jax
import jax.numpy as jnp
from jax import lax
from jax.experimental import pallas as pl
from jax.experimental.pallas import tpu as pltpu
from jax.sharding import PartitionSpec as P

HEADS = 16
HD = 72
SMALL_PER = 4
ATT_ROWS = 256
EPS = 1e-6
MASKED = -1e30
MESH = pl.DeviceIdType.MESH
F32 = jnp.float32
BF16 = jnp.bfloat16


def remote(src, dst, send_sem, recv_sem, target):
    return pltpu.make_async_remote_copy(
        src_ref=src,
        dst_ref=dst,
        send_sem=send_sem,
        recv_sem=recv_sem,
        device_id=target,
        device_id_type=MESH,
    )


def when(condition, run):
    pl.when(condition)(run)


def position():
    me = lax.axis_index("dp")
    return me // 4, (me // 2) % 2, me % 2


def at(line, pair, core):
    return {"dp": (line * 2 + pair) * 2 + core}


def greet(length, a, b, c):
    has_up, has_down = a < length - 1, a > 0
    barrier = pltpu.get_barrier_semaphore()

    def tell(target):
        pl.semaphore_signal(barrier, inc=1, device_id=target, device_id_type=MESH)

    tell(at(a, 1 - b, c))
    tell(at(a, b, 1 - c))
    when(has_up, lambda: tell(at(a + 1, b, c)))
    when(has_down, lambda: tell(at(a - 1, b, c)))
    pl.semaphore_wait(barrier, 2 + has_up.astype(jnp.int32) + has_down.astype(jnp.int32))
    return has_up, has_down


def piece(ref, lead, plan_entry):
    _, low, size, _ = plan_entry
    if size == 0:
        return ref.at[lead + (low,)]
    return ref.at[lead + (slice(None), pl.ds(low, size))]


def gather_moves(length, plan, sources, outs, sems, a, b, c):
    up_s, up_r, down_s, down_r, pair_s, pair_r, core_s, core_r, own_sem = sems
    has_up, has_down = a < length - 1, a > 0
    chunks = range(len(plan))
    line_first = [plan[i][3] == "line" for i in chunks]

    def slot(i, aa, bb, cc):
        return piece(outs[plan[i][0]], (aa, bb, cc), plan[i])

    def own(i):
        return piece(sources[plan[i][0]], (), plan[i])

    def rows_of(i):
        return (b,) if line_first[i] else (b, 1 - b)

    def up(i, k, bb, src=None):
        s = slot(i, a - k, bb, c)
        return remote(s if src is None else src, s, up_s.at[i, k, bb], up_r.at[i, k, bb], at(a + 1, b, c))

    def up_arrival(i, k, bb):
        s = slot(i, a - 1 - k, bb, c)
        return remote(s, s, up_s.at[i, k, bb], up_r.at[i, k, bb], at(a + 1, b, c))

    def down(i, k, bb, src=None):
        s = slot(i, a + k, bb, c)
        return remote(s if src is None else src, s, down_s.at[i, k, bb], down_r.at[i, k, bb], at(a - 1, b, c))

    def down_arrival(i, k, bb):
        s = slot(i, a + 1 + k, bb, c)
        return remote(s, s, down_s.at[i, k, bb], down_r.at[i, k, bb], at(a - 1, b, c))

    def across(i, aa, src=None):
        s = slot(i, aa, b, c)
        return remote(s if src is None else src, s, pair_s.at[i, aa], pair_r.at[i, aa], at(a, 1 - b, c))

    def across_arrival(i, aa):
        s = slot(i, aa, 1 - b, c)
        return remote(s, s, pair_s.at[i, aa], pair_r.at[i, aa], at(a, 1 - b, c))

    def to_core(i, aa, bb, src=None):
        s = slot(i, aa, bb, c)
        return remote(s if src is None else src, s, core_s.at[i, aa, bb], core_r.at[i, aa, bb], at(a, b, 1 - c))

    def core_arrival(i, aa, bb):
        s = slot(i, aa, bb, 1 - c)
        return remote(s, s, core_s.at[i, aa, bb], core_r.at[i, aa, bb], at(a, b, 1 - c))

    def after_across(i, aa):
        across_arrival(i, aa).wait_recv()
        to_core(i, aa, 1 - b).start()

    def issue(i):
        src = own(i)
        pltpu.make_async_copy(src, slot(i, a, b, c), own_sem.at[i]).start()
        across(i, a, src).start()
        when(has_up, lambda: up(i, 0, b, src).start())
        when(has_down, lambda: down(i, 0, b, src).start())
        to_core(i, a, b, src).start()

    def pair_step(i):
        across_arrival(i, a).wait_recv()
        when(has_up, lambda: up(i, 0, 1 - b).start())
        when(has_down, lambda: down(i, 0, 1 - b).start())
        to_core(i, a, 1 - b).start()

    def line_step(i, k):
        for bb in rows_of(i):

            def from_below():
                up_arrival(i, k - 1, bb).wait_recv()
                when(has_up, lambda: up(i, k, bb).start())
                if line_first[i]:
                    across(i, a - k).start()
                to_core(i, a - k, bb).start()

            def from_above():
                down_arrival(i, k - 1, bb).wait_recv()
                when(has_down, lambda: down(i, k, bb).start())
                if line_first[i]:
                    across(i, a + k).start()
                to_core(i, a + k, bb).start()

            when(a - k >= 0, from_below)
            when(a + k <= length - 1, from_above)

    def across_step(i, k):
        if not line_first[i]:
            return
        if k == 0:
            after_across(i, a)
        else:
            when(a - k >= 0, lambda: after_across(i, a - k))
            when(a + k <= length - 1, lambda: after_across(i, a + k))

    def complete(i):
        pltpu.make_async_copy(own(i), slot(i, a, b, c), own_sem.at[i]).wait()
        for aa in range(length):
            for bb in range(2):
                core_arrival(i, aa, bb).wait_recv()

    def drain(i):
        for aa in range(length):
            for bb in range(2):
                to_core(i, aa, bb).wait_send()
            if line_first[i]:
                across(i, aa).wait_send()
        if not line_first[i]:
            across(i, a).wait_send()
        for k in range(length - 1):
            for bb in rows_of(i):
                when(jnp.logical_and(has_up, a - k >= 0), lambda: up(i, k, bb).wait_send())
                when(
                    jnp.logical_and(has_down, a + k <= length - 1),
                    lambda: down(i, k, bb).wait_send(),
                )

    def move(t, ahead):
        n = len(plan)
        if t + ahead < n:
            issue(t + ahead)
        if t < n and not line_first[t]:
            pair_step(t)
        for k in range(1, length):
            i = t - k + 1
            if 0 <= i < n:
                line_step(i, k)
        for k in range(length):
            i = t - k
            if 0 <= i < n:
                across_step(i, k)

    return issue, move, complete, drain


def scatter_kernel(length, plan, slots, pair_slots, *refs):
    lefts, rights = refs[:4], refs[4:8]
    outs = refs[8:12]
    (
        raw, right, left_t, held, sent, core_in, pair_in, pair_late, up_in, down_in,
    ) = refs[12:22]
    (
        raw_sem, right_sem, core_s, core_r, pair_s, pair_r, up_s, up_r, down_s, down_r, out_sem,
        core_credit, pair_credit,
    ) = refs[22:]
    a, b, c = position()
    greet(length, a, b, c)
    n = len(plan)
    rows, width = held.shape[3:]
    total_rows = raw.shape[1]
    encoder = lax.axis_index("section") == 0
    used_rows = jnp.where(encoder, total_rows // 2, total_rows)
    pair_first = [p[3] == "pair" for p in plan]
    order = [sum(pair_first[:i]) if pair_first[i] else i - sum(pair_first[:i]) for i in range(n)]
    base, total = [], 0
    for i in range(n):
        base.append(total)
        total += (length - 1) * (1 if pair_first[i] else 2)
    groups = 2 * length

    def blocks_of(w):
        return lefts[w].shape[1] // width

    raw_jobs = []
    right_jobs = []
    for i, (w, low, size, _) in enumerate(plan):
        if i == 0 or plan[i - 1][0] != w:
            raw_jobs += [(w, k) for k in range(blocks_of(w))]
        if size != 0 or plan[i - 1][0] != w:
            right_jobs.append(i)

    def raw_load(x):
        w, k = raw_jobs[x]
        src = lefts[w].at[:, pl.ds(k * width, width)]
        return pltpu.make_async_copy(src, raw.at[x % 2], raw_sem.at[x])

    def right_load(x):
        w, low, size, _ = plan[right_jobs[x]]
        src = rights[w].at[:, pl.ds(low if size else 0, width)]
        return pltpu.make_async_copy(src, right.at[x % 2], right_sem.at[x])

    progress = {"raw": 0, "right": -1}

    def turn(w):
        count = blocks_of(w)
        for k in range(count):
            x = progress["raw"]
            progress["raw"] += 1
            raw_load(x).wait()
            slot = x % 2

            def body(r, carry):
                start = pl.multiple_of(r * 128, 128)
                block = raw[slot, pl.ds(start, 128), :].astype(F32).T
                if count == 1:
                    split = block.reshape(groups, 2, rows, 128)
                    for q in range(2):
                        part = split[:, q].reshape(groups * rows, 128)
                        left_t[q, :, pl.ds(start, 128)] = part.astype(BF16)
                else:
                    near = groups // count
                    split = block.reshape(near, 2, count, rows, 128)
                    for q in range(2):
                        for j in range(count):
                            part = split[:, q, j].reshape(near * rows, 128)
                            left_t[
                                q * count + j, pl.ds(k * near * rows, near * rows), pl.ds(start, 128)
                            ] = part.astype(BF16)
                return carry

            lax.fori_loop(0, used_rows // 128, body, 0)
            if x + 2 < len(raw_jobs):
                raw_load(x + 2).start()

    def product(i, q, put):
        w, low, size, _ = plan[i]
        count = blocks_of(w)
        row_set = q if count == 1 else q * count + low
        slot = progress["right"] % 2
        tile = width // 3

        def body(k, carry):
            columns = pl.ds(pl.multiple_of(k * tile, 128), tile)

            def multiply(depth):
                result = dot(left_t[row_set, :, :depth], right[slot, :depth, columns])
                for s in range(groups):
                    put(s, columns, result[s * rows : (s + 1) * rows].astype(BF16))

            when(encoder, lambda: multiply(total_rows // 2))
            when(jnp.logical_not(encoder), lambda: multiply(total_rows))
            return carry

        lax.fori_loop(0, 3, body, 0)

    def to_core(i):
        return remote(sent.at[i % slots], core_in.at[i % slots], core_s.at[i], core_r.at[i], at(a, b, 1 - c))

    def across(i):
        target = at(a, 1 - b, c)
        if pair_first[i]:
            return remote(
                held.at[i, :, 1 - b], pair_in.at[order[i] % pair_slots], pair_s.at[i], pair_r.at[i], target
            )
        return remote(held.at[i, a, 1 - b], pair_late.at[order[i]], pair_s.at[i], pair_r.at[i], target)

    def rows_of(i):
        return (b,) if pair_first[i] else (b, 1 - b)

    def flow_index(i, dest, bb):
        if pair_first[i]:
            return base[i] + dest
        return base[i] + dest * 2 + bb

    def up(i, line, dest, bb):
        x = flow_index(i, dest - 1, bb)
        return remote(held.at[i, dest, bb], up_in.at[x], up_s.at[x], up_r.at[x], at(line + 1, b, c))

    def down(i, line, dest, bb):
        x = flow_index(i, dest, bb)
        return remote(held.at[i, dest, bb], down_in.at[x], down_s.at[x], down_r.at[x], at(line - 1, b, c))

    def add(dst, src):
        dst[...] = dst[...] + src[...]

    def credit(sem, target):
        pl.semaphore_signal(sem, inc=1, device_id=target, device_id_type=MESH)

    def produce(i):
        w = plan[i][0]
        if i == 0 or plan[i - 1][0] != w:
            turn(w)
        if progress["right"] + 1 < len(right_jobs) and right_jobs[progress["right"] + 1] == i:
            progress["right"] += 1
            right_load(progress["right"]).wait()
            if progress["right"] + 1 < len(right_jobs):
                right_load(progress["right"] + 1).start()
        if i >= slots:
            to_core(i - slots).wait_send()

        def put_sent(s, columns, value):
            sent[i % slots, s // 2, s % 2, :, columns] = value

        def put_held(s, columns, value):
            held[i, s // 2, s % 2, :, columns] = value

        product(i, 1 - c, put_sent)
        if i >= slots:
            pl.semaphore_wait(core_credit, 1)
        to_core(i).start()
        product(i, c, put_held)

    def first_add(i):
        to_core(i).wait_recv()

        def body(s, carry):
            add(held.at[i, s // 2, s % 2], core_in.at[i % slots, s // 2, s % 2])
            return carry

        lax.fori_loop(0, groups, body, 0)
        if i + slots < n:
            credit(core_credit, at(a, b, 1 - c))
        if pair_first[i]:
            if order[i] >= pair_slots:
                pl.semaphore_wait(pair_credit, 1)
            across(i).start()

    def second_add(i):
        if not pair_first[i]:
            return
        across(i).wait_recv()

        def body(s, carry):
            add(held.at[i, s, b], pair_in.at[order[i] % pair_slots, s])
            return carry

        lax.fori_loop(0, length, body, 0)
        if order[i] + pair_slots < sum(pair_first):
            credit(pair_credit, at(a, 1 - b, c))

    def line_step(i, j):
        def going_up():
            for dest in range(length - 1, j - 1, -1):
                for bb in rows_of(i):
                    if j > 0:
                        up(i, j - 1, dest, bb).wait_recv()
                        add(held.at[i, dest, bb], up_in.at[flow_index(i, dest - 1, bb)])
                    if dest > j:
                        up(i, j, dest, bb).start()

        def going_down():
            here = length - 1 - j
            for dest in range(0, here + 1):
                for bb in rows_of(i):
                    if j > 0:
                        down(i, here + 1, dest, bb).wait_recv()
                        add(held.at[i, dest, bb], down_in.at[flow_index(i, dest, bb)])
                    if dest < here:
                        down(i, here, dest, bb).start()

        when(a == j, going_up)
        when(a == length - 1 - j, going_down)

    def result(i):
        w, low, size, _ = plan[i]
        dst = outs[w].at[low] if size == 0 else outs[w].at[:, pl.ds(low, size)]
        return pltpu.make_async_copy(held.at[i, a, b], dst, out_sem.at[i])

    def finish(i):
        if pair_first[i]:
            result(i).start()
        else:
            across(i).start()

    def finish_late(i):
        if not pair_first[i]:
            across(i).wait_recv()
            add(held.at[i, a, b], pair_late.at[order[i]])
            result(i).start()

    raw_load(0).start()
    right_load(0).start()
    raw_load(1).start()
    produce(0)
    for t in range(n + length + 3):
        if t < n:
            first_add(t)
        if t + 1 < n:
            produce(t + 1)
        if 0 <= t - 1 < n:
            second_add(t - 1)
        for j in range(length):
            if 0 <= t - 2 - j < n:
                line_step(t - 2 - j, j)
        if 0 <= t - 1 - length < n:
            finish(t - 1 - length)
        if 0 <= t - 2 - length < n:
            finish_late(t - 2 - length)
    for i in range(n):
        if i >= n - slots:
            to_core(i).wait_send()
        across(i).wait_send()
        result(i).wait()
        for bb in rows_of(i):
            for here in range(length):

                def gone():
                    for dest in range(here + 1, length):
                        up(i, here, dest, bb).wait_send()
                    for dest in range(0, here):
                        down(i, here, dest, bb).wait_send()

                when(a == here, gone)


def scatter_all(lefts, rights, shard_shapes, plan, length):
    n = len(plan)
    slots, pair_slots = 2, 4
    total_rows = lefts[0].shape[0]
    rows, width = shard_shapes[0][0], plan[0][2]
    late = sum(p[3] != "pair" for p in plan)
    flows = (length - 1) * (n + late)
    lead = shard_shapes[-1][0]
    dma = pltpu.SemaphoreType.DMA
    anywhere = pl.BlockSpec(memory_space=pl.ANY)
    slab = (rows, width)
    return pl.pallas_call(
        functools.partial(scatter_kernel, length, plan, slots, pair_slots),
        out_shape=tuple(jax.ShapeDtypeStruct(s, BF16) for s in shard_shapes),
        in_specs=[anywhere] * 8,
        out_specs=[anywhere] * 4,
        scratch_shapes=[
            pltpu.VMEM((2, total_rows, width), BF16),
            pltpu.VMEM((2, total_rows, width), BF16),
            pltpu.VMEM((2 * lead, 2 * length * rows, total_rows), BF16),
            pltpu.VMEM((n, length, 2) + slab, BF16),
            pltpu.VMEM((slots, length, 2) + slab, BF16),
            pltpu.VMEM((slots, length, 2) + slab, BF16),
            pltpu.VMEM((pair_slots, length) + slab, BF16),
            pltpu.VMEM((late,) + slab, BF16),
            pltpu.VMEM((flows,) + slab, BF16),
            pltpu.VMEM((flows,) + slab, BF16),
            dma((lead + 3,)), dma((n,)), dma((n,)), dma((n,)), dma((n,)), dma((n,)),
            dma((flows,)), dma((flows,)), dma((flows,)), dma((flows,)), dma((n,)),
            pltpu.SemaphoreType.REGULAR, pltpu.SemaphoreType.REGULAR,
        ],
        compiler_params=pltpu.CompilerParams(
            collective_id=1, has_side_effects=True, vmem_limit_bytes=62 * 1024 * 1024
        ),
        name="scatter_grads",
    )(*lefts, *rights)


def small_gather_kernel(length, sum_sections, own_ref, out_ref, other, *sems):
    line_s, line_r, pair_s, pair_r, core_s, core_r, side_s, side_r = sems
    a, b, c = position()
    partner = {"section": 1 - lax.axis_index("section")}
    barrier = pltpu.get_barrier_semaphore()

    def tell(target):
        pl.semaphore_signal(barrier, inc=1, device_id=target, device_id_type=MESH)

    tell(at(a, 1 - b, c))
    tell(at(a, b, 1 - c))
    for k in range(1, length):
        tell(at(lax.rem(a + k, length), b, c))
    if sum_sections:
        tell(partner)
    pl.semaphore_wait(barrier, length + 1 + int(sum_sections))
    value = own_ref[...]
    if sum_sections:
        side = remote(own_ref, other, side_s, side_r, partner)
        side.start()
        side.wait()
        value = value + other[...]
    out_ref[a, b, c] = value
    mine = out_ref.at[a, b, c]
    copies = []
    for k in range(1, length):
        to = lax.rem(a + k, length)
        copy = remote(mine, mine, line_s.at[k - 1], line_r.at[k - 1], at(to, b, c))
        copy.start()
        copies.append(copy)
    for k in range(1, length):
        source = lax.rem(a + length - k, length)
        slab = out_ref.at[source, b, c]
        remote(slab, slab, line_s.at[k - 1], line_r.at[k - 1], at(a, 1 - b, c)).wait_recv()
        copies[k - 1].wait_send()
    for go, come, s, r, to in (
        (out_ref.at[:, b, c], out_ref.at[:, 1 - b, c], pair_s, pair_r, at(a, 1 - b, c)),
        (out_ref.at[:, :, c], out_ref.at[:, :, 1 - c], core_s, core_r, at(a, b, 1 - c)),
    ):
        copy = remote(go, go, s, r, to)
        copy.start()
        remote(come, come, s, r, to).wait_recv()
        copy.wait_send()


def small_gather(own, length, sum_sections, collective_id):
    dma = pltpu.SemaphoreType.DMA
    vmem = pl.BlockSpec(memory_space=pltpu.VMEM)
    shape = (length, 2, 2) + own.shape
    return pl.pallas_call(
        functools.partial(small_gather_kernel, length, sum_sections),
        out_shape=jax.ShapeDtypeStruct(shape, own.dtype),
        in_specs=[vmem],
        out_specs=vmem,
        scratch_shapes=[
            pltpu.VMEM(own.shape, own.dtype), dma((length - 1,)), dma((length - 1,)), dma, dma, dma, dma, dma, dma,
        ],
        compiler_params=pltpu.CompilerParams(collective_id=collective_id, has_side_effects=True),
        name="small_gather",
    )(own).reshape((4 * length,) + own.shape)


def head_window(h):
    low, high = h * HD, h * HD + HD
    start = low // 128 * 128
    return low, high, start, -(-high // 128) * 128


def contract(x, y, dims):
    return lax.dot_general(x, y, ((dims[0], dims[1]), ((), ())), preferred_element_type=F32)


def head_operands(qkv_ref, rows, h):
    width = qkv_ref.shape[1] // 3
    low, high, start, stop = head_window(h)
    lane = lax.broadcasted_iota(jnp.int32, (1, stop - start), 1) + start
    inside = jnp.logical_and(lane >= low, lane < high)
    parts = [qkv_ref[rows, j * width + start : j * width + stop] for j in range(3)]
    return inside, slice(start, stop), parts


def only(inside, x):
    return jnp.where(inside, x, jnp.zeros_like(x))


def softmax_of(query, key, allowed):
    scores = jnp.where(allowed, contract(query, key, ((1,), (1,))) * HD**-0.5, MASKED)
    weights = jnp.exp(scores - jnp.max(scores, axis=-1, keepdims=True))
    return weights * (1.0 / jnp.sum(weights, axis=-1, keepdims=True))


def attend(qkv_ref, rows, allowed, total, out_ref):
    width = out_ref.shape[1]
    total[:, :width] = jnp.zeros((total.shape[0], width), F32)
    for h in range(HEADS):
        inside, window, (query, key, value) = head_operands(qkv_ref, rows, h)
        probs = softmax_of(only(inside, query), key, allowed).astype(BF16)
        mixed = contract(probs, value, ((1,), (0,)))
        total[:, window] += only(inside, mixed)
    out_ref[rows, :] = total[:, :width].astype(BF16)


def attend_back(qkv_ref, grad_ref, rows, allowed, total, out_ref):
    width = grad_ref.shape[1]
    total[...] = jnp.zeros_like(total)
    for h in range(HEADS):
        inside, window, (query, key, value) = head_operands(qkv_ref, rows, h)
        query, key = only(inside, query), only(inside, key)
        grad = only(inside, grad_ref[rows, window])
        probs = softmax_of(query, key, allowed)
        grad_probs = contract(grad, value, ((1,), (1,)))
        centre = jnp.sum(probs * grad_probs, axis=-1, keepdims=True)
        grad_scores = (probs * (grad_probs - centre)).astype(BF16)
        start, stop = window.start, window.stop
        total[:, start:stop] += contract(grad_scores, key, ((1,), (0,))) * HD**-0.5
        total[:, width + start : width + stop] += contract(grad_scores, query, ((0,), (0,))) * HD**-0.5
        total[:, 2 * width + start : 2 * width + stop] += contract(probs.astype(BF16), grad, ((0,), (0,)))
    out_ref[rows, :] = total[...].astype(BF16)


def dot(x, y):
    return jnp.dot(x, y, preferred_element_type=F32)


def dot_back(x, y):
    return lax.dot_general(x, y, (((1,), (1,)), ((), ())), preferred_element_type=F32)


def dot_rows(x, y):
    return lax.dot_general(x, y, (((0,), (0,)), ((), ())), preferred_element_type=F32)


def normal(x):
    centred = x - jnp.mean(x, axis=-1, keepdims=True)
    scale = lax.rsqrt(jnp.mean(centred * centred, axis=-1, keepdims=True) + EPS)
    return centred * scale, scale


TILE = 384
DEPTH = 3
GELU = math.sqrt(2.0 / math.pi)


def columns_of(t):
    if isinstance(t, int):
        return pl.ds(t * TILE, TILE)
    return pl.ds(pl.multiple_of(t * TILE, 128), TILE)


class Stream:
    def __init__(self, wide, tall, sems, width):
        self.wide, self.tall, self.sems, self.width = wide, tall, sems, width
        self.stages = []

    def add(self, weight, back, inner, outer):
        self.stages.append((weight, back, inner, outer))

    def tile(self, stage, n, k):
        weight, back, inner, _ = self.stages[stage]
        t = n * inner + k
        slot = lax.rem(t, DEPTH) if not isinstance(t, int) else t % DEPTH
        deep = pl.ds(pl.multiple_of(k * self.width, 128), self.width)
        side = columns_of(n)
        ring = self.tall if back else self.wide
        src = weight.at[side, deep] if back else weight.at[deep, side]
        buffer = ring.at[stage % 2, slot]
        return pltpu.make_async_copy(src, buffer, self.sems.at[stage % 2, slot]), buffer

    def begin(self, stage):
        if stage < len(self.stages):
            _, _, inner, outer = self.stages[stage]
            for t in range(min(DEPTH, inner * outer)):
                self.tile(stage, t // inner, t % inner)[0].start()

    def run(self, stage, use, ahead=True):
        _, _, inner, outer = self.stages[stage]
        if ahead:
            self.begin(stage + 1)
        count = inner * outer

        def body(n, carry):
            def product(k, left, back):
                copy, buffer = self.tile(stage, n, k)
                copy.wait()
                result = (dot_back if back else dot)(left, buffer[...])
                t = n * inner + k + DEPTH

                def refill():
                    self.tile(stage, lax.div(t, inner), lax.rem(t, inner))[0].start()

                when(t < count, refill)
                return result

            use(n, product)
            return carry

        lax.fori_loop(0, outer, body, 0)


def each_quarter(rows, run):
    def body(q, carry):
        run(q, pl.ds(pl.multiple_of(q * rows, rows), rows))
        return carry

    lax.fori_loop(0, 8, body, 0)


def piece_of(mod_ref, q, p, width, columns=None):
    if columns is None:
        return mod_ref[q, :, p * width : (p + 1) * width]
    return mod_ref[q, :, pl.ds(p * width + columns.start, columns.size)]


def modulate(x_ref, mod_ref, out_ref, first, quarter_rows):
    width = x_ref.shape[1]

    def run(q, rows):
        hat = normal(x_ref[rows, :])[0]
        shift, scale = piece_of(mod_ref, q, first, width), piece_of(mod_ref, q, first + 1, width)
        out_ref[rows, :] = (hat * (1.0 + scale) + shift).astype(BF16)

    each_quarter(quarter_rows, run)


def modulate_back(grad, x, scale):
    hat, inverse = normal(x)
    inner = grad * (1.0 + scale)
    along = jnp.mean(inner * hat, axis=-1, keepdims=True)
    grad_x = inverse * (inner - jnp.mean(inner, axis=-1, keepdims=True) - hat * along)
    return grad_x, jnp.sum(grad, axis=0, keepdims=True), jnp.sum(grad * hat, axis=0, keepdims=True)


def split_quarters(quarter_rows, run):
    for q in range(8):
        run(q, slice(q * quarter_rows, (q + 1) * quarter_rows))


def allowed_of(row_ref, column_ref, block):
    rows = pl.ds(pl.multiple_of(block * ATT_ROWS, ATT_ROWS), ATT_ROWS)
    return rows, row_ref[rows, :] == column_ref[block]


def each_block(total_rows, run):
    def body(block, carry):
        run(block)
        return carry

    lax.fori_loop(0, total_rows // ATT_ROWS, body, 0)


def forward_stages(stream, weights):
    width = weights[0].shape[0]
    qkv, proj, up, down = weights
    stream.add(qkv, False, 1, qkv.shape[1] // TILE)
    stream.add(proj, False, 1, width // TILE)
    stream.add(up, False, 1, up.shape[1] // TILE)
    stream.add(down, False, down.shape[0] // width, width // TILE)


def backward_stages(stream, weights):
    width = weights[0].shape[0]
    qkv, proj, up, down = weights
    stream.add(down, True, 1, down.shape[0] // TILE)
    stream.add(up, True, up.shape[1] // width, width // TILE)
    stream.add(proj, True, 1, width // TILE)
    stream.add(qkv, True, qkv.shape[1] // width, width // TILE)


def proj_tile(r, mod_ref, quarter_rows, columns, branch):
    width = r["x"].shape[1]
    r["branch"][:, columns] = branch.astype(BF16)

    def gated(q, rows):
        gate = piece_of(mod_ref, q, 2, width, columns)
        r["x2"][rows, columns] = r["x"][rows, columns] + gate * branch[rows]

    split_quarters(quarter_rows, gated)


def up_tile(r, columns, h):
    square = h * h
    t = jnp.tanh(h * (GELU + (GELU * 0.044715) * square))
    half = 0.5 + 0.5 * t
    r["act"][:, columns] = (h * half).astype(BF16)
    slope = half + (0.5 * h) * (1.0 - t * t) * (GELU + (3.0 * GELU * 0.044715) * square)
    r["slope"][:, columns] = slope.astype(BF16)


def out_tile(r, mod_ref, quarter_rows, columns, mlp):
    width = r["x"].shape[1]
    r["mlp"][:, columns] = mlp.astype(BF16)

    def gated(q, rows):
        gate = piece_of(mod_ref, q, 5, width, columns)
        r["out"][rows, columns] = (r["x2"][rows, columns] + gate * mlp[rows]).astype(BF16)

    split_quarters(quarter_rows, gated)


def run_forward(stream, r, mod_ref, segments, quarter_rows, finish_tile, done):
    width = r["x"].shape[1]
    total_rows = r["x"].shape[0]
    modulate(r["x"], mod_ref, r["a1"], 0, quarter_rows)

    def qkv(n, product):
        r["qkv"][:, columns_of(n)] = product(0, r["a1"][...], False).astype(BF16)

    stream.run(0, qkv)
    done("a1")

    def mix(block):
        rows, allowed = allowed_of(*segments, block)
        attend(r["qkv"], rows, allowed, r["total"], r["att"])

    each_block(total_rows, mix)

    def proj(n, product):
        proj_tile(r, mod_ref, quarter_rows, columns_of(n), product(0, r["att"][...], False))

    stream.run(1, proj)
    done("att")
    modulate(r["x2"], mod_ref, r["a2"], 3, quarter_rows)

    def up(n, product):
        up_tile(r, columns_of(n), product(0, r["a2"][...], False))

    stream.run(2, up)
    done("a2")

    def down(n, product):
        mlp = None
        for k in range(r["act"].shape[1] // width):
            part = product(k, r["act"][:, k * width : (k + 1) * width], False)
            mlp = part if mlp is None else mlp + part
        finish_tile(n, columns_of(n), mlp)

    stream.run(3, down)
    done("act")


def run_backward(stream, first, r, mod_ref, segments, quarter_rows, grad_of, finish, done):
    width = r["x"].shape[1]
    total_rows = r["x"].shape[0]

    def down(n, product):
        columns = columns_of(n)
        grad = product(0, r["dmlp"][...], True)
        r["slope"][:, columns] = (grad * r["slope"][:, columns].astype(F32)).astype(BF16)

    stream.run(first, down)
    done("dmlp")
    done("slope")

    def up(n, product):
        grad = None
        for k in range(r["slope"].shape[1] // width):
            part = product(k, r["slope"][:, k * width : (k + 1) * width], True)
            grad = part if grad is None else grad + part
        r["dx2"][:, columns_of(n)] = grad

    stream.run(first + 1, up)

    def middle(q, rows):
        scale, gate = piece_of(mod_ref, q, 4, width), piece_of(mod_ref, q, 2, width)
        grad, shift_grad, scale_grad = modulate_back(r["dx2"][rows, :], r["x2"][rows, :], scale)
        grad = grad + grad_of(rows)
        r["dx2"][rows, :] = grad
        r["dmod"][q, :, 3 * width : 4 * width] = shift_grad
        r["dmod"][q, :, 4 * width : 5 * width] = scale_grad
        r["dmod"][q, :, 2 * width : 3 * width] = jnp.sum(
            grad * r["branch"][rows, :].astype(F32), axis=0, keepdims=True
        )
        r["dbranch"][rows, :] = (gate * grad).astype(BF16)

    each_quarter(quarter_rows, middle)

    def proj(n, product):
        r["datt"][:, columns_of(n)] = product(0, r["dbranch"][...], True).astype(BF16)

    stream.run(first + 2, proj)
    done("dbranch")

    def mix(block):
        rows, allowed = allowed_of(*segments, block)
        attend_back(r["qkv"], r["datt"], rows, allowed, r["total"], r["dqkv"])

    each_block(total_rows, mix)
    done("dqkv")

    def qkv(n, product):
        grad = None
        for k in range(3):
            part = product(k, r["dqkv"][:, k * width : (k + 1) * width], True)
            grad = part if grad is None else grad + part
        r["da1"][:, columns_of(n)] = grad

    stream.run(first + 3, qkv, ahead=False)

    def outer(q, rows):
        scale = piece_of(mod_ref, q, 1, width)
        grad, shift_grad, scale_grad = modulate_back(r["da1"][rows, :], r["x"][rows, :], scale)
        r["dmod"][q, :, :width] = shift_grad
        r["dmod"][q, :, width : 2 * width] = scale_grad
        finish(q, rows, grad + r["dx2"][rows, :])

    each_quarter(quarter_rows, outer)
    done("dmod")


def placed(kept_ref, m, slot):
    kept = kept_ref[m]
    positions = lax.broadcasted_iota(jnp.int32, (slot, kept.shape[1]), 0)
    return jnp.where(positions == kept, 1.0, 0.0).astype(BF16)


class Copies:
    def __init__(self, sems):
        self.sems, self.count, self.pending = sems, 0, []

    def start(self, src, dst):
        copy = pltpu.make_async_copy(src, dst, self.sems.at[self.count])
        self.count += 1
        copy.start()
        self.pending.append(copy)
        return copy

    def finish(self):
        for copy in self.pending:
            copy.wait()
        self.pending = []


def encode_kernel(names, tokens, kept_ref, mod_ref, row_ref, column_ref, wq, wp, wu, wd, *rest):
    outs, scratch = rest[: len(names)], rest[len(names) :]
    r = dict(zip(names + ("total",), scratch[: len(names) + 1]))
    loaded, wide, tall, stream_sems, sems = scratch[len(names) + 1 :]
    width = loaded.shape[2]
    slot = loaded.shape[1]

    def work():
        stream = Stream(wide, tall, stream_sems, width)
        forward_stages(stream, (wq, wp, wu, wd))
        copies = Copies(sems)
        copies.start(tokens, loaded)
        stream.begin(0)
        copies.finish()
        kept = kept_ref.shape[2]
        for m in range(2):
            r["x"][m * kept : (m + 1) * kept, :] = dot_rows(placed(kept_ref, m, slot), loaded[m])
        total_rows = r["x"].shape[0]
        out_of = dict(zip(names, outs))

        def done(name):
            copies.start(r[name], out_of[name].at[pl.ds(0, total_rows)])

        def finish_tile(n, columns, mlp):
            out_tile(r, mod_ref, total_rows // 8, columns, mlp)

        run_forward(stream, r, mod_ref, (row_ref, column_ref), total_rows // 8, finish_tile, done)
        for name in ("x", "x2", "qkv", "branch", "slope", "mlp", "out"):
            done(name)
        copies.finish()

    when(lax.axis_index("section") == 0, work)


def decode_kernel(
    names, rights, received, cotangent, kept_ref, mask_ref, mod_ref, row_ref, column_ref, wq, wp, wu, wd,
    a1, att, a2, act, *rest,
):
    outs, scratch = rest[: 4 + len(rights) + 4], rest[4 + len(rights) + 4 :]
    lefts = dict(zip(("a1", "att", "a2", "act"), outs[:4]))
    right_outs = dict(zip(rights, outs[4 : 4 + len(rights)]))
    dmod_out, decoded, back, mask_out = outs[4 + len(rights) :]
    r = dict(zip(names, scratch[: len(names)]))
    got, wide, tall, stream_sems, sems = scratch[len(names) :]
    width = got.shape[2]

    def work():
        stream = Stream(wide, tall, stream_sems, width)
        forward_stages(stream, (wq, wp, wu, wd))
        backward_stages(stream, (wq, wp, wu, wd))
        copies = Copies(sems)
        copies.start(received, got)
        copies.start(cotangent, r["dy"])
        stream.begin(0)
        copies.finish()
        total_rows = r["x"].shape[0]
        slot, kept = total_rows // 2, kept_ref.shape[2]
        for m in range(2):
            place = placed(kept_ref, m, slot)
            flags = jnp.sum(place.astype(F32), axis=1, keepdims=True)
            r["free"][m * slot : (m + 1) * slot, :] = jnp.broadcast_to(1.0 - flags, (slot, 128))
            filled = dot(place, got[m]) + (1.0 - flags) * mask_ref[...].astype(F32)
            r["x"][m * slot : (m + 1) * slot, :] = filled
        out_of = {**lefts, **right_outs, "dmod": dmod_out, "slope": right_outs["dhid"]}

        def done(name):
            copies.start(r[name], out_of[name])

        def finish_tile(n, columns, mlp):
            def gated(q, rows):
                gate = piece_of(mod_ref, q, 5, width, columns)
                dy = r["dy"][rows, columns].astype(F32)
                part = mlp[rows]
                r["out"][rows, columns] = (r["x2"][rows, columns] + gate * part).astype(BF16)
                r["dmlp"][rows, columns] = (gate * dy).astype(BF16)
                r["dmod"][q, :, pl.ds(5 * width + columns.start, TILE)] = jnp.sum(
                    dy * part, axis=0, keepdims=True
                )

            split_quarters(total_rows // 8, gated)

        segments = (row_ref, column_ref)
        run_forward(stream, r, mod_ref, segments, total_rows // 8, finish_tile, done)
        copies.start(r["out"], decoded)
        r["mask"][...] = jnp.zeros_like(r["mask"])

        def finish(q, rows, grad):
            r["mask"][...] += jnp.sum(grad * r["free"][rows, :1], axis=0, keepdims=True)
            r["dbranch"][rows, :] = grad.astype(BF16)

        def grad_of(rows):
            return r["dy"][rows, :].astype(F32)

        def done_back(name):
            if name == "dbranch":
                copies.start(r[name], out_of[name]).wait()
                copies.pending.pop()
            else:
                done(name)

        run_backward(stream, 4, r, mod_ref, segments, total_rows // 8, grad_of, finish, done_back)
        for m in range(2):
            place = placed(kept_ref, m, slot)
            got[m] = dot_rows(place, r["dbranch"][m * slot : (m + 1) * slot, :]).astype(BF16)
        copies.start(got, back)
        copies.start(r["mask"], mask_out)
        copies.finish()

    when(lax.axis_index("section") == 1, work)


def encode_back_kernel(
    names, rights, saved, received, kept_ref, mod_ref, row_ref, column_ref, wq, wp, wu, wd, *rest
):
    kept_in = dict(zip(saved, rest[: len(saved)]))
    rest = rest[len(saved) + len(rights) + 1 :]
    right_outs = dict(zip(rights, rest[: len(rights)]))
    dmod_out, token_out = rest[len(rights) : len(rights) + 2]
    scratch = rest[len(rights) + 2 :]
    r = dict(zip(names, scratch[: len(names)]))
    wide, tall, stream_sems, sems = scratch[len(names) :]
    width = r["x"].shape[1]

    def work():
        stream = Stream(wide, tall, stream_sems, width)
        backward_stages(stream, (wq, wp, wu, wd))
        copies = Copies(sems)
        copies.start(received, r["dy"])
        for name in saved:
            copies.start(kept_in[name], r[name])
        stream.begin(0)
        copies.finish()
        total_rows = r["x"].shape[0]
        out_of = {**right_outs, "dmod": dmod_out, "slope": right_outs["dhid"]}

        def done(name):
            if name == "dmod":
                copies.start(r[name], out_of[name])
            else:
                copies.start(r[name], out_of[name].at[pl.ds(0, total_rows)])

        def start(q, rows):
            gate = piece_of(mod_ref, q, 5, width)
            dy = r["dy"][rows, :].astype(F32)
            r["dmlp"][rows, :] = (gate * dy).astype(BF16)
            r["dmod"][q, :, 5 * width :] = jnp.sum(dy * r["mlp"][rows, :].astype(F32), axis=0, keepdims=True)

        each_quarter(total_rows // 8, start)

        def finish(q, rows, grad):
            r["mlp"][rows, :] = grad.astype(BF16)

        def grad_of(rows):
            return r["dy"][rows, :].astype(F32)

        segments = (row_ref, column_ref)
        run_backward(stream, 0, r, mod_ref, segments, total_rows // 8, grad_of, finish, done)
        kept = kept_ref.shape[2]
        slot = token_out.shape[1]
        for m in range(2):
            place = placed(kept_ref, m, slot)
            r["tokens"][m] = dot(place, r["mlp"][m * kept : (m + 1) * kept, :]).astype(BF16)
        copies.start(r["tokens"], token_out)
        copies.finish()

    when(lax.axis_index("section") == 0, work)


VMEM_BYTES = 60 * 1024 * 1024
LEFTS = ("a1", "att", "a2", "act")
RIGHTS = ("dqkv", "dbranch", "dhid", "dmlp")
SAVED = ("x", "x2", "qkv", "branch", "slope", "mlp")
anywhere = pl.BlockSpec(memory_space=pl.ANY)
in_vmem = pl.BlockSpec(memory_space=pltpu.VMEM)


def buffer_shapes(rows, width, wide_width):
    full, broad = lambda t: ((rows, width), t), lambda n, t: ((rows, n), t)
    return {
        "x": full(F32), "x2": full(F32), "dx2": full(F32), "da1": full(F32), "a1": full(BF16),
        "att": full(BF16), "a2": full(BF16), "branch": full(BF16), "mlp": full(BF16), "out": full(BF16),
        "dy": full(BF16), "dmlp": full(BF16), "dbranch": full(BF16), "datt": full(BF16),
        "qkv": broad(3 * width, BF16), "dqkv": broad(3 * width, BF16), "act": broad(wide_width, BF16),
        "slope": broad(wide_width, BF16), "dhid": broad(wide_width, BF16),
        "dmod": ((8, 1, 6 * width), F32), "mask": ((1, width), F32), "free": ((rows, 128), F32),
        "total": ((ATT_ROWS, 3 * width), F32),
    }


def rings(width, forward, backward):
    dma = pltpu.SemaphoreType.DMA
    none = (2, 1, 8, 128)
    return [
        pltpu.VMEM((2, DEPTH, width, TILE) if forward else none, BF16),
        pltpu.VMEM((2, DEPTH, TILE, width) if backward else none, BF16),
        dma((2, DEPTH)),
        dma((24,)),
    ]


def encode(tokens, kept, modulation, segments, weights, rows, all_rows):
    width, wide_width = weights[0].shape[0], weights[2].shape[1]
    shapes = buffer_shapes(rows, width, wide_width)
    names = LEFTS + SAVED + ("out",)
    outs = [jax.ShapeDtypeStruct(((all_rows if n in LEFTS else rows), shapes[n][0][1]), shapes[n][1]) for n in names]
    results = pl.pallas_call(
        functools.partial(encode_kernel, names),
        out_shape=outs,
        in_specs=[anywhere] + [in_vmem] * 4 + [anywhere] * 4,
        out_specs=[anywhere] * len(names),
        scratch_shapes=[pltpu.VMEM(*shapes[n]) for n in names + ("total",)]
        + [pltpu.VMEM(tokens.shape, BF16)]
        + rings(width, True, False),
        compiler_params=pltpu.CompilerParams(vmem_limit_bytes=VMEM_BYTES),
        name="encode",
    )(tokens, kept, modulation, *segments, *weights)
    return results[:4], results[4:-1], results[-1]


def decode(received, cotangent, kept, mask_token, modulation, segments, weights, lefts):
    width, wide_width = weights[0].shape[0], weights[2].shape[1]
    rows = cotangent.shape[0]
    shapes = buffer_shapes(rows, width, wide_width)
    names = LEFTS + (
        "x", "x2", "qkv", "branch", "slope", "out", "dy", "dmlp", "dbranch", "datt", "dqkv", "dmod",
        "mask", "free", "total",
    )
    scratch = [pltpu.VMEM(*shapes[n]) for n in names]
    names += ("dx2", "da1")
    scratch += [pltpu.VMEM(*shapes["dx2"]), pltpu.VMEM(*shapes["da1"])]
    outs = [jax.ShapeDtypeStruct(*shapes[n]) for n in LEFTS + RIGHTS + ("dmod", "out")]
    outs += [jax.ShapeDtypeStruct(received.shape, BF16), jax.ShapeDtypeStruct((1, width), F32)]
    results = pl.pallas_call(
        functools.partial(decode_kernel, names, RIGHTS),
        out_shape=outs,
        in_specs=[anywhere] * 2 + [in_vmem] * 5 + [anywhere] * 8,
        out_specs=[anywhere] * len(outs),
        scratch_shapes=scratch + [pltpu.VMEM(received.shape, BF16)] + rings(width, True, True),
        input_output_aliases={11 + j: j for j in range(4)},
        compiler_params=pltpu.CompilerParams(vmem_limit_bytes=VMEM_BYTES),
        name="decode",
    )(received, cotangent, kept, mask_token, modulation, *segments, *weights, *lefts)
    return results[:4], results[4:8], results[8:]


def encode_back(received, kept, modulation, segments, weights, saved, rights, grad_mod, token_shape):
    width, wide_width = weights[0].shape[0], weights[2].shape[1]
    rows = received.shape[0]
    shapes = buffer_shapes(rows, width, wide_width)
    names = SAVED + ("dy", "dmlp", "dbranch", "datt", "dqkv", "dmod", "dx2", "da1", "total", "tokens")
    shapes["tokens"] = (token_shape, BF16)
    outs = [jax.ShapeDtypeStruct(x.shape, x.dtype) for x in tuple(rights) + (grad_mod,)]
    outs.append(jax.ShapeDtypeStruct(token_shape, BF16))
    before = 9 + len(saved)
    results = pl.pallas_call(
        functools.partial(encode_back_kernel, names, RIGHTS, SAVED),
        out_shape=outs,
        in_specs=[anywhere] + [in_vmem] * 4 + [anywhere] * (4 + len(saved) + 5),
        out_specs=[anywhere] * len(outs),
        scratch_shapes=[pltpu.VMEM(*shapes[n]) for n in names] + rings(width, False, True),
        input_output_aliases={before + j: j for j in range(5)},
        compiler_params=pltpu.CompilerParams(vmem_limit_bytes=VMEM_BYTES),
        name="encode_back",
    )(received, kept, modulation, *segments, *weights, *saved, *rights, grad_mod)
    return results[:4], results[4], results[5]


def gather_encode_kernel(length, plan, names, *refs):
    sources, (partial, big_ref, tokens, kept_ref, row_ref, column_ref) = refs[:4], refs[4:10]
    outs, (mod_out, received) = refs[10:14], refs[14:16]
    saved_outs = refs[16 : 16 + len(names)]
    rest = refs[16 + len(names) :]
    r = dict(zip(names + ("out", "total"), rest[: len(names) + 2]))
    (
        loaded, mod_ref, tiles, last_tile, part_held, part_core, part_pair, part_line,
    ) = rest[len(names) + 2 : len(names) + 10]
    sems = rest[len(names) + 10 : len(names) + 19]
    part_sems, line_sems, tile_sems, out_sems, copy_sems = rest[len(names) + 19 :]
    a, b, c = position()
    encoder = lax.axis_index("section") == 0
    other = {"section": 1 - lax.axis_index("section")}
    barrier = pltpu.get_barrier_semaphore()

    def tell(target):
        pl.semaphore_signal(barrier, inc=1, device_id=target, device_id_type=MESH)

    tell(at(a, 1 - b, c))
    tell(at(a, b, 1 - c))
    tell(other)
    for k in range(1, length):
        tell(at(lax.rem(a + k, length), b, c))
    pl.semaphore_wait(barrier, length + 2)

    n = len(plan)
    width = r["x"].shape[1]
    total_rows = r["x"].shape[0]
    quarter_rows = total_rows // 8
    issue, move, complete, drain = gather_moves(length, plan, sources, outs, sems, a, b, c)
    copies = Copies(copy_sems)
    out_of = dict(zip(names, saved_outs))

    part_load = pltpu.make_async_copy(partial.at[:, :, c], part_held, part_sems.at[0])
    part_to_core = remote(partial.at[:, :, 1 - c], part_core, part_sems.at[1], part_sems.at[2], at(a, b, 1 - c))
    part_across = remote(part_held.at[:, 1 - b], part_pair, part_sems.at[3], part_sems.at[4], at(a, 1 - b, c))

    def part_to_line(k):
        to = lax.rem(a + k, length)
        return remote(
            part_held.at[to, b], part_line.at[k - 1], line_sems.at[0, k - 1], line_sems.at[1, k - 1], at(to, b, c)
        )

    def add_part(where, got):
        part_held[where] = part_held[where] + got

    def part_first():
        part_to_core.wait_recv()
        part_load.wait()
        for s in range(2 * length):
            add_part((s // 2, s % 2), part_core[s // 2, s % 2])
        part_across.start()

    def part_second():
        part_across.wait()
        for aa in range(length):
            add_part((aa, b), part_pair[aa])
        for k in range(1, length):
            part_to_line(k).start()

    def part_last():
        total = part_held[a, b].astype(F32)
        for k in range(1, length):
            part_to_line(k).wait_recv()
            total = total + part_line[k - 1].astype(F32)
        for q in range(8):
            first = q // SMALL_PER * SMALL_PER
            mod_ref[q] = jnp.where(big_ref[q] > 0, total[first : first + 1], total[q : q + 1])
        copies.start(mod_ref, mod_out)

    def load_tile(w, low, t):
        src = outs[w].at[:, :, :, :, pl.ds(low + t * TILE, TILE)]
        return pltpu.make_async_copy(src, tiles.at[t % 2], tile_sems.at[t % 2])

    def products(w, low, left, put):
        count = width // TILE
        for t in range(min(2, count)):
            load_tile(w, low, t).start()
        for t in range(count):
            load_tile(w, low, t).wait()
            tile = tiles[t % 2].astype(F32).reshape(width, TILE).astype(BF16)
            result = dot(r[left][...], tile)
            if t + 2 < count:
                load_tile(w, low, t + 2).start()
            put(columns_of(low // TILE + t), result)

    def done(name):
        copies.start(r[name], out_of[name].at[pl.ds(0, total_rows)])

    def start_encode():
        fetch = pltpu.make_async_copy(tokens, loaded, tile_sems.at[2])
        fetch.start()
        fetch.wait()
        kept, slot = kept_ref.shape[2], loaded.shape[1]
        for m in range(2):
            r["x"][m * kept : (m + 1) * kept, :] = dot_rows(placed(kept_ref, m, slot), loaded[m])

    def put_qkv(columns, result):
        r["qkv"][:, columns] = result.astype(BF16)

    def put_proj(columns, result):
        proj_tile(r, mod_ref, quarter_rows, columns, result)

    def put_up(columns, result):
        up_tile(r, columns, result)

    def send_out(t):
        columns = columns_of(t)
        return remote(
            r["out"].at[:, columns], received.at[:, columns], out_sems.at[0, t], out_sems.at[1, t], other
        )

    def encode_chunk(i):
        w, low, _, _ = plan[i]
        if w == 0:
            if i == 0:
                modulate(r["x"], mod_ref, r["a1"], 0, quarter_rows)
            products(w, low, "a1", put_qkv)
        elif w == 1:
            rows, allowed = slice(0, total_rows), row_ref[...] == column_ref[0]
            attend(r["qkv"], rows, allowed, r["total"], r["att"])
            products(w, low, "att", put_proj)
            modulate(r["x2"], mod_ref, r["a2"], 3, quarter_rows)
        elif w == 2:
            products(w, low, "a2", put_up)
        else:
            src = outs[w].at[:, :, :, :, pl.ds(low, TILE)]
            fetch = pltpu.make_async_copy(src, last_tile, tile_sems.at[2])
            fetch.start()
            fetch.wait()
            tile = last_tile[...].reshape(r["act"].shape[1], TILE)
            out_tile(r, mod_ref, quarter_rows, columns_of(low // TILE), dot(r["act"][...], tile))
            send_out(low // TILE).start()

    part_load.start()
    part_to_core.start()
    issue(0)
    when(encoder, start_encode)
    part_first()
    for i in range(1, AHEAD):
        issue(i)
    for t in range(n + length - 1):
        move(t, AHEAD)
        if t == 0:
            part_second()
        if t == 1:
            part_last()
        i = t - length + 1
        if i >= 0:
            complete(i)
            when(encoder, lambda: encode_chunk(i))
    for i in range(n):
        drain(i)
    part_to_core.wait_send()
    for k in range(1, length):
        part_to_line(k).wait_send()

    def close():
        for name in names:
            done(name)
        for copy in copies.pending[1:]:
            copy.wait()
        for t in range(width // TILE):
            send_out(t).wait_send()

    when(encoder, close)
    copies.pending[0].wait()

    def arrive():
        for t in range(width // TILE):
            send_out(t).wait_recv()

    when(jnp.logical_not(encoder), arrive)


AHEAD = 4


def gather_encode(shards, partial, big, tokens, kept, segments, plan, length, rows, all_rows):
    n = len(plan)
    width, wide_width = shards[1].shape[1], shards[2].shape[1]
    shapes = buffer_shapes(rows, width, wide_width)
    names = LEFTS + SAVED
    quarters = partial.shape[3]
    part_slab = partial.shape[3:]
    dma = pltpu.SemaphoreType.DMA
    outs = [jax.ShapeDtypeStruct((length, 2, 2) + s.shape, BF16) for s in shards]
    outs += [jax.ShapeDtypeStruct((quarters, 1, 6 * width), F32), jax.ShapeDtypeStruct((rows, width), BF16)]
    outs += [jax.ShapeDtypeStruct(((all_rows if m in LEFTS else rows), shapes[m][0][1]), shapes[m][1]) for m in names]
    results = pl.pallas_call(
        functools.partial(gather_encode_kernel, length, plan, names),
        out_shape=outs,
        in_specs=[anywhere] * 5 + [in_vmem, anywhere] + [in_vmem] * 3,
        out_specs=[anywhere] * len(outs),
        scratch_shapes=[pltpu.VMEM(*shapes[m]) for m in names + ("out", "total")]
        + [
            pltpu.VMEM(tokens.shape, BF16),
            pltpu.VMEM((quarters, 1, 6 * width), F32),
            pltpu.VMEM((2, length, 2, 2, shards[0].shape[0], TILE), BF16),
            pltpu.VMEM((length, 2, 2, shards[3].shape[0], TILE), BF16),
            pltpu.VMEM((length, 2) + part_slab, BF16),
            pltpu.VMEM((length, 2) + part_slab, BF16),
            pltpu.VMEM((length,) + part_slab, BF16),
            pltpu.VMEM((length - 1,) + part_slab, BF16),
        ]
        + [dma((n, length, 2))] * 4
        + [dma((n, length))] * 2
        + [dma((n, length, 2))] * 2
        + [dma((n,)), dma((5,)), dma((2, length - 1)), dma((3,)), dma((2, width // TILE)), dma((len(names) + 1,))],
        compiler_params=pltpu.CompilerParams(
            collective_id=0, has_side_effects=True, vmem_limit_bytes=VMEM_BYTES
        ),
        name="gather_encode",
    )(*shards, partial, big, tokens, kept, *segments)
    return results[:4], results[4], results[5], results[6:10], results[10:]


def plan_of(widths, lead, unit, line_first):
    plan = [(w, low, unit) for w, width in enumerate(widths) for low in range(0, width, unit)]
    plan += [(len(widths), j, 0) for j in range(lead)]
    return tuple(p + ("line" if i in line_first else "pair",) for i, p in enumerate(plan))


def swap_sections(x):
    return lax.ppermute(x, "section", [(0, 1), (1, 0)])


def on_device(
    tokens, kept_index, big_image, timesteps, labels, cotangent, mask_token, time_weight, class_table,
    ada_weight, ada_bias, qkv_weight, proj_weight, up_weight, down_weight,
):
    section = lax.axis_index("section")
    me = lax.axis_index("dp")
    devices = lax.axis_size("dp")
    micro, slot, width = tokens.shape
    kept_count = kept_index.shape[1]
    own_width = ada_weight.shape[1]
    images = micro * SMALL_PER
    quarters = micro * SMALL_PER
    ada = ada_weight[0]

    length = devices // 4
    ids = jnp.concatenate([timesteps.reshape(1, images), labels.reshape(1, images)])
    if length == 4:
        ids = small_gather(jnp.pad(ids, ((0, 6), (0, 128 - images))), length, False, 2)
    else:
        ids = lax.all_gather(ids, "dp", axis=0)
    times = ids[:, 0, :images].reshape(devices * images)
    classes = ids[:, 1, :images].reshape(devices * images)
    half = time_weight.shape[0] // 2
    frequencies = jnp.exp(-math.log(10000.0) * jnp.arange(half, dtype=F32) / half)
    angles = times.astype(F32)[:, None] * frequencies[None, :]
    embedding = jnp.concatenate([jnp.cos(angles), jnp.sin(angles)], axis=-1).astype(BF16)
    onehot = (classes[:, None] == jnp.arange(class_table.shape[0])[None, :]).astype(BF16)
    cond = dot(embedding, time_weight) + dot(onehot, class_table)
    cond = lax.dynamic_slice_in_dim(cond, me * own_width, own_width, axis=1)
    lifted = jax.nn.silu(cond).astype(BF16)
    bias_width = ada_bias.shape[1]
    bias = lax.dynamic_update_slice_in_dim(
        jnp.zeros((1, 6 * width), F32), ada_bias.astype(F32), me * bias_width, axis=1
    )
    partial = (dot(lifted, ada) + bias).astype(BF16).reshape(devices, images, 6 * width)

    big = big_image[:, :1] > 0
    quarter_ids = jnp.arange(quarters, dtype=jnp.int32).reshape(micro, SMALL_PER)
    segment_of = jnp.where(big, quarter_ids[:, :1], quarter_ids).reshape(quarters)
    kept = kept_index.reshape(micro, 1, kept_count)

    def segments(quarter_rows):
        ids = jnp.repeat(segment_of, quarter_rows)
        return ids.reshape(-1, 1), ids.reshape(-1, 1, ATT_ROWS)

    enc_rows, dec_rows = micro * kept_count, micro * slot
    enc_segments = segments(enc_rows // quarters)
    dec_segments = segments(dec_rows // quarters)

    shards = (qkv_weight[0], proj_weight[0], up_weight[0])
    lead = down_weight.shape[1] // qkv_weight.shape[1]
    widths = [x.shape[1] for x in shards]
    if length == 4:
        plan = [(w, low, width, "line") for w in range(3) for low in range(0, widths[w], width)]
        plan += [(3, low, TILE, "line") for low in range(0, width, TILE)]
        plan = tuple(p[:3] + ("pair" if i in (1, 7) else "line",) for i, p in enumerate(plan))
        flags = jnp.repeat(big[:, 0], SMALL_PER).astype(jnp.int32).reshape(quarters, 1, 1)
        whole, modulation, received, lefts, saved = gather_encode(
            shards + (down_weight[0],), partial.reshape((length, 2, 2) + partial.shape[1:]), flags, tokens, kept,
            enc_segments, plan, length, enc_rows, dec_rows,
        )
        weights = tuple(w.reshape(-1, w.shape[-1]) for w in whole)
        received = received.reshape(micro, kept_count, width)
    else:
        whole = (lax.all_gather(x, "dp", axis=0, tiled=True) for x in shards + (down_weight[0],))
        weights = tuple(whole)
        modulation = lax.psum_scatter(partial, "dp", scatter_dimension=0, tiled=False).astype(F32)
        modulation = modulation.reshape(micro, SMALL_PER, 6 * width)
        modulation = jnp.where(big[:, :, None], modulation[:, :1], modulation).reshape(quarters, 1, 6 * width)
        lefts, saved, encoded = encode(tokens, kept, modulation, enc_segments, weights, enc_rows, dec_rows)
        received = swap_sections(encoded).reshape(micro, kept_count, width)

    lefts, rights, (grad_mod, decoded, back, mask_part) = decode(
        received, cotangent.reshape(dec_rows, width), kept, mask_token.reshape(1, width), modulation,
        dec_segments, weights, lefts,
    )
    received = swap_sections(back).reshape(enc_rows, width)
    rights, grad_mod, token_grad = encode_back(
        received, kept, modulation, enc_segments, weights, saved, rights, grad_mod, (micro, slot, width)
    )
    decoded = decoded.reshape(micro, slot, width)
    mask_part = jnp.where(section == 1, mask_part, 0.0).reshape(width)

    half_width = width // 2
    outgoing = jnp.where(section == 0, token_grad[:, :, half_width:], decoded[:, :, :half_width])
    incoming = swap_sections(outgoing)
    decoded_half = jnp.where(section == 0, incoming, decoded[:, :, half_width:])
    token_half = jnp.where(section == 0, token_grad[:, :, :half_width], incoming)

    grad_mod = grad_mod.reshape(micro, SMALL_PER, 6 * width)
    first_only = (jnp.arange(SMALL_PER) == 0)[None, :, None]
    grad_mod = jnp.where(
        big[:, :, None], jnp.where(first_only, jnp.sum(grad_mod, axis=1, keepdims=True), 0.0), grad_mod
    )
    grad_mod = grad_mod.reshape(images, 6 * width).astype(BF16)
    every_mod = lax.all_gather(grad_mod, "dp", axis=0, tiled=True)
    ada_grad = dot_rows(lifted, every_mod)
    bias_grad = jnp.sum(
        lax.dynamic_slice_in_dim(every_mod, me * bias_width, bias_width, axis=1).astype(F32), axis=0
    )
    grad_lifted = dot_back(every_mod, ada)
    _, pull = jax.vjp(jax.nn.silu, cond)
    grad_cond = pull(grad_lifted)[0]
    mask_rows = mask_part.reshape(-1, devices * images) if length == 4 else None
    if length == 4:
        payload = jnp.concatenate([grad_cond.T, mask_rows])
        extra = -payload.shape[0] % 8
        payload = small_gather(jnp.pad(payload, ((0, extra), (0, 0))), length, True, 3)
        every_cond = payload[:, :own_width].reshape(width, devices * images)
        mask_grad = jnp.sum(payload[:, own_width : own_width + mask_rows.shape[0]], axis=0).reshape(width)
    else:
        every_cond = lax.psum(lax.all_gather(grad_cond.T, "dp", axis=0, tiled=True), "section")
        mask_grad = lax.psum(mask_part, ("section", "dp"))
    inputs = jnp.concatenate([embedding, onehot], axis=1)
    shared = lax.dot_general(
        inputs, every_cond.astype(BF16), (((0,), (1,)), ((), ())), preferred_element_type=F32
    )
    time_grad, table_grad = shared[: time_weight.shape[0]], shared[time_weight.shape[0] :]

    shapes = tuple(x.shape for x in shards) + ((lead, own_width, width),)
    half_rows = jnp.arange(dec_rows)[:, None] < jnp.where(section == 0, enc_rows, dec_rows)
    if length == 4:
        plan = plan_of(widths, lead, width, (0, 6))
        mine = scatter_all(lefts, rights, shapes, plan, length)
    else:
        lefts, rights = ([jnp.where(half_rows, x, jnp.zeros_like(x)) for x in xs] for xs in (lefts, rights))
        split = (dot_rows(x, y).astype(BF16).reshape((devices,) + s) for x, y, s in zip(lefts, rights, shapes))
        mine = tuple(lax.psum_scatter(g, "dp", scatter_dimension=0) for g in split)
    qkv_grad, proj_grad, up_grad, down_grad = (g.astype(F32) for g in mine)
    return (
        decoded_half,
        token_half,
        mask_grad,
        time_grad,
        table_grad,
        ada_grad[None],
        bias_grad[None],
        qkv_grad[None],
        proj_grad[None],
        up_grad[None],
        down_grad.reshape(down_weight.shape),
    )


def solution(mesh):
    rows = P(None, "dp", None)
    ids = P(None, "dp")
    weight = P("section", "dp", None)
    halves = P(None, "dp", "section")
    in_specs = (rows, ids, ids, ids, ids, rows, P(), P(), P(), weight, P("section", "dp")) + (weight,) * 4
    out_specs = (halves, halves, P(), P(), P(), weight, P("section", "dp")) + (weight,) * 4
    return jax.shard_map(
        on_device, mesh=mesh, in_specs=in_specs, out_specs=out_specs, check_vma=False
    )
```

```python
import functools
import math

import jax
import jax.numpy as jnp
from jax import lax
from jax.experimental import pallas as pl
from jax.experimental.pallas import tpu as pltpu
from jax.sharding import PartitionSpec as P

HEADS = 16
HD = 72
SMALL_PER = 4
ATT_ROWS = 256
EPS = 1e-6
MASKED = -1e30
MESH = pl.DeviceIdType.MESH
F32 = jnp.float32
BF16 = jnp.bfloat16


anywhere = pl.BlockSpec(memory_space=pl.ANY)
in_vmem = pl.BlockSpec(memory_space=pltpu.VMEM)


def remote(src, dst, send_sem, recv_sem, target):
    return pltpu.make_async_remote_copy(
        src_ref=src,
        dst_ref=dst,
        send_sem=send_sem,
        recv_sem=recv_sem,
        device_id=target,
        device_id_type=MESH,
    )


def when(condition, run):
    pl.when(condition)(run)


def position():
    me = lax.axis_index("dp")
    return me // 4, (me // 2) % 2, me % 2


def at(line, pair, core):
    return {"dp": (line * 2 + pair) * 2 + core}


def greet(length, a, b, c):
    has_up, has_down = a < length - 1, a > 0
    barrier = pltpu.get_barrier_semaphore()

    def tell(target):
        pl.semaphore_signal(barrier, inc=1, device_id=target, device_id_type=MESH)

    tell(at(a, 1 - b, c))
    tell(at(a, b, 1 - c))
    when(has_up, lambda: tell(at(a + 1, b, c)))
    when(has_down, lambda: tell(at(a - 1, b, c)))
    pl.semaphore_wait(barrier, 2 + has_up.astype(jnp.int32) + has_down.astype(jnp.int32))
    return has_up, has_down


def piece(ref, lead, plan_entry):
    _, low, size, _ = plan_entry
    if size == 0:
        return ref.at[lead + (low,)]
    return ref.at[lead + (slice(None), pl.ds(low, size))]


def gather_moves(length, plan, sources, outs, sems, a, b, c):
    up_s, up_r, down_s, down_r, pair_s, pair_r, core_s, core_r, own_sem = sems
    has_up, has_down = a < length - 1, a > 0
    chunks = range(len(plan))
    line_first = [plan[i][3] == "line" for i in chunks]

    def slot(i, aa, bb, cc):
        return piece(outs[plan[i][0]], (aa, bb, cc), plan[i])

    def own(i):
        return piece(sources[plan[i][0]], (), plan[i])

    def rows_of(i):
        return (b,) if line_first[i] else (b, 1 - b)

    def up(i, k, bb, src=None):
        s = slot(i, a - k, bb, c)
        return remote(s if src is None else src, s, up_s.at[i, k, bb], up_r.at[i, k, bb], at(a + 1, b, c))

    def up_arrival(i, k, bb):
        s = slot(i, a - 1 - k, bb, c)
        return remote(s, s, up_s.at[i, k, bb], up_r.at[i, k, bb], at(a + 1, b, c))

    def down(i, k, bb, src=None):
        s = slot(i, a + k, bb, c)
        return remote(s if src is None else src, s, down_s.at[i, k, bb], down_r.at[i, k, bb], at(a - 1, b, c))

    def down_arrival(i, k, bb):
        s = slot(i, a + 1 + k, bb, c)
        return remote(s, s, down_s.at[i, k, bb], down_r.at[i, k, bb], at(a - 1, b, c))

    def across(i, aa, src=None):
        s = slot(i, aa, b, c)
        return remote(s if src is None else src, s, pair_s.at[i, aa], pair_r.at[i, aa], at(a, 1 - b, c))

    def across_arrival(i, aa):
        s = slot(i, aa, 1 - b, c)
        return remote(s, s, pair_s.at[i, aa], pair_r.at[i, aa], at(a, 1 - b, c))

    def to_core(i, aa, bb, src=None):
        s = slot(i, aa, bb, c)
        return remote(s if src is None else src, s, core_s.at[i, aa, bb], core_r.at[i, aa, bb], at(a, b, 1 - c))

    def core_arrival(i, aa, bb):
        s = slot(i, aa, bb, 1 - c)
        return remote(s, s, core_s.at[i, aa, bb], core_r.at[i, aa, bb], at(a, b, 1 - c))

    def after_across(i, aa):
        across_arrival(i, aa).wait_recv()
        to_core(i, aa, 1 - b).start()

    def issue(i):
        src = own(i)
        pltpu.make_async_copy(src, slot(i, a, b, c), own_sem.at[i]).start()
        across(i, a, src).start()
        when(has_up, lambda: up(i, 0, b, src).start())
        when(has_down, lambda: down(i, 0, b, src).start())
        to_core(i, a, b, src).start()

    def pair_step(i):
        across_arrival(i, a).wait_recv()
        when(has_up, lambda: up(i, 0, 1 - b).start())
        when(has_down, lambda: down(i, 0, 1 - b).start())
        to_core(i, a, 1 - b).start()

    def line_step(i, k):
        for bb in rows_of(i):

            def from_below():
                up_arrival(i, k - 1, bb).wait_recv()
                when(has_up, lambda: up(i, k, bb).start())
                if line_first[i]:
                    across(i, a - k).start()
                to_core(i, a - k, bb).start()

            def from_above():
                down_arrival(i, k - 1, bb).wait_recv()
                when(has_down, lambda: down(i, k, bb).start())
                if line_first[i]:
                    across(i, a + k).start()
                to_core(i, a + k, bb).start()

            when(a - k >= 0, from_below)
            when(a + k <= length - 1, from_above)

    def across_step(i, k):
        if not line_first[i]:
            return
        if k == 0:
            after_across(i, a)
        else:
            when(a - k >= 0, lambda: after_across(i, a - k))
            when(a + k <= length - 1, lambda: after_across(i, a + k))

    def complete(i):
        pltpu.make_async_copy(own(i), slot(i, a, b, c), own_sem.at[i]).wait()
        for aa in range(length):
            for bb in range(2):
                core_arrival(i, aa, bb).wait_recv()

    def drain(i):
        for aa in range(length):
            for bb in range(2):
                to_core(i, aa, bb).wait_send()
            if line_first[i]:
                across(i, aa).wait_send()
        if not line_first[i]:
            across(i, a).wait_send()
        for k in range(length - 1):
            for bb in rows_of(i):
                when(jnp.logical_and(has_up, a - k >= 0), lambda: up(i, k, bb).wait_send())
                when(
                    jnp.logical_and(has_down, a + k <= length - 1),
                    lambda: down(i, k, bb).wait_send(),
                )

    def move(t, ahead):
        n = len(plan)
        if t + ahead < n:
            issue(t + ahead)
        if t < n and not line_first[t]:
            pair_step(t)
        for k in range(1, length):
            i = t - k + 1
            if 0 <= i < n:
                line_step(i, k)
        for k in range(length):
            i = t - k
            if 0 <= i < n:
                across_step(i, k)

    return issue, move, complete, drain


SIDE_TIMES = (2, 4, 5, 6, 8, 10)


def greet_all(length, a, b, c):
    barrier = pltpu.get_barrier_semaphore()

    def tell(target):
        pl.semaphore_signal(barrier, inc=1, device_id=target, device_id_type=MESH)

    tell(at(a, 1 - b, c))
    tell(at(a, b, 1 - c))
    tell({"section": 1 - lax.axis_index("section")})
    for k in range(1, length):
        tell(at(lax.rem(a + k, length), b, c))
    pl.semaphore_wait(barrier, length + 2)


def spread(length, buffer, sems, a, b, c):
    line_s, line_r, pair_core = sems

    def to_line(k):
        mine = buffer.at[a, b, c]
        return remote(mine, mine, line_s.at[k - 1], line_r.at[k - 1], at(lax.rem(a + k, length), b, c))

    def from_line(k):
        slab = buffer.at[lax.rem(a + length - k, length), b, c]
        return remote(slab, slab, line_s.at[k - 1], line_r.at[k - 1], at(a, 1 - b, c))

    def across(bb):
        part = buffer.at[:, bb, c]
        return remote(part, part, pair_core.at[0], pair_core.at[1], at(a, 1 - b, c))

    def to_core(cc):
        part = buffer.at[:, :, cc]
        return remote(part, part, pair_core.at[2], pair_core.at[3], at(a, b, 1 - c))

    def start():
        for k in range(1, length):
            to_line(k).start()

    def second():
        for k in range(1, length):
            from_line(k).wait_recv()
            to_line(k).wait_send()
        across(b).start()

    def third():
        across(1 - b).wait_recv()
        across(b).wait_send()
        to_core(c).start()

    def end():
        to_core(1 - c).wait_recv()
        to_core(c).wait_send()

    return start, second, third, end


def conditioning_steps(length, inputs, outputs, scratch, a, b, c):
    grad_mod, lifted_t, slope_t, ada, mask_rows = inputs
    ada_grad, bias_sum, shared = outputs
    every, stage, payload, other = scratch[:4]
    mod_sems, shared_sems, side_sems, stage_sems = scratch[4:7], scratch[7:10], scratch[10], scratch[11]
    mod_start, mod_second, mod_third, mod_end = spread(length, every, mod_sems, a, b, c)
    shared_start, shared_second, shared_third, shared_end = spread(length, shared, shared_sems, a, b, c)
    own_rows, images = lifted_t.shape
    mask_count = mask_rows.shape[0]
    width = stage.shape[2]
    count = grad_mod.shape[1] // width
    side = remote(payload, other, side_sems.at[0], side_sems.at[1], {"section": 1 - lax.axis_index("section")})

    def save(j):
        return pltpu.make_async_copy(
            stage.at[j % 2], ada_grad.at[:, pl.ds(j * width, width)], stage_sems.at[j % 2]
        )

    def begin():
        every[a, b, c] = grad_mod[...]
        mod_start()

    def compute():
        mod_end()
        total = None
        for j in range(count):
            columns = slice(j * width, (j + 1) * width)
            rows = every[:, :, :, :, columns].astype(F32).reshape(images, width)
            bias_sum[:, columns] = jnp.sum(rows, axis=0, keepdims=True)
            rows = rows.astype(BF16)
            if j >= 2:
                save(j - 2).wait()
            stage[j % 2] = dot(lifted_t[...], rows)
            save(j).start()
            part = dot_back(ada[:, columns], rows)
            total = part if total is None else total + part
        payload[...] = jnp.zeros_like(payload)
        payload[:own_rows, :] = total * slope_t[...]
        payload[own_rows : own_rows + mask_count, :] = mask_rows[...]
        side.start()

    def add():
        side.wait()
        shared[a, b, c] = payload[...] + other[...]
        shared_start()

    def end():
        shared_end()
        for j in range(count - 2, count):
            save(j).wait()

    return begin, mod_second, mod_third, compute, add, shared_second, shared_third, end


def scatter_kernel(length, plan, slots, pair_slots, *refs):
    lefts, rights = refs[:4], refs[4:8]
    extras = refs[8:13]
    outs = refs[13:17]
    extra_outs = refs[17:20]
    (
        raw, right, left_t, held, sent, core_in, pair_in, pair_late, up_in, down_in,
    ) = refs[20:30]
    (
        raw_sem, right_sem, core_s, core_r, pair_s, pair_r, up_s, up_r, down_s, down_r, out_sem,
        core_credit, pair_credit,
    ) = refs[30:43]
    a, b, c = position()
    greet_all(length, a, b, c)
    side_steps = conditioning_steps(length, extras, extra_outs, refs[43:], a, b, c)
    n = len(plan)
    rows, width = held.shape[3:]
    total_rows = raw.shape[1]
    encoder = lax.axis_index("section") == 0
    used_rows = jnp.where(encoder, total_rows // 2, total_rows)
    pair_first = [p[3] == "pair" for p in plan]
    order = [sum(pair_first[:i]) if pair_first[i] else i - sum(pair_first[:i]) for i in range(n)]
    base, total = [], 0
    for i in range(n):
        base.append(total)
        total += (length - 1) * (1 if pair_first[i] else 2)
    groups = 2 * length

    def blocks_of(w):
        return lefts[w].shape[1] // width

    raw_jobs = []
    right_jobs = []
    for i, (w, low, size, _) in enumerate(plan):
        if i == 0 or plan[i - 1][0] != w:
            raw_jobs += [(w, k) for k in range(blocks_of(w))]
        if size != 0 or plan[i - 1][0] != w:
            right_jobs.append(i)

    def raw_load(x):
        w, k = raw_jobs[x]
        src = lefts[w].at[:, pl.ds(k * width, width)]
        return pltpu.make_async_copy(src, raw.at[x % 2], raw_sem.at[x])

    def right_load(x):
        w, low, size, _ = plan[right_jobs[x]]
        src = rights[w].at[:, pl.ds(low if size else 0, width)]
        return pltpu.make_async_copy(src, right.at[x % 2], right_sem.at[x])

    progress = {"raw": 0, "right": -1}

    def turn(w):
        count = blocks_of(w)
        for k in range(count):
            x = progress["raw"]
            progress["raw"] += 1
            raw_load(x).wait()
            slot = x % 2

            def body(r, carry):
                start = pl.multiple_of(r * 128, 128)
                block = raw[slot, pl.ds(start, 128), :].astype(F32).T
                if count == 1:
                    split = block.reshape(groups, 2, rows, 128)
                    for q in range(2):
                        part = split[:, q].reshape(groups * rows, 128)
                        left_t[q, :, pl.ds(start, 128)] = part.astype(BF16)
                else:
                    near = groups // count
                    split = block.reshape(near, 2, count, rows, 128)
                    for q in range(2):
                        for j in range(count):
                            part = split[:, q, j].reshape(near * rows, 128)
                            left_t[
                                q * count + j, pl.ds(k * near * rows, near * rows), pl.ds(start, 128)
                            ] = part.astype(BF16)
                return carry

            lax.fori_loop(0, used_rows // 128, body, 0)
            if x + 2 < len(raw_jobs):
                raw_load(x + 2).start()

    def product(i, q, put):
        w, low, size, _ = plan[i]
        count = blocks_of(w)
        row_set = q if count == 1 else q * count + low
        slot = progress["right"] % 2
        tile = width // 3

        def body(k, carry):
            columns = pl.ds(pl.multiple_of(k * tile, 128), tile)

            def multiply(depth):
                result = dot(left_t[row_set, :, :depth], right[slot, :depth, columns])
                for s in range(groups):
                    put(s, columns, result[s * rows : (s + 1) * rows].astype(BF16))

            when(encoder, lambda: multiply(total_rows // 2))
            when(jnp.logical_not(encoder), lambda: multiply(total_rows))
            return carry

        lax.fori_loop(0, 3, body, 0)

    def to_core(i):
        return remote(sent.at[i % slots], core_in.at[i % slots], core_s.at[i], core_r.at[i], at(a, b, 1 - c))

    def across(i):
        target = at(a, 1 - b, c)
        if pair_first[i]:
            return remote(
                held.at[i, :, 1 - b], pair_in.at[order[i] % pair_slots], pair_s.at[i], pair_r.at[i], target
            )
        return remote(held.at[i, a, 1 - b], pair_late.at[order[i]], pair_s.at[i], pair_r.at[i], target)

    def rows_of(i):
        return (b,) if pair_first[i] else (b, 1 - b)

    def flow_index(i, dest, bb):
        if pair_first[i]:
            return base[i] + dest
        return base[i] + dest * 2 + bb

    def up(i, line, dest, bb):
        x = flow_index(i, dest - 1, bb)
        return remote(held.at[i, dest, bb], up_in.at[x], up_s.at[x], up_r.at[x], at(line + 1, b, c))

    def down(i, line, dest, bb):
        x = flow_index(i, dest, bb)
        return remote(held.at[i, dest, bb], down_in.at[x], down_s.at[x], down_r.at[x], at(line - 1, b, c))

    def add(dst, src):
        dst[...] = dst[...] + src[...]

    def credit(sem, target):
        pl.semaphore_signal(sem, inc=1, device_id=target, device_id_type=MESH)

    def produce(i):
        w = plan[i][0]
        if i == 0 or plan[i - 1][0] != w:
            turn(w)
        if progress["right"] + 1 < len(right_jobs) and right_jobs[progress["right"] + 1] == i:
            progress["right"] += 1
            right_load(progress["right"]).wait()
            if progress["right"] + 1 < len(right_jobs):
                right_load(progress["right"] + 1).start()
        if i >= slots:
            to_core(i - slots).wait_send()

        def put_sent(s, columns, value):
            sent[i % slots, s // 2, s % 2, :, columns] = value

        def put_held(s, columns, value):
            held[i, s // 2, s % 2, :, columns] = value

        product(i, 1 - c, put_sent)
        if i >= slots:
            pl.semaphore_wait(core_credit, 1)
        to_core(i).start()
        product(i, c, put_held)

    def first_add(i):
        to_core(i).wait_recv()

        def body(s, carry):
            add(held.at[i, s // 2, s % 2], core_in.at[i % slots, s // 2, s % 2])
            return carry

        lax.fori_loop(0, groups, body, 0)
        if i + slots < n:
            credit(core_credit, at(a, b, 1 - c))
        if pair_first[i]:
            if order[i] >= pair_slots:
                pl.semaphore_wait(pair_credit, 1)
            across(i).start()

    def second_add(i):
        if not pair_first[i]:
            return
        across(i).wait_recv()

        def body(s, carry):
            add(held.at[i, s, b], pair_in.at[order[i] % pair_slots, s])
            return carry

        lax.fori_loop(0, length, body, 0)
        if order[i] + pair_slots < sum(pair_first):
            credit(pair_credit, at(a, 1 - b, c))

    def line_step(i, j):
        def going_up():
            for dest in range(length - 1, j - 1, -1):
                for bb in rows_of(i):
                    if j > 0:
                        up(i, j - 1, dest, bb).wait_recv()
                        add(held.at[i, dest, bb], up_in.at[flow_index(i, dest - 1, bb)])
                    if dest > j:
                        up(i, j, dest, bb).start()

        def going_down():
            here = length - 1 - j
            for dest in range(0, here + 1):
                for bb in rows_of(i):
                    if j > 0:
                        down(i, here + 1, dest, bb).wait_recv()
                        add(held.at[i, dest, bb], down_in.at[flow_index(i, dest, bb)])
                    if dest < here:
                        down(i, here, dest, bb).start()

        when(a == j, going_up)
        when(a == length - 1 - j, going_down)

    def result(i):
        w, low, size, _ = plan[i]
        dst = outs[w].at[low] if size == 0 else outs[w].at[:, pl.ds(low, size)]
        return pltpu.make_async_copy(held.at[i, a, b], dst, out_sem.at[i])

    def finish(i):
        if pair_first[i]:
            result(i).start()
        else:
            across(i).start()

    def finish_late(i):
        if not pair_first[i]:
            across(i).wait_recv()
            add(held.at[i, a, b], pair_late.at[order[i]])
            result(i).start()

    side_steps[0]()
    raw_load(0).start()
    right_load(0).start()
    raw_load(1).start()
    produce(0)
    for t in range(n + length + 3):
        if t in SIDE_TIMES:
            side_steps[SIDE_TIMES.index(t) + 1]()
        if t < n:
            first_add(t)
        if t + 1 < n:
            produce(t + 1)
        if 0 <= t - 1 < n:
            second_add(t - 1)
        for j in range(length):
            if 0 <= t - 2 - j < n:
                line_step(t - 2 - j, j)
        if 0 <= t - 1 - length < n:
            finish(t - 1 - length)
        if 0 <= t - 2 - length < n:
            finish_late(t - 2 - length)
    side_steps[-1]()
    for i in range(n):
        if i >= n - slots:
            to_core(i).wait_send()
        across(i).wait_send()
        result(i).wait()
        for bb in rows_of(i):
            for here in range(length):

                def gone():
                    for dest in range(here + 1, length):
                        up(i, here, dest, bb).wait_send()
                    for dest in range(0, here):
                        down(i, here, dest, bb).wait_send()

                when(a == here, gone)


def scatter_all(lefts, rights, extras, shard_shapes, plan, length):
    n = len(plan)
    slots, pair_slots = 2, 4
    total_rows = lefts[0].shape[0]
    rows, width = shard_shapes[0][0], plan[0][2]
    late = sum(p[3] != "pair" for p in plan)
    flows = (length - 1) * (n + late)
    lead = shard_shapes[-1][0]
    dma = pltpu.SemaphoreType.DMA
    grad_mod, lifted_t, slope_t, ada, mask_rows = extras
    images = lifted_t.shape[1]
    payload = (-(-(rows + mask_rows.shape[0]) // 8) * 8, images)
    small = [dma((length - 1,)), dma((length - 1,)), dma((4,))]
    slab = (rows, width)
    return pl.pallas_call(
        functools.partial(scatter_kernel, length, plan, slots, pair_slots),
        out_shape=tuple(jax.ShapeDtypeStruct(s, BF16) for s in shard_shapes)
        + (
            jax.ShapeDtypeStruct(ada.shape, F32),
            jax.ShapeDtypeStruct((1, ada.shape[1]), F32),
            jax.ShapeDtypeStruct((length, 2, 2) + payload, F32),
        ),
        in_specs=[anywhere] * 8 + [in_vmem] * 5,
        out_specs=[anywhere] * 5 + [in_vmem] * 2,
        scratch_shapes=[
            pltpu.VMEM((2, total_rows, width), BF16),
            pltpu.VMEM((2, total_rows, width), BF16),
            pltpu.VMEM((2 * lead, 2 * length * rows, total_rows), BF16),
            pltpu.VMEM((n, length, 2) + slab, BF16),
            pltpu.VMEM((slots, length, 2) + slab, BF16),
            pltpu.VMEM((slots, length, 2) + slab, BF16),
            pltpu.VMEM((pair_slots, length) + slab, BF16),
            pltpu.VMEM((late,) + slab, BF16),
            pltpu.VMEM((flows,) + slab, BF16),
            pltpu.VMEM((flows,) + slab, BF16),
            dma((lead + 3,)), dma((n,)), dma((n,)), dma((n,)), dma((n,)), dma((n,)),
            dma((flows,)), dma((flows,)), dma((flows,)), dma((flows,)), dma((n,)),
            pltpu.SemaphoreType.REGULAR, pltpu.SemaphoreType.REGULAR,
            pltpu.VMEM((length, 2, 2) + grad_mod.shape, BF16),
            pltpu.VMEM((2, rows, width), F32),
            pltpu.VMEM(payload, F32),
            pltpu.VMEM(payload, F32),
        ]
        + small
        + small
        + [dma((2,)), dma((2,))],
        compiler_params=pltpu.CompilerParams(
            collective_id=1, has_side_effects=True, vmem_limit_bytes=62 * 1024 * 1024
        ),
        name="scatter_grads",
    )(*lefts, *rights, *extras)


def small_gather_kernel(length, sum_sections, own_ref, out_ref, other, *sems):
    line_s, line_r, pair_s, pair_r, core_s, core_r, side_s, side_r = sems
    a, b, c = position()
    partner = {"section": 1 - lax.axis_index("section")}
    barrier = pltpu.get_barrier_semaphore()

    def tell(target):
        pl.semaphore_signal(barrier, inc=1, device_id=target, device_id_type=MESH)

    tell(at(a, 1 - b, c))
    tell(at(a, b, 1 - c))
    for k in range(1, length):
        tell(at(lax.rem(a + k, length), b, c))
    if sum_sections:
        tell(partner)
    pl.semaphore_wait(barrier, length + 1 + int(sum_sections))
    value = own_ref[...]
    if sum_sections:
        side = remote(own_ref, other, side_s, side_r, partner)
        side.start()
        side.wait()
        value = value + other[...]
    out_ref[a, b, c] = value
    mine = out_ref.at[a, b, c]
    copies = []
    for k in range(1, length):
        to = lax.rem(a + k, length)
        copy = remote(mine, mine, line_s.at[k - 1], line_r.at[k - 1], at(to, b, c))
        copy.start()
        copies.append(copy)
    for k in range(1, length):
        source = lax.rem(a + length - k, length)
        slab = out_ref.at[source, b, c]
        remote(slab, slab, line_s.at[k - 1], line_r.at[k - 1], at(a, 1 - b, c)).wait_recv()
        copies[k - 1].wait_send()
    for go, come, s, r, to in (
        (out_ref.at[:, b, c], out_ref.at[:, 1 - b, c], pair_s, pair_r, at(a, 1 - b, c)),
        (out_ref.at[:, :, c], out_ref.at[:, :, 1 - c], core_s, core_r, at(a, b, 1 - c)),
    ):
        copy = remote(go, go, s, r, to)
        copy.start()
        remote(come, come, s, r, to).wait_recv()
        copy.wait_send()


def small_gather(own, length, sum_sections, collective_id):
    dma = pltpu.SemaphoreType.DMA
    vmem = pl.BlockSpec(memory_space=pltpu.VMEM)
    shape = (length, 2, 2) + own.shape
    return pl.pallas_call(
        functools.partial(small_gather_kernel, length, sum_sections),
        out_shape=jax.ShapeDtypeStruct(shape, own.dtype),
        in_specs=[vmem],
        out_specs=vmem,
        scratch_shapes=[
            pltpu.VMEM(own.shape, own.dtype), dma((length - 1,)), dma((length - 1,)), dma, dma, dma, dma, dma, dma,
        ],
        compiler_params=pltpu.CompilerParams(collective_id=collective_id, has_side_effects=True),
        name="small_gather",
    )(own).reshape((4 * length,) + own.shape)


def head_window(h):
    low, high = h * HD, h * HD + HD
    start = low // 128 * 128
    return low, high, start, -(-high // 128) * 128


def contract(x, y, dims):
    return lax.dot_general(x, y, ((dims[0], dims[1]), ((), ())), preferred_element_type=F32)


def head_operands(qkv_ref, rows, h):
    width = qkv_ref.shape[1] // 3
    low, high, start, stop = head_window(h)
    lane = lax.broadcasted_iota(jnp.int32, (1, stop - start), 1) + start
    inside = jnp.logical_and(lane >= low, lane < high)
    parts = [qkv_ref[rows, j * width + start : j * width + stop] for j in range(3)]
    return inside, slice(start, stop), parts


def only(inside, x):
    return jnp.where(inside, x, jnp.zeros_like(x))


def softmax_of(query, key, allowed):
    scores = jnp.where(allowed, contract(query, key, ((1,), (1,))) * HD**-0.5, MASKED)
    weights = jnp.exp(scores - jnp.max(scores, axis=-1, keepdims=True))
    return weights * (1.0 / jnp.sum(weights, axis=-1, keepdims=True))


def attend(qkv_ref, rows, allowed, total, out_ref):
    width = out_ref.shape[1]
    total[:, :width] = jnp.zeros((total.shape[0], width), F32)
    for h in range(HEADS):
        inside, window, (query, key, value) = head_operands(qkv_ref, rows, h)
        probs = softmax_of(only(inside, query), key, allowed).astype(BF16)
        mixed = contract(probs, value, ((1,), (0,)))
        total[:, window] += only(inside, mixed)
    out_ref[rows, :] = total[:, :width].astype(BF16)


def attend_back(qkv_ref, grad_ref, rows, allowed, total, out_ref):
    width = grad_ref.shape[1]
    total[...] = jnp.zeros_like(total)
    for h in range(HEADS):
        inside, window, (query, key, value) = head_operands(qkv_ref, rows, h)
        query, key = only(inside, query), only(inside, key)
        grad = only(inside, grad_ref[rows, window])
        probs = softmax_of(query, key, allowed)
        grad_probs = contract(grad, value, ((1,), (1,)))
        centre = jnp.sum(probs * grad_probs, axis=-1, keepdims=True)
        grad_scores = (probs * (grad_probs - centre)).astype(BF16)
        start, stop = window.start, window.stop
        total[:, start:stop] += contract(grad_scores, key, ((1,), (0,))) * HD**-0.5
        total[:, width + start : width + stop] += contract(grad_scores, query, ((0,), (0,))) * HD**-0.5
        total[:, 2 * width + start : 2 * width + stop] += contract(probs.astype(BF16), grad, ((0,), (0,)))
    out_ref[rows, :] = total[...].astype(BF16)


def dot(x, y):
    return jnp.dot(x, y, preferred_element_type=F32)


def dot_back(x, y):
    return lax.dot_general(x, y, (((1,), (1,)), ((), ())), preferred_element_type=F32)


def dot_rows(x, y):
    return lax.dot_general(x, y, (((0,), (0,)), ((), ())), preferred_element_type=F32)


def normal(x):
    centred = x - jnp.mean(x, axis=-1, keepdims=True)
    scale = lax.rsqrt(jnp.mean(centred * centred, axis=-1, keepdims=True) + EPS)
    return centred * scale, scale


TILE = 384
DEPTH = 2
GELU = math.sqrt(2.0 / math.pi)


def columns_of(t):
    if isinstance(t, int):
        return pl.ds(t * TILE, TILE)
    return pl.ds(pl.multiple_of(t * TILE, 128), TILE)


def unit_of(t, width):
    if isinstance(t, int):
        return pl.ds(t * width, width)
    return pl.ds(pl.multiple_of(t * width, 128), width)


class Stream:
    def __init__(self, ring, sems, width):
        self.ring, self.sems, self.width = ring, sems, width
        self.stages = []

    def add(self, weight, back, inner, outer):
        self.stages.append((weight, back, inner, outer))

    def tile(self, stage, n, k):
        weight, back, inner, _ = self.stages[stage]
        t = n * inner + k
        slot = t % DEPTH if isinstance(t, int) else lax.rem(t, DEPTH)
        deep, side = unit_of(k, self.width), unit_of(n, self.width)
        src = weight.at[side, deep] if back else weight.at[deep, side]
        buffer = self.ring.at[stage % 2, slot]
        return pltpu.make_async_copy(src, buffer, self.sems.at[stage % 2, slot]), buffer

    def begin(self, stage):
        if stage < len(self.stages):
            _, _, inner, outer = self.stages[stage]
            for t in range(min(DEPTH, inner * outer)):
                self.tile(stage, t // inner, t % inner)[0].start()

    def run(self, stage, use, ahead=True):
        _, _, inner, outer = self.stages[stage]
        if ahead:
            self.begin(stage + 1)
        count = inner * outer

        def group(n):
            def product(k, left, back):
                copy, buffer = self.tile(stage, n, k)
                copy.wait()
                result = (dot_back if back else dot)(left, buffer[...])
                t = n * inner + k + DEPTH

                def refill():
                    self.tile(stage, lax.div(t, inner), lax.rem(t, inner))[0].start()

                if not isinstance(t, int):
                    when(t < count, refill)
                elif t < count:
                    self.tile(stage, t // inner, t % inner)[0].start()
                return result

            use(n, product)

        def body(n, carry):
            group(n)
            return carry

        if outer == 1:
            group(0)
        else:
            lax.fori_loop(0, outer, body, 0)


def each_quarter(rows, run):
    def body(q, carry):
        run(q, pl.ds(pl.multiple_of(q * rows, rows), rows))
        return carry

    lax.fori_loop(0, 8, body, 0)


def piece_of(mod_ref, q, p, width, columns=None):
    if columns is None:
        return mod_ref[q, :, p * width : (p + 1) * width]
    return mod_ref[q, :, pl.ds(p * width + columns.start, TILE)]


def modulate(x_ref, mod_ref, out_ref, first, quarter_rows):
    width = x_ref.shape[1]

    def run(q, rows):
        hat = normal(x_ref[rows, :])[0]
        shift, scale = piece_of(mod_ref, q, first, width), piece_of(mod_ref, q, first + 1, width)
        out_ref[rows, :] = (hat * (1.0 + scale) + shift).astype(BF16)

    each_quarter(quarter_rows, run)


def modulate_back(grad, x, scale):
    hat, inverse = normal(x)
    inner = grad * (1.0 + scale)
    along = jnp.mean(inner * hat, axis=-1, keepdims=True)
    grad_x = inverse * (inner - jnp.mean(inner, axis=-1, keepdims=True) - hat * along)
    return grad_x, jnp.sum(grad, axis=0, keepdims=True), jnp.sum(grad * hat, axis=0, keepdims=True)


def split_quarters(quarter_rows, run):
    for q in range(8):
        run(q, slice(q * quarter_rows, (q + 1) * quarter_rows))


def allowed_of(row_ref, column_ref, block):
    rows = pl.ds(pl.multiple_of(block * ATT_ROWS, ATT_ROWS), ATT_ROWS)
    return rows, row_ref[rows, :] == column_ref[block]


def each_block(total_rows, run):
    def body(block, carry):
        run(block)
        return carry

    lax.fori_loop(0, total_rows // ATT_ROWS, body, 0)


def forward_stages(stream, weights):
    width = weights[0].shape[0]
    qkv, proj, up, down = weights
    stream.add(qkv, False, 1, qkv.shape[1] // width)
    stream.add(proj, False, 1, 1)
    stream.add(up, False, 1, up.shape[1] // width)
    stream.add(down, False, down.shape[0] // width, 1)


def backward_stages(stream, weights):
    width = weights[0].shape[0]
    qkv, proj, up, down = weights
    stream.add(down, True, 1, down.shape[0] // width)
    stream.add(up, True, up.shape[1] // width, 1)
    stream.add(proj, True, 1, 1)
    stream.add(qkv, True, qkv.shape[1] // width, 1)


def by_parts(quarter_rows, width, run):
    def one(q, rows):
        for t in range(width // TILE):
            run(q, rows, slice(t * TILE, (t + 1) * TILE))

    each_quarter(quarter_rows, one)


def proj_tile(r, mod_ref, quarter_rows, columns, branch):
    width = r["x"].shape[1]
    r["branch"][:, columns] = branch.astype(BF16)

    def gated(q, rows):
        gate = piece_of(mod_ref, q, 2, width, columns)
        r["x2"][rows, columns] = r["x"][rows, columns] + gate * branch[rows]

    split_quarters(quarter_rows, gated)


def gelu_parts(h):
    square = h * h
    t = jnp.tanh(h * (GELU + (GELU * 0.044715) * square))
    half = 0.5 + 0.5 * t
    return h * half, half + (0.5 * h) * (1.0 - t * t) * (GELU + (3.0 * GELU * 0.044715) * square)


def up_tile(r, columns, h):
    act, slope = gelu_parts(h)
    r["act"][:, columns] = act.astype(BF16)
    r["slope"][:, columns] = slope.astype(BF16)


def out_tile(r, mod_ref, quarter_rows, columns, mlp):
    width = r["x"].shape[1]
    r["mlp"][:, columns] = mlp.astype(BF16)

    def gated(q, rows):
        gate = piece_of(mod_ref, q, 5, width, columns)
        r["out"][rows, columns] = (r["x2"][rows, columns] + gate * mlp[rows]).astype(BF16)

    split_quarters(quarter_rows, gated)


def run_forward(stream, r, mod_ref, segments, quarter_rows, finish_part, done):
    width = r["x"].shape[1]
    total_rows = r["x"].shape[0]
    modulate(r["x"], mod_ref, r["a1"], 0, quarter_rows)

    def qkv(n, product):
        r["qkv"][:, unit_of(n, width)] = product(0, r["a1"][...], False).astype(BF16)

    stream.run(0, qkv)
    done("a1")

    def mix(block):
        rows, allowed = allowed_of(*segments, block)
        attend(r["qkv"], rows, allowed, r["total"], r["att"])

    each_block(total_rows, mix)

    def proj(n, product):
        r["acc"][...] = product(0, r["att"][...], False)

    stream.run(1, proj)
    done("att")

    def gated(q, rows, columns):
        branch = r["acc"][rows, columns]
        r["branch"][rows, columns] = branch.astype(BF16)
        gate = piece_of(mod_ref, q, 2, width, columns)
        r["x2"][rows, columns] = r["x"][rows, columns] + gate * branch

    by_parts(quarter_rows, width, gated)
    modulate(r["x2"], mod_ref, r["a2"], 3, quarter_rows)

    def up(n, product):
        r["acc"][...] = product(0, r["a2"][...], False)

        def part(q, rows, columns):
            into = pl.ds(pl.multiple_of(n * width + columns.start, 128), TILE)
            act, slope = gelu_parts(r["acc"][rows, columns])
            r["act"][rows, into] = act.astype(BF16)
            r["slope"][rows, into] = slope.astype(BF16)

        by_parts(quarter_rows, width, part)

    stream.run(2, up)
    done("a2")

    def down(n, product):
        for k in range(r["act"].shape[1] // width):
            part = product(k, r["act"][:, k * width : (k + 1) * width], False)
            if k == 0:
                r["acc"][...] = part
            else:
                r["acc"][...] += part

    stream.run(3, down)
    done("act")
    by_parts(quarter_rows, width, lambda q, rows, columns: finish_part(q, rows, columns, r["acc"][rows, columns]))


def run_backward(stream, first, r, mod_ref, segments, quarter_rows, grad_of, finish, done):
    width = r["x"].shape[1]
    total_rows = r["x"].shape[0]

    def down(n, product):
        columns = unit_of(n, width)
        grad = product(0, r["dmlp"][...], True)
        r["slope"][:, columns] = (grad * r["slope"][:, columns].astype(F32)).astype(BF16)

    stream.run(first, down)
    done("dmlp")
    done("slope")

    def up(n, product):
        for k in range(r["slope"].shape[1] // width):
            part = product(k, r["slope"][:, k * width : (k + 1) * width], True)
            if k == 0:
                r["dx2"][...] = part
            else:
                r["dx2"][...] += part

    stream.run(first + 1, up)

    def middle(q, rows):
        scale, gate = piece_of(mod_ref, q, 4, width), piece_of(mod_ref, q, 2, width)
        grad, shift_grad, scale_grad = modulate_back(r["dx2"][rows, :], r["x2"][rows, :], scale)
        grad = grad + grad_of(rows)
        r["dx2"][rows, :] = grad
        r["dmod"][q, :, 3 * width : 4 * width] = shift_grad
        r["dmod"][q, :, 4 * width : 5 * width] = scale_grad
        r["dmod"][q, :, 2 * width : 3 * width] = jnp.sum(
            grad * r["branch"][rows, :].astype(F32), axis=0, keepdims=True
        )
        r["dbranch"][rows, :] = (gate * grad).astype(BF16)

    each_quarter(quarter_rows, middle)

    def proj(n, product):
        r["datt"][...] = product(0, r["dbranch"][...], True).astype(BF16)

    stream.run(first + 2, proj)
    done("dbranch")

    def mix(block):
        rows, allowed = allowed_of(*segments, block)
        attend_back(r["qkv"], r["datt"], rows, allowed, r["total"], r["dqkv"])

    each_block(total_rows, mix)
    done("dqkv")

    def qkv(n, product):
        for k in range(3):
            part = product(k, r["dqkv"][:, k * width : (k + 1) * width], True)
            if k == 0:
                r["acc"][...] = part
            else:
                r["acc"][...] += part

    stream.run(first + 3, qkv, ahead=False)

    def outer(q, rows):
        scale = piece_of(mod_ref, q, 1, width)
        grad, shift_grad, scale_grad = modulate_back(r["acc"][rows, :], r["x"][rows, :], scale)
        r["dmod"][q, :, :width] = shift_grad
        r["dmod"][q, :, width : 2 * width] = scale_grad
        finish(q, rows, grad + r["dx2"][rows, :])

    each_quarter(quarter_rows, outer)
    done("dmod")


def placed(kept_ref, m, slot):
    kept = kept_ref[m]
    positions = lax.broadcasted_iota(jnp.int32, (slot, kept.shape[1]), 0)
    return jnp.where(positions == kept, 1.0, 0.0).astype(BF16)


class Copies:
    def __init__(self, sems):
        self.sems, self.count, self.pending = sems, 0, []

    def start(self, src, dst):
        copy = pltpu.make_async_copy(src, dst, self.sems.at[self.count])
        self.count += 1
        copy.start()
        self.pending.append(copy)
        return copy

    def finish(self):
        for copy in self.pending:
            copy.wait()
        self.pending = []


def encode_kernel(names, tokens, kept_ref, mod_ref, row_ref, column_ref, wq, wp, wu, wd, *rest):
    outs, scratch = rest[: len(names)], rest[len(names) :]
    r = dict(zip(names + ("total", "acc"), scratch[: len(names) + 2]))
    loaded, ring, stream_sems, sems = scratch[len(names) + 2 :]
    width = loaded.shape[2]
    slot = loaded.shape[1]

    def work():
        stream = Stream(ring, stream_sems, width)
        forward_stages(stream, (wq, wp, wu, wd))
        copies = Copies(sems)
        copies.start(tokens, loaded)
        stream.begin(0)
        copies.finish()
        kept = kept_ref.shape[2]
        for m in range(2):
            r["x"][m * kept : (m + 1) * kept, :] = dot_rows(placed(kept_ref, m, slot), loaded[m])
        total_rows = r["x"].shape[0]
        out_of = dict(zip(names, outs))

        def done(name):
            copies.start(r[name], out_of[name].at[pl.ds(0, total_rows)])

        def finish_part(q, rows, columns, mlp):
            r["mlp"][rows, columns] = mlp.astype(BF16)
            gate = piece_of(mod_ref, q, 5, width, columns)
            r["out"][rows, columns] = (r["x2"][rows, columns] + gate * mlp).astype(BF16)

        run_forward(stream, r, mod_ref, (row_ref, column_ref), total_rows // 8, finish_part, done)
        for name in ("x", "x2", "qkv", "branch", "slope", "mlp", "out"):
            done(name)
        copies.finish()

    when(lax.axis_index("section") == 0, work)


def decode_kernel(
    names, rights, received, cotangent, kept_ref, mask_ref, mod_ref, row_ref, column_ref, wq, wp, wu, wd,
    a1, att, a2, act, *rest,
):
    outs, scratch = rest[: 4 + len(rights) + 4], rest[4 + len(rights) + 4 :]
    lefts = dict(zip(("a1", "att", "a2", "act"), outs[:4]))
    right_outs = dict(zip(rights, outs[4 : 4 + len(rights)]))
    dmod_out, decoded, back, mask_out = outs[4 + len(rights) :]
    r = dict(zip(names, scratch[: len(names)]))
    got, ring, stream_sems, sems = scratch[len(names) :]
    width = got.shape[2]

    def work():
        stream = Stream(ring, stream_sems, width)
        forward_stages(stream, (wq, wp, wu, wd))
        backward_stages(stream, (wq, wp, wu, wd))
        copies = Copies(sems)
        copies.start(received, got)
        copies.start(cotangent, r["dy"])
        stream.begin(0)
        copies.finish()
        total_rows = r["x"].shape[0]
        slot, kept = total_rows // 2, kept_ref.shape[2]
        for m in range(2):
            place = placed(kept_ref, m, slot)
            flags = jnp.sum(place.astype(F32), axis=1, keepdims=True)
            r["free"][m * slot : (m + 1) * slot, :] = jnp.broadcast_to(1.0 - flags, (slot, 128))
            filled = dot(place, got[m]) + (1.0 - flags) * mask_ref[...].astype(F32)
            r["x"][m * slot : (m + 1) * slot, :] = filled
        out_of = {**lefts, **right_outs, "dmod": dmod_out, "slope": right_outs["dhid"]}

        def done(name):
            copies.start(r[name], out_of[name])

        def finish_part(q, rows, columns, part):
            gate = piece_of(mod_ref, q, 5, width, columns)
            dy = r["dy"][rows, columns].astype(F32)
            r["out"][rows, columns] = (r["x2"][rows, columns] + gate * part).astype(BF16)
            r["dmlp"][rows, columns] = (gate * dy).astype(BF16)
            r["dmod"][q, :, 5 * width + columns.start : 5 * width + columns.stop] = jnp.sum(
                dy * part, axis=0, keepdims=True
            )

        segments = (row_ref, column_ref)
        run_forward(stream, r, mod_ref, segments, total_rows // 8, finish_part, done)
        copies.start(r["out"], decoded)
        r["mask"][...] = jnp.zeros_like(r["mask"])

        def finish(q, rows, grad):
            r["mask"][...] += jnp.sum(grad * r["free"][rows, :1], axis=0, keepdims=True)
            r["dbranch"][rows, :] = grad.astype(BF16)

        def grad_of(rows):
            return r["dy"][rows, :].astype(F32)

        def done_back(name):
            if name == "dbranch":
                copies.start(r[name], out_of[name]).wait()
                copies.pending.pop()
            else:
                done(name)

        run_backward(stream, 4, r, mod_ref, segments, total_rows // 8, grad_of, finish, done_back)
        for m in range(2):
            place = placed(kept_ref, m, slot)
            got[m] = dot_rows(place, r["dbranch"][m * slot : (m + 1) * slot, :]).astype(BF16)
        copies.start(got, back)
        copies.start(r["mask"], mask_out)
        copies.finish()

    when(lax.axis_index("section") == 1, work)


def encode_back_kernel(
    names, rights, saved, received, kept_ref, mod_ref, row_ref, column_ref, wq, wp, wu, wd, *rest
):
    kept_in = dict(zip(saved, rest[: len(saved)]))
    rest = rest[len(saved) + len(rights) + 1 :]
    right_outs = dict(zip(rights, rest[: len(rights)]))
    dmod_out, token_out = rest[len(rights) : len(rights) + 2]
    scratch = rest[len(rights) + 2 :]
    r = dict(zip(names, scratch[: len(names)]))
    ring, stream_sems, sems = scratch[len(names) :]
    width = r["x"].shape[1]

    def work():
        stream = Stream(ring, stream_sems, width)
        backward_stages(stream, (wq, wp, wu, wd))
        copies = Copies(sems)
        copies.start(received, r["dy"])
        for name in saved:
            copies.start(kept_in[name], r[name])
        stream.begin(0)
        copies.finish()
        total_rows = r["x"].shape[0]
        out_of = {**right_outs, "dmod": dmod_out, "slope": right_outs["dhid"]}

        def done(name):
            if name == "dmod":
                copies.start(r[name], out_of[name])
            else:
                copies.start(r[name], out_of[name].at[pl.ds(0, total_rows)])

        def start(q, rows):
            gate = piece_of(mod_ref, q, 5, width)
            dy = r["dy"][rows, :].astype(F32)
            r["dmlp"][rows, :] = (gate * dy).astype(BF16)
            r["dmod"][q, :, 5 * width :] = jnp.sum(dy * r["mlp"][rows, :].astype(F32), axis=0, keepdims=True)

        each_quarter(total_rows // 8, start)

        def finish(q, rows, grad):
            r["mlp"][rows, :] = grad.astype(BF16)

        def grad_of(rows):
            return r["dy"][rows, :].astype(F32)

        segments = (row_ref, column_ref)
        run_backward(stream, 0, r, mod_ref, segments, total_rows // 8, grad_of, finish, done)
        kept = kept_ref.shape[2]
        slot = token_out.shape[1]
        for m in range(2):
            place = placed(kept_ref, m, slot)
            r["tokens"][m] = dot(place, r["mlp"][m * kept : (m + 1) * kept, :]).astype(BF16)
        copies.start(r["tokens"], token_out)
        copies.finish()

    when(lax.axis_index("section") == 0, work)


VMEM_BYTES = 60 * 1024 * 1024
LEFTS = ("a1", "att", "a2", "act")
RIGHTS = ("dqkv", "dbranch", "dhid", "dmlp")
SAVED = ("x", "x2", "qkv", "branch", "slope", "mlp")


def buffer_shapes(rows, width, wide_width):
    full, broad = lambda t: ((rows, width), t), lambda n, t: ((rows, n), t)
    return {
        "x": full(F32), "x2": full(F32), "dx2": full(F32), "acc": full(F32), "a1": full(BF16),
        "att": full(BF16), "a2": full(BF16), "branch": full(BF16), "mlp": full(BF16), "out": full(BF16),
        "dy": full(BF16), "dmlp": full(BF16), "dbranch": full(BF16), "datt": full(BF16),
        "qkv": broad(3 * width, BF16), "dqkv": broad(3 * width, BF16), "act": broad(wide_width, BF16),
        "slope": broad(wide_width, BF16), "dhid": broad(wide_width, BF16),
        "dmod": ((8, 1, 6 * width), F32), "mask": ((1, width), F32), "free": ((rows, 128), F32),
        "total": ((ATT_ROWS, 3 * width), F32),
    }


def rings(width):
    dma = pltpu.SemaphoreType.DMA
    return [pltpu.VMEM((2, DEPTH, width, width), BF16), dma((2, DEPTH)), dma((24,))]


def encode(tokens, kept, modulation, segments, weights, rows, all_rows):
    width, wide_width = weights[0].shape[0], weights[2].shape[1]
    shapes = buffer_shapes(rows, width, wide_width)
    names = LEFTS + SAVED + ("out",)
    outs = [jax.ShapeDtypeStruct(((all_rows if n in LEFTS else rows), shapes[n][0][1]), shapes[n][1]) for n in names]
    results = pl.pallas_call(
        functools.partial(encode_kernel, names),
        out_shape=outs,
        in_specs=[anywhere] + [in_vmem] * 4 + [anywhere] * 4,
        out_specs=[anywhere] * len(names),
        scratch_shapes=[pltpu.VMEM(*shapes[n]) for n in names + ("total", "acc")]
        + [pltpu.VMEM(tokens.shape, BF16)]
        + rings(width),
        compiler_params=pltpu.CompilerParams(vmem_limit_bytes=VMEM_BYTES),
        name="encode",
    )(tokens, kept, modulation, *segments, *weights)
    return results[:4], results[4:-1], results[-1]


def decode(received, cotangent, kept, mask_token, modulation, segments, weights, lefts):
    width, wide_width = weights[0].shape[0], weights[2].shape[1]
    rows = cotangent.shape[0]
    shapes = buffer_shapes(rows, width, wide_width)
    names = LEFTS + (
        "x", "x2", "qkv", "branch", "slope", "out", "dy", "dmlp", "dbranch", "datt", "dqkv", "dmod",
        "mask", "free", "total",
    )
    scratch = [pltpu.VMEM(*shapes[n]) for n in names]
    names += ("dx2", "acc")
    scratch += [pltpu.VMEM(*shapes["dx2"]), pltpu.VMEM(*shapes["acc"])]
    outs = [jax.ShapeDtypeStruct(*shapes[n]) for n in LEFTS + RIGHTS + ("dmod", "out")]
    outs += [jax.ShapeDtypeStruct(received.shape, BF16), jax.ShapeDtypeStruct((1, width), F32)]
    results = pl.pallas_call(
        functools.partial(decode_kernel, names, RIGHTS),
        out_shape=outs,
        in_specs=[anywhere] * 2 + [in_vmem] * 5 + [anywhere] * 8,
        out_specs=[anywhere] * len(outs),
        scratch_shapes=scratch + [pltpu.VMEM(received.shape, BF16)] + rings(width),
        input_output_aliases={11 + j: j for j in range(4)},
        compiler_params=pltpu.CompilerParams(vmem_limit_bytes=VMEM_BYTES),
        name="decode",
    )(received, cotangent, kept, mask_token, modulation, *segments, *weights, *lefts)
    return results[:4], results[4:8], results[8:]


def encode_back(received, kept, modulation, segments, weights, saved, rights, grad_mod, token_shape):
    width, wide_width = weights[0].shape[0], weights[2].shape[1]
    rows = received.shape[0]
    shapes = buffer_shapes(rows, width, wide_width)
    names = SAVED + ("dy", "dmlp", "dbranch", "datt", "dqkv", "dmod", "dx2", "acc", "total", "tokens")
    shapes["tokens"] = (token_shape, BF16)
    outs = [jax.ShapeDtypeStruct(x.shape, x.dtype) for x in tuple(rights) + (grad_mod,)]
    outs.append(jax.ShapeDtypeStruct(token_shape, BF16))
    before = 9 + len(saved)
    results = pl.pallas_call(
        functools.partial(encode_back_kernel, names, RIGHTS, SAVED),
        out_shape=outs,
        in_specs=[anywhere] + [in_vmem] * 4 + [anywhere] * (4 + len(saved) + 5),
        out_specs=[anywhere] * len(outs),
        scratch_shapes=[pltpu.VMEM(*shapes[n]) for n in names] + rings(width),
        input_output_aliases={before + j: j for j in range(5)},
        compiler_params=pltpu.CompilerParams(vmem_limit_bytes=VMEM_BYTES),
        name="encode_back",
    )(received, kept, modulation, *segments, *weights, *saved, *rights, grad_mod)
    return results[:4], results[4], results[5]


def gather_encode_kernel(length, plan, names, *refs):
    sources, (partial, big_ref, tokens, kept_ref, row_ref, column_ref) = refs[:4], refs[4:10]
    outs, (mod_out, received) = refs[10:14], refs[14:16]
    saved_outs = refs[16 : 16 + len(names)]
    rest = refs[16 + len(names) :]
    r = dict(zip(names + ("out", "total"), rest[: len(names) + 2]))
    (
        loaded, mod_ref, tiles, last_tile, part_held, part_core, part_pair, part_line,
    ) = rest[len(names) + 2 : len(names) + 10]
    sems = rest[len(names) + 10 : len(names) + 19]
    part_sems, line_sems, tile_sems, out_sems, copy_sems = rest[len(names) + 19 :]
    a, b, c = position()
    encoder = lax.axis_index("section") == 0
    other = {"section": 1 - lax.axis_index("section")}
    barrier = pltpu.get_barrier_semaphore()

    def tell(target):
        pl.semaphore_signal(barrier, inc=1, device_id=target, device_id_type=MESH)

    tell(at(a, 1 - b, c))
    tell(at(a, b, 1 - c))
    tell(other)
    for k in range(1, length):
        tell(at(lax.rem(a + k, length), b, c))
    pl.semaphore_wait(barrier, length + 2)

    n = len(plan)
    width = r["x"].shape[1]
    total_rows = r["x"].shape[0]
    quarter_rows = total_rows // 8
    issue, move, complete, drain = gather_moves(length, plan, sources, outs, sems, a, b, c)
    copies = Copies(copy_sems)
    out_of = dict(zip(names, saved_outs))

    part_load = pltpu.make_async_copy(partial.at[:, :, c], part_held, part_sems.at[0])
    part_to_core = remote(partial.at[:, :, 1 - c], part_core, part_sems.at[1], part_sems.at[2], at(a, b, 1 - c))
    part_across = remote(part_held.at[:, 1 - b], part_pair, part_sems.at[3], part_sems.at[4], at(a, 1 - b, c))

    def part_to_line(k):
        to = lax.rem(a + k, length)
        return remote(
            part_held.at[to, b], part_line.at[k - 1], line_sems.at[0, k - 1], line_sems.at[1, k - 1], at(to, b, c)
        )

    def add_part(where, got):
        part_held[where] = part_held[where] + got

    def part_first():
        part_to_core.wait_recv()
        part_load.wait()
        for s in range(2 * length):
            add_part((s // 2, s % 2), part_core[s // 2, s % 2])
        part_across.start()

    def part_second():
        part_across.wait()
        for aa in range(length):
            add_part((aa, b), part_pair[aa])
        for k in range(1, length):
            part_to_line(k).start()

    def part_last():
        total = part_held[a, b].astype(F32)
        for k in range(1, length):
            part_to_line(k).wait_recv()
            total = total + part_line[k - 1].astype(F32)
        for q in range(8):
            first = q // SMALL_PER * SMALL_PER
            mod_ref[q] = jnp.where(big_ref[q] > 0, total[first : first + 1], total[q : q + 1])
        copies.start(mod_ref, mod_out)

    def load_tile(w, low, t):
        src = outs[w].at[:, :, :, :, pl.ds(low + t * TILE, TILE)]
        return pltpu.make_async_copy(src, tiles.at[t % 2], tile_sems.at[t % 2])

    def products(w, low, left, put):
        count = width // TILE
        for t in range(min(2, count)):
            load_tile(w, low, t).start()
        for t in range(count):
            load_tile(w, low, t).wait()
            tile = tiles[t % 2].astype(F32).reshape(width, TILE).astype(BF16)
            result = dot(r[left][...], tile)
            if t + 2 < count:
                load_tile(w, low, t + 2).start()
            put(columns_of(low // TILE + t), result)

    def done(name):
        copies.start(r[name], out_of[name].at[pl.ds(0, total_rows)])

    def start_encode():
        fetch = pltpu.make_async_copy(tokens, loaded, tile_sems.at[2])
        fetch.start()
        fetch.wait()
        kept, slot = kept_ref.shape[2], loaded.shape[1]
        for m in range(2):
            r["x"][m * kept : (m + 1) * kept, :] = dot_rows(placed(kept_ref, m, slot), loaded[m])

    def put_qkv(columns, result):
        r["qkv"][:, columns] = result.astype(BF16)

    def put_proj(columns, result):
        proj_tile(r, mod_ref, quarter_rows, columns, result)

    def put_up(columns, result):
        up_tile(r, columns, result)

    def send_out(t):
        columns = columns_of(t)
        return remote(
            r["out"].at[:, columns], received.at[:, columns], out_sems.at[0, t], out_sems.at[1, t], other
        )

    def encode_chunk(i):
        w, low, _, _ = plan[i]
        if w == 0:
            if i == 0:
                modulate(r["x"], mod_ref, r["a1"], 0, quarter_rows)
            products(w, low, "a1", put_qkv)
        elif w == 1:
            rows, allowed = slice(0, total_rows), row_ref[...] == column_ref[0]
            attend(r["qkv"], rows, allowed, r["total"], r["att"])
            products(w, low, "att", put_proj)
            modulate(r["x2"], mod_ref, r["a2"], 3, quarter_rows)
        elif w == 2:
            products(w, low, "a2", put_up)
        else:
            src = outs[w].at[:, :, :, :, pl.ds(low, TILE)]
            fetch = pltpu.make_async_copy(src, last_tile, tile_sems.at[2])
            fetch.start()
            fetch.wait()
            tile = last_tile[...].reshape(r["act"].shape[1], TILE)
            out_tile(r, mod_ref, quarter_rows, columns_of(low // TILE), dot(r["act"][...], tile))
            send_out(low // TILE).start()

    part_load.start()
    part_to_core.start()
    issue(0)
    when(encoder, start_encode)
    part_first()
    for i in range(1, AHEAD):
        issue(i)
    for t in range(n + length - 1):
        move(t, AHEAD)
        if t == 0:
            part_second()
        if t == 1:
            part_last()
        i = t - length + 1
        if i >= 0:
            complete(i)
            when(encoder, lambda: encode_chunk(i))
    for i in range(n):
        drain(i)
    part_to_core.wait_send()
    for k in range(1, length):
        part_to_line(k).wait_send()

    def close():
        for name in names:
            done(name)
        for copy in copies.pending[1:]:
            copy.wait()
        for t in range(width // TILE):
            send_out(t).wait_send()

    when(encoder, close)
    copies.pending[0].wait()

    def arrive():
        for t in range(width // TILE):
            send_out(t).wait_recv()

    when(jnp.logical_not(encoder), arrive)


AHEAD = 4


def gather_encode(shards, partial, big, tokens, kept, segments, plan, length, rows, all_rows):
    n = len(plan)
    width, wide_width = shards[1].shape[1], shards[2].shape[1]
    shapes = buffer_shapes(rows, width, wide_width)
    names = LEFTS + SAVED
    quarters = partial.shape[3]
    part_slab = partial.shape[3:]
    dma = pltpu.SemaphoreType.DMA
    outs = [jax.ShapeDtypeStruct((length, 2, 2) + s.shape, BF16) for s in shards]
    outs += [jax.ShapeDtypeStruct((quarters, 1, 6 * width), F32), jax.ShapeDtypeStruct((rows, width), BF16)]
    outs += [jax.ShapeDtypeStruct(((all_rows if m in LEFTS else rows), shapes[m][0][1]), shapes[m][1]) for m in names]
    results = pl.pallas_call(
        functools.partial(gather_encode_kernel, length, plan, names),
        out_shape=outs,
        in_specs=[anywhere] * 5 + [in_vmem, anywhere] + [in_vmem] * 3,
        out_specs=[anywhere] * len(outs),
        scratch_shapes=[pltpu.VMEM(*shapes[m]) for m in names + ("out", "total")]
        + [
            pltpu.VMEM(tokens.shape, BF16),
            pltpu.VMEM((quarters, 1, 6 * width), F32),
            pltpu.VMEM((2, length, 2, 2, shards[0].shape[0], TILE), BF16),
            pltpu.VMEM((length, 2, 2, shards[3].shape[0], TILE), BF16),
            pltpu.VMEM((length, 2) + part_slab, BF16),
            pltpu.VMEM((length, 2) + part_slab, BF16),
            pltpu.VMEM((length,) + part_slab, BF16),
            pltpu.VMEM((length - 1,) + part_slab, BF16),
        ]
        + [dma((n, length, 2))] * 4
        + [dma((n, length))] * 2
        + [dma((n, length, 2))] * 2
        + [dma((n,)), dma((5,)), dma((2, length - 1)), dma((3,)), dma((2, width // TILE)), dma((len(names) + 1,))],
        compiler_params=pltpu.CompilerParams(
            collective_id=0, has_side_effects=True, vmem_limit_bytes=VMEM_BYTES
        ),
        name="gather_encode",
    )(*shards, partial, big, tokens, kept, *segments)
    return results[:4], results[4], results[5], results[6:10], results[10:]


def plan_of(widths, lead, unit, line_first):
    plan = [(w, low, unit) for w, width in enumerate(widths) for low in range(0, width, unit)]
    plan += [(len(widths), j, 0) for j in range(lead)]
    return tuple(p + ("line" if i in line_first else "pair",) for i, p in enumerate(plan))


def swap_sections(x):
    return lax.ppermute(x, "section", [(0, 1), (1, 0)])


def on_device(
    tokens, kept_index, big_image, timesteps, labels, cotangent, mask_token, time_weight, class_table,
    ada_weight, ada_bias, qkv_weight, proj_weight, up_weight, down_weight,
):
    section = lax.axis_index("section")
    me = lax.axis_index("dp")
    devices = lax.axis_size("dp")
    micro, slot, width = tokens.shape
    kept_count = kept_index.shape[1]
    own_width = ada_weight.shape[1]
    images = micro * SMALL_PER
    quarters = micro * SMALL_PER
    ada = ada_weight[0]

    length = devices // 4
    ids = jnp.concatenate([timesteps.reshape(1, images), labels.reshape(1, images)])
    if length == 4:
        ids = small_gather(jnp.pad(ids, ((0, 6), (0, 128 - images))), length, False, 2)
    else:
        ids = lax.all_gather(ids, "dp", axis=0)
    times = ids[:, 0, :images].reshape(devices * images)
    classes = ids[:, 1, :images].reshape(devices * images)
    half = time_weight.shape[0] // 2
    frequencies = jnp.exp(-math.log(10000.0) * jnp.arange(half, dtype=F32) / half)
    angles = times.astype(F32)[:, None] * frequencies[None, :]
    embedding = jnp.concatenate([jnp.cos(angles), jnp.sin(angles)], axis=-1).astype(BF16)
    onehot = (classes[:, None] == jnp.arange(class_table.shape[0])[None, :]).astype(BF16)
    cond = dot(embedding, time_weight) + dot(onehot, class_table)
    cond = lax.dynamic_slice_in_dim(cond, me * own_width, own_width, axis=1)
    lifted = jax.nn.silu(cond).astype(BF16)
    bias_width = ada_bias.shape[1]
    bias = lax.dynamic_update_slice_in_dim(
        jnp.zeros((1, 6 * width), F32), ada_bias.astype(F32), me * bias_width, axis=1
    )
    partial = (dot(lifted, ada) + bias).astype(BF16).reshape(devices, images, 6 * width)

    big = big_image[:, :1] > 0
    quarter_ids = jnp.arange(quarters, dtype=jnp.int32).reshape(micro, SMALL_PER)
    segment_of = jnp.where(big, quarter_ids[:, :1], quarter_ids).reshape(quarters)
    kept = kept_index.reshape(micro, 1, kept_count)

    def segments(quarter_rows):
        ids = jnp.repeat(segment_of, quarter_rows)
        return ids.reshape(-1, 1), ids.reshape(-1, 1, ATT_ROWS)

    enc_rows, dec_rows = micro * kept_count, micro * slot
    enc_segments = segments(enc_rows // quarters)
    dec_segments = segments(dec_rows // quarters)

    shards = (qkv_weight[0], proj_weight[0], up_weight[0])
    lead = down_weight.shape[1] // qkv_weight.shape[1]
    widths = [x.shape[1] for x in shards]
    if length == 4:
        plan = [(w, low, width, "line") for w in range(3) for low in range(0, widths[w], width)]
        plan += [(3, low, TILE, "line") for low in range(0, width, TILE)]
        plan = tuple(p[:3] + ("pair" if i in (1, 7) else "line",) for i, p in enumerate(plan))
        flags = jnp.repeat(big[:, 0], SMALL_PER).astype(jnp.int32).reshape(quarters, 1, 1)
        whole, modulation, received, lefts, saved = gather_encode(
            shards + (down_weight[0],), partial.reshape((length, 2, 2) + partial.shape[1:]), flags, tokens, kept,
            enc_segments, plan, length, enc_rows, dec_rows,
        )
        weights = tuple(w.reshape(-1, w.shape[-1]) for w in whole)
        received = received.reshape(micro, kept_count, width)
    else:
        whole = (lax.all_gather(x, "dp", axis=0, tiled=True) for x in shards + (down_weight[0],))
        weights = tuple(whole)
        modulation = lax.psum_scatter(partial, "dp", scatter_dimension=0, tiled=False).astype(F32)
        modulation = modulation.reshape(micro, SMALL_PER, 6 * width)
        modulation = jnp.where(big[:, :, None], modulation[:, :1], modulation).reshape(quarters, 1, 6 * width)
        lefts, saved, encoded = encode(tokens, kept, modulation, enc_segments, weights, enc_rows, dec_rows)
        received = swap_sections(encoded).reshape(micro, kept_count, width)

    lefts, rights, (grad_mod, decoded, back, mask_part) = decode(
        received, cotangent.reshape(dec_rows, width), kept, mask_token.reshape(1, width), modulation,
        dec_segments, weights, lefts,
    )
    received = swap_sections(back).reshape(enc_rows, width)
    rights, grad_mod, token_grad = encode_back(
        received, kept, modulation, enc_segments, weights, saved, rights, grad_mod, (micro, slot, width)
    )
    decoded = decoded.reshape(micro, slot, width)
    mask_part = jnp.where(section == 1, mask_part, 0.0).reshape(width)

    half_width = width // 2
    outgoing = jnp.where(section == 0, token_grad[:, :, half_width:], decoded[:, :, :half_width])
    incoming = swap_sections(outgoing)
    decoded_half = jnp.where(section == 0, incoming, decoded[:, :, half_width:])
    token_half = jnp.where(section == 0, token_grad[:, :, :half_width], incoming)

    grad_mod = grad_mod.reshape(micro, SMALL_PER, 6 * width)
    first_only = (jnp.arange(SMALL_PER) == 0)[None, :, None]
    grad_mod = jnp.where(
        big[:, :, None], jnp.where(first_only, jnp.sum(grad_mod, axis=1, keepdims=True), 0.0), grad_mod
    )
    grad_mod = grad_mod.reshape(images, 6 * width).astype(BF16)
    silu_slope = jax.vjp(jax.nn.silu, cond)[1](jnp.ones_like(cond))[0]
    shapes = tuple(x.shape for x in shards) + ((lead, own_width, width),)
    every_image = devices * images
    if length == 4:
        mask_rows = mask_part.reshape(-1, every_image)
        extras = (grad_mod, lifted.T, silu_slope.T, ada, mask_rows)
        plan = plan_of(widths, lead, width, (0, 6))
        *mine, ada_grad, bias_sum, shared = scatter_all(lefts, rights, extras, shapes, plan, length)
        shared = shared.reshape(devices, -1, every_image)
        every_cond = shared[:, :own_width].reshape(width, every_image)
        mask_grad = jnp.sum(shared[:, own_width : own_width + mask_rows.shape[0]], axis=0).reshape(width)
        bias_grad = lax.dynamic_slice_in_dim(bias_sum, me * bias_width, bias_width, axis=1)
    else:
        every_mod = lax.all_gather(grad_mod, "dp", axis=0, tiled=True)
        ada_grad = dot_rows(lifted, every_mod)
        bias_sum = jnp.sum(every_mod.astype(F32), axis=0, keepdims=True)
        bias_grad = lax.dynamic_slice_in_dim(bias_sum, me * bias_width, bias_width, axis=1)
        grad_cond = dot_back(every_mod, ada) * silu_slope
        every_cond = lax.psum(lax.all_gather(grad_cond.T, "dp", axis=0, tiled=True), "section")
        mask_grad = lax.psum(mask_part, ("section", "dp"))
        half_rows = jnp.arange(dec_rows)[:, None] < jnp.where(section == 0, enc_rows, dec_rows)
        lefts, rights = ([jnp.where(half_rows, x, jnp.zeros_like(x)) for x in xs] for xs in (lefts, rights))
        split = (dot_rows(x, y).astype(BF16).reshape((devices,) + s) for x, y, s in zip(lefts, rights, shapes))
        mine = tuple(lax.psum_scatter(g, "dp", scatter_dimension=0) for g in split)
    inputs = jnp.concatenate([embedding, onehot], axis=1)
    shared_grad = lax.dot_general(
        inputs, every_cond.astype(BF16), (((0,), (1,)), ((), ())), preferred_element_type=F32
    )
    time_grad, table_grad = shared_grad[: time_weight.shape[0]], shared_grad[time_weight.shape[0] :]
    qkv_grad, proj_grad, up_grad, down_grad = (g.astype(F32) for g in mine)
    return (
        decoded_half,
        token_half,
        mask_grad,
        time_grad,
        table_grad,
        ada_grad[None],
        bias_grad,
        qkv_grad[None],
        proj_grad[None],
        up_grad[None],
        down_grad.reshape(down_weight.shape),
    )


def solution(mesh):
    rows = P(None, "dp", None)
    ids = P(None, "dp")
    weight = P("section", "dp", None)
    halves = P(None, "dp", "section")
    in_specs = (rows, ids, ids, ids, ids, rows, P(), P(), P(), weight, P("section", "dp")) + (weight,) * 4
    out_specs = (halves, halves, P(), P(), P(), weight, P("section", "dp")) + (weight,) * 4
    return jax.shard_map(
        on_device, mesh=mesh, in_specs=in_specs, out_specs=out_specs, check_vma=False
    )
```

```python
import functools
import math
from types import SimpleNamespace

import jax
import jax.numpy as jnp
from jax import lax
from jax.experimental import pallas as pl
from jax.experimental.pallas import tpu as pltpu
from jax.sharding import PartitionSpec as P

HEADS = 16
HD = 72
SMALL_PER = 4
ATT_ROWS = 256
EPS = 1e-6
MASKED = -1e30
MESH = pl.DeviceIdType.MESH
F32 = jnp.float32
BF16 = jnp.bfloat16


anywhere = pl.BlockSpec(memory_space=pl.ANY)
in_vmem = pl.BlockSpec(memory_space=pltpu.VMEM)


def remote(src, dst, send_sem, recv_sem, target):
    return pltpu.make_async_remote_copy(
        src_ref=src,
        dst_ref=dst,
        send_sem=send_sem,
        recv_sem=recv_sem,
        device_id=target,
        device_id_type=MESH,
    )


def when(condition, run):
    pl.when(condition)(run)


def position():
    me = lax.axis_index("dp")
    return me // 4, (me // 2) % 2, me % 2


def at(line, pair, core):
    return {"dp": (line * 2 + pair) * 2 + core}


def greet(length, a, b, c):
    has_up, has_down = a < length - 1, a > 0
    barrier = pltpu.get_barrier_semaphore()

    def tell(target):
        pl.semaphore_signal(barrier, inc=1, device_id=target, device_id_type=MESH)

    tell(at(a, 1 - b, c))
    tell(at(a, b, 1 - c))
    when(has_up, lambda: tell(at(a + 1, b, c)))
    when(has_down, lambda: tell(at(a - 1, b, c)))
    pl.semaphore_wait(barrier, 2 + has_up.astype(jnp.int32) + has_down.astype(jnp.int32))
    return has_up, has_down


def piece(ref, lead, plan_entry):
    _, low, size, _ = plan_entry
    if size == 0:
        return ref.at[lead + (low,)]
    return ref.at[lead + (slice(None), pl.ds(low, size))]


def gather_moves(length, plan, sources, outs, sems, a, b, c):
    up_s, up_r, down_s, down_r, pair_s, pair_r, core_s, core_r, own_sem = sems
    has_up, has_down = a < length - 1, a > 0
    chunks = range(len(plan))
    line_first = [plan[i][3] == "line" for i in chunks]

    def slot(i, aa, bb, cc):
        return piece(outs[plan[i][0]], (aa, bb, cc), plan[i])

    def own(i):
        return piece(sources[plan[i][0]], (), plan[i])

    def rows_of(i):
        return (b,) if line_first[i] else (b, 1 - b)

    def up(i, k, bb, src=None):
        s = slot(i, a - k, bb, c)
        return remote(s if src is None else src, s, up_s.at[i, k, bb], up_r.at[i, k, bb], at(a + 1, b, c))

    def up_arrival(i, k, bb):
        s = slot(i, a - 1 - k, bb, c)
        return remote(s, s, up_s.at[i, k, bb], up_r.at[i, k, bb], at(a + 1, b, c))

    def down(i, k, bb, src=None):
        s = slot(i, a + k, bb, c)
        return remote(s if src is None else src, s, down_s.at[i, k, bb], down_r.at[i, k, bb], at(a - 1, b, c))

    def down_arrival(i, k, bb):
        s = slot(i, a + 1 + k, bb, c)
        return remote(s, s, down_s.at[i, k, bb], down_r.at[i, k, bb], at(a - 1, b, c))

    def across(i, aa, src=None):
        s = slot(i, aa, b, c)
        return remote(s if src is None else src, s, pair_s.at[i, aa], pair_r.at[i, aa], at(a, 1 - b, c))

    def across_arrival(i, aa):
        s = slot(i, aa, 1 - b, c)
        return remote(s, s, pair_s.at[i, aa], pair_r.at[i, aa], at(a, 1 - b, c))

    def to_core(i, aa, bb, src=None):
        s = slot(i, aa, bb, c)
        return remote(s if src is None else src, s, core_s.at[i, aa, bb], core_r.at[i, aa, bb], at(a, b, 1 - c))

    def core_arrival(i, aa, bb):
        s = slot(i, aa, bb, 1 - c)
        return remote(s, s, core_s.at[i, aa, bb], core_r.at[i, aa, bb], at(a, b, 1 - c))

    def after_across(i, aa):
        across_arrival(i, aa).wait_recv()
        to_core(i, aa, 1 - b).start()

    def issue(i):
        src = own(i)
        pltpu.make_async_copy(src, slot(i, a, b, c), own_sem.at[i]).start()
        across(i, a, src).start()
        when(has_up, lambda: up(i, 0, b, src).start())
        when(has_down, lambda: down(i, 0, b, src).start())
        to_core(i, a, b, src).start()

    def pair_step(i):
        across_arrival(i, a).wait_recv()
        when(has_up, lambda: up(i, 0, 1 - b).start())
        when(has_down, lambda: down(i, 0, 1 - b).start())
        to_core(i, a, 1 - b).start()

    def line_step(i, k):
        for bb in rows_of(i):

            def from_below():
                up_arrival(i, k - 1, bb).wait_recv()
                when(has_up, lambda: up(i, k, bb).start())
                if line_first[i]:
                    across(i, a - k).start()
                to_core(i, a - k, bb).start()

            def from_above():
                down_arrival(i, k - 1, bb).wait_recv()
                when(has_down, lambda: down(i, k, bb).start())
                if line_first[i]:
                    across(i, a + k).start()
                to_core(i, a + k, bb).start()

            when(a - k >= 0, from_below)
            when(a + k <= length - 1, from_above)

    def across_step(i, k):
        if not line_first[i]:
            return
        if k == 0:
            after_across(i, a)
        else:
            when(a - k >= 0, lambda: after_across(i, a - k))
            when(a + k <= length - 1, lambda: after_across(i, a + k))

    def complete(i):
        pltpu.make_async_copy(own(i), slot(i, a, b, c), own_sem.at[i]).wait()
        for aa in range(length):
            for bb in range(2):
                core_arrival(i, aa, bb).wait_recv()

    def drain(i):
        for aa in range(length):
            for bb in range(2):
                to_core(i, aa, bb).wait_send()
            if line_first[i]:
                across(i, aa).wait_send()
        if not line_first[i]:
            across(i, a).wait_send()
        for k in range(length - 1):
            for bb in rows_of(i):
                when(jnp.logical_and(has_up, a - k >= 0), lambda: up(i, k, bb).wait_send())
                when(
                    jnp.logical_and(has_down, a + k <= length - 1),
                    lambda: down(i, k, bb).wait_send(),
                )

    def move(t, ahead):
        n = len(plan)
        if t + ahead < n:
            issue(t + ahead)
        if t < n and not line_first[t]:
            pair_step(t)
        for k in range(1, length):
            i = t - k + 1
            if 0 <= i < n:
                line_step(i, k)
        for k in range(length):
            i = t - k
            if 0 <= i < n:
                across_step(i, k)

    return issue, move, complete, drain


SIDE_TIMES = (2, 4, 5, 6, 8, 10)


def greet_all(length, a, b, c):
    barrier = pltpu.get_barrier_semaphore()

    def tell(target):
        pl.semaphore_signal(barrier, inc=1, device_id=target, device_id_type=MESH)

    tell(at(a, 1 - b, c))
    tell(at(a, b, 1 - c))
    tell({"section": 1 - lax.axis_index("section")})
    for k in range(1, length):
        tell(at(lax.rem(a + k, length), b, c))
    pl.semaphore_wait(barrier, length + 2)


def spread(length, buffer, sems, a, b, c):
    line_s, line_r, pair_core = sems

    def to_line(k):
        mine = buffer.at[a, b, c]
        return remote(mine, mine, line_s.at[k - 1], line_r.at[k - 1], at(lax.rem(a + k, length), b, c))

    def from_line(k):
        slab = buffer.at[lax.rem(a + length - k, length), b, c]
        return remote(slab, slab, line_s.at[k - 1], line_r.at[k - 1], at(a, 1 - b, c))

    def across(bb):
        part = buffer.at[:, bb, c]
        return remote(part, part, pair_core.at[0], pair_core.at[1], at(a, 1 - b, c))

    def to_core(cc):
        part = buffer.at[:, :, cc]
        return remote(part, part, pair_core.at[2], pair_core.at[3], at(a, b, 1 - c))

    def start():
        for k in range(1, length):
            to_line(k).start()

    def second():
        for k in range(1, length):
            from_line(k).wait_recv()
            to_line(k).wait_send()
        across(b).start()

    def third():
        across(1 - b).wait_recv()
        across(b).wait_send()
        to_core(c).start()

    def end():
        to_core(1 - c).wait_recv()
        to_core(c).wait_send()

    return start, second, third, end


def conditioning_steps(length, inputs, outputs, scratch, a, b, c):
    grad_mod, lifted_t, slope_t, ada, mask_rows = inputs
    ada_grad, bias_sum, shared = outputs
    every, stage, payload, other = scratch[:4]
    mod_sems, shared_sems, side_sems, stage_sems = scratch[4:7], scratch[7:10], scratch[10], scratch[11]
    mod_start, mod_second, mod_third, mod_end = spread(length, every, mod_sems, a, b, c)
    shared_start, shared_second, shared_third, shared_end = spread(length, shared, shared_sems, a, b, c)
    own_rows, images = lifted_t.shape
    mask_count = mask_rows.shape[0]
    width = stage.shape[2]
    count = grad_mod.shape[1] // width
    side = remote(payload, other, side_sems.at[0], side_sems.at[1], {"section": 1 - lax.axis_index("section")})

    def save(j):
        return pltpu.make_async_copy(
            stage.at[j % 2], ada_grad.at[:, pl.ds(j * width, width)], stage_sems.at[j % 2]
        )

    def begin():
        every[a, b, c] = grad_mod[...]
        mod_start()

    def compute():
        mod_end()
        total = None
        for j in range(count):
            columns = slice(j * width, (j + 1) * width)
            rows = every[:, :, :, :, columns].astype(F32).reshape(images, width)
            bias_sum[:, columns] = jnp.sum(rows, axis=0, keepdims=True)
            rows = rows.astype(BF16)
            if j >= 2:
                save(j - 2).wait()
            stage[j % 2] = dot(lifted_t[...], rows)
            save(j).start()
            part = dot_back(ada[:, columns], rows)
            total = part if total is None else total + part
        payload[...] = jnp.zeros_like(payload)
        payload[:own_rows, :] = total * slope_t[...]
        payload[own_rows : own_rows + mask_count, :] = mask_rows[...]
        side.start()

    def add():
        side.wait()
        shared[a, b, c] = payload[...] + other[...]
        shared_start()

    def end():
        shared_end()
        for j in range(count - 2, count):
            save(j).wait()

    return begin, mod_second, mod_third, compute, add, shared_second, shared_third, end


def scatter_kernel(length, plan, slots, pair_slots, *refs):
    lefts, rights = refs[:4], refs[4:8]
    extras, outgoing = refs[8:13], refs[13]
    outs = refs[14:18]
    extra_outs, incoming = refs[18:21], refs[21]
    (
        raw, right, left_t, held, sent, core_in, pair_in, pair_late, up_in, down_in,
    ) = refs[22:32]
    (
        raw_sem, right_sem, core_s, core_r, pair_s, pair_r, up_s, up_r, down_s, down_r, out_sem,
        core_credit, pair_credit,
    ) = refs[32:45]
    a, b, c = position()
    greet_all(length, a, b, c)
    side_steps = conditioning_steps(length, extras, extra_outs, refs[45:-1], a, b, c)
    swap_sem = refs[-1]
    swap = remote(
        outgoing, incoming, swap_sem.at[0], swap_sem.at[1], {"section": 1 - lax.axis_index("section")}
    )
    swap.start()
    n = len(plan)
    rows, width = held.shape[3:]
    total_rows = raw.shape[1]
    encoder = lax.axis_index("section") == 0
    used_rows = jnp.where(encoder, total_rows // 2, total_rows)
    pair_first = [p[3] == "pair" for p in plan]
    order = [sum(pair_first[:i]) if pair_first[i] else i - sum(pair_first[:i]) for i in range(n)]
    base, total = [], 0
    for i in range(n):
        base.append(total)
        total += (length - 1) * (1 if pair_first[i] else 2)
    groups = 2 * length

    def blocks_of(w):
        return lefts[w].shape[1] // width

    raw_jobs = []
    right_jobs = []
    for i, (w, low, size, _) in enumerate(plan):
        if i == 0 or plan[i - 1][0] != w:
            raw_jobs += [(w, k) for k in range(blocks_of(w))]
        if size != 0 or plan[i - 1][0] != w:
            right_jobs.append(i)

    def raw_load(x):
        w, k = raw_jobs[x]
        src = lefts[w].at[:, pl.ds(k * width, width)]
        return pltpu.make_async_copy(src, raw.at[x % 2], raw_sem.at[x])

    def right_load(x):
        w, low, size, _ = plan[right_jobs[x]]
        src = rights[w].at[:, pl.ds(low if size else 0, width)]
        return pltpu.make_async_copy(src, right.at[x % 2], right_sem.at[x])

    progress = {"raw": 0, "right": -1}

    def turn(w):
        count = blocks_of(w)
        for k in range(count):
            x = progress["raw"]
            progress["raw"] += 1
            raw_load(x).wait()
            slot = x % 2

            def body(r, carry):
                start = pl.multiple_of(r * 128, 128)
                block = raw[slot, pl.ds(start, 128), :].astype(F32).T
                if count == 1:
                    split = block.reshape(groups, 2, rows, 128)
                    for q in range(2):
                        part = split[:, q].reshape(groups * rows, 128)
                        left_t[q, :, pl.ds(start, 128)] = part.astype(BF16)
                else:
                    near = groups // count
                    split = block.reshape(near, 2, count, rows, 128)
                    for q in range(2):
                        for j in range(count):
                            part = split[:, q, j].reshape(near * rows, 128)
                            left_t[
                                q * count + j, pl.ds(k * near * rows, near * rows), pl.ds(start, 128)
                            ] = part.astype(BF16)
                return carry

            lax.fori_loop(0, used_rows // 128, body, 0)
            if x + 2 < len(raw_jobs):
                raw_load(x + 2).start()

    def product(i, q, put):
        w, low, size, _ = plan[i]
        count = blocks_of(w)
        row_set = q if count == 1 else q * count + low
        slot = progress["right"] % 2
        tile = width // 3

        def body(k, carry):
            columns = pl.ds(pl.multiple_of(k * tile, 128), tile)

            def multiply(depth):
                result = dot(left_t[row_set, :, :depth], right[slot, :depth, columns])
                for s in range(groups):
                    put(s, columns, result[s * rows : (s + 1) * rows].astype(BF16))

            when(encoder, lambda: multiply(total_rows // 2))
            when(jnp.logical_not(encoder), lambda: multiply(total_rows))
            return carry

        lax.fori_loop(0, 3, body, 0)

    def to_core(i):
        return remote(sent.at[i % slots], core_in.at[i % slots], core_s.at[i], core_r.at[i], at(a, b, 1 - c))

    def across(i):
        target = at(a, 1 - b, c)
        if pair_first[i]:
            return remote(
                held.at[i, :, 1 - b], pair_in.at[order[i] % pair_slots], pair_s.at[i], pair_r.at[i], target
            )
        return remote(held.at[i, a, 1 - b], pair_late.at[order[i]], pair_s.at[i], pair_r.at[i], target)

    def rows_of(i):
        return (b,) if pair_first[i] else (b, 1 - b)

    def flow_index(i, dest, bb):
        if pair_first[i]:
            return base[i] + dest
        return base[i] + dest * 2 + bb

    def up(i, line, dest, bb):
        x = flow_index(i, dest - 1, bb)
        return remote(held.at[i, dest, bb], up_in.at[x], up_s.at[x], up_r.at[x], at(line + 1, b, c))

    def down(i, line, dest, bb):
        x = flow_index(i, dest, bb)
        return remote(held.at[i, dest, bb], down_in.at[x], down_s.at[x], down_r.at[x], at(line - 1, b, c))

    def add(dst, src):
        dst[...] = dst[...] + src[...]

    def credit(sem, target):
        pl.semaphore_signal(sem, inc=1, device_id=target, device_id_type=MESH)

    def produce(i):
        w = plan[i][0]
        if i == 0 or plan[i - 1][0] != w:
            turn(w)
        if progress["right"] + 1 < len(right_jobs) and right_jobs[progress["right"] + 1] == i:
            progress["right"] += 1
            right_load(progress["right"]).wait()
            if progress["right"] + 1 < len(right_jobs):
                right_load(progress["right"] + 1).start()
        if i >= slots:
            to_core(i - slots).wait_send()

        def put_sent(s, columns, value):
            sent[i % slots, s // 2, s % 2, :, columns] = value

        def put_held(s, columns, value):
            held[i, s // 2, s % 2, :, columns] = value

        product(i, 1 - c, put_sent)
        if i >= slots:
            pl.semaphore_wait(core_credit, 1)
        to_core(i).start()
        product(i, c, put_held)

    def first_add(i):
        to_core(i).wait_recv()

        def body(s, carry):
            add(held.at[i, s // 2, s % 2], core_in.at[i % slots, s // 2, s % 2])
            return carry

        lax.fori_loop(0, groups, body, 0)
        if i + slots < n:
            credit(core_credit, at(a, b, 1 - c))
        if pair_first[i]:
            if order[i] >= pair_slots:
                pl.semaphore_wait(pair_credit, 1)
            across(i).start()

    def second_add(i):
        if not pair_first[i]:
            return
        across(i).wait_recv()

        def body(s, carry):
            add(held.at[i, s, b], pair_in.at[order[i] % pair_slots, s])
            return carry

        lax.fori_loop(0, length, body, 0)
        if order[i] + pair_slots < sum(pair_first):
            credit(pair_credit, at(a, 1 - b, c))

    def line_step(i, j):
        def going_up():
            for dest in range(length - 1, j - 1, -1):
                for bb in rows_of(i):
                    if j > 0:
                        up(i, j - 1, dest, bb).wait_recv()
                        add(held.at[i, dest, bb], up_in.at[flow_index(i, dest - 1, bb)])
                    if dest > j:
                        up(i, j, dest, bb).start()

        def going_down():
            here = length - 1 - j
            for dest in range(0, here + 1):
                for bb in rows_of(i):
                    if j > 0:
                        down(i, here + 1, dest, bb).wait_recv()
                        add(held.at[i, dest, bb], down_in.at[flow_index(i, dest, bb)])
                    if dest < here:
                        down(i, here, dest, bb).start()

        when(a == j, going_up)
        when(a == length - 1 - j, going_down)

    def result(i):
        w, low, size, _ = plan[i]
        dst = outs[w].at[low] if size == 0 else outs[w].at[:, pl.ds(low, size)]
        return pltpu.make_async_copy(held.at[i, a, b], dst, out_sem.at[i])

    def finish(i):
        if pair_first[i]:
            result(i).start()
        else:
            across(i).start()

    def finish_late(i):
        if not pair_first[i]:
            across(i).wait_recv()
            add(held.at[i, a, b], pair_late.at[order[i]])
            result(i).start()

    side_steps[0]()
    raw_load(0).start()
    right_load(0).start()
    raw_load(1).start()
    produce(0)
    for t in range(n + length + 3):
        if t in SIDE_TIMES:
            side_steps[SIDE_TIMES.index(t) + 1]()
        if t < n:
            first_add(t)
        if t + 1 < n:
            produce(t + 1)
        if 0 <= t - 1 < n:
            second_add(t - 1)
        for j in range(length):
            if 0 <= t - 2 - j < n:
                line_step(t - 2 - j, j)
        if 0 <= t - 1 - length < n:
            finish(t - 1 - length)
        if 0 <= t - 2 - length < n:
            finish_late(t - 2 - length)
    side_steps[-1]()
    swap.wait()
    for i in range(n):
        if i >= n - slots:
            to_core(i).wait_send()
        across(i).wait_send()
        result(i).wait()
        for bb in rows_of(i):
            for here in range(length):

                def gone():
                    for dest in range(here + 1, length):
                        up(i, here, dest, bb).wait_send()
                    for dest in range(0, here):
                        down(i, here, dest, bb).wait_send()

                when(a == here, gone)


def scatter_all(lefts, rights, extras, outgoing, shard_shapes, plan, length):
    n = len(plan)
    slots, pair_slots = 2, 4
    total_rows = lefts[0].shape[0]
    rows, width = shard_shapes[0][0], plan[0][2]
    late = sum(p[3] != "pair" for p in plan)
    flows = (length - 1) * (n + late)
    lead = shard_shapes[-1][0]
    dma = pltpu.SemaphoreType.DMA
    grad_mod, lifted_t, slope_t, ada, mask_rows = extras
    images = lifted_t.shape[1]
    payload = (-(-(rows + mask_rows.shape[0]) // 8) * 8, images)
    small = [dma((length - 1,)), dma((length - 1,)), dma((4,))]
    slab = (rows, width)
    return pl.pallas_call(
        functools.partial(scatter_kernel, length, plan, slots, pair_slots),
        out_shape=tuple(jax.ShapeDtypeStruct(s, BF16) for s in shard_shapes)
        + (
            jax.ShapeDtypeStruct(ada.shape, F32),
            jax.ShapeDtypeStruct((1, ada.shape[1]), F32),
            jax.ShapeDtypeStruct((length, 2, 2) + payload, F32),
            jax.ShapeDtypeStruct(outgoing.shape, BF16),
        ),
        in_specs=[anywhere] * 8 + [in_vmem] * 5 + [anywhere],
        out_specs=[anywhere] * 5 + [in_vmem] * 2 + [anywhere],
        scratch_shapes=[
            pltpu.VMEM((2, total_rows, width), BF16),
            pltpu.VMEM((2, total_rows, width), BF16),
            pltpu.VMEM((2 * lead, 2 * length * rows, total_rows), BF16),
            pltpu.VMEM((n, length, 2) + slab, BF16),
            pltpu.VMEM((slots, length, 2) + slab, BF16),
            pltpu.VMEM((slots, length, 2) + slab, BF16),
            pltpu.VMEM((pair_slots, length) + slab, BF16),
            pltpu.VMEM((late,) + slab, BF16),
            pltpu.VMEM((flows,) + slab, BF16),
            pltpu.VMEM((flows,) + slab, BF16),
            dma((lead + 3,)), dma((n,)), dma((n,)), dma((n,)), dma((n,)), dma((n,)),
            dma((flows,)), dma((flows,)), dma((flows,)), dma((flows,)), dma((n,)),
            pltpu.SemaphoreType.REGULAR, pltpu.SemaphoreType.REGULAR,
            pltpu.VMEM((length, 2, 2) + grad_mod.shape, BF16),
            pltpu.VMEM((2, rows, width), F32),
            pltpu.VMEM(payload, F32),
            pltpu.VMEM(payload, F32),
        ]
        + small
        + small
        + [dma((2,)), dma((2,)), dma((2,))],
        compiler_params=pltpu.CompilerParams(
            collective_id=1, has_side_effects=True, vmem_limit_bytes=62 * 1024 * 1024
        ),
        name="scatter_grads",
    )(*lefts, *rights, *extras, outgoing)


def small_gather_kernel(length, sum_sections, own_ref, out_ref, other, *sems):
    line_s, line_r, pair_s, pair_r, core_s, core_r, side_s, side_r = sems
    a, b, c = position()
    partner = {"section": 1 - lax.axis_index("section")}
    barrier = pltpu.get_barrier_semaphore()

    def tell(target):
        pl.semaphore_signal(barrier, inc=1, device_id=target, device_id_type=MESH)

    tell(at(a, 1 - b, c))
    tell(at(a, b, 1 - c))
    for k in range(1, length):
        tell(at(lax.rem(a + k, length), b, c))
    if sum_sections:
        tell(partner)
    pl.semaphore_wait(barrier, length + 1 + int(sum_sections))
    value = own_ref[...]
    if sum_sections:
        side = remote(own_ref, other, side_s, side_r, partner)
        side.start()
        side.wait()
        value = value + other[...]
    out_ref[a, b, c] = value
    mine = out_ref.at[a, b, c]
    copies = []
    for k in range(1, length):
        to = lax.rem(a + k, length)
        copy = remote(mine, mine, line_s.at[k - 1], line_r.at[k - 1], at(to, b, c))
        copy.start()
        copies.append(copy)
    for k in range(1, length):
        source = lax.rem(a + length - k, length)
        slab = out_ref.at[source, b, c]
        remote(slab, slab, line_s.at[k - 1], line_r.at[k - 1], at(a, 1 - b, c)).wait_recv()
        copies[k - 1].wait_send()
    for go, come, s, r, to in (
        (out_ref.at[:, b, c], out_ref.at[:, 1 - b, c], pair_s, pair_r, at(a, 1 - b, c)),
        (out_ref.at[:, :, c], out_ref.at[:, :, 1 - c], core_s, core_r, at(a, b, 1 - c)),
    ):
        copy = remote(go, go, s, r, to)
        copy.start()
        remote(come, come, s, r, to).wait_recv()
        copy.wait_send()


def small_gather(own, length, sum_sections, collective_id):
    dma = pltpu.SemaphoreType.DMA
    vmem = pl.BlockSpec(memory_space=pltpu.VMEM)
    shape = (length, 2, 2) + own.shape
    return pl.pallas_call(
        functools.partial(small_gather_kernel, length, sum_sections),
        out_shape=jax.ShapeDtypeStruct(shape, own.dtype),
        in_specs=[vmem],
        out_specs=vmem,
        scratch_shapes=[
            pltpu.VMEM(own.shape, own.dtype), dma((length - 1,)), dma((length - 1,)), dma, dma, dma, dma, dma, dma,
        ],
        compiler_params=pltpu.CompilerParams(collective_id=collective_id, has_side_effects=True),
        name="small_gather",
    )(own).reshape((4 * length,) + own.shape)


def head_window(h):
    low, high = h * HD, h * HD + HD
    start = low // 128 * 128
    return low, high, start, -(-high // 128) * 128


def contract(x, y, dims):
    return lax.dot_general(x, y, ((dims[0], dims[1]), ((), ())), preferred_element_type=F32)


def head_operands(qkv_ref, rows, h):
    width = qkv_ref.shape[1] // 3
    low, high, start, stop = head_window(h)
    lane = lax.broadcasted_iota(jnp.int32, (1, stop - start), 1) + start
    inside = jnp.logical_and(lane >= low, lane < high)
    parts = [qkv_ref[rows, j * width + start : j * width + stop] for j in range(3)]
    return inside, slice(start, stop), parts


def only(inside, x):
    return jnp.where(inside, x, jnp.zeros_like(x))


def softmax_of(query, key, allowed):
    scores = jnp.where(allowed, contract(query, key, ((1,), (1,))) * HD**-0.5, MASKED)
    weights = jnp.exp(scores - jnp.max(scores, axis=-1, keepdims=True))
    return weights * (1.0 / jnp.sum(weights, axis=-1, keepdims=True))


def place(out_ref, rows, start, inside, value):
    window = slice(start, start + value.shape[1])
    out_ref[rows, window] = jnp.where(inside, value.astype(BF16), out_ref[rows, window])


def attend(qkv_ref, rows, allowed, out_ref):
    for h in range(HEADS):
        inside, window, (query, key, value) = head_operands(qkv_ref, rows, h)
        probs = softmax_of(only(inside, query), key, allowed).astype(BF16)
        place(out_ref, rows, window.start, inside, contract(probs, value, ((1,), (0,))))


def attend_back(qkv_ref, grad_ref, rows, allowed, out_ref):
    width = grad_ref.shape[1]
    for h in range(HEADS):
        inside, window, (query, key, value) = head_operands(qkv_ref, rows, h)
        query, grad = only(inside, query), only(inside, grad_ref[rows, window])
        scores = jnp.where(allowed, contract(key, query, ((1,), (1,))) * HD**-0.5, MASKED)
        weights = jnp.exp(scores - jnp.max(scores, axis=0, keepdims=True))
        probs = weights * (1.0 / jnp.sum(weights, axis=0, keepdims=True))
        grad_probs = contract(value, grad, ((1,), (1,)))
        centre = jnp.sum(probs * grad_probs, axis=0, keepdims=True)
        grad_scores = (probs * (grad_probs - centre)).astype(BF16)
        start = window.start
        place(out_ref, rows, 2 * width + start, inside, contract(probs.astype(BF16), grad, ((1,), (0,))))
        place(out_ref, rows, width + start, inside, contract(grad_scores, query, ((1,), (0,))) * HD**-0.5)
        place(out_ref, rows, start, inside, contract(grad_scores, key, ((0,), (0,))) * HD**-0.5)


def dot(x, y):
    return jnp.dot(x, y, preferred_element_type=F32)


def dot_back(x, y):
    return lax.dot_general(x, y, (((1,), (1,)), ((), ())), preferred_element_type=F32)


def dot_rows(x, y):
    return lax.dot_general(x, y, (((0,), (0,)), ((), ())), preferred_element_type=F32)


def normal(x):
    centred = x - jnp.mean(x, axis=-1, keepdims=True)
    scale = lax.rsqrt(jnp.mean(centred * centred, axis=-1, keepdims=True) + EPS)
    return centred * scale, scale


TILE = 384
DEPTH = 2
GELU = math.sqrt(2.0 / math.pi)


def columns_of(t):
    if isinstance(t, int):
        return pl.ds(t * TILE, TILE)
    return pl.ds(pl.multiple_of(t * TILE, 128), TILE)


def unit_of(t, width):
    if isinstance(t, int):
        return pl.ds(t * width, width)
    return pl.ds(pl.multiple_of(t * width, 128), width)


class Stream:
    def __init__(self, ring, sems, width):
        self.ring, self.sems, self.width = ring, sems, width
        self.stages = []

    def add(self, weight, back, inner, outer):
        self.stages.append((weight, back, inner, outer))

    def tile(self, stage, n, k):
        weight, back, inner, _ = self.stages[stage]
        t = n * inner + k
        slot = t % DEPTH if isinstance(t, int) else lax.rem(t, DEPTH)
        deep, side = unit_of(k, self.width), unit_of(n, self.width)
        src = weight.at[side, deep] if back else weight.at[deep, side]
        buffer = self.ring.at[stage % 2, slot]
        return pltpu.make_async_copy(src, buffer, self.sems.at[stage % 2, slot]), buffer

    def begin(self, stage):
        if stage < len(self.stages):
            _, _, inner, outer = self.stages[stage]
            for t in range(min(DEPTH, inner * outer)):
                self.tile(stage, t // inner, t % inner)[0].start()

    def run(self, stage, use, ahead=True):
        _, _, inner, outer = self.stages[stage]
        if ahead:
            self.begin(stage + 1)
        count = inner * outer

        def group(n):
            def product(k, left, back):
                copy, buffer = self.tile(stage, n, k)
                copy.wait()
                result = (dot_back if back else dot)(left, buffer[...])
                t = n * inner + k + DEPTH

                def refill():
                    self.tile(stage, lax.div(t, inner), lax.rem(t, inner))[0].start()

                if not isinstance(t, int):
                    when(t < count, refill)
                elif t < count:
                    self.tile(stage, t // inner, t % inner)[0].start()
                return result

            use(n, product)

        def body(n, carry):
            group(n)
            return carry

        if outer == 1:
            group(0)
        else:
            lax.fori_loop(0, outer, body, 0)


def each_quarter(rows, run):
    def body(q, carry):
        run(q, pl.ds(pl.multiple_of(q * rows, rows), rows))
        return carry

    lax.fori_loop(0, 8, body, 0)


def piece_of(mod_ref, q, p, width, columns=None):
    if columns is None:
        return mod_ref[q, :, p * width : (p + 1) * width]
    return mod_ref[q, :, pl.ds(p * width + columns.start, TILE)]


def modulate(x_ref, mod_ref, out_ref, first, quarter_rows):
    width = x_ref.shape[1]

    def run(q, rows):
        hat = normal(x_ref[rows, :])[0]
        shift, scale = piece_of(mod_ref, q, first, width), piece_of(mod_ref, q, first + 1, width)
        out_ref[rows, :] = (hat * (1.0 + scale) + shift).astype(BF16)

    each_quarter(quarter_rows, run)


def modulate_back(grad, x, scale):
    hat, inverse = normal(x)
    inner = grad * (1.0 + scale)
    along = jnp.mean(inner * hat, axis=-1, keepdims=True)
    grad_x = inverse * (inner - jnp.mean(inner, axis=-1, keepdims=True) - hat * along)
    return grad_x, jnp.sum(grad, axis=0, keepdims=True), jnp.sum(grad * hat, axis=0, keepdims=True)


def split_quarters(quarter_rows, run):
    for q in range(8):
        run(q, slice(q * quarter_rows, (q + 1) * quarter_rows))


def allowed_of(row_ref, column_ref, block):
    rows = pl.ds(pl.multiple_of(block * ATT_ROWS, ATT_ROWS), ATT_ROWS)
    return rows, row_ref[rows, :] == column_ref[block]


def each_block(total_rows, run):
    def body(block, carry):
        run(block)
        return carry

    lax.fori_loop(0, total_rows // ATT_ROWS, body, 0)


def forward_stages(stream, weights):
    width = weights[0].shape[0]
    qkv, proj, up, down = weights
    stream.add(qkv, False, 1, qkv.shape[1] // width)
    stream.add(proj, False, 1, 1)
    stream.add(up, False, 1, up.shape[1] // width)
    stream.add(down, False, down.shape[0] // width, 1)


def backward_stages(stream, weights):
    width = weights[0].shape[0]
    qkv, proj, up, down = weights
    stream.add(down, True, 1, down.shape[0] // width)
    stream.add(up, True, up.shape[1] // width, 1)
    stream.add(proj, True, 1, 1)
    stream.add(qkv, True, qkv.shape[1] // width, 1)


def by_parts(quarter_rows, width, run):
    def one(q, rows):
        for t in range(width // TILE):
            run(q, rows, slice(t * TILE, (t + 1) * TILE))

    each_quarter(quarter_rows, one)


def proj_tile(r, mod_ref, quarter_rows, columns, branch):
    width = r.x.shape[1]
    r.branch[:, columns] = branch.astype(BF16)

    def gated(q, rows):
        gate = piece_of(mod_ref, q, 2, width, columns)
        r.x2[rows, columns] = r.x[rows, columns] + gate * branch[rows]

    split_quarters(quarter_rows, gated)


def gelu_parts(h):
    square = h * h
    t = jnp.tanh(h * (GELU + (GELU * 0.044715) * square))
    half = 0.5 + 0.5 * t
    return h * half, half + (0.5 * h) * (1.0 - t * t) * (GELU + (3.0 * GELU * 0.044715) * square)


def up_tile(r, columns, h):
    act, slope = gelu_parts(h)
    r.act[:, columns] = act.astype(BF16)
    r.slope[:, columns] = slope.astype(BF16)


def out_tile(r, mod_ref, quarter_rows, columns, mlp):
    width = r.x.shape[1]
    r.mlp[:, columns] = mlp.astype(BF16)

    def gated(q, rows):
        gate = piece_of(mod_ref, q, 5, width, columns)
        r.out[rows, columns] = (r.x2[rows, columns] + gate * mlp[rows]).astype(BF16)

    split_quarters(quarter_rows, gated)


def run_forward(stream, r, mod_ref, segments, quarter_rows, finish_part, done):
    width = r.x.shape[1]
    total_rows = r.x.shape[0]
    modulate(r.x, mod_ref, r.a1, 0, quarter_rows)

    def qkv(n, product):
        r.qkv[:, unit_of(n, width)] = product(0, r.a1[...], False).astype(BF16)

    stream.run(0, qkv)
    done("a1")

    def mix(block):
        rows, allowed = allowed_of(*segments, block)
        attend(r.qkv, rows, allowed, r.att)

    each_block(total_rows, mix)

    def proj(n, product):
        r.acc[...] = product(0, r.att[...], False)

    stream.run(1, proj)
    done("att")

    def gated(q, rows, columns):
        branch = r.acc[rows, columns]
        r.branch[rows, columns] = branch.astype(BF16)
        gate = piece_of(mod_ref, q, 2, width, columns)
        r.x2[rows, columns] = r.x[rows, columns] + gate * branch

    by_parts(quarter_rows, width, gated)
    modulate(r.x2, mod_ref, r.a2, 3, quarter_rows)

    def up(n, product):
        r.acc[...] = product(0, r.a2[...], False)

        def part(q, rows, columns):
            into = pl.ds(pl.multiple_of(n * width + columns.start, 128), TILE)
            act, slope = gelu_parts(r.acc[rows, columns])
            r.act[rows, into] = act.astype(BF16)
            r.slope[rows, into] = slope.astype(BF16)

        by_parts(quarter_rows, width, part)

    stream.run(2, up)
    done("a2")

    def down(n, product):
        for k in range(r.act.shape[1] // width):
            part = product(k, r.act[:, k * width : (k + 1) * width], False)
            if k == 0:
                r.acc[...] = part
            else:
                r.acc[...] += part

    stream.run(3, down)
    done("act")
    by_parts(quarter_rows, width, lambda q, rows, columns: finish_part(q, rows, columns, r.acc[rows, columns]))


def run_backward(stream, first, r, mod_ref, segments, quarter_rows, grad_of, finish, done):
    width = r.x.shape[1]
    total_rows = r.x.shape[0]

    def down(n, product):
        columns = unit_of(n, width)
        grad = product(0, r.dmlp[...], True)
        r.slope[:, columns] = (grad * r.slope[:, columns].astype(F32)).astype(BF16)

    stream.run(first, down)
    done("dmlp")
    done("slope")

    def up(n, product):
        for k in range(r.slope.shape[1] // width):
            part = product(k, r.slope[:, k * width : (k + 1) * width], True)
            if k == 0:
                r.dx2[...] = part
            else:
                r.dx2[...] += part

    stream.run(first + 1, up)

    def middle(q, rows):
        scale, gate = piece_of(mod_ref, q, 4, width), piece_of(mod_ref, q, 2, width)
        grad, shift_grad, scale_grad = modulate_back(r.dx2[rows, :], r.x2[rows, :], scale)
        grad = grad + grad_of(rows)
        r.dx2[rows, :] = grad
        r.dmod[q, :, 3 * width : 4 * width] = shift_grad
        r.dmod[q, :, 4 * width : 5 * width] = scale_grad
        r.dmod[q, :, 2 * width : 3 * width] = jnp.sum(
            grad * r.branch[rows, :].astype(F32), axis=0, keepdims=True
        )
        r.dbranch[rows, :] = (gate * grad).astype(BF16)

    each_quarter(quarter_rows, middle)

    def proj(n, product):
        r.datt[...] = product(0, r.dbranch[...], True).astype(BF16)

    stream.run(first + 2, proj)
    done("dbranch")

    def mix(block):
        rows, allowed = allowed_of(*segments, block)
        attend_back(r.qkv, r.datt, rows, allowed, r.dqkv)

    each_block(total_rows, mix)
    done("dqkv")

    def qkv(n, product):
        for k in range(3):
            part = product(k, r.dqkv[:, k * width : (k + 1) * width], True)
            if k == 0:
                r.acc[...] = part
            else:
                r.acc[...] += part

    stream.run(first + 3, qkv, ahead=False)

    def outer(q, rows):
        scale = piece_of(mod_ref, q, 1, width)
        grad, shift_grad, scale_grad = modulate_back(r.acc[rows, :], r.x[rows, :], scale)
        r.dmod[q, :, :width] = shift_grad
        r.dmod[q, :, width : 2 * width] = scale_grad
        finish(q, rows, grad + r.dx2[rows, :])

    each_quarter(quarter_rows, outer)
    done("dmod")


def placed(kept_ref, m, slot):
    kept = kept_ref[m]
    positions = lax.broadcasted_iota(jnp.int32, (slot, kept.shape[1]), 0)
    return jnp.where(positions == kept, 1.0, 0.0).astype(BF16)


class Copies:
    def __init__(self, sems):
        self.sems, self.count, self.pending = sems, 0, []

    def start(self, src, dst):
        copy = pltpu.make_async_copy(src, dst, self.sems.at[self.count])
        self.count += 1
        copy.start()
        self.pending.append(copy)
        return copy

    def finish(self):
        for copy in self.pending:
            copy.wait()
        self.pending = []


def encode_kernel(names, tokens, kept_ref, mod_ref, row_ref, column_ref, wq, wp, wu, wd, *rest):
    outs, scratch = rest[: len(names)], rest[len(names) :]
    r = SimpleNamespace(**dict(zip(names + ("acc",), scratch[: len(names) + 1])))
    loaded, ring, stream_sems, sems = scratch[len(names) + 1 :]
    width = loaded.shape[2]
    slot = loaded.shape[1]

    def work():
        stream = Stream(ring, stream_sems, width)
        forward_stages(stream, (wq, wp, wu, wd))
        copies = Copies(sems)
        copies.start(tokens, loaded)
        stream.begin(0)
        copies.finish()
        kept = kept_ref.shape[2]
        for m in range(2):
            r.x[m * kept : (m + 1) * kept, :] = dot_rows(placed(kept_ref, m, slot), loaded[m])
        total_rows = r.x.shape[0]
        out_of = dict(zip(names, outs))

        def done(name):
            copies.start(getattr(r, name), out_of[name].at[pl.ds(0, total_rows)])

        def finish_part(q, rows, columns, mlp):
            r.mlp[rows, columns] = mlp.astype(BF16)
            gate = piece_of(mod_ref, q, 5, width, columns)
            r.out[rows, columns] = (r.x2[rows, columns] + gate * mlp).astype(BF16)

        run_forward(stream, r, mod_ref, (row_ref, column_ref), total_rows // 8, finish_part, done)
        for name in ("x", "x2", "qkv", "branch", "slope", "mlp", "out"):
            done(name)
        copies.finish()

    when(lax.axis_index("section") == 0, work)


def decode_kernel(
    names, rights, received, cotangent, kept_ref, mask_ref, mod_ref, row_ref, column_ref, wq, wp, wu, wd,
    a1, att, a2, act, *rest,
):
    outs, scratch = rest[: 4 + len(rights) + 4], rest[4 + len(rights) + 4 :]
    lefts = dict(zip(("a1", "att", "a2", "act"), outs[:4]))
    right_outs = dict(zip(rights, outs[4 : 4 + len(rights)]))
    dmod_out, decoded, back, mask_out = outs[4 + len(rights) :]
    r = SimpleNamespace(**dict(zip(names, scratch[: len(names)])))
    got, ring, stream_sems, sems = scratch[len(names) :]
    width = got.shape[2]

    def work():
        stream = Stream(ring, stream_sems, width)
        forward_stages(stream, (wq, wp, wu, wd))
        backward_stages(stream, (wq, wp, wu, wd))
        copies = Copies(sems)
        copies.start(received, got)
        copies.start(cotangent, r.dy)
        stream.begin(0)
        copies.finish()
        total_rows = r.x.shape[0]
        slot, kept = total_rows // 2, kept_ref.shape[2]
        for m in range(2):
            place = placed(kept_ref, m, slot)
            flags = jnp.sum(place.astype(F32), axis=1, keepdims=True)
            r.free[m * slot : (m + 1) * slot, :] = jnp.broadcast_to(1.0 - flags, (slot, 128))
            filled = dot(place, got[m]) + (1.0 - flags) * mask_ref[...].astype(F32)
            r.x[m * slot : (m + 1) * slot, :] = filled
        out_of = {**lefts, **right_outs, "dmod": dmod_out, "slope": right_outs["dhid"]}

        def done(name):
            copies.start(getattr(r, name), out_of[name])

        def finish_part(q, rows, columns, part):
            gate = piece_of(mod_ref, q, 5, width, columns)
            dy = r.dy[rows, columns].astype(F32)
            r.out[rows, columns] = (r.x2[rows, columns] + gate * part).astype(BF16)
            r.dmlp[rows, columns] = (gate * dy).astype(BF16)
            r.dmod[q, :, 5 * width + columns.start : 5 * width + columns.stop] = jnp.sum(
                dy * part, axis=0, keepdims=True
            )

        segments = (row_ref, column_ref)
        run_forward(stream, r, mod_ref, segments, total_rows // 8, finish_part, done)
        copies.start(r.out, decoded)
        r.mask[...] = jnp.zeros_like(r.mask)

        def finish(q, rows, grad):
            r.mask[...] += jnp.sum(grad * r.free[rows, :1], axis=0, keepdims=True)
            r.dbranch[rows, :] = grad.astype(BF16)

        def grad_of(rows):
            return r.dy[rows, :].astype(F32)

        def done_back(name):
            if name == "dbranch":
                copies.start(getattr(r, name), out_of[name]).wait()
                copies.pending.pop()
            else:
                done(name)

        run_backward(stream, 4, r, mod_ref, segments, total_rows // 8, grad_of, finish, done_back)
        for m in range(2):
            place = placed(kept_ref, m, slot)
            got[m] = dot_rows(place, r.dbranch[m * slot : (m + 1) * slot, :]).astype(BF16)
        copies.start(got, back)
        copies.start(r.mask, mask_out)
        copies.finish()

    when(lax.axis_index("section") == 1, work)


def encode_back_kernel(
    names, rights, saved, received, kept_ref, mod_ref, row_ref, column_ref, wq, wp, wu, wd, *rest
):
    kept_in = dict(zip(saved, rest[: len(saved)]))
    rest = rest[len(saved) + len(rights) + 1 :]
    right_outs = dict(zip(rights, rest[: len(rights)]))
    dmod_out, token_out = rest[len(rights) : len(rights) + 2]
    scratch = rest[len(rights) + 2 :]
    r = SimpleNamespace(**dict(zip(names, scratch[: len(names)])))
    ring, stream_sems, sems = scratch[len(names) :]
    width = r.x.shape[1]

    def work():
        stream = Stream(ring, stream_sems, width)
        backward_stages(stream, (wq, wp, wu, wd))
        copies = Copies(sems)
        copies.start(received, r.dy)
        for name in saved:
            copies.start(kept_in[name], getattr(r, name))
        stream.begin(0)
        copies.finish()
        total_rows = r.x.shape[0]
        out_of = {**right_outs, "dmod": dmod_out, "slope": right_outs["dhid"]}

        def done(name):
            if name == "dmod":
                copies.start(getattr(r, name), out_of[name])
            else:
                copies.start(getattr(r, name), out_of[name].at[pl.ds(0, total_rows)])

        def start(q, rows):
            gate = piece_of(mod_ref, q, 5, width)
            dy = r.dy[rows, :].astype(F32)
            r.dmlp[rows, :] = (gate * dy).astype(BF16)
            r.dmod[q, :, 5 * width :] = jnp.sum(dy * r.mlp[rows, :].astype(F32), axis=0, keepdims=True)

        each_quarter(total_rows // 8, start)

        def finish(q, rows, grad):
            r.mlp[rows, :] = grad.astype(BF16)

        def grad_of(rows):
            return r.dy[rows, :].astype(F32)

        segments = (row_ref, column_ref)
        run_backward(stream, 0, r, mod_ref, segments, total_rows // 8, grad_of, finish, done)
        kept = kept_ref.shape[2]
        slot = token_out.shape[1]
        for m in range(2):
            place = placed(kept_ref, m, slot)
            r.tokens[m] = dot(place, r.mlp[m * kept : (m + 1) * kept, :]).astype(BF16)
        copies.start(r.tokens, token_out)
        copies.finish()

    when(lax.axis_index("section") == 0, work)


VMEM_BYTES = 60 * 1024 * 1024
LEFTS = ("a1", "att", "a2", "act")
RIGHTS = ("dqkv", "dbranch", "dhid", "dmlp")
SAVED = ("x", "x2", "qkv", "branch", "slope", "mlp")


def buffer_shapes(rows, width, wide_width):
    full, broad = lambda t: ((rows, width), t), lambda n, t: ((rows, n), t)
    return dict(
        x=full(F32), x2=full(F32), dx2=full(F32), acc=full(F32), a1=full(BF16),
        att=full(BF16), a2=full(BF16), branch=full(BF16), mlp=full(BF16), out=full(BF16),
        dy=full(BF16), dmlp=full(BF16), dbranch=full(BF16), datt=full(BF16),
        qkv=broad(3 * width, BF16), dqkv=broad(3 * width, BF16), act=broad(wide_width, BF16),
        slope=broad(wide_width, BF16), dhid=broad(wide_width, BF16),
        dmod=((8, 1, 6 * width), F32), mask=((1, width), F32), free=((rows, 128), F32),
    )


def rings(width):
    dma = pltpu.SemaphoreType.DMA
    return [pltpu.VMEM((2, DEPTH, width, width), BF16), dma((2, DEPTH)), dma((24,))]


def encode(tokens, kept, modulation, segments, weights, rows, all_rows):
    width, wide_width = weights[0].shape[0], weights[2].shape[1]
    shapes = buffer_shapes(rows, width, wide_width)
    names = LEFTS + SAVED + ("out",)
    outs = [jax.ShapeDtypeStruct(((all_rows if n in LEFTS else rows), shapes[n][0][1]), shapes[n][1]) for n in names]
    results = pl.pallas_call(
        functools.partial(encode_kernel, names),
        out_shape=outs,
        in_specs=[anywhere] + [in_vmem] * 4 + [anywhere] * 4,
        out_specs=[anywhere] * len(names),
        scratch_shapes=[pltpu.VMEM(*shapes[n]) for n in names + ("acc",)]
        + [pltpu.VMEM(tokens.shape, BF16)]
        + rings(width),
        compiler_params=pltpu.CompilerParams(vmem_limit_bytes=VMEM_BYTES),
        name="encode",
    )(tokens, kept, modulation, *segments, *weights)
    return results[:4], results[4:-1], results[-1]


def decode(received, cotangent, kept, mask_token, modulation, segments, weights, lefts):
    width, wide_width = weights[0].shape[0], weights[2].shape[1]
    rows = cotangent.shape[0]
    shapes = buffer_shapes(rows, width, wide_width)
    names = LEFTS + (
        "x", "x2", "qkv", "branch", "slope", "out", "dy", "dmlp", "dbranch", "datt", "dqkv", "dmod",
        "mask", "free",
    )
    scratch = [pltpu.VMEM(*shapes[n]) for n in names]
    names += ("dx2", "acc")
    scratch += [pltpu.VMEM(*shapes["dx2"]), pltpu.VMEM(*shapes["acc"])]
    outs = [jax.ShapeDtypeStruct(*shapes[n]) for n in LEFTS + RIGHTS + ("dmod", "out")]
    outs += [jax.ShapeDtypeStruct(received.shape, BF16), jax.ShapeDtypeStruct((1, width), F32)]
    results = pl.pallas_call(
        functools.partial(decode_kernel, names, RIGHTS),
        out_shape=outs,
        in_specs=[anywhere] * 2 + [in_vmem] * 5 + [anywhere] * 8,
        out_specs=[anywhere] * len(outs),
        scratch_shapes=scratch + [pltpu.VMEM(received.shape, BF16)] + rings(width),
        input_output_aliases={11 + j: j for j in range(4)},
        compiler_params=pltpu.CompilerParams(vmem_limit_bytes=VMEM_BYTES),
        name="decode",
    )(received, cotangent, kept, mask_token, modulation, *segments, *weights, *lefts)
    return results[:4], results[4:8], results[8:]


def encode_back(received, kept, modulation, segments, weights, saved, rights, grad_mod, token_shape):
    width, wide_width = weights[0].shape[0], weights[2].shape[1]
    rows = received.shape[0]
    shapes = buffer_shapes(rows, width, wide_width)
    names = SAVED + ("dy", "dmlp", "dbranch", "datt", "dqkv", "dmod", "dx2", "acc", "tokens")
    shapes["tokens"] = (token_shape, BF16)
    outs = [jax.ShapeDtypeStruct(x.shape, x.dtype) for x in tuple(rights) + (grad_mod,)]
    outs.append(jax.ShapeDtypeStruct(token_shape, BF16))
    before = 9 + len(saved)
    results = pl.pallas_call(
        functools.partial(encode_back_kernel, names, RIGHTS, SAVED),
        out_shape=outs,
        in_specs=[anywhere] + [in_vmem] * 4 + [anywhere] * (4 + len(saved) + 5),
        out_specs=[anywhere] * len(outs),
        scratch_shapes=[pltpu.VMEM(*shapes[n]) for n in names] + rings(width),
        input_output_aliases={before + j: j for j in range(5)},
        compiler_params=pltpu.CompilerParams(vmem_limit_bytes=VMEM_BYTES),
        name="encode_back",
    )(received, kept, modulation, *segments, *weights, *saved, *rights, grad_mod)
    return results[:4], results[4], results[5]


def gather_encode_kernel(length, plan, names, *refs):
    sources, (partial, big_ref, tokens, kept_ref, row_ref, column_ref) = refs[:4], refs[4:10]
    outs, (mod_out, received) = refs[10:14], refs[14:16]
    saved_outs = refs[16 : 16 + len(names)]
    rest = refs[16 + len(names) :]
    r = SimpleNamespace(**dict(zip(names + ("out",), rest[: len(names) + 1])))
    (
        loaded, mod_ref, tiles, last_tile, part_held, part_core, part_pair, part_line,
    ) = rest[len(names) + 1 : len(names) + 9]
    sems = rest[len(names) + 9 : len(names) + 18]
    part_sems, line_sems, tile_sems, out_sems, copy_sems = rest[len(names) + 18 :]
    a, b, c = position()
    encoder = lax.axis_index("section") == 0
    other = {"section": 1 - lax.axis_index("section")}
    barrier = pltpu.get_barrier_semaphore()

    def tell(target):
        pl.semaphore_signal(barrier, inc=1, device_id=target, device_id_type=MESH)

    tell(at(a, 1 - b, c))
    tell(at(a, b, 1 - c))
    tell(other)
    for k in range(1, length):
        tell(at(lax.rem(a + k, length), b, c))
    pl.semaphore_wait(barrier, length + 2)

    n = len(plan)
    width = r.x.shape[1]
    total_rows = r.x.shape[0]
    quarter_rows = total_rows // 8
    issue, move, complete, drain = gather_moves(length, plan, sources, outs, sems, a, b, c)
    copies = Copies(copy_sems)
    out_of = dict(zip(names, saved_outs))

    part_load = pltpu.make_async_copy(partial.at[:, :, c], part_held, part_sems.at[0])
    part_to_core = remote(partial.at[:, :, 1 - c], part_core, part_sems.at[1], part_sems.at[2], at(a, b, 1 - c))
    part_across = remote(part_held.at[:, 1 - b], part_pair, part_sems.at[3], part_sems.at[4], at(a, 1 - b, c))

    def part_to_line(k):
        to = lax.rem(a + k, length)
        return remote(
            part_held.at[to, b], part_line.at[k - 1], line_sems.at[0, k - 1], line_sems.at[1, k - 1], at(to, b, c)
        )

    def add_part(where, got):
        part_held[where] = part_held[where] + got

    def part_first():
        part_to_core.wait_recv()
        part_load.wait()
        for s in range(2 * length):
            add_part((s // 2, s % 2), part_core[s // 2, s % 2])
        part_across.start()

    def part_second():
        part_across.wait()
        for aa in range(length):
            add_part((aa, b), part_pair[aa])
        for k in range(1, length):
            part_to_line(k).start()

    def part_last():
        total = part_held[a, b].astype(F32)
        for k in range(1, length):
            part_to_line(k).wait_recv()
            total = total + part_line[k - 1].astype(F32)
        for q in range(8):
            first = q // SMALL_PER * SMALL_PER
            mod_ref[q] = jnp.where(big_ref[q] > 0, total[first : first + 1], total[q : q + 1])
        copies.start(mod_ref, mod_out)

    def load_tile(w, low, t):
        src = outs[w].at[:, :, :, :, pl.ds(low + t * TILE, TILE)]
        return pltpu.make_async_copy(src, tiles.at[t % 2], tile_sems.at[t % 2])

    def products(w, low, left, put):
        count = width // TILE
        for t in range(min(2, count)):
            load_tile(w, low, t).start()
        for t in range(count):
            load_tile(w, low, t).wait()
            tile = tiles[t % 2].astype(F32).reshape(width, TILE).astype(BF16)
            result = dot(getattr(r, left)[...], tile)
            if t + 2 < count:
                load_tile(w, low, t + 2).start()
            put(columns_of(low // TILE + t), result)

    def done(name):
        copies.start(getattr(r, name), out_of[name].at[pl.ds(0, total_rows)])

    def start_encode():
        fetch = pltpu.make_async_copy(tokens, loaded, tile_sems.at[2])
        fetch.start()
        fetch.wait()
        kept, slot = kept_ref.shape[2], loaded.shape[1]
        for m in range(2):
            r.x[m * kept : (m + 1) * kept, :] = dot_rows(placed(kept_ref, m, slot), loaded[m])

    def put_qkv(columns, result):
        r.qkv[:, columns] = result.astype(BF16)

    def put_proj(columns, result):
        proj_tile(r, mod_ref, quarter_rows, columns, result)

    def put_up(columns, result):
        up_tile(r, columns, result)

    def send_out(t):
        columns = columns_of(t)
        return remote(
            r.out.at[:, columns], received.at[:, columns], out_sems.at[0, t], out_sems.at[1, t], other
        )

    def encode_chunk(i):
        w, low, _, _ = plan[i]
        if w == 0:
            if i == 0:
                modulate(r.x, mod_ref, r.a1, 0, quarter_rows)
            products(w, low, "a1", put_qkv)
        elif w == 1:
            rows, allowed = slice(0, total_rows), row_ref[...] == column_ref[0]
            attend(r.qkv, rows, allowed, r.att)
            products(w, low, "att", put_proj)
            modulate(r.x2, mod_ref, r.a2, 3, quarter_rows)
        elif w == 2:
            products(w, low, "a2", put_up)
        else:
            src = outs[w].at[:, :, :, :, pl.ds(low, TILE)]
            fetch = pltpu.make_async_copy(src, last_tile, tile_sems.at[2])
            fetch.start()
            fetch.wait()
            tile = last_tile[...].reshape(r.act.shape[1], TILE)
            out_tile(r, mod_ref, quarter_rows, columns_of(low // TILE), dot(r.act[...], tile))
            send_out(low // TILE).start()

    part_load.start()
    part_to_core.start()
    issue(0)
    when(encoder, start_encode)
    part_first()
    for i in range(1, AHEAD):
        issue(i)
    for t in range(n + length - 1):
        move(t, AHEAD)
        if t == 0:
            part_second()
        if t == 1:
            part_last()
        i = t - length + 1
        if i >= 0:
            complete(i)
            when(encoder, lambda: encode_chunk(i))
    for i in range(n):
        drain(i)
    part_to_core.wait_send()
    for k in range(1, length):
        part_to_line(k).wait_send()

    def close():
        for name in names:
            done(name)
        for copy in copies.pending[1:]:
            copy.wait()
        for t in range(width // TILE):
            send_out(t).wait_send()

    when(encoder, close)
    copies.pending[0].wait()

    def arrive():
        for t in range(width // TILE):
            send_out(t).wait_recv()

    when(jnp.logical_not(encoder), arrive)


AHEAD = 4


def gather_encode(shards, partial, big, tokens, kept, segments, plan, length, rows, all_rows):
    n = len(plan)
    width, wide_width = shards[1].shape[1], shards[2].shape[1]
    shapes = buffer_shapes(rows, width, wide_width)
    names = LEFTS + SAVED
    quarters = partial.shape[3]
    part_slab = partial.shape[3:]
    dma = pltpu.SemaphoreType.DMA
    outs = [jax.ShapeDtypeStruct((length, 2, 2) + s.shape, BF16) for s in shards]
    outs += [jax.ShapeDtypeStruct((quarters, 1, 6 * width), F32), jax.ShapeDtypeStruct((rows, width), BF16)]
    outs += [jax.ShapeDtypeStruct(((all_rows if m in LEFTS else rows), shapes[m][0][1]), shapes[m][1]) for m in names]
    results = pl.pallas_call(
        functools.partial(gather_encode_kernel, length, plan, names),
        out_shape=outs,
        in_specs=[anywhere] * 5 + [in_vmem, anywhere] + [in_vmem] * 3,
        out_specs=[anywhere] * len(outs),
        scratch_shapes=[pltpu.VMEM(*shapes[m]) for m in names + ("out",)]
        + [
            pltpu.VMEM(tokens.shape, BF16),
            pltpu.VMEM((quarters, 1, 6 * width), F32),
            pltpu.VMEM((2, length, 2, 2, shards[0].shape[0], TILE), BF16),
            pltpu.VMEM((length, 2, 2, shards[3].shape[0], TILE), BF16),
            pltpu.VMEM((length, 2) + part_slab, BF16),
            pltpu.VMEM((length, 2) + part_slab, BF16),
            pltpu.VMEM((length,) + part_slab, BF16),
            pltpu.VMEM((length - 1,) + part_slab, BF16),
        ]
        + [dma((n, length, 2))] * 4
        + [dma((n, length))] * 2
        + [dma((n, length, 2))] * 2
        + [dma((n,)), dma((5,)), dma((2, length - 1)), dma((3,)), dma((2, width // TILE)), dma((len(names) + 1,))],
        compiler_params=pltpu.CompilerParams(
            collective_id=0, has_side_effects=True, vmem_limit_bytes=VMEM_BYTES
        ),
        name="gather_encode",
    )(*shards, partial, big, tokens, kept, *segments)
    return results[:4], results[4], results[5], results[6:10], results[10:]


def plan_of(widths, lead, unit, line_first):
    plan = [(w, low, unit) for w, width in enumerate(widths) for low in range(0, width, unit)]
    plan += [(len(widths), j, 0) for j in range(lead)]
    return tuple(p + ("line" if i in line_first else "pair",) for i, p in enumerate(plan))


def swap_sections(x):
    return lax.ppermute(x, "section", [(0, 1), (1, 0)])


def on_device(
    tokens, kept_index, big_image, timesteps, labels, cotangent, mask_token, time_weight, class_table,
    ada_weight, ada_bias, qkv_weight, proj_weight, up_weight, down_weight,
):
    section = lax.axis_index("section")
    me = lax.axis_index("dp")
    devices = lax.axis_size("dp")
    micro, slot, width = tokens.shape
    kept_count = kept_index.shape[1]
    own_width = ada_weight.shape[1]
    images = micro * SMALL_PER
    quarters = micro * SMALL_PER
    ada = ada_weight[0]

    length = devices // 4
    ids = jnp.concatenate([timesteps.reshape(1, images), labels.reshape(1, images)])
    if length == 4:
        ids = small_gather(jnp.pad(ids, ((0, 6), (0, 128 - images))), length, False, 2)
    else:
        ids = lax.all_gather(ids, "dp", axis=0)
    times = ids[:, 0, :images].reshape(devices * images)
    classes = ids[:, 1, :images].reshape(devices * images)
    half = time_weight.shape[0] // 2
    frequencies = jnp.exp(-math.log(10000.0) * jnp.arange(half, dtype=F32) / half)
    angles = times.astype(F32)[:, None] * frequencies[None, :]
    embedding = jnp.concatenate([jnp.cos(angles), jnp.sin(angles)], axis=-1).astype(BF16)
    onehot = (classes[:, None] == jnp.arange(class_table.shape[0])[None, :]).astype(BF16)
    cond = dot(embedding, time_weight) + dot(onehot, class_table)
    cond = lax.dynamic_slice_in_dim(cond, me * own_width, own_width, axis=1)
    lifted = jax.nn.silu(cond).astype(BF16)
    bias_width = ada_bias.shape[1]
    bias = lax.dynamic_update_slice_in_dim(
        jnp.zeros((1, 6 * width), F32), ada_bias.astype(F32), me * bias_width, axis=1
    )
    partial = (dot(lifted, ada) + bias).astype(BF16).reshape(devices, images, 6 * width)

    big = big_image[:, :1] > 0
    quarter_ids = jnp.arange(quarters, dtype=jnp.int32).reshape(micro, SMALL_PER)
    segment_of = jnp.where(big, quarter_ids[:, :1], quarter_ids).reshape(quarters)
    kept = kept_index.reshape(micro, 1, kept_count)

    def segments(quarter_rows):
        ids = jnp.repeat(segment_of, quarter_rows)
        return ids.reshape(-1, 1), ids.reshape(-1, 1, ATT_ROWS)

    enc_rows, dec_rows = micro * kept_count, micro * slot
    enc_segments = segments(enc_rows // quarters)
    dec_segments = segments(dec_rows // quarters)

    shards = (qkv_weight[0], proj_weight[0], up_weight[0])
    lead = down_weight.shape[1] // qkv_weight.shape[1]
    widths = [x.shape[1] for x in shards]
    if length == 4:
        plan = [(w, low, width, "line") for w in range(3) for low in range(0, widths[w], width)]
        plan += [(3, low, TILE, "line") for low in range(0, width, TILE)]
        plan = tuple(p[:3] + ("pair" if i in (1, 7) else "line",) for i, p in enumerate(plan))
        flags = jnp.repeat(big[:, 0], SMALL_PER).astype(jnp.int32).reshape(quarters, 1, 1)
        whole, modulation, received, lefts, saved = gather_encode(
            shards + (down_weight[0],), partial.reshape((length, 2, 2) + partial.shape[1:]), flags, tokens, kept,
            enc_segments, plan, length, enc_rows, dec_rows,
        )
        weights = tuple(w.reshape(-1, w.shape[-1]) for w in whole)
        received = received.reshape(micro, kept_count, width)
    else:
        whole = (lax.all_gather(x, "dp", axis=0, tiled=True) for x in shards + (down_weight[0],))
        weights = tuple(whole)
        modulation = lax.psum_scatter(partial, "dp", scatter_dimension=0, tiled=False).astype(F32)
        modulation = modulation.reshape(micro, SMALL_PER, 6 * width)
        modulation = jnp.where(big[:, :, None], modulation[:, :1], modulation).reshape(quarters, 1, 6 * width)
        lefts, saved, encoded = encode(tokens, kept, modulation, enc_segments, weights, enc_rows, dec_rows)
        received = swap_sections(encoded).reshape(micro, kept_count, width)

    lefts, rights, (grad_mod, decoded, back, mask_part) = decode(
        received, cotangent.reshape(dec_rows, width), kept, mask_token.reshape(1, width), modulation,
        dec_segments, weights, lefts,
    )
    received = swap_sections(back).reshape(enc_rows, width)
    rights, grad_mod, token_grad = encode_back(
        received, kept, modulation, enc_segments, weights, saved, rights, grad_mod, (micro, slot, width)
    )
    decoded = decoded.reshape(micro, slot, width)
    mask_part = jnp.where(section == 1, mask_part, 0.0).reshape(width)

    half_width = width // 2
    outgoing = jnp.where(section == 0, token_grad[:, :, half_width:], decoded[:, :, :half_width])

    grad_mod = grad_mod.reshape(micro, SMALL_PER, 6 * width)
    first_only = (jnp.arange(SMALL_PER) == 0)[None, :, None]
    grad_mod = jnp.where(
        big[:, :, None], jnp.where(first_only, jnp.sum(grad_mod, axis=1, keepdims=True), 0.0), grad_mod
    )
    grad_mod = grad_mod.reshape(images, 6 * width).astype(BF16)
    silu_slope = jax.vjp(jax.nn.silu, cond)[1](jnp.ones_like(cond))[0]
    shapes = tuple(x.shape for x in shards) + ((lead, own_width, width),)
    every_image = devices * images
    if length == 4:
        mask_rows = mask_part.reshape(-1, every_image)
        extras = (grad_mod, lifted.T, silu_slope.T, ada, mask_rows)
        plan = plan_of(widths, lead, width, (0, 6))
        *mine, ada_grad, bias_sum, shared, incoming = scatter_all(
            lefts, rights, extras, outgoing, shapes, plan, length
        )
        shared = shared.reshape(devices, -1, every_image)
        every_cond = shared[:, :own_width].reshape(width, every_image)
        mask_grad = jnp.sum(shared[:, own_width : own_width + mask_rows.shape[0]], axis=0).reshape(width)
        bias_grad = lax.dynamic_slice_in_dim(bias_sum, me * bias_width, bias_width, axis=1)
    else:
        incoming = swap_sections(outgoing)
        every_mod = lax.all_gather(grad_mod, "dp", axis=0, tiled=True)
        ada_grad = dot_rows(lifted, every_mod)
        bias_sum = jnp.sum(every_mod.astype(F32), axis=0, keepdims=True)
        bias_grad = lax.dynamic_slice_in_dim(bias_sum, me * bias_width, bias_width, axis=1)
        grad_cond = dot_back(every_mod, ada) * silu_slope
        every_cond = lax.psum(lax.all_gather(grad_cond.T, "dp", axis=0, tiled=True), "section")
        mask_grad = lax.psum(mask_part, ("section", "dp"))
        half_rows = jnp.arange(dec_rows)[:, None] < jnp.where(section == 0, enc_rows, dec_rows)
        lefts, rights = ([jnp.where(half_rows, x, jnp.zeros_like(x)) for x in xs] for xs in (lefts, rights))
        split = (dot_rows(x, y).astype(BF16).reshape((devices,) + s) for x, y, s in zip(lefts, rights, shapes))
        mine = tuple(lax.psum_scatter(g, "dp", scatter_dimension=0) for g in split)
    decoded_half = jnp.where(section == 0, incoming, decoded[:, :, half_width:])
    token_half = jnp.where(section == 0, token_grad[:, :, :half_width], incoming)
    every_cond = every_cond.astype(BF16)
    time_grad, table_grad = (
        lax.dot_general(x, every_cond, (((0,), (1,)), ((), ())), preferred_element_type=F32)
        for x in (embedding, onehot)
    )
    qkv_grad, proj_grad, up_grad, down_grad = (g.astype(F32) for g in mine)
    return (
        decoded_half,
        token_half,
        mask_grad,
        time_grad,
        table_grad,
        ada_grad[None],
        bias_grad,
        qkv_grad[None],
        proj_grad[None],
        up_grad[None],
        down_grad.reshape(down_weight.shape),
    )


def solution(mesh):
    rows = P(None, "dp", None)
    ids = P(None, "dp")
    weight = P("section", "dp", None)
    halves = P(None, "dp", "section")
    in_specs = (rows, ids, ids, ids, ids, rows, P(), P(), P(), weight, P("section", "dp")) + (weight,) * 4
    out_specs = (halves, halves, P(), P(), P(), weight, P("section", "dp")) + (weight,) * 4
    return jax.shard_map(
        on_device, mesh=mesh, in_specs=in_specs, out_specs=out_specs, check_vma=False
    )
```

```python
import functools
import math
from types import SimpleNamespace

import jax
import jax.numpy as jnp
from jax import lax
from jax.experimental import pallas as pl
from jax.experimental.pallas import tpu as pltpu
from jax.sharding import PartitionSpec as P

HEADS = 16
HD = 72
SMALL_PER = 4
ATT_ROWS = 256
EPS = 1e-6
MASKED = -1e30
MESH = pl.DeviceIdType.MESH
F32 = jnp.float32
BF16 = jnp.bfloat16


anywhere = pl.BlockSpec(memory_space=pl.ANY)
in_vmem = pl.BlockSpec(memory_space=pltpu.VMEM)


def remote(src, dst, send_sem, recv_sem, target):
    return pltpu.make_async_remote_copy(
        src_ref=src,
        dst_ref=dst,
        send_sem=send_sem,
        recv_sem=recv_sem,
        device_id=target,
        device_id_type=MESH,
    )


def when(condition, run):
    pl.when(condition)(run)


def position():
    me = lax.axis_index("dp")
    return me // 4, (me // 2) % 2, me % 2


def at(line, pair, core):
    return {"dp": (line * 2 + pair) * 2 + core}


def greet(length, a, b, c):
    has_up, has_down = a < length - 1, a > 0
    barrier = pltpu.get_barrier_semaphore()

    def tell(target):
        pl.semaphore_signal(barrier, inc=1, device_id=target, device_id_type=MESH)

    tell(at(a, 1 - b, c))
    tell(at(a, b, 1 - c))
    when(has_up, lambda: tell(at(a + 1, b, c)))
    when(has_down, lambda: tell(at(a - 1, b, c)))
    pl.semaphore_wait(barrier, 2 + has_up.astype(jnp.int32) + has_down.astype(jnp.int32))
    return has_up, has_down


def piece(ref, lead, plan_entry):
    _, low, size, _ = plan_entry
    if size == 0:
        return ref.at[lead + (low,)]
    return ref.at[lead + (slice(None), pl.ds(low, size))]


def gather_moves(length, plan, sources, outs, sems, a, b, c):
    up_s, up_r, down_s, down_r, pair_s, pair_r, core_s, core_r, own_sem = sems
    has_up, has_down = a < length - 1, a > 0
    chunks = range(len(plan))
    line_first = [plan[i][3] == "line" for i in chunks]

    def slot(i, aa, bb, cc):
        return piece(outs[plan[i][0]], (aa, bb, cc), plan[i])

    def own(i):
        return piece(sources[plan[i][0]], (), plan[i])

    def rows_of(i):
        return (b,) if line_first[i] else (b, 1 - b)

    def up(i, k, bb, src=None):
        s = slot(i, a - k, bb, c)
        return remote(s if src is None else src, s, up_s.at[i, k, bb], up_r.at[i, k, bb], at(a + 1, b, c))

    def up_arrival(i, k, bb):
        s = slot(i, a - 1 - k, bb, c)
        return remote(s, s, up_s.at[i, k, bb], up_r.at[i, k, bb], at(a + 1, b, c))

    def down(i, k, bb, src=None):
        s = slot(i, a + k, bb, c)
        return remote(s if src is None else src, s, down_s.at[i, k, bb], down_r.at[i, k, bb], at(a - 1, b, c))

    def down_arrival(i, k, bb):
        s = slot(i, a + 1 + k, bb, c)
        return remote(s, s, down_s.at[i, k, bb], down_r.at[i, k, bb], at(a - 1, b, c))

    def across(i, aa, src=None):
        s = slot(i, aa, b, c)
        return remote(s if src is None else src, s, pair_s.at[i, aa], pair_r.at[i, aa], at(a, 1 - b, c))

    def across_arrival(i, aa):
        s = slot(i, aa, 1 - b, c)
        return remote(s, s, pair_s.at[i, aa], pair_r.at[i, aa], at(a, 1 - b, c))

    def to_core(i, aa, bb, src=None):
        s = slot(i, aa, bb, c)
        return remote(s if src is None else src, s, core_s.at[i, aa, bb], core_r.at[i, aa, bb], at(a, b, 1 - c))

    def core_arrival(i, aa, bb):
        s = slot(i, aa, bb, 1 - c)
        return remote(s, s, core_s.at[i, aa, bb], core_r.at[i, aa, bb], at(a, b, 1 - c))

    def after_across(i, aa):
        across_arrival(i, aa).wait_recv()
        to_core(i, aa, 1 - b).start()

    def issue(i):
        src = own(i)
        pltpu.make_async_copy(src, slot(i, a, b, c), own_sem.at[i]).start()
        across(i, a, src).start()
        when(has_up, lambda: up(i, 0, b, src).start())
        when(has_down, lambda: down(i, 0, b, src).start())
        to_core(i, a, b, src).start()

    def pair_step(i):
        across_arrival(i, a).wait_recv()
        when(has_up, lambda: up(i, 0, 1 - b).start())
        when(has_down, lambda: down(i, 0, 1 - b).start())
        to_core(i, a, 1 - b).start()

    def line_step(i, k):
        for bb in rows_of(i):

            def from_below():
                up_arrival(i, k - 1, bb).wait_recv()
                when(has_up, lambda: up(i, k, bb).start())
                if line_first[i]:
                    across(i, a - k).start()
                to_core(i, a - k, bb).start()

            def from_above():
                down_arrival(i, k - 1, bb).wait_recv()
                when(has_down, lambda: down(i, k, bb).start())
                if line_first[i]:
                    across(i, a + k).start()
                to_core(i, a + k, bb).start()

            when(a - k >= 0, from_below)
            when(a + k <= length - 1, from_above)

    def across_step(i, k):
        if not line_first[i]:
            return
        if k == 0:
            after_across(i, a)
        else:
            when(a - k >= 0, lambda: after_across(i, a - k))
            when(a + k <= length - 1, lambda: after_across(i, a + k))

    def complete(i):
        pltpu.make_async_copy(own(i), slot(i, a, b, c), own_sem.at[i]).wait()
        for aa in range(length):
            for bb in range(2):
                core_arrival(i, aa, bb).wait_recv()

    def drain(i):
        for aa in range(length):
            for bb in range(2):
                to_core(i, aa, bb).wait_send()
            if line_first[i]:
                across(i, aa).wait_send()
        if not line_first[i]:
            across(i, a).wait_send()
        for k in range(length - 1):
            for bb in rows_of(i):
                when(jnp.logical_and(has_up, a - k >= 0), lambda: up(i, k, bb).wait_send())
                when(
                    jnp.logical_and(has_down, a + k <= length - 1),
                    lambda: down(i, k, bb).wait_send(),
                )

    def move(t, ahead):
        n = len(plan)
        if t + ahead < n:
            issue(t + ahead)
        if t < n and not line_first[t]:
            pair_step(t)
        for k in range(1, length):
            i = t - k + 1
            if 0 <= i < n:
                line_step(i, k)
        for k in range(length):
            i = t - k
            if 0 <= i < n:
                across_step(i, k)

    return issue, move, complete, drain


SIDE_TIMES = (2, 4, 5, 6, 8, 10)
LAG, LINE_LAG = 1, (0, 1, 2, 3)


def greet_all(length, a, b, c):
    barrier = pltpu.get_barrier_semaphore()

    def tell(target):
        pl.semaphore_signal(barrier, inc=1, device_id=target, device_id_type=MESH)

    tell(at(a, 1 - b, c))
    tell(at(a, b, 1 - c))
    tell({"section": 1 - lax.axis_index("section")})
    for k in range(1, length):
        tell(at(lax.rem(a + k, length), b, c))
    pl.semaphore_wait(barrier, length + 2)


def spread(length, buffer, sems, a, b, c):
    line_s, line_r, pair_core = sems

    def to_line(k):
        mine = buffer.at[a, b, c]
        return remote(mine, mine, line_s.at[k - 1], line_r.at[k - 1], at(lax.rem(a + k, length), b, c))

    def from_line(k):
        slab = buffer.at[lax.rem(a + length - k, length), b, c]
        return remote(slab, slab, line_s.at[k - 1], line_r.at[k - 1], at(a, 1 - b, c))

    def across(bb):
        part = buffer.at[:, bb, c]
        return remote(part, part, pair_core.at[0], pair_core.at[1], at(a, 1 - b, c))

    def to_core(cc):
        part = buffer.at[:, :, cc]
        return remote(part, part, pair_core.at[2], pair_core.at[3], at(a, b, 1 - c))

    def start():
        for k in range(1, length):
            to_line(k).start()

    def second():
        for k in range(1, length):
            from_line(k).wait_recv()
            to_line(k).wait_send()
        across(b).start()

    def third():
        across(1 - b).wait_recv()
        across(b).wait_send()
        to_core(c).start()

    def end():
        to_core(1 - c).wait_recv()
        to_core(c).wait_send()

    return start, second, third, end


def conditioning_steps(length, inputs, outputs, scratch, a, b, c):
    grad_mod, lifted_t, slope_t, ada, mask_rows = inputs
    ada_grad, bias_sum, shared = outputs
    every, stage, payload, other = scratch[:4]
    mod_sems, shared_sems, side_sems, stage_sems = scratch[4:7], scratch[7:10], scratch[10], scratch[11]
    mod_start, mod_second, mod_third, mod_end = spread(length, every, mod_sems, a, b, c)
    shared_start, shared_second, shared_third, shared_end = spread(length, shared, shared_sems, a, b, c)
    own_rows, images = lifted_t.shape
    mask_count = mask_rows.shape[0]
    width = stage.shape[2]
    count = grad_mod.shape[1] // width
    side = remote(payload, other, side_sems.at[0], side_sems.at[1], {"section": 1 - lax.axis_index("section")})

    def save(j):
        return pltpu.make_async_copy(
            stage.at[j % 2], ada_grad.at[:, pl.ds(j * width, width)], stage_sems.at[j % 2]
        )

    def begin():
        every[a, b, c] = grad_mod[...]
        mod_start()

    def compute():
        mod_end()
        total = None
        for j in range(count):
            columns = slice(j * width, (j + 1) * width)
            rows = every[:, :, :, :, columns].astype(F32).reshape(images, width)
            bias_sum[:, columns] = jnp.sum(rows, axis=0, keepdims=True)
            rows = rows.astype(BF16)
            if j >= 2:
                save(j - 2).wait()
            stage[j % 2] = dot(lifted_t[...], rows)
            save(j).start()
            part = dot_back(ada[:, columns], rows)
            total = part if total is None else total + part
        payload[...] = jnp.zeros_like(payload)
        payload[:own_rows, :] = total * slope_t[...]
        payload[own_rows : own_rows + mask_count, :] = mask_rows[...]
        side.start()

    def add():
        side.wait()
        shared[a, b, c] = payload[...] + other[...]
        shared_start()

    def end():
        shared_end()
        for j in range(count - 2, count):
            save(j).wait()

    return begin, mod_second, mod_third, compute, add, shared_second, shared_third, end


def scatter_kernel(length, plan, slots, pair_slots, *refs):
    lefts, rights = refs[:4], refs[4:8]
    extras, outgoing = refs[8:13], refs[13]
    outs = refs[14:18]
    extra_outs, incoming = refs[18:21], refs[21]
    (
        raw, right, left_t, held, sent, core_in, pair_in, pair_late, up_in, down_in,
    ) = refs[22:32]
    (
        raw_sem, right_sem, core_s, core_r, pair_s, pair_r, up_s, up_r, down_s, down_r, out_sem,
        core_credit, pair_credit,
    ) = refs[32:45]
    a, b, c = position()
    greet_all(length, a, b, c)
    side_steps = conditioning_steps(length, extras, extra_outs, refs[45:-1], a, b, c)
    swap_sem = refs[-1]
    swap = remote(
        outgoing, incoming, swap_sem.at[0], swap_sem.at[1], {"section": 1 - lax.axis_index("section")}
    )
    swap.start()
    n = len(plan)
    rows, width = held.shape[3:]
    total_rows = raw.shape[1]
    encoder = lax.axis_index("section") == 0
    used_rows = jnp.where(encoder, total_rows // 2, total_rows)
    pair_first = [p[3] == "pair" for p in plan]
    order = [sum(pair_first[:i]) if pair_first[i] else i - sum(pair_first[:i]) for i in range(n)]
    base, total = [], 0
    for i in range(n):
        base.append(total)
        total += (length - 1) * (1 if pair_first[i] else 2)
    groups = 2 * length

    def blocks_of(w):
        return lefts[w].shape[1] // width

    raw_jobs = []
    right_jobs = []
    for i, (w, low, size, _) in enumerate(plan):
        if i == 0 or plan[i - 1][0] != w:
            raw_jobs += [(w, k) for k in range(blocks_of(w))]
        if size != 0 or plan[i - 1][0] != w:
            right_jobs.append(i)

    def raw_load(x):
        w, k = raw_jobs[x]
        src = lefts[w].at[:, pl.ds(k * width, width)]
        return pltpu.make_async_copy(src, raw.at[x % 2], raw_sem.at[x])

    def right_load(x):
        w, low, size, _ = plan[right_jobs[x]]
        src = rights[w].at[:, pl.ds(low if size else 0, width)]
        return pltpu.make_async_copy(src, right.at[x % 2], right_sem.at[x])

    progress = {"raw": 0, "right": -1}

    def turn(w):
        count = blocks_of(w)
        for k in range(count):
            x = progress["raw"]
            progress["raw"] += 1
            raw_load(x).wait()
            slot = x % 2

            def body(r, carry):
                start = pl.multiple_of(r * 128, 128)
                block = raw[slot, pl.ds(start, 128), :].astype(F32).T
                if count == 1:
                    split = block.reshape(groups, 2, rows, 128)
                    for q in range(2):
                        part = split[:, q].reshape(groups * rows, 128)
                        left_t[q, :, pl.ds(start, 128)] = part.astype(BF16)
                else:
                    near = groups // count
                    split = block.reshape(near, 2, count, rows, 128)
                    for q in range(2):
                        for j in range(count):
                            part = split[:, q, j].reshape(near * rows, 128)
                            left_t[
                                q * count + j, pl.ds(k * near * rows, near * rows), pl.ds(start, 128)
                            ] = part.astype(BF16)
                return carry

            lax.fori_loop(0, used_rows // 128, body, 0)
            if x + 2 < len(raw_jobs):
                raw_load(x + 2).start()

    def product(i, q, put):
        w, low, size, _ = plan[i]
        count = blocks_of(w)
        row_set = q if count == 1 else q * count + low
        slot = progress["right"] % 2
        tile = width // 3

        def body(k, carry):
            columns = pl.ds(pl.multiple_of(k * tile, 128), tile)

            def multiply(depth):
                result = dot(left_t[row_set, :, :depth], right[slot, :depth, columns])
                for s in range(groups):
                    put(s, columns, result[s * rows : (s + 1) * rows].astype(BF16))

            when(encoder, lambda: multiply(total_rows // 2))
            when(jnp.logical_not(encoder), lambda: multiply(total_rows))
            return carry

        lax.fori_loop(0, 3, body, 0)

    def to_core(i):
        return remote(sent.at[i % slots], core_in.at[i % slots], core_s.at[i], core_r.at[i], at(a, b, 1 - c))

    def across(i):
        target = at(a, 1 - b, c)
        if pair_first[i]:
            return remote(
                held.at[i, :, 1 - b], pair_in.at[order[i] % pair_slots], pair_s.at[i], pair_r.at[i], target
            )
        return remote(held.at[i, a, 1 - b], pair_late.at[order[i]], pair_s.at[i], pair_r.at[i], target)

    def rows_of(i):
        return (b,) if pair_first[i] else (b, 1 - b)

    def flow_index(i, dest, bb):
        if pair_first[i]:
            return base[i] + dest
        return base[i] + dest * 2 + bb

    def up(i, line, dest, bb):
        x = flow_index(i, dest - 1, bb)
        return remote(held.at[i, dest, bb], up_in.at[x], up_s.at[x], up_r.at[x], at(line + 1, b, c))

    def down(i, line, dest, bb):
        x = flow_index(i, dest, bb)
        return remote(held.at[i, dest, bb], down_in.at[x], down_s.at[x], down_r.at[x], at(line - 1, b, c))

    def add(dst, src):
        dst[...] = dst[...] + src[...]

    def credit(sem, target):
        pl.semaphore_signal(sem, inc=1, device_id=target, device_id_type=MESH)

    def produce(i):
        w = plan[i][0]
        if i == 0 or plan[i - 1][0] != w:
            turn(w)
        if progress["right"] + 1 < len(right_jobs) and right_jobs[progress["right"] + 1] == i:
            progress["right"] += 1
            right_load(progress["right"]).wait()
            if progress["right"] + 1 < len(right_jobs):
                right_load(progress["right"] + 1).start()
        if i >= slots:
            to_core(i - slots).wait_send()

        def put_sent(s, columns, value):
            sent[i % slots, s // 2, s % 2, :, columns] = value

        def put_held(s, columns, value):
            held[i, s // 2, s % 2, :, columns] = value

        product(i, 1 - c, put_sent)
        if i >= slots:
            pl.semaphore_wait(core_credit, 1)
        to_core(i).start()
        product(i, c, put_held)

    def first_add(i):
        to_core(i).wait_recv()

        def body(s, carry):
            add(held.at[i, s // 2, s % 2], core_in.at[i % slots, s // 2, s % 2])
            return carry

        lax.fori_loop(0, groups, body, 0)
        if i + slots < n:
            credit(core_credit, at(a, b, 1 - c))
        if pair_first[i]:
            if order[i] >= pair_slots:
                pl.semaphore_wait(pair_credit, 1)
            across(i).start()

    def second_add(i):
        if not pair_first[i]:
            return
        across(i).wait_recv()

        def body(s, carry):
            add(held.at[i, s, b], pair_in.at[order[i] % pair_slots, s])
            return carry

        lax.fori_loop(0, length, body, 0)
        if order[i] + pair_slots < sum(pair_first):
            credit(pair_credit, at(a, 1 - b, c))

    def line_step(i, j):
        def going_up():
            for dest in range(length - 1, j - 1, -1):
                for bb in rows_of(i):
                    if j > 0:
                        up(i, j - 1, dest, bb).wait_recv()
                        add(held.at[i, dest, bb], up_in.at[flow_index(i, dest - 1, bb)])
                    if dest > j:
                        up(i, j, dest, bb).start()

        def going_down():
            here = length - 1 - j
            for dest in range(0, here + 1):
                for bb in rows_of(i):
                    if j > 0:
                        down(i, here + 1, dest, bb).wait_recv()
                        add(held.at[i, dest, bb], down_in.at[flow_index(i, dest, bb)])
                    if dest < here:
                        down(i, here, dest, bb).start()

        when(a == j, going_up)
        when(a == length - 1 - j, going_down)

    def result(i):
        w, low, size, _ = plan[i]
        dst = outs[w].at[low] if size == 0 else outs[w].at[:, pl.ds(low, size)]
        return pltpu.make_async_copy(held.at[i, a, b], dst, out_sem.at[i])

    def finish(i):
        if pair_first[i]:
            result(i).start()
        else:
            across(i).start()

    def finish_late(i):
        if not pair_first[i]:
            across(i).wait_recv()
            add(held.at[i, a, b], pair_late.at[order[i]])
            result(i).start()

    side_steps[0]()
    raw_load(0).start()
    right_load(0).start()
    raw_load(1).start()
    produce(0)
    for t in range(n + LAG + LINE_LAG[-1] + 1):
        if t in SIDE_TIMES:
            side_steps[SIDE_TIMES.index(t) + 1]()
        if t < n:
            first_add(t)
        if t + 1 < n:
            produce(t + 1)
        if 0 <= t - LAG < n:
            second_add(t - LAG)
        for j in range(length):
            i = t - LAG - LINE_LAG[j]
            if 0 <= i < n:
                line_step(i, j)
        i = t - LAG - LINE_LAG[length - 1]
        if 0 <= i < n:
            finish(i)
        if 0 <= i - 1 < n:
            finish_late(i - 1)
    side_steps[-1]()
    swap.wait()
    for i in range(n):
        if i >= n - slots:
            to_core(i).wait_send()
        across(i).wait_send()
        result(i).wait()
        for bb in rows_of(i):
            for here in range(length):

                def gone():
                    for dest in range(here + 1, length):
                        up(i, here, dest, bb).wait_send()
                    for dest in range(0, here):
                        down(i, here, dest, bb).wait_send()

                when(a == here, gone)


def scatter_all(lefts, rights, extras, outgoing, shard_shapes, plan, length):
    n = len(plan)
    slots, pair_slots = 2, 4
    total_rows = lefts[0].shape[0]
    rows, width = shard_shapes[0][0], plan[0][2]
    late = sum(p[3] != "pair" for p in plan)
    flows = (length - 1) * (n + late)
    lead = shard_shapes[-1][0]
    dma = pltpu.SemaphoreType.DMA
    grad_mod, lifted_t, slope_t, ada, mask_rows = extras
    images = lifted_t.shape[1]
    payload = (-(-(rows + mask_rows.shape[0]) // 8) * 8, images)
    small = [dma((length - 1,)), dma((length - 1,)), dma((4,))]
    slab = (rows, width)
    return pl.pallas_call(
        functools.partial(scatter_kernel, length, plan, slots, pair_slots),
        out_shape=tuple(jax.ShapeDtypeStruct(s, BF16) for s in shard_shapes)
        + (
            jax.ShapeDtypeStruct(ada.shape, F32),
            jax.ShapeDtypeStruct((1, ada.shape[1]), F32),
            jax.ShapeDtypeStruct((length, 2, 2) + payload, F32),
            jax.ShapeDtypeStruct(outgoing.shape, BF16),
        ),
        in_specs=[anywhere] * 8 + [in_vmem] * 5 + [anywhere],
        out_specs=[anywhere] * 5 + [in_vmem] * 2 + [anywhere],
        scratch_shapes=[
            pltpu.VMEM((2, total_rows, width), BF16),
            pltpu.VMEM((2, total_rows, width), BF16),
            pltpu.VMEM((2 * lead, 2 * length * rows, total_rows), BF16),
            pltpu.VMEM((n, length, 2) + slab, BF16),
            pltpu.VMEM((slots, length, 2) + slab, BF16),
            pltpu.VMEM((slots, length, 2) + slab, BF16),
            pltpu.VMEM((pair_slots, length) + slab, BF16),
            pltpu.VMEM((late,) + slab, BF16),
            pltpu.VMEM((flows,) + slab, BF16),
            pltpu.VMEM((flows,) + slab, BF16),
            dma((lead + 3,)), dma((n,)), dma((n,)), dma((n,)), dma((n,)), dma((n,)),
            dma((flows,)), dma((flows,)), dma((flows,)), dma((flows,)), dma((n,)),
            pltpu.SemaphoreType.REGULAR, pltpu.SemaphoreType.REGULAR,
            pltpu.VMEM((length, 2, 2) + grad_mod.shape, BF16),
            pltpu.VMEM((2, rows, width), F32),
            pltpu.VMEM(payload, F32),
            pltpu.VMEM(payload, F32),
        ]
        + small
        + small
        + [dma((2,)), dma((2,)), dma((2,))],
        compiler_params=pltpu.CompilerParams(
            collective_id=1, has_side_effects=True, vmem_limit_bytes=62 * 1024 * 1024
        ),
        name="scatter_grads",
    )(*lefts, *rights, *extras, outgoing)


def small_gather_kernel(devices, own_ref, out_ref, send, recv):
    me = lax.axis_index("dp")
    barrier = pltpu.get_barrier_semaphore()
    ahead = [lax.rem(me + k, devices) for k in range(1, devices)]
    for target in ahead:
        pl.semaphore_signal(barrier, inc=1, device_id={"dp": target}, device_id_type=MESH)
    pl.semaphore_wait(barrier, devices - 1)
    out_ref[me] = own_ref[...]
    mine = out_ref.at[me]
    copies = [remote(mine, mine, send.at[k], recv.at[k], {"dp": to}) for k, to in enumerate(ahead)]
    for copy in copies:
        copy.start()
    for k, copy in enumerate(copies):
        slab = out_ref.at[lax.rem(me + devices - 1 - k, devices)]
        remote(slab, slab, send.at[k], recv.at[k], {"dp": ahead[k]}).wait_recv()
        copy.wait_send()


def small_gather(own, devices, collective_id):
    dma = pltpu.SemaphoreType.DMA
    return pl.pallas_call(
        functools.partial(small_gather_kernel, devices),
        out_shape=jax.ShapeDtypeStruct((devices,) + own.shape, own.dtype),
        in_specs=[in_vmem],
        out_specs=in_vmem,
        scratch_shapes=[dma((devices - 1,)), dma((devices - 1,))],
        compiler_params=pltpu.CompilerParams(collective_id=collective_id, has_side_effects=True),
        name="small_gather",
    )(own)


def head_window(h):
    low, high = h * HD, h * HD + HD
    start = low // 128 * 128
    return low, high, start, -(-high // 128) * 128


def contract(x, y, dims):
    return lax.dot_general(x, y, ((dims[0], dims[1]), ((), ())), preferred_element_type=F32)


def head_operands(qkv_ref, rows, h):
    width = qkv_ref.shape[1] // 3
    low, high, start, stop = head_window(h)
    lane = lax.broadcasted_iota(jnp.int32, (1, stop - start), 1) + start
    inside = jnp.logical_and(lane >= low, lane < high)
    parts = [qkv_ref[rows, j * width + start : j * width + stop] for j in range(3)]
    return inside, slice(start, stop), parts


def only(inside, x):
    return jnp.where(inside, x, jnp.zeros_like(x))


def softmax_of(query, key, allowed):
    scores = jnp.where(allowed, contract(query, key, ((1,), (1,))) * HD**-0.5, MASKED)
    weights = jnp.exp(scores - jnp.max(scores, axis=-1, keepdims=True))
    return weights * (1.0 / jnp.sum(weights, axis=-1, keepdims=True))


def place(out_ref, rows, start, inside, value):
    window = slice(start, start + value.shape[1])
    out_ref[rows, window] = jnp.where(inside, value.astype(BF16), out_ref[rows, window])


def attend(qkv_ref, rows, allowed, out_ref):
    for h in range(HEADS):
        inside, window, (query, key, value) = head_operands(qkv_ref, rows, h)
        probs = softmax_of(only(inside, query), key, allowed).astype(BF16)
        place(out_ref, rows, window.start, inside, contract(probs, value, ((1,), (0,))))


def attend_back(qkv_ref, grad_ref, rows, allowed, out_ref):
    width = grad_ref.shape[1]
    for h in range(HEADS):
        inside, window, (query, key, value) = head_operands(qkv_ref, rows, h)
        query, grad = only(inside, query), only(inside, grad_ref[rows, window])
        scores = jnp.where(allowed, contract(key, query, ((1,), (1,))) * HD**-0.5, MASKED)
        weights = jnp.exp(scores - jnp.max(scores, axis=0, keepdims=True))
        probs = weights * (1.0 / jnp.sum(weights, axis=0, keepdims=True))
        grad_probs = contract(value, grad, ((1,), (1,)))
        centre = jnp.sum(probs * grad_probs, axis=0, keepdims=True)
        grad_scores = (probs * (grad_probs - centre)).astype(BF16)
        start = window.start
        place(out_ref, rows, 2 * width + start, inside, contract(probs.astype(BF16), grad, ((1,), (0,))))
        place(out_ref, rows, width + start, inside, contract(grad_scores, query, ((1,), (0,))) * HD**-0.5)
        place(out_ref, rows, start, inside, contract(grad_scores, key, ((0,), (0,))) * HD**-0.5)


def dot(x, y):
    return jnp.dot(x, y, preferred_element_type=F32)


def dot_back(x, y):
    return lax.dot_general(x, y, (((1,), (1,)), ((), ())), preferred_element_type=F32)


def dot_rows(x, y):
    return lax.dot_general(x, y, (((0,), (0,)), ((), ())), preferred_element_type=F32)


def normal(x):
    centred = x - jnp.mean(x, axis=-1, keepdims=True)
    scale = lax.rsqrt(jnp.mean(centred * centred, axis=-1, keepdims=True) + EPS)
    return centred * scale, scale


TILE = 384
DEPTH = 2
GELU = math.sqrt(2.0 / math.pi)


def columns_of(t):
    if isinstance(t, int):
        return pl.ds(t * TILE, TILE)
    return pl.ds(pl.multiple_of(t * TILE, 128), TILE)


def unit_of(t, width):
    if isinstance(t, int):
        return pl.ds(t * width, width)
    return pl.ds(pl.multiple_of(t * width, 128), width)


class Stream:
    def __init__(self, ring, sems, width):
        self.ring, self.sems, self.width = ring, sems, width
        self.stages = []

    def add(self, weight, back, inner, outer):
        self.stages.append((weight, back, inner, outer))

    def tile(self, stage, n, k):
        weight, back, inner, _ = self.stages[stage]
        t = n * inner + k
        slot = t % DEPTH if isinstance(t, int) else lax.rem(t, DEPTH)
        deep, side = unit_of(k, self.width), unit_of(n, self.width)
        src = weight.at[side, deep] if back else weight.at[deep, side]
        buffer = self.ring.at[stage % 2, slot]
        return pltpu.make_async_copy(src, buffer, self.sems.at[stage % 2, slot]), buffer

    def begin(self, stage):
        if stage < len(self.stages):
            _, _, inner, outer = self.stages[stage]
            for t in range(min(DEPTH, inner * outer)):
                self.tile(stage, t // inner, t % inner)[0].start()

    def run(self, stage, use, ahead=True):
        _, _, inner, outer = self.stages[stage]
        if ahead:
            self.begin(stage + 1)
        count = inner * outer

        def group(n):
            def product(k, left, back):
                copy, buffer = self.tile(stage, n, k)
                copy.wait()
                result = (dot_back if back else dot)(left, buffer[...])
                t = n * inner + k + DEPTH

                def refill():
                    self.tile(stage, lax.div(t, inner), lax.rem(t, inner))[0].start()

                if not isinstance(t, int):
                    when(t < count, refill)
                elif t < count:
                    self.tile(stage, t // inner, t % inner)[0].start()
                return result

            use(n, product)

        def body(n, carry):
            group(n)
            return carry

        if outer == 1:
            group(0)
        else:
            lax.fori_loop(0, outer, body, 0)


def each_quarter(rows, run):
    def body(q, carry):
        run(q, pl.ds(pl.multiple_of(q * rows, rows), rows))
        return carry

    lax.fori_loop(0, 8, body, 0)


def piece_of(mod_ref, q, p, width, columns=None):
    if columns is None:
        return mod_ref[q, :, p * width : (p + 1) * width]
    return mod_ref[q, :, pl.ds(p * width + columns.start, TILE)]


def modulate(x_ref, mod_ref, out_ref, first, quarter_rows):
    width = x_ref.shape[1]

    def run(q, rows):
        hat = normal(x_ref[rows, :])[0]
        shift, scale = piece_of(mod_ref, q, first, width), piece_of(mod_ref, q, first + 1, width)
        out_ref[rows, :] = (hat * (1.0 + scale) + shift).astype(BF16)

    each_quarter(quarter_rows, run)


def modulate_back(grad, x, scale):
    hat, inverse = normal(x)
    inner = grad * (1.0 + scale)
    along = jnp.mean(inner * hat, axis=-1, keepdims=True)
    grad_x = inverse * (inner - jnp.mean(inner, axis=-1, keepdims=True) - hat * along)
    return grad_x, jnp.sum(grad, axis=0, keepdims=True), jnp.sum(grad * hat, axis=0, keepdims=True)


def split_quarters(quarter_rows, run):
    for q in range(8):
        run(q, slice(q * quarter_rows, (q + 1) * quarter_rows))


def allowed_of(row_ref, column_ref, block):
    rows = pl.ds(pl.multiple_of(block * ATT_ROWS, ATT_ROWS), ATT_ROWS)
    return rows, row_ref[rows, :] == column_ref[block]


def each_block(total_rows, run):
    def body(block, carry):
        run(block)
        return carry

    lax.fori_loop(0, total_rows // ATT_ROWS, body, 0)


def forward_stages(stream, weights):
    width = weights[0].shape[0]
    qkv, proj, up, down = weights
    stream.add(qkv, False, 1, qkv.shape[1] // width)
    stream.add(proj, False, 1, 1)
    stream.add(up, False, 1, up.shape[1] // width)
    stream.add(down, False, down.shape[0] // width, 1)


def backward_stages(stream, weights):
    width = weights[0].shape[0]
    qkv, proj, up, down = weights
    stream.add(down, True, 1, down.shape[0] // width)
    stream.add(up, True, up.shape[1] // width, 1)
    stream.add(proj, True, 1, 1)
    stream.add(qkv, True, qkv.shape[1] // width, 1)


def by_parts(quarter_rows, width, run):
    def one(q, rows):
        for t in range(width // TILE):
            run(q, rows, slice(t * TILE, (t + 1) * TILE))

    each_quarter(quarter_rows, one)


def proj_tile(r, mod_ref, quarter_rows, columns, branch):
    width = r.x.shape[1]
    r.branch[:, columns] = branch.astype(BF16)

    def gated(q, rows):
        gate = piece_of(mod_ref, q, 2, width, columns)
        r.x2[rows, columns] = r.x[rows, columns] + gate * branch[rows]

    split_quarters(quarter_rows, gated)


def gelu_parts(h):
    square = h * h
    t = jnp.tanh(h * (GELU + (GELU * 0.044715) * square))
    half = 0.5 + 0.5 * t
    return h * half, half + (0.5 * h) * (1.0 - t * t) * (GELU + (3.0 * GELU * 0.044715) * square)


def up_tile(r, columns, h):
    act, slope = gelu_parts(h)
    r.act[:, columns] = act.astype(BF16)
    r.slope[:, columns] = slope.astype(BF16)


def out_tile(r, mod_ref, quarter_rows, columns, mlp):
    width = r.x.shape[1]
    r.mlp[:, columns] = mlp.astype(BF16)

    def gated(q, rows):
        gate = piece_of(mod_ref, q, 5, width, columns)
        r.out[rows, columns] = (r.x2[rows, columns] + gate * mlp[rows]).astype(BF16)

    split_quarters(quarter_rows, gated)


def run_forward(stream, r, mod_ref, segments, quarter_rows, finish_part, done):
    width = r.x.shape[1]
    total_rows = r.x.shape[0]
    modulate(r.x, mod_ref, r.a1, 0, quarter_rows)

    def qkv(n, product):
        r.qkv[:, unit_of(n, width)] = product(0, r.a1[...], False).astype(BF16)

    stream.run(0, qkv)
    done("a1")

    def mix(block):
        rows, allowed = allowed_of(*segments, block)
        attend(r.qkv, rows, allowed, r.att)

    each_block(total_rows, mix)

    def proj(n, product):
        r.acc[...] = product(0, r.att[...], False)

    stream.run(1, proj)
    done("att")

    def gated(q, rows, columns):
        branch = r.acc[rows, columns]
        r.branch[rows, columns] = branch.astype(BF16)
        gate = piece_of(mod_ref, q, 2, width, columns)
        r.x2[rows, columns] = r.x[rows, columns] + gate * branch

    by_parts(quarter_rows, width, gated)
    modulate(r.x2, mod_ref, r.a2, 3, quarter_rows)

    def up(n, product):
        r.acc[...] = product(0, r.a2[...], False)

        def part(q, rows, columns):
            into = pl.ds(pl.multiple_of(n * width + columns.start, 128), TILE)
            act, slope = gelu_parts(r.acc[rows, columns])
            r.act[rows, into] = act.astype(BF16)
            r.slope[rows, into] = slope.astype(BF16)

        by_parts(quarter_rows, width, part)

    stream.run(2, up)
    done("a2")

    def down(n, product):
        for k in range(r.act.shape[1] // width):
            part = product(k, r.act[:, k * width : (k + 1) * width], False)
            if k == 0:
                r.acc[...] = part
            else:
                r.acc[...] += part

    stream.run(3, down)
    done("act")
    by_parts(quarter_rows, width, lambda q, rows, columns: finish_part(q, rows, columns, r.acc[rows, columns]))


def run_backward(stream, first, r, mod_ref, segments, quarter_rows, grad_of, finish, done):
    width = r.x.shape[1]
    total_rows = r.x.shape[0]

    def down(n, product):
        columns = unit_of(n, width)
        grad = product(0, r.dmlp[...], True)
        r.slope[:, columns] = (grad * r.slope[:, columns].astype(F32)).astype(BF16)

    stream.run(first, down)
    done("dmlp")
    done("slope")

    def up(n, product):
        for k in range(r.slope.shape[1] // width):
            part = product(k, r.slope[:, k * width : (k + 1) * width], True)
            if k == 0:
                r.dx2[...] = part
            else:
                r.dx2[...] += part

    stream.run(first + 1, up)

    def middle(q, rows):
        scale, gate = piece_of(mod_ref, q, 4, width), piece_of(mod_ref, q, 2, width)
        grad, shift_grad, scale_grad = modulate_back(r.dx2[rows, :], r.x2[rows, :], scale)
        grad = grad + grad_of(rows)
        r.dx2[rows, :] = grad
        r.dmod[q, :, 3 * width : 4 * width] = shift_grad
        r.dmod[q, :, 4 * width : 5 * width] = scale_grad
        r.dmod[q, :, 2 * width : 3 * width] = jnp.sum(
            grad * r.branch[rows, :].astype(F32), axis=0, keepdims=True
        )
        r.dbranch[rows, :] = (gate * grad).astype(BF16)

    each_quarter(quarter_rows, middle)

    def proj(n, product):
        r.datt[...] = product(0, r.dbranch[...], True).astype(BF16)

    stream.run(first + 2, proj)
    done("dbranch")

    def mix(block):
        rows, allowed = allowed_of(*segments, block)
        attend_back(r.qkv, r.datt, rows, allowed, r.dqkv)

    each_block(total_rows, mix)
    done("dqkv")

    def qkv(n, product):
        for k in range(3):
            part = product(k, r.dqkv[:, k * width : (k + 1) * width], True)
            if k == 0:
                r.acc[...] = part
            else:
                r.acc[...] += part

    stream.run(first + 3, qkv, ahead=False)

    def outer(q, rows):
        scale = piece_of(mod_ref, q, 1, width)
        grad, shift_grad, scale_grad = modulate_back(r.acc[rows, :], r.x[rows, :], scale)
        r.dmod[q, :, :width] = shift_grad
        r.dmod[q, :, width : 2 * width] = scale_grad
        finish(q, rows, grad + r.dx2[rows, :])

    each_quarter(quarter_rows, outer)
    done("dmod")


def placed(kept_ref, m, slot):
    kept = kept_ref[m]
    positions = lax.broadcasted_iota(jnp.int32, (slot, kept.shape[1]), 0)
    return jnp.where(positions == kept, 1.0, 0.0).astype(BF16)


class Copies:
    def __init__(self, sems):
        self.sems, self.count, self.pending = sems, 0, []

    def start(self, src, dst):
        copy = pltpu.make_async_copy(src, dst, self.sems.at[self.count])
        self.count += 1
        copy.start()
        self.pending.append(copy)
        return copy

    def finish(self):
        for copy in self.pending:
            copy.wait()
        self.pending = []


def encode_kernel(names, tokens, kept_ref, mod_ref, row_ref, column_ref, wq, wp, wu, wd, *rest):
    outs, scratch = rest[: len(names)], rest[len(names) :]
    r = SimpleNamespace(**dict(zip(names + ("acc",), scratch[: len(names) + 1])))
    loaded, ring, stream_sems, sems = scratch[len(names) + 1 :]
    width = loaded.shape[2]
    slot = loaded.shape[1]

    def work():
        stream = Stream(ring, stream_sems, width)
        forward_stages(stream, (wq, wp, wu, wd))
        copies = Copies(sems)
        copies.start(tokens, loaded)
        stream.begin(0)
        copies.finish()
        kept = kept_ref.shape[2]
        for m in range(2):
            r.x[m * kept : (m + 1) * kept, :] = dot_rows(placed(kept_ref, m, slot), loaded[m])
        total_rows = r.x.shape[0]
        out_of = dict(zip(names, outs))

        def done(name):
            copies.start(getattr(r, name), out_of[name].at[pl.ds(0, total_rows)])

        def finish_part(q, rows, columns, mlp):
            r.mlp[rows, columns] = mlp.astype(BF16)
            gate = piece_of(mod_ref, q, 5, width, columns)
            r.out[rows, columns] = (r.x2[rows, columns] + gate * mlp).astype(BF16)

        run_forward(stream, r, mod_ref, (row_ref, column_ref), total_rows // 8, finish_part, done)
        for name in ("x", "x2", "qkv", "branch", "slope", "mlp", "out"):
            done(name)
        copies.finish()

    when(lax.axis_index("section") == 0, work)


def decode_kernel(
    names, rights, received, cotangent, kept_ref, mask_ref, mod_ref, row_ref, column_ref, wq, wp, wu, wd,
    a1, att, a2, act, *rest,
):
    outs, scratch = rest[: 4 + len(rights) + 4], rest[4 + len(rights) + 4 :]
    lefts = dict(zip(("a1", "att", "a2", "act"), outs[:4]))
    right_outs = dict(zip(rights, outs[4 : 4 + len(rights)]))
    dmod_out, decoded, back, mask_out = outs[4 + len(rights) :]
    r = SimpleNamespace(**dict(zip(names, scratch[: len(names)])))
    got, ring, stream_sems, sems = scratch[len(names) :]
    width = got.shape[2]

    def work():
        stream = Stream(ring, stream_sems, width)
        forward_stages(stream, (wq, wp, wu, wd))
        backward_stages(stream, (wq, wp, wu, wd))
        copies = Copies(sems)
        copies.start(received, got)
        copies.start(cotangent, r.dy)
        stream.begin(0)
        copies.finish()
        total_rows = r.x.shape[0]
        slot, kept = total_rows // 2, kept_ref.shape[2]
        for m in range(2):
            place = placed(kept_ref, m, slot)
            flags = jnp.sum(place.astype(F32), axis=1, keepdims=True)
            r.free[m * slot : (m + 1) * slot, :] = jnp.broadcast_to(1.0 - flags, (slot, 128))
            filled = dot(place, got[m]) + (1.0 - flags) * mask_ref[...].astype(F32)
            r.x[m * slot : (m + 1) * slot, :] = filled
        out_of = {**lefts, **right_outs, "dmod": dmod_out, "slope": right_outs["dhid"]}

        def done(name):
            copies.start(getattr(r, name), out_of[name])

        def finish_part(q, rows, columns, part):
            gate = piece_of(mod_ref, q, 5, width, columns)
            dy = r.dy[rows, columns].astype(F32)
            r.out[rows, columns] = (r.x2[rows, columns] + gate * part).astype(BF16)
            r.dmlp[rows, columns] = (gate * dy).astype(BF16)
            r.dmod[q, :, 5 * width + columns.start : 5 * width + columns.stop] = jnp.sum(
                dy * part, axis=0, keepdims=True
            )

        segments = (row_ref, column_ref)
        run_forward(stream, r, mod_ref, segments, total_rows // 8, finish_part, done)
        copies.start(r.out, decoded)
        r.mask[...] = jnp.zeros_like(r.mask)

        def finish(q, rows, grad):
            r.mask[...] += jnp.sum(grad * r.free[rows, :1], axis=0, keepdims=True)
            r.dbranch[rows, :] = grad.astype(BF16)

        def grad_of(rows):
            return r.dy[rows, :].astype(F32)

        def done_back(name):
            if name == "dbranch":
                copies.start(getattr(r, name), out_of[name]).wait()
                copies.pending.pop()
            else:
                done(name)

        run_backward(stream, 4, r, mod_ref, segments, total_rows // 8, grad_of, finish, done_back)
        for m in range(2):
            place = placed(kept_ref, m, slot)
            got[m] = dot_rows(place, r.dbranch[m * slot : (m + 1) * slot, :]).astype(BF16)
        copies.start(got, back)
        copies.start(r.mask, mask_out)
        copies.finish()

    when(lax.axis_index("section") == 1, work)


def encode_back_kernel(
    names, rights, saved, received, kept_ref, mod_ref, row_ref, column_ref, wq, wp, wu, wd, *rest
):
    kept_in = dict(zip(saved, rest[: len(saved)]))
    rest = rest[len(saved) + len(rights) + 1 :]
    right_outs = dict(zip(rights, rest[: len(rights)]))
    dmod_out, token_out = rest[len(rights) : len(rights) + 2]
    scratch = rest[len(rights) + 2 :]
    r = SimpleNamespace(**dict(zip(names, scratch[: len(names)])))
    ring, stream_sems, sems = scratch[len(names) :]
    width = r.x.shape[1]

    def work():
        stream = Stream(ring, stream_sems, width)
        backward_stages(stream, (wq, wp, wu, wd))
        copies = Copies(sems)
        first = [copies.start(received, r.dy)]
        for name in reversed(saved):
            first.append(copies.start(kept_in[name], getattr(r, name)))
        stream.begin(0)
        for copy in first[:2]:
            copy.wait()
        total_rows = r.x.shape[0]
        out_of = {**right_outs, "dmod": dmod_out, "slope": right_outs["dhid"]}

        def done(name):
            if name == "dmod":
                copies.start(getattr(r, name), out_of[name])
            else:
                copies.start(getattr(r, name), out_of[name].at[pl.ds(0, total_rows)])

        def start(q, rows):
            gate = piece_of(mod_ref, q, 5, width)
            dy = r.dy[rows, :].astype(F32)
            r.dmlp[rows, :] = (gate * dy).astype(BF16)
            r.dmod[q, :, 5 * width :] = jnp.sum(dy * r.mlp[rows, :].astype(F32), axis=0, keepdims=True)

        each_quarter(total_rows // 8, start)
        for copy in first[2:]:
            copy.wait()
        copies.pending = []

        def finish(q, rows, grad):
            r.mlp[rows, :] = grad.astype(BF16)

        def grad_of(rows):
            return r.dy[rows, :].astype(F32)

        segments = (row_ref, column_ref)
        run_backward(stream, 0, r, mod_ref, segments, total_rows // 8, grad_of, finish, done)
        kept = kept_ref.shape[2]
        slot = token_out.shape[1]
        for m in range(2):
            place = placed(kept_ref, m, slot)
            r.tokens[m] = dot(place, r.mlp[m * kept : (m + 1) * kept, :]).astype(BF16)
        copies.start(r.tokens, token_out)
        copies.finish()

    when(lax.axis_index("section") == 0, work)


VMEM_BYTES = 60 * 1024 * 1024
LEFTS = ("a1", "att", "a2", "act")
RIGHTS = ("dqkv", "dbranch", "dhid", "dmlp")
SAVED = ("x", "x2", "qkv", "branch", "slope", "mlp")


def buffer_shapes(rows, width, wide_width):
    full, broad = lambda t: ((rows, width), t), lambda n, t: ((rows, n), t)
    return dict(
        x=full(F32), x2=full(F32), dx2=full(F32), acc=full(F32), a1=full(BF16),
        att=full(BF16), a2=full(BF16), branch=full(BF16), mlp=full(BF16), out=full(BF16),
        dy=full(BF16), dmlp=full(BF16), dbranch=full(BF16), datt=full(BF16),
        qkv=broad(3 * width, BF16), dqkv=broad(3 * width, BF16), act=broad(wide_width, BF16),
        slope=broad(wide_width, BF16), dhid=broad(wide_width, BF16),
        dmod=((8, 1, 6 * width), F32), mask=((1, width), F32), free=((rows, 128), F32),
    )


def rings(width):
    dma = pltpu.SemaphoreType.DMA
    return [pltpu.VMEM((2, DEPTH, width, width), BF16), dma((2, DEPTH)), dma((24,))]


def encode(tokens, kept, modulation, segments, weights, rows, all_rows):
    width, wide_width = weights[0].shape[0], weights[2].shape[1]
    shapes = buffer_shapes(rows, width, wide_width)
    names = LEFTS + SAVED + ("out",)
    outs = [jax.ShapeDtypeStruct(((all_rows if n in LEFTS else rows), shapes[n][0][1]), shapes[n][1]) for n in names]
    results = pl.pallas_call(
        functools.partial(encode_kernel, names),
        out_shape=outs,
        in_specs=[anywhere] + [in_vmem] * 4 + [anywhere] * 4,
        out_specs=[anywhere] * len(names),
        scratch_shapes=[pltpu.VMEM(*shapes[n]) for n in names + ("acc",)]
        + [pltpu.VMEM(tokens.shape, BF16)]
        + rings(width),
        compiler_params=pltpu.CompilerParams(vmem_limit_bytes=VMEM_BYTES),
        name="encode",
    )(tokens, kept, modulation, *segments, *weights)
    return results[:4], results[4:-1], results[-1]


def decode(received, cotangent, kept, mask_token, modulation, segments, weights, lefts):
    width, wide_width = weights[0].shape[0], weights[2].shape[1]
    rows = cotangent.shape[0]
    shapes = buffer_shapes(rows, width, wide_width)
    names = LEFTS + (
        "x", "x2", "qkv", "branch", "slope", "out", "dy", "dmlp", "dbranch", "datt", "dqkv", "dmod",
        "mask", "free",
    )
    scratch = [pltpu.VMEM(*shapes[n]) for n in names]
    names += ("dx2", "acc")
    scratch += [pltpu.VMEM(*shapes["dx2"]), pltpu.VMEM(*shapes["acc"])]
    outs = [jax.ShapeDtypeStruct(*shapes[n]) for n in LEFTS + RIGHTS + ("dmod", "out")]
    outs += [jax.ShapeDtypeStruct(received.shape, BF16), jax.ShapeDtypeStruct((1, width), F32)]
    results = pl.pallas_call(
        functools.partial(decode_kernel, names, RIGHTS),
        out_shape=outs,
        in_specs=[anywhere] * 2 + [in_vmem] * 5 + [anywhere] * 8,
        out_specs=[anywhere] * len(outs),
        scratch_shapes=scratch + [pltpu.VMEM(received.shape, BF16)] + rings(width),
        input_output_aliases={11 + j: j for j in range(4)},
        compiler_params=pltpu.CompilerParams(vmem_limit_bytes=VMEM_BYTES),
        name="decode",
    )(received, cotangent, kept, mask_token, modulation, *segments, *weights, *lefts)
    return results[:4], results[4:8], results[8:]


def encode_back(received, kept, modulation, segments, weights, saved, rights, grad_mod, token_shape):
    width, wide_width = weights[0].shape[0], weights[2].shape[1]
    rows = received.shape[0]
    shapes = buffer_shapes(rows, width, wide_width)
    names = SAVED + ("dy", "dmlp", "dbranch", "datt", "dqkv", "dmod", "dx2", "acc", "tokens")
    shapes["tokens"] = (token_shape, BF16)
    outs = [jax.ShapeDtypeStruct(x.shape, x.dtype) for x in tuple(rights) + (grad_mod,)]
    outs.append(jax.ShapeDtypeStruct(token_shape, BF16))
    before = 9 + len(saved)
    results = pl.pallas_call(
        functools.partial(encode_back_kernel, names, RIGHTS, SAVED),
        out_shape=outs,
        in_specs=[anywhere] + [in_vmem] * 4 + [anywhere] * (4 + len(saved) + 5),
        out_specs=[anywhere] * len(outs),
        scratch_shapes=[pltpu.VMEM(*shapes[n]) for n in names] + rings(width),
        input_output_aliases={before + j: j for j in range(5)},
        compiler_params=pltpu.CompilerParams(vmem_limit_bytes=VMEM_BYTES),
        name="encode_back",
    )(received, kept, modulation, *segments, *weights, *saved, *rights, grad_mod)
    return results[:4], results[4], results[5]


def gather_encode_kernel(length, plan, names, *refs):
    sources, (partial, big_ref, tokens, kept_ref, row_ref, column_ref) = refs[:4], refs[4:10]
    outs, (mod_out, received) = refs[10:14], refs[14:16]
    saved_outs = refs[16 : 16 + len(names)]
    rest = refs[16 + len(names) :]
    r = SimpleNamespace(**dict(zip(names + ("out",), rest[: len(names) + 1])))
    (
        loaded, mod_ref, tiles, last_tile, part_held, part_core, part_pair, part_line,
    ) = rest[len(names) + 1 : len(names) + 9]
    sems = rest[len(names) + 9 : len(names) + 18]
    part_sems, line_sems, tile_sems, out_sems, copy_sems = rest[len(names) + 18 :]
    a, b, c = position()
    encoder = lax.axis_index("section") == 0
    other = {"section": 1 - lax.axis_index("section")}
    barrier = pltpu.get_barrier_semaphore()

    def tell(target):
        pl.semaphore_signal(barrier, inc=1, device_id=target, device_id_type=MESH)

    tell(at(a, 1 - b, c))
    tell(at(a, b, 1 - c))
    tell(other)
    for k in range(1, length):
        tell(at(lax.rem(a + k, length), b, c))
    pl.semaphore_wait(barrier, length + 2)

    n = len(plan)
    width = r.x.shape[1]
    total_rows = r.x.shape[0]
    quarter_rows = total_rows // 8
    issue, move, complete, drain = gather_moves(length, plan, sources, outs, sems, a, b, c)
    copies = Copies(copy_sems)
    out_of = dict(zip(names, saved_outs))

    part_load = pltpu.make_async_copy(partial.at[:, :, c], part_held, part_sems.at[0])
    part_to_core = remote(partial.at[:, :, 1 - c], part_core, part_sems.at[1], part_sems.at[2], at(a, b, 1 - c))
    part_across = remote(part_held.at[:, 1 - b], part_pair, part_sems.at[3], part_sems.at[4], at(a, 1 - b, c))

    def part_to_line(k):
        to = lax.rem(a + k, length)
        return remote(
            part_held.at[to, b], part_line.at[k - 1], line_sems.at[0, k - 1], line_sems.at[1, k - 1], at(to, b, c)
        )

    def add_part(where, got):
        part_held[where] = part_held[where] + got

    def part_first():
        part_to_core.wait_recv()
        part_load.wait()
        for s in range(2 * length):
            add_part((s // 2, s % 2), part_core[s // 2, s % 2])
        part_across.start()

    def part_second():
        part_across.wait()
        for aa in range(length):
            add_part((aa, b), part_pair[aa])
        for k in range(1, length):
            part_to_line(k).start()

    def part_last():
        total = part_held[a, b].astype(F32)
        for k in range(1, length):
            part_to_line(k).wait_recv()
            total = total + part_line[k - 1].astype(F32)
        for q in range(8):
            first = q // SMALL_PER * SMALL_PER
            mod_ref[q] = jnp.where(big_ref[q] > 0, total[first : first + 1], total[q : q + 1])
        copies.start(mod_ref, mod_out)

    def load_tile(w, low, t):
        src = outs[w].at[:, :, :, :, pl.ds(low + t * TILE, TILE)]
        return pltpu.make_async_copy(src, tiles.at[t % 2], tile_sems.at[t % 2])

    def products(w, low, left, put):
        count = width // TILE
        for t in range(min(2, count)):
            load_tile(w, low, t).start()
        for t in range(count):
            load_tile(w, low, t).wait()
            tile = tiles[t % 2].astype(F32).reshape(width, TILE).astype(BF16)
            result = dot(getattr(r, left)[...], tile)
            if t + 2 < count:
                load_tile(w, low, t + 2).start()
            put(columns_of(low // TILE + t), result)

    def done(name):
        copies.start(getattr(r, name), out_of[name].at[pl.ds(0, total_rows)])

    def start_encode():
        fetch = pltpu.make_async_copy(tokens, loaded, tile_sems.at[2])
        fetch.start()
        fetch.wait()
        kept, slot = kept_ref.shape[2], loaded.shape[1]
        for m in range(2):
            r.x[m * kept : (m + 1) * kept, :] = dot_rows(placed(kept_ref, m, slot), loaded[m])

    def put_qkv(columns, result):
        r.qkv[:, columns] = result.astype(BF16)

    def put_proj(columns, result):
        proj_tile(r, mod_ref, quarter_rows, columns, result)

    def put_up(columns, result):
        up_tile(r, columns, result)

    def send_out(t):
        columns = columns_of(t)
        return remote(
            r.out.at[:, columns], received.at[:, columns], out_sems.at[0, t], out_sems.at[1, t], other
        )

    def encode_chunk(i):
        w, low, _, _ = plan[i]
        if w == 0:
            if i == 0:
                modulate(r.x, mod_ref, r.a1, 0, quarter_rows)
            products(w, low, "a1", put_qkv)
        elif w == 1:
            rows, allowed = slice(0, total_rows), row_ref[...] == column_ref[0]
            attend(r.qkv, rows, allowed, r.att)
            products(w, low, "att", put_proj)
            modulate(r.x2, mod_ref, r.a2, 3, quarter_rows)
        elif w == 2:
            products(w, low, "a2", put_up)
        else:
            src = outs[w].at[:, :, :, :, pl.ds(low, TILE)]
            fetch = pltpu.make_async_copy(src, last_tile, tile_sems.at[2])
            fetch.start()
            fetch.wait()
            tile = last_tile[...].reshape(r.act.shape[1], TILE)
            out_tile(r, mod_ref, quarter_rows, columns_of(low // TILE), dot(r.act[...], tile))
            send_out(low // TILE).start()

    part_load.start()
    part_to_core.start()
    issue(0)
    when(encoder, start_encode)
    part_first()
    for i in range(1, AHEAD):
        issue(i)
    for t in range(n + length - 1):
        move(t, AHEAD)
        if t == 0:
            part_second()
        if t == 1:
            part_last()
        i = t - length + 1
        if i >= 0:
            complete(i)
            when(encoder, lambda: encode_chunk(i))
    for i in range(n):
        drain(i)
    part_to_core.wait_send()
    for k in range(1, length):
        part_to_line(k).wait_send()

    def close():
        for name in names:
            done(name)
        for copy in copies.pending[1:]:
            copy.wait()
        for t in range(width // TILE):
            send_out(t).wait_send()

    when(encoder, close)
    copies.pending[0].wait()

    def arrive():
        for t in range(width // TILE):
            send_out(t).wait_recv()

    when(jnp.logical_not(encoder), arrive)


AHEAD = 4


def gather_encode(shards, partial, big, tokens, kept, segments, plan, length, rows, all_rows):
    n = len(plan)
    width, wide_width = shards[1].shape[1], shards[2].shape[1]
    shapes = buffer_shapes(rows, width, wide_width)
    names = LEFTS + SAVED
    quarters = partial.shape[3]
    part_slab = partial.shape[3:]
    dma = pltpu.SemaphoreType.DMA
    outs = [jax.ShapeDtypeStruct((length, 2, 2) + s.shape, BF16) for s in shards]
    outs += [jax.ShapeDtypeStruct((quarters, 1, 6 * width), F32), jax.ShapeDtypeStruct((rows, width), BF16)]
    outs += [jax.ShapeDtypeStruct(((all_rows if m in LEFTS else rows), shapes[m][0][1]), shapes[m][1]) for m in names]
    results = pl.pallas_call(
        functools.partial(gather_encode_kernel, length, plan, names),
        out_shape=outs,
        in_specs=[anywhere] * 5 + [in_vmem, anywhere] + [in_vmem] * 3,
        out_specs=[anywhere] * len(outs),
        scratch_shapes=[pltpu.VMEM(*shapes[m]) for m in names + ("out",)]
        + [
            pltpu.VMEM(tokens.shape, BF16),
            pltpu.VMEM((quarters, 1, 6 * width), F32),
            pltpu.VMEM((2, length, 2, 2, shards[0].shape[0], TILE), BF16),
            pltpu.VMEM((length, 2, 2, shards[3].shape[0], TILE), BF16),
            pltpu.VMEM((length, 2) + part_slab, BF16),
            pltpu.VMEM((length, 2) + part_slab, BF16),
            pltpu.VMEM((length,) + part_slab, BF16),
            pltpu.VMEM((length - 1,) + part_slab, BF16),
        ]
        + [dma((n, length, 2))] * 4
        + [dma((n, length))] * 2
        + [dma((n, length, 2))] * 2
        + [dma((n,)), dma((5,)), dma((2, length - 1)), dma((3,)), dma((2, width // TILE)), dma((len(names) + 1,))],
        compiler_params=pltpu.CompilerParams(
            collective_id=0, has_side_effects=True, vmem_limit_bytes=VMEM_BYTES
        ),
        name="gather_encode",
    )(*shards, partial, big, tokens, kept, *segments)
    return results[:4], results[4], results[5], results[6:10], results[10:]


def plan_of(widths, lead, unit, line_first):
    plan = [(w, low, unit) for w, width in enumerate(widths) for low in range(0, width, unit)]
    plan += [(len(widths), j, 0) for j in range(lead)]
    return tuple(p + ("line" if i in line_first else "pair",) for i, p in enumerate(plan))


def swap_sections(x):
    return lax.ppermute(x, "section", [(0, 1), (1, 0)])


def on_device(
    tokens, kept_index, big_image, timesteps, labels, cotangent, mask_token, time_weight, class_table,
    ada_weight, ada_bias, qkv_weight, proj_weight, up_weight, down_weight,
):
    section = lax.axis_index("section")
    me = lax.axis_index("dp")
    devices = lax.axis_size("dp")
    micro, slot, width = tokens.shape
    kept_count = kept_index.shape[1]
    own_width = ada_weight.shape[1]
    images = micro * SMALL_PER
    quarters = micro * SMALL_PER
    ada = ada_weight[0]

    length = devices // 4
    ids = jnp.concatenate([timesteps.reshape(1, images), labels.reshape(1, images)])
    if length == 4:
        ids = small_gather(jnp.pad(ids, ((0, 6), (0, 128 - images))), devices, 2)
    else:
        ids = lax.all_gather(ids, "dp", axis=0)
    times = ids[:, 0, :images].reshape(devices * images)
    classes = ids[:, 1, :images].reshape(devices * images)
    half = time_weight.shape[0] // 2
    frequencies = jnp.exp(-math.log(10000.0) * jnp.arange(half, dtype=F32) / half)
    angles = times.astype(F32)[:, None] * frequencies[None, :]
    embedding = jnp.concatenate([jnp.cos(angles), jnp.sin(angles)], axis=-1).astype(BF16)
    onehot = (classes[:, None] == jnp.arange(class_table.shape[0])[None, :]).astype(BF16)
    cond = dot(embedding, time_weight) + dot(onehot, class_table)
    cond = lax.dynamic_slice_in_dim(cond, me * own_width, own_width, axis=1)
    lifted = jax.nn.silu(cond).astype(BF16)
    bias_width = ada_bias.shape[1]
    bias = lax.dynamic_update_slice_in_dim(
        jnp.zeros((1, 6 * width), F32), ada_bias.astype(F32), me * bias_width, axis=1
    )
    partial = (dot(lifted, ada) + bias).astype(BF16).reshape(devices, images, 6 * width)

    big = big_image[:, :1] > 0
    quarter_ids = jnp.arange(quarters, dtype=jnp.int32).reshape(micro, SMALL_PER)
    segment_of = jnp.where(big, quarter_ids[:, :1], quarter_ids).reshape(quarters)
    kept = kept_index.reshape(micro, 1, kept_count)

    def segments(quarter_rows):
        ids = jnp.repeat(segment_of, quarter_rows)
        return ids.reshape(-1, 1), ids.reshape(-1, 1, ATT_ROWS)

    enc_rows, dec_rows = micro * kept_count, micro * slot
    enc_segments = segments(enc_rows // quarters)
    dec_segments = segments(dec_rows // quarters)

    shards = (qkv_weight[0], proj_weight[0], up_weight[0])
    lead = down_weight.shape[1] // qkv_weight.shape[1]
    widths = [x.shape[1] for x in shards]
    if length == 4:
        plan = [(w, low, width, "line") for w in range(3) for low in range(0, widths[w], width)]
        plan += [(3, low, TILE, "line") for low in range(0, width, TILE)]
        plan = tuple(p[:3] + ("pair" if i in (1, 7) else "line",) for i, p in enumerate(plan))
        flags = jnp.repeat(big[:, 0], SMALL_PER).astype(jnp.int32).reshape(quarters, 1, 1)
        whole, modulation, received, lefts, saved = gather_encode(
            shards + (down_weight[0],), partial.reshape((length, 2, 2) + partial.shape[1:]), flags, tokens, kept,
            enc_segments, plan, length, enc_rows, dec_rows,
        )
        weights = tuple(w.reshape(-1, w.shape[-1]) for w in whole)
        received = received.reshape(micro, kept_count, width)
    else:
        whole = (lax.all_gather(x, "dp", axis=0, tiled=True) for x in shards + (down_weight[0],))
        weights = tuple(whole)
        modulation = lax.psum_scatter(partial, "dp", scatter_dimension=0, tiled=False).astype(F32)
        modulation = modulation.reshape(micro, SMALL_PER, 6 * width)
        modulation = jnp.where(big[:, :, None], modulation[:, :1], modulation).reshape(quarters, 1, 6 * width)
        lefts, saved, encoded = encode(tokens, kept, modulation, enc_segments, weights, enc_rows, dec_rows)
        received = swap_sections(encoded).reshape(micro, kept_count, width)

    lefts, rights, (grad_mod, decoded, back, mask_part) = decode(
        received, cotangent.reshape(dec_rows, width), kept, mask_token.reshape(1, width), modulation,
        dec_segments, weights, lefts,
    )
    received = swap_sections(back).reshape(enc_rows, width)
    rights, grad_mod, token_grad = encode_back(
        received, kept, modulation, enc_segments, weights, saved, rights, grad_mod, (micro, slot, width)
    )
    decoded = decoded.reshape(micro, slot, width)
    mask_part = jnp.where(section == 1, mask_part, 0.0).reshape(width)

    half_width = width // 2
    outgoing = jnp.where(section == 0, token_grad[:, :, half_width:], decoded[:, :, :half_width])

    grad_mod = grad_mod.reshape(micro, SMALL_PER, 6 * width)
    first_only = (jnp.arange(SMALL_PER) == 0)[None, :, None]
    grad_mod = jnp.where(
        big[:, :, None], jnp.where(first_only, jnp.sum(grad_mod, axis=1, keepdims=True), 0.0), grad_mod
    )
    grad_mod = grad_mod.reshape(images, 6 * width).astype(BF16)
    silu_slope = jax.vjp(jax.nn.silu, cond)[1](jnp.ones_like(cond))[0]
    shapes = tuple(x.shape for x in shards) + ((lead, own_width, width),)
    every_image = devices * images
    if length == 4:
        mask_rows = mask_part.reshape(-1, every_image)
        extras = (grad_mod, lifted.T, silu_slope.T, ada, mask_rows)
        plan = plan_of(widths, lead, width, (0, 6))
        *mine, ada_grad, bias_sum, shared, incoming = scatter_all(
            lefts, rights, extras, outgoing, shapes, plan, length
        )
        shared = shared.reshape(devices, -1, every_image)
        every_cond = shared[:, :own_width].reshape(width, every_image)
        mask_grad = jnp.sum(shared[:, own_width : own_width + mask_rows.shape[0]], axis=0).reshape(width)
        bias_grad = lax.dynamic_slice_in_dim(bias_sum, me * bias_width, bias_width, axis=1)
    else:
        incoming = swap_sections(outgoing)
        every_mod = lax.all_gather(grad_mod, "dp", axis=0, tiled=True)
        ada_grad = dot_rows(lifted, every_mod)
        bias_sum = jnp.sum(every_mod.astype(F32), axis=0, keepdims=True)
        bias_grad = lax.dynamic_slice_in_dim(bias_sum, me * bias_width, bias_width, axis=1)
        grad_cond = dot_back(every_mod, ada) * silu_slope
        every_cond = lax.psum(lax.all_gather(grad_cond.T, "dp", axis=0, tiled=True), "section")
        mask_grad = lax.psum(mask_part, ("section", "dp"))
        half_rows = jnp.arange(dec_rows)[:, None] < jnp.where(section == 0, enc_rows, dec_rows)
        lefts, rights = ([jnp.where(half_rows, x, jnp.zeros_like(x)) for x in xs] for xs in (lefts, rights))
        split = (dot_rows(x, y).astype(BF16).reshape((devices,) + s) for x, y, s in zip(lefts, rights, shapes))
        mine = tuple(lax.psum_scatter(g, "dp", scatter_dimension=0) for g in split)
    decoded_half = jnp.where(section == 0, incoming, decoded[:, :, half_width:])
    token_half = jnp.where(section == 0, token_grad[:, :, :half_width], incoming)
    every_cond = every_cond.astype(BF16)
    time_grad, table_grad = (
        lax.dot_general(x, every_cond, (((0,), (1,)), ((), ())), preferred_element_type=F32)
        for x in (embedding, onehot)
    )
    qkv_grad, proj_grad, up_grad, down_grad = (g.astype(F32) for g in mine)
    return (
        decoded_half,
        token_half,
        mask_grad,
        time_grad,
        table_grad,
        ada_grad[None],
        bias_grad,
        qkv_grad[None],
        proj_grad[None],
        up_grad[None],
        down_grad.reshape(down_weight.shape),
    )


def solution(mesh):
    rows = P(None, "dp", None)
    ids = P(None, "dp")
    weight = P("section", "dp", None)
    halves = P(None, "dp", "section")
    in_specs = (rows, ids, ids, ids, ids, rows, P(), P(), P(), weight, P("section", "dp")) + (weight,) * 4
    out_specs = (halves, halves, P(), P(), P(), weight, P("section", "dp")) + (weight,) * 4
    return jax.shard_map(
        on_device, mesh=mesh, in_specs=in_specs, out_specs=out_specs, check_vma=False
    )
```

```python
import functools
import math
from types import SimpleNamespace

import jax
import jax.numpy as jnp
from jax import lax
from jax.experimental import pallas as pl
from jax.experimental.pallas import tpu as pltpu
from jax.sharding import PartitionSpec as P

HEADS = 16
HD = 72
SMALL_PER = 4
ATT_ROWS = 256
EPS = 1e-6
MASKED = -1e30
MESH = pl.DeviceIdType.MESH
F32 = jnp.float32
BF16 = jnp.bfloat16


anywhere = pl.BlockSpec(memory_space=pl.ANY)
in_vmem = pl.BlockSpec(memory_space=pltpu.VMEM)


def remote(src, dst, send_sem, recv_sem, target):
    return pltpu.make_async_remote_copy(
        src_ref=src,
        dst_ref=dst,
        send_sem=send_sem,
        recv_sem=recv_sem,
        device_id=target,
        device_id_type=MESH,
    )


def when(condition, run):
    pl.when(condition)(run)


def position():
    me = lax.axis_index("dp")
    return me // 4, (me // 2) % 2, me % 2


def at(line, pair, core):
    return {"dp": (line * 2 + pair) * 2 + core}


def greet(length, a, b, c):
    has_up, has_down = a < length - 1, a > 0
    barrier = pltpu.get_barrier_semaphore()

    def tell(target):
        pl.semaphore_signal(barrier, inc=1, device_id=target, device_id_type=MESH)

    tell(at(a, 1 - b, c))
    tell(at(a, b, 1 - c))
    when(has_up, lambda: tell(at(a + 1, b, c)))
    when(has_down, lambda: tell(at(a - 1, b, c)))
    pl.semaphore_wait(barrier, 2 + has_up.astype(jnp.int32) + has_down.astype(jnp.int32))
    return has_up, has_down


def piece(ref, lead, plan_entry):
    _, low, size, _ = plan_entry
    if size == 0:
        return ref.at[lead + (low,)]
    return ref.at[lead + (slice(None), pl.ds(low, size))]


def gather_moves(length, plan, sources, outs, sems, a, b, c):
    up_s, up_r, down_s, down_r, pair_s, pair_r, core_s, core_r, own_sem = sems
    has_up, has_down = a < length - 1, a > 0
    chunks = range(len(plan))
    line_first = [plan[i][3] == "line" for i in chunks]

    def slot(i, aa, bb, cc):
        return piece(outs[plan[i][0]], (aa, bb, cc), plan[i])

    def own(i):
        return piece(sources[plan[i][0]], (), plan[i])

    def rows_of(i):
        return (b,) if line_first[i] else (b, 1 - b)

    def up(i, k, bb, src=None):
        s = slot(i, a - k, bb, c)
        return remote(s if src is None else src, s, up_s.at[i, k, bb], up_r.at[i, k, bb], at(a + 1, b, c))

    def up_arrival(i, k, bb):
        s = slot(i, a - 1 - k, bb, c)
        return remote(s, s, up_s.at[i, k, bb], up_r.at[i, k, bb], at(a + 1, b, c))

    def down(i, k, bb, src=None):
        s = slot(i, a + k, bb, c)
        return remote(s if src is None else src, s, down_s.at[i, k, bb], down_r.at[i, k, bb], at(a - 1, b, c))

    def down_arrival(i, k, bb):
        s = slot(i, a + 1 + k, bb, c)
        return remote(s, s, down_s.at[i, k, bb], down_r.at[i, k, bb], at(a - 1, b, c))

    def across(i, aa, src=None):
        s = slot(i, aa, b, c)
        return remote(s if src is None else src, s, pair_s.at[i, aa], pair_r.at[i, aa], at(a, 1 - b, c))

    def across_arrival(i, aa):
        s = slot(i, aa, 1 - b, c)
        return remote(s, s, pair_s.at[i, aa], pair_r.at[i, aa], at(a, 1 - b, c))

    def to_core(i, aa, bb, src=None):
        s = slot(i, aa, bb, c)
        return remote(s if src is None else src, s, core_s.at[i, aa, bb], core_r.at[i, aa, bb], at(a, b, 1 - c))

    def core_arrival(i, aa, bb):
        s = slot(i, aa, bb, 1 - c)
        return remote(s, s, core_s.at[i, aa, bb], core_r.at[i, aa, bb], at(a, b, 1 - c))

    def after_across(i, aa):
        across_arrival(i, aa).wait_recv()
        to_core(i, aa, 1 - b).start()

    def issue(i):
        src = own(i)
        pltpu.make_async_copy(src, slot(i, a, b, c), own_sem.at[i]).start()
        across(i, a, src).start()
        when(has_up, lambda: up(i, 0, b, src).start())
        when(has_down, lambda: down(i, 0, b, src).start())
        to_core(i, a, b, src).start()

    def pair_step(i):
        across_arrival(i, a).wait_recv()
        when(has_up, lambda: up(i, 0, 1 - b).start())
        when(has_down, lambda: down(i, 0, 1 - b).start())
        to_core(i, a, 1 - b).start()

    def line_step(i, k):
        for bb in rows_of(i):

            def from_below():
                up_arrival(i, k - 1, bb).wait_recv()
                when(has_up, lambda: up(i, k, bb).start())
                if line_first[i]:
                    across(i, a - k).start()
                to_core(i, a - k, bb).start()

            def from_above():
                down_arrival(i, k - 1, bb).wait_recv()
                when(has_down, lambda: down(i, k, bb).start())
                if line_first[i]:
                    across(i, a + k).start()
                to_core(i, a + k, bb).start()

            when(a - k >= 0, from_below)
            when(a + k <= length - 1, from_above)

    def across_step(i, k):
        if not line_first[i]:
            return
        if k == 0:
            after_across(i, a)
        else:
            when(a - k >= 0, lambda: after_across(i, a - k))
            when(a + k <= length - 1, lambda: after_across(i, a + k))

    def complete(i):
        pltpu.make_async_copy(own(i), slot(i, a, b, c), own_sem.at[i]).wait()
        for aa in range(length):
            for bb in range(2):
                core_arrival(i, aa, bb).wait_recv()

    def drain(i):
        for aa in range(length):
            for bb in range(2):
                to_core(i, aa, bb).wait_send()
            if line_first[i]:
                across(i, aa).wait_send()
        if not line_first[i]:
            across(i, a).wait_send()
        for k in range(length - 1):
            for bb in rows_of(i):
                when(jnp.logical_and(has_up, a - k >= 0), lambda: up(i, k, bb).wait_send())
                when(
                    jnp.logical_and(has_down, a + k <= length - 1),
                    lambda: down(i, k, bb).wait_send(),
                )

    def move(t, ahead):
        n = len(plan)
        if t + ahead < n:
            issue(t + ahead)
        if t < n and not line_first[t]:
            pair_step(t)
        for k in range(1, length):
            i = t - k + 1
            if 0 <= i < n:
                line_step(i, k)
        for k in range(length):
            i = t - k
            if 0 <= i < n:
                across_step(i, k)

    return issue, move, complete, drain


SIDE_TIMES = (2, 4, 5, 6, 8, 10)
LAG, LINE_LAG = 1, (0, 1, 2, 3)


def greet_all(length, a, b, c):
    barrier = pltpu.get_barrier_semaphore()

    def tell(target):
        pl.semaphore_signal(barrier, inc=1, device_id=target, device_id_type=MESH)

    tell(at(a, 1 - b, c))
    tell(at(a, b, 1 - c))
    tell({"section": 1 - lax.axis_index("section")})
    for k in range(1, length):
        tell(at(lax.rem(a + k, length), b, c))
    pl.semaphore_wait(barrier, length + 2)


def spread(length, buffer, sems, a, b, c):
    line_s, line_r, pair_core = sems

    def to_line(k):
        mine = buffer.at[a, b, c]
        return remote(mine, mine, line_s.at[k - 1], line_r.at[k - 1], at(lax.rem(a + k, length), b, c))

    def from_line(k):
        slab = buffer.at[lax.rem(a + length - k, length), b, c]
        return remote(slab, slab, line_s.at[k - 1], line_r.at[k - 1], at(a, 1 - b, c))

    def across(bb):
        part = buffer.at[:, bb, c]
        return remote(part, part, pair_core.at[0], pair_core.at[1], at(a, 1 - b, c))

    def to_core(cc):
        part = buffer.at[:, :, cc]
        return remote(part, part, pair_core.at[2], pair_core.at[3], at(a, b, 1 - c))

    def start():
        for k in range(1, length):
            to_line(k).start()

    def second():
        for k in range(1, length):
            from_line(k).wait_recv()
            to_line(k).wait_send()
        across(b).start()

    def third():
        across(1 - b).wait_recv()
        across(b).wait_send()
        to_core(c).start()

    def end():
        to_core(1 - c).wait_recv()
        to_core(c).wait_send()

    return start, second, third, end


def conditioning_steps(length, inputs, outputs, scratch, a, b, c):
    grad_mod, lifted_t, slope_t, ada, mask_rows = inputs
    ada_grad, bias_sum, shared = outputs
    every, stage, payload, other = scratch[:4]
    mod_sems, shared_sems, side_sems, stage_sems = scratch[4:7], scratch[7:10], scratch[10], scratch[11]
    mod_start, mod_second, mod_third, mod_end = spread(length, every, mod_sems, a, b, c)
    shared_start, shared_second, shared_third, shared_end = spread(length, shared, shared_sems, a, b, c)
    own_rows, images = lifted_t.shape
    mask_count = mask_rows.shape[0]
    width = stage.shape[2]
    count = grad_mod.shape[1] // width
    side = remote(payload, other, side_sems.at[0], side_sems.at[1], {"section": 1 - lax.axis_index("section")})

    def save(j):
        return pltpu.make_async_copy(
            stage.at[j % 2], ada_grad.at[:, pl.ds(j * width, width)], stage_sems.at[j % 2]
        )

    def begin():
        every[a, b, c] = grad_mod[...]
        mod_start()

    def compute():
        mod_end()
        total = None
        for j in range(count):
            columns = slice(j * width, (j + 1) * width)
            rows = every[:, :, :, :, columns].astype(F32).reshape(images, width)
            bias_sum[:, columns] = jnp.sum(rows, axis=0, keepdims=True)
            rows = rows.astype(BF16)
            if j >= 2:
                save(j - 2).wait()
            stage[j % 2] = dot(lifted_t[...], rows)
            save(j).start()
            part = dot_back(ada[:, columns], rows)
            total = part if total is None else total + part
        payload[...] = jnp.zeros_like(payload)
        payload[:own_rows, :] = total * slope_t[...]
        payload[own_rows : own_rows + mask_count, :] = mask_rows[...]
        side.start()

    def add():
        side.wait()
        shared[a, b, c] = payload[...] + other[...]
        shared_start()

    def end():
        shared_end()
        for j in range(count - 2, count):
            save(j).wait()

    return begin, mod_second, mod_third, compute, add, shared_second, shared_third, end


def scatter_kernel(length, plan, slots, pair_slots, *refs):
    lefts, rights = refs[:4], refs[4:8]
    extras, outgoing = refs[8:13], refs[13]
    outs = refs[14:18]
    extra_outs, incoming = refs[18:21], refs[21]
    (
        raw, right, left_t, held, sent, core_in, pair_in, pair_late, up_in, down_in,
    ) = refs[22:32]
    (
        raw_sem, right_sem, core_s, core_r, pair_s, pair_r, up_s, up_r, down_s, down_r, out_sem,
        core_credit, pair_credit,
    ) = refs[32:45]
    a, b, c = position()
    side_steps = conditioning_steps(length, extras, extra_outs, refs[45:-1], a, b, c)
    swap_sem = refs[-1]
    swap = remote(
        outgoing, incoming, swap_sem.at[0], swap_sem.at[1], {"section": 1 - lax.axis_index("section")}
    )
    n = len(plan)
    rows, width = held.shape[3:]
    total_rows = raw.shape[1]
    encoder = lax.axis_index("section") == 0
    used_rows = jnp.where(encoder, total_rows // 2, total_rows)
    pair_first = [p[3] == "pair" for p in plan]
    order = [sum(pair_first[:i]) if pair_first[i] else i - sum(pair_first[:i]) for i in range(n)]
    base, total = [], 0
    for i in range(n):
        base.append(total)
        total += (length - 1) * (1 if pair_first[i] else 2)
    groups = 2 * length

    def blocks_of(w):
        return lefts[w].shape[1] // width

    raw_jobs = []
    right_jobs = []
    for i, (w, low, size, _) in enumerate(plan):
        if i == 0 or plan[i - 1][0] != w:
            raw_jobs += [(w, k) for k in range(blocks_of(w))]
        if size != 0 or plan[i - 1][0] != w:
            right_jobs.append(i)

    def raw_load(x):
        w, k = raw_jobs[x]
        src = lefts[w].at[:, pl.ds(k * width, width)]
        return pltpu.make_async_copy(src, raw.at[x % 2], raw_sem.at[x])

    def right_load(x):
        w, low, size, _ = plan[right_jobs[x]]
        src = rights[w].at[:, pl.ds(low if size else 0, width)]
        return pltpu.make_async_copy(src, right.at[x % 2], right_sem.at[x])

    progress = {"raw": 0, "right": -1}

    def turn(w):
        count = blocks_of(w)
        for k in range(count):
            x = progress["raw"]
            progress["raw"] += 1
            raw_load(x).wait()
            slot = x % 2

            def body(r, carry):
                start = pl.multiple_of(r * 128, 128)
                block = raw[slot, pl.ds(start, 128), :].astype(F32).T
                if count == 1:
                    split = block.reshape(groups, 2, rows, 128)
                    for q in range(2):
                        part = split[:, q].reshape(groups * rows, 128)
                        left_t[q, :, pl.ds(start, 128)] = part.astype(BF16)
                else:
                    near = groups // count
                    split = block.reshape(near, 2, count, rows, 128)
                    for q in range(2):
                        for j in range(count):
                            part = split[:, q, j].reshape(near * rows, 128)
                            left_t[
                                q * count + j, pl.ds(k * near * rows, near * rows), pl.ds(start, 128)
                            ] = part.astype(BF16)
                return carry

            lax.fori_loop(0, used_rows // 128, body, 0)
            if x + 2 < len(raw_jobs):
                raw_load(x + 2).start()

    def product(i, q, put):
        w, low, size, _ = plan[i]
        count = blocks_of(w)
        row_set = q if count == 1 else q * count + low
        slot = progress["right"] % 2
        tile = width // 3

        def body(k, carry):
            columns = pl.ds(pl.multiple_of(k * tile, 128), tile)

            def multiply(depth):
                result = dot(left_t[row_set, :, :depth], right[slot, :depth, columns])
                for s in range(groups):
                    put(s, columns, result[s * rows : (s + 1) * rows].astype(BF16))

            when(encoder, lambda: multiply(total_rows // 2))
            when(jnp.logical_not(encoder), lambda: multiply(total_rows))
            return carry

        lax.fori_loop(0, 3, body, 0)

    def to_core(i):
        return remote(sent.at[i % slots], core_in.at[i % slots], core_s.at[i], core_r.at[i], at(a, b, 1 - c))

    def across(i):
        target = at(a, 1 - b, c)
        if pair_first[i]:
            return remote(
                held.at[i, :, 1 - b], pair_in.at[order[i] % pair_slots], pair_s.at[i], pair_r.at[i], target
            )
        return remote(held.at[i, a, 1 - b], pair_late.at[order[i]], pair_s.at[i], pair_r.at[i], target)

    def rows_of(i):
        return (b,) if pair_first[i] else (b, 1 - b)

    def flow_index(i, dest, bb):
        if pair_first[i]:
            return base[i] + dest
        return base[i] + dest * 2 + bb

    def up(i, line, dest, bb):
        x = flow_index(i, dest - 1, bb)
        return remote(held.at[i, dest, bb], up_in.at[x], up_s.at[x], up_r.at[x], at(line + 1, b, c))

    def down(i, line, dest, bb):
        x = flow_index(i, dest, bb)
        return remote(held.at[i, dest, bb], down_in.at[x], down_s.at[x], down_r.at[x], at(line - 1, b, c))

    def add(dst, src):
        dst[...] = dst[...] + src[...]

    def credit(sem, target):
        pl.semaphore_signal(sem, inc=1, device_id=target, device_id_type=MESH)

    def produce(i):
        w = plan[i][0]
        if i == 0 or plan[i - 1][0] != w:
            turn(w)
        if progress["right"] + 1 < len(right_jobs) and right_jobs[progress["right"] + 1] == i:
            progress["right"] += 1
            right_load(progress["right"]).wait()
            if progress["right"] + 1 < len(right_jobs):
                right_load(progress["right"] + 1).start()
        if i >= slots:
            to_core(i - slots).wait_send()

        def put_sent(s, columns, value):
            sent[i % slots, s // 2, s % 2, :, columns] = value

        def put_held(s, columns, value):
            held[i, s // 2, s % 2, :, columns] = value

        product(i, 1 - c, put_sent)
        if i >= slots:
            pl.semaphore_wait(core_credit, 1)
        to_core(i).start()
        product(i, c, put_held)

    def first_add(i):
        to_core(i).wait_recv()

        def body(s, carry):
            add(held.at[i, s // 2, s % 2], core_in.at[i % slots, s // 2, s % 2])
            return carry

        lax.fori_loop(0, groups, body, 0)
        if i + slots < n:
            credit(core_credit, at(a, b, 1 - c))
        if pair_first[i]:
            if order[i] >= pair_slots:
                pl.semaphore_wait(pair_credit, 1)
            across(i).start()

    def second_add(i):
        if not pair_first[i]:
            return
        across(i).wait_recv()

        def body(s, carry):
            add(held.at[i, s, b], pair_in.at[order[i] % pair_slots, s])
            return carry

        lax.fori_loop(0, length, body, 0)
        if order[i] + pair_slots < sum(pair_first):
            credit(pair_credit, at(a, 1 - b, c))

    def line_step(i, j):
        def going_up():
            for dest in range(length - 1, j - 1, -1):
                for bb in rows_of(i):
                    if j > 0:
                        up(i, j - 1, dest, bb).wait_recv()
                        add(held.at[i, dest, bb], up_in.at[flow_index(i, dest - 1, bb)])
                    if dest > j:
                        up(i, j, dest, bb).start()

        def going_down():
            here = length - 1 - j
            for dest in range(0, here + 1):
                for bb in rows_of(i):
                    if j > 0:
                        down(i, here + 1, dest, bb).wait_recv()
                        add(held.at[i, dest, bb], down_in.at[flow_index(i, dest, bb)])
                    if dest < here:
                        down(i, here, dest, bb).start()

        when(a == j, going_up)
        when(a == length - 1 - j, going_down)

    def result(i):
        w, low, size, _ = plan[i]
        dst = outs[w].at[low] if size == 0 else outs[w].at[:, pl.ds(low, size)]
        return pltpu.make_async_copy(held.at[i, a, b], dst, out_sem.at[i])

    def finish(i):
        if pair_first[i]:
            result(i).start()
        else:
            across(i).start()

    def finish_late(i):
        if not pair_first[i]:
            across(i).wait_recv()
            add(held.at[i, a, b], pair_late.at[order[i]])
            result(i).start()

    raw_load(0).start()
    right_load(0).start()
    raw_load(1).start()
    greet_all(length, a, b, c)
    side_steps[0]()
    swap.start()
    produce(0)
    for t in range(n + LAG + LINE_LAG[-1] + 1):
        if t in SIDE_TIMES:
            side_steps[SIDE_TIMES.index(t) + 1]()
        if t < n:
            first_add(t)
        if t + 1 < n:
            produce(t + 1)
        if 0 <= t - LAG < n:
            second_add(t - LAG)
        for j in range(length):
            i = t - LAG - LINE_LAG[j]
            if 0 <= i < n:
                line_step(i, j)
        i = t - LAG - LINE_LAG[length - 1]
        if 0 <= i < n:
            finish(i)
        if 0 <= i - 1 < n:
            finish_late(i - 1)
    side_steps[-1]()
    swap.wait()
    for i in range(n):
        if i >= n - slots:
            to_core(i).wait_send()
        across(i).wait_send()
        result(i).wait()
        for bb in rows_of(i):
            for here in range(length):

                def gone():
                    for dest in range(here + 1, length):
                        up(i, here, dest, bb).wait_send()
                    for dest in range(0, here):
                        down(i, here, dest, bb).wait_send()

                when(a == here, gone)


def scatter_all(lefts, rights, extras, outgoing, shard_shapes, plan, length):
    n = len(plan)
    slots, pair_slots = 2, 4
    total_rows = lefts[0].shape[0]
    rows, width = shard_shapes[0][0], plan[0][2]
    late = sum(p[3] != "pair" for p in plan)
    flows = (length - 1) * (n + late)
    lead = shard_shapes[-1][0]
    dma = pltpu.SemaphoreType.DMA
    grad_mod, lifted_t, slope_t, ada, mask_rows = extras
    images = lifted_t.shape[1]
    payload = (-(-(rows + mask_rows.shape[0]) // 8) * 8, images)
    small = [dma((length - 1,)), dma((length - 1,)), dma((4,))]
    slab = (rows, width)
    return pl.pallas_call(
        functools.partial(scatter_kernel, length, plan, slots, pair_slots),
        out_shape=tuple(jax.ShapeDtypeStruct(s, BF16) for s in shard_shapes)
        + (
            jax.ShapeDtypeStruct(ada.shape, F32),
            jax.ShapeDtypeStruct((1, ada.shape[1]), F32),
            jax.ShapeDtypeStruct((length, 2, 2) + payload, F32),
            jax.ShapeDtypeStruct(outgoing.shape, BF16),
        ),
        in_specs=[anywhere] * 8 + [in_vmem] * 5 + [anywhere],
        out_specs=[anywhere] * 5 + [in_vmem] * 2 + [anywhere],
        scratch_shapes=[
            pltpu.VMEM((2, total_rows, width), BF16),
            pltpu.VMEM((2, total_rows, width), BF16),
            pltpu.VMEM((2 * lead, 2 * length * rows, total_rows), BF16),
            pltpu.VMEM((n, length, 2) + slab, BF16),
            pltpu.VMEM((slots, length, 2) + slab, BF16),
            pltpu.VMEM((slots, length, 2) + slab, BF16),
            pltpu.VMEM((pair_slots, length) + slab, BF16),
            pltpu.VMEM((late,) + slab, BF16),
            pltpu.VMEM((flows,) + slab, BF16),
            pltpu.VMEM((flows,) + slab, BF16),
            dma((lead + 3,)), dma((n,)), dma((n,)), dma((n,)), dma((n,)), dma((n,)),
            dma((flows,)), dma((flows,)), dma((flows,)), dma((flows,)), dma((n,)),
            pltpu.SemaphoreType.REGULAR, pltpu.SemaphoreType.REGULAR,
            pltpu.VMEM((length, 2, 2) + grad_mod.shape, BF16),
            pltpu.VMEM((2, rows, width), F32),
            pltpu.VMEM(payload, F32),
            pltpu.VMEM(payload, F32),
        ]
        + small
        + small
        + [dma((2,)), dma((2,)), dma((2,))],
        compiler_params=pltpu.CompilerParams(
            collective_id=1, has_side_effects=True, vmem_limit_bytes=62 * 1024 * 1024
        ),
        name="scatter_grads",
    )(*lefts, *rights, *extras, outgoing)


def small_gather_kernel(devices, own_ref, out_ref, send, recv):
    me = lax.axis_index("dp")
    barrier = pltpu.get_barrier_semaphore()
    ahead = [lax.rem(me + k, devices) for k in range(1, devices)]
    for target in ahead:
        pl.semaphore_signal(barrier, inc=1, device_id={"dp": target}, device_id_type=MESH)
    pl.semaphore_wait(barrier, devices - 1)
    out_ref[me] = own_ref[...]
    mine = out_ref.at[me]
    copies = [remote(mine, mine, send.at[k], recv.at[k], {"dp": to}) for k, to in enumerate(ahead)]
    for copy in copies:
        copy.start()
    for k, copy in enumerate(copies):
        slab = out_ref.at[lax.rem(me + devices - 1 - k, devices)]
        remote(slab, slab, send.at[k], recv.at[k], {"dp": ahead[k]}).wait_recv()
        copy.wait_send()


def small_gather(own, devices, collective_id):
    dma = pltpu.SemaphoreType.DMA
    return pl.pallas_call(
        functools.partial(small_gather_kernel, devices),
        out_shape=jax.ShapeDtypeStruct((devices,) + own.shape, own.dtype),
        in_specs=[in_vmem],
        out_specs=in_vmem,
        scratch_shapes=[dma((devices - 1,)), dma((devices - 1,))],
        compiler_params=pltpu.CompilerParams(collective_id=collective_id, has_side_effects=True),
        name="small_gather",
    )(own)


def head_window(h):
    low, high = h * HD, h * HD + HD
    start = low // 128 * 128
    return low, high, start, -(-high // 128) * 128


def contract(x, y, dims):
    return lax.dot_general(x, y, ((dims[0], dims[1]), ((), ())), preferred_element_type=F32)


def head_operands(qkv_ref, rows, h):
    width = qkv_ref.shape[1] // 3
    low, high, start, stop = head_window(h)
    lane = lax.broadcasted_iota(jnp.int32, (1, stop - start), 1) + start
    inside = jnp.logical_and(lane >= low, lane < high)
    parts = [qkv_ref[rows, j * width + start : j * width + stop] for j in range(3)]
    return inside, slice(start, stop), parts


def only(inside, x):
    return jnp.where(inside, x, jnp.zeros_like(x))


def softmax_of(query, key, allowed):
    scores = jnp.where(allowed, contract(query, key, ((1,), (1,))) * HD**-0.5, MASKED)
    weights = jnp.exp(scores - jnp.max(scores, axis=-1, keepdims=True))
    return weights * (1.0 / jnp.sum(weights, axis=-1, keepdims=True))


def place(out_ref, rows, start, inside, value):
    window = slice(start, start + value.shape[1])
    out_ref[rows, window] = jnp.where(inside, value.astype(BF16), out_ref[rows, window])


def attend(qkv_ref, rows, allowed, out_ref):
    for h in range(HEADS):
        inside, window, (query, key, value) = head_operands(qkv_ref, rows, h)
        probs = softmax_of(only(inside, query), key, allowed).astype(BF16)
        place(out_ref, rows, window.start, inside, contract(probs, value, ((1,), (0,))))


def attend_back(qkv_ref, grad_ref, rows, allowed, out_ref):
    width = grad_ref.shape[1]
    for h in range(HEADS):
        inside, window, (query, key, value) = head_operands(qkv_ref, rows, h)
        query, grad = only(inside, query), only(inside, grad_ref[rows, window])
        scores = jnp.where(allowed, contract(key, query, ((1,), (1,))) * HD**-0.5, MASKED)
        weights = jnp.exp(scores - jnp.max(scores, axis=0, keepdims=True))
        probs = weights * (1.0 / jnp.sum(weights, axis=0, keepdims=True))
        grad_probs = contract(value, grad, ((1,), (1,)))
        centre = jnp.sum(probs * grad_probs, axis=0, keepdims=True)
        grad_scores = (probs * (grad_probs - centre)).astype(BF16)
        start = window.start
        place(out_ref, rows, 2 * width + start, inside, contract(probs.astype(BF16), grad, ((1,), (0,))))
        place(out_ref, rows, width + start, inside, contract(grad_scores, query, ((1,), (0,))) * HD**-0.5)
        place(out_ref, rows, start, inside, contract(grad_scores, key, ((0,), (0,))) * HD**-0.5)


def dot(x, y):
    return jnp.dot(x, y, preferred_element_type=F32)


def dot_back(x, y):
    return lax.dot_general(x, y, (((1,), (1,)), ((), ())), preferred_element_type=F32)


def dot_rows(x, y):
    return lax.dot_general(x, y, (((0,), (0,)), ((), ())), preferred_element_type=F32)


def normal(x):
    centred = x - jnp.mean(x, axis=-1, keepdims=True)
    scale = lax.rsqrt(jnp.mean(centred * centred, axis=-1, keepdims=True) + EPS)
    return centred * scale, scale


TILE = 384
DEPTH = 2
GELU = math.sqrt(2.0 / math.pi)


def columns_of(t):
    if isinstance(t, int):
        return pl.ds(t * TILE, TILE)
    return pl.ds(pl.multiple_of(t * TILE, 128), TILE)


def unit_of(t, width):
    if isinstance(t, int):
        return pl.ds(t * width, width)
    return pl.ds(pl.multiple_of(t * width, 128), width)


class Stream:
    def __init__(self, ring, sems, width):
        self.ring, self.sems, self.width = ring, sems, width
        self.stages = []

    def add(self, weight, back, inner, outer):
        self.stages.append((weight, back, inner, outer))

    def tile(self, stage, n, k):
        weight, back, inner, _ = self.stages[stage]
        t = n * inner + k
        slot = t % DEPTH if isinstance(t, int) else lax.rem(t, DEPTH)
        deep, side = unit_of(k, self.width), unit_of(n, self.width)
        src = weight.at[side, deep] if back else weight.at[deep, side]
        buffer = self.ring.at[stage % 2, slot]
        return pltpu.make_async_copy(src, buffer, self.sems.at[stage % 2, slot]), buffer

    def begin(self, stage):
        if stage < len(self.stages):
            _, _, inner, outer = self.stages[stage]
            for t in range(min(DEPTH, inner * outer)):
                self.tile(stage, t // inner, t % inner)[0].start()

    def run(self, stage, use, ahead=True):
        _, _, inner, outer = self.stages[stage]
        if ahead:
            self.begin(stage + 1)
        count = inner * outer

        def group(n):
            def product(k, left, back):
                copy, buffer = self.tile(stage, n, k)
                copy.wait()
                result = (dot_back if back else dot)(left, buffer[...])
                t = n * inner + k + DEPTH

                def refill():
                    self.tile(stage, lax.div(t, inner), lax.rem(t, inner))[0].start()

                if not isinstance(t, int):
                    when(t < count, refill)
                elif t < count:
                    self.tile(stage, t // inner, t % inner)[0].start()
                return result

            use(n, product)

        def body(n, carry):
            group(n)
            return carry

        if outer == 1:
            group(0)
        else:
            lax.fori_loop(0, outer, body, 0)


def each_quarter(rows, run):
    def body(q, carry):
        run(q, pl.ds(pl.multiple_of(q * rows, rows), rows))
        return carry

    lax.fori_loop(0, 8, body, 0)


def piece_of(mod_ref, q, p, width, columns=None):
    if columns is None:
        return mod_ref[q, :, p * width : (p + 1) * width]
    return mod_ref[q, :, pl.ds(p * width + columns.start, TILE)]


def modulate(x_ref, mod_ref, out_ref, first, quarter_rows):
    width = x_ref.shape[1]

    def run(q, rows):
        hat = normal(x_ref[rows, :])[0]
        shift, scale = piece_of(mod_ref, q, first, width), piece_of(mod_ref, q, first + 1, width)
        out_ref[rows, :] = (hat * (1.0 + scale) + shift).astype(BF16)

    each_quarter(quarter_rows, run)


def modulate_back(grad, x, scale):
    hat, inverse = normal(x)
    inner = grad * (1.0 + scale)
    along = jnp.mean(inner * hat, axis=-1, keepdims=True)
    grad_x = inverse * (inner - jnp.mean(inner, axis=-1, keepdims=True) - hat * along)
    return grad_x, jnp.sum(grad, axis=0, keepdims=True), jnp.sum(grad * hat, axis=0, keepdims=True)


def split_quarters(quarter_rows, run):
    for q in range(8):
        run(q, slice(q * quarter_rows, (q + 1) * quarter_rows))


def allowed_of(row_ref, column_ref, block):
    rows = pl.ds(pl.multiple_of(block * ATT_ROWS, ATT_ROWS), ATT_ROWS)
    return rows, row_ref[rows, :] == column_ref[block]


def each_block(total_rows, run):
    def body(block, carry):
        run(block)
        return carry

    lax.fori_loop(0, total_rows // ATT_ROWS, body, 0)


def forward_stages(stream, weights):
    width = weights[0].shape[0]
    qkv, proj, up, down = weights
    stream.add(qkv, False, 1, qkv.shape[1] // width)
    stream.add(proj, False, 1, 1)
    stream.add(up, False, 1, up.shape[1] // width)
    stream.add(down, False, down.shape[0] // width, 1)


def backward_stages(stream, weights):
    width = weights[0].shape[0]
    qkv, proj, up, down = weights
    stream.add(down, True, 1, down.shape[0] // width)
    stream.add(up, True, up.shape[1] // width, 1)
    stream.add(proj, True, 1, 1)
    stream.add(qkv, True, qkv.shape[1] // width, 1)


def by_parts(quarter_rows, width, run):
    def one(q, rows):
        for t in range(width // TILE):
            run(q, rows, slice(t * TILE, (t + 1) * TILE))

    each_quarter(quarter_rows, one)


def proj_tile(r, mod_ref, quarter_rows, columns, branch):
    width = r.x.shape[1]
    r.branch[:, columns] = branch.astype(BF16)

    def gated(q, rows):
        gate = piece_of(mod_ref, q, 2, width, columns)
        r.x2[rows, columns] = r.x[rows, columns] + gate * branch[rows]

    split_quarters(quarter_rows, gated)


def gelu_parts(h):
    square = h * h
    t = jnp.tanh(h * (GELU + (GELU * 0.044715) * square))
    half = 0.5 + 0.5 * t
    return h * half, half + (0.5 * h) * (1.0 - t * t) * (GELU + (3.0 * GELU * 0.044715) * square)


def up_tile(r, columns, h):
    act, slope = gelu_parts(h)
    r.act[:, columns] = act.astype(BF16)
    r.slope[:, columns] = slope.astype(BF16)


def out_tile(r, mod_ref, quarter_rows, columns, mlp):
    width = r.x.shape[1]
    r.mlp[:, columns] = mlp.astype(BF16)

    def gated(q, rows):
        gate = piece_of(mod_ref, q, 5, width, columns)
        r.out[rows, columns] = (r.x2[rows, columns] + gate * mlp[rows]).astype(BF16)

    split_quarters(quarter_rows, gated)


def run_forward(stream, r, mod_ref, segments, quarter_rows, finish_part, done):
    width = r.x.shape[1]
    total_rows = r.x.shape[0]
    modulate(r.x, mod_ref, r.a1, 0, quarter_rows)

    def qkv(n, product):
        r.qkv[:, unit_of(n, width)] = product(0, r.a1[...], False).astype(BF16)

    stream.run(0, qkv)
    done("a1")

    def mix(block):
        rows, allowed = allowed_of(*segments, block)
        attend(r.qkv, rows, allowed, r.att)

    each_block(total_rows, mix)

    def proj(n, product):
        r.acc[...] = product(0, r.att[...], False)

    stream.run(1, proj)
    done("att")

    def gated(q, rows, columns):
        branch = r.acc[rows, columns]
        r.branch[rows, columns] = branch.astype(BF16)
        gate = piece_of(mod_ref, q, 2, width, columns)
        r.x2[rows, columns] = r.x[rows, columns] + gate * branch

    by_parts(quarter_rows, width, gated)
    modulate(r.x2, mod_ref, r.a2, 3, quarter_rows)

    def up(n, product):
        r.acc[...] = product(0, r.a2[...], False)

        def part(q, rows, columns):
            into = pl.ds(pl.multiple_of(n * width + columns.start, 128), TILE)
            act, slope = gelu_parts(r.acc[rows, columns])
            r.act[rows, into] = act.astype(BF16)
            r.slope[rows, into] = slope.astype(BF16)

        by_parts(quarter_rows, width, part)

    stream.run(2, up)
    done("a2")

    def down(n, product):
        for k in range(r.act.shape[1] // width):
            part = product(k, r.act[:, k * width : (k + 1) * width], False)
            if k == 0:
                r.acc[...] = part
            else:
                r.acc[...] += part

    stream.run(3, down)
    done("act")
    by_parts(quarter_rows, width, lambda q, rows, columns: finish_part(q, rows, columns, r.acc[rows, columns]))


def run_backward(stream, first, r, mod_ref, segments, quarter_rows, grad_of, finish, done):
    width = r.x.shape[1]
    total_rows = r.x.shape[0]

    def down(n, product):
        columns = unit_of(n, width)
        grad = product(0, r.dmlp[...], True)
        r.slope[:, columns] = (grad * r.slope[:, columns].astype(F32)).astype(BF16)

    stream.run(first, down)
    done("dmlp")
    done("slope")

    def up(n, product):
        for k in range(r.slope.shape[1] // width):
            part = product(k, r.slope[:, k * width : (k + 1) * width], True)
            if k == 0:
                r.dx2[...] = part
            else:
                r.dx2[...] += part

    stream.run(first + 1, up)

    def middle(q, rows):
        scale, gate = piece_of(mod_ref, q, 4, width), piece_of(mod_ref, q, 2, width)
        grad, shift_grad, scale_grad = modulate_back(r.dx2[rows, :], r.x2[rows, :], scale)
        grad = grad + grad_of(rows)
        r.dx2[rows, :] = grad
        r.dmod[q, :, 3 * width : 4 * width] = shift_grad
        r.dmod[q, :, 4 * width : 5 * width] = scale_grad
        r.dmod[q, :, 2 * width : 3 * width] = jnp.sum(
            grad * r.branch[rows, :].astype(F32), axis=0, keepdims=True
        )
        r.dbranch[rows, :] = (gate * grad).astype(BF16)

    each_quarter(quarter_rows, middle)

    def proj(n, product):
        r.datt[...] = product(0, r.dbranch[...], True).astype(BF16)

    stream.run(first + 2, proj)
    done("dbranch")

    def mix(block):
        rows, allowed = allowed_of(*segments, block)
        attend_back(r.qkv, r.datt, rows, allowed, r.dqkv)

    each_block(total_rows, mix)
    done("dqkv")

    def qkv(n, product):
        for k in range(3):
            part = product(k, r.dqkv[:, k * width : (k + 1) * width], True)
            if k == 0:
                r.acc[...] = part
            else:
                r.acc[...] += part

    stream.run(first + 3, qkv, ahead=False)

    def outer(q, rows):
        scale = piece_of(mod_ref, q, 1, width)
        grad, shift_grad, scale_grad = modulate_back(r.acc[rows, :], r.x[rows, :], scale)
        r.dmod[q, :, :width] = shift_grad
        r.dmod[q, :, width : 2 * width] = scale_grad
        finish(q, rows, grad + r.dx2[rows, :])

    each_quarter(quarter_rows, outer)
    done("dmod")


def placed(kept_ref, m, slot):
    kept = kept_ref[m]
    positions = lax.broadcasted_iota(jnp.int32, (slot, kept.shape[1]), 0)
    return jnp.where(positions == kept, 1.0, 0.0).astype(BF16)


class Copies:
    def __init__(self, sems):
        self.sems, self.count, self.pending = sems, 0, []

    def start(self, src, dst):
        copy = pltpu.make_async_copy(src, dst, self.sems.at[self.count])
        self.count += 1
        copy.start()
        self.pending.append(copy)
        return copy

    def finish(self):
        for copy in self.pending:
            copy.wait()
        self.pending = []


def encode_kernel(names, tokens, kept_ref, mod_ref, row_ref, column_ref, wq, wp, wu, wd, *rest):
    outs, scratch = rest[: len(names)], rest[len(names) :]
    r = SimpleNamespace(**dict(zip(names + ("acc",), scratch[: len(names) + 1])))
    loaded, ring, stream_sems, sems = scratch[len(names) + 1 :]
    width = loaded.shape[2]
    slot = loaded.shape[1]

    def work():
        stream = Stream(ring, stream_sems, width)
        forward_stages(stream, (wq, wp, wu, wd))
        copies = Copies(sems)
        copies.start(tokens, loaded)
        stream.begin(0)
        copies.finish()
        kept = kept_ref.shape[2]
        for m in range(2):
            r.x[m * kept : (m + 1) * kept, :] = dot_rows(placed(kept_ref, m, slot), loaded[m])
        total_rows = r.x.shape[0]
        out_of = dict(zip(names, outs))

        def done(name):
            copies.start(getattr(r, name), out_of[name].at[pl.ds(0, total_rows)])

        def finish_part(q, rows, columns, mlp):
            r.mlp[rows, columns] = mlp.astype(BF16)
            gate = piece_of(mod_ref, q, 5, width, columns)
            r.out[rows, columns] = (r.x2[rows, columns] + gate * mlp).astype(BF16)

        run_forward(stream, r, mod_ref, (row_ref, column_ref), total_rows // 8, finish_part, done)
        for name in ("x", "x2", "qkv", "branch", "slope", "mlp", "out"):
            done(name)
        copies.finish()

    when(lax.axis_index("section") == 0, work)


def decode_kernel(
    names, rights, received, cotangent, kept_ref, mask_ref, mod_ref, row_ref, column_ref, wq, wp, wu, wd,
    a1, att, a2, act, *rest,
):
    outs, scratch = rest[: 4 + len(rights) + 4], rest[4 + len(rights) + 4 :]
    lefts = dict(zip(("a1", "att", "a2", "act"), outs[:4]))
    right_outs = dict(zip(rights, outs[4 : 4 + len(rights)]))
    dmod_out, decoded, back, mask_out = outs[4 + len(rights) :]
    r = SimpleNamespace(**dict(zip(names, scratch[: len(names)])))
    got, ring, stream_sems, sems = scratch[len(names) :]
    width = got.shape[2]

    def work():
        stream = Stream(ring, stream_sems, width)
        forward_stages(stream, (wq, wp, wu, wd))
        backward_stages(stream, (wq, wp, wu, wd))
        copies = Copies(sems)
        copies.start(received, got)
        copies.start(cotangent, r.dy)
        stream.begin(0)
        copies.finish()
        total_rows = r.x.shape[0]
        slot, kept = total_rows // 2, kept_ref.shape[2]
        for m in range(2):
            place = placed(kept_ref, m, slot)
            flags = jnp.sum(place.astype(F32), axis=1, keepdims=True)
            r.free[m * slot : (m + 1) * slot, :] = jnp.broadcast_to(1.0 - flags, (slot, 128))
            filled = dot(place, got[m]) + (1.0 - flags) * mask_ref[...].astype(F32)
            r.x[m * slot : (m + 1) * slot, :] = filled
        out_of = {**lefts, **right_outs, "dmod": dmod_out, "slope": right_outs["dhid"]}

        def done(name):
            copies.start(getattr(r, name), out_of[name])

        def finish_part(q, rows, columns, part):
            gate = piece_of(mod_ref, q, 5, width, columns)
            dy = r.dy[rows, columns].astype(F32)
            r.out[rows, columns] = (r.x2[rows, columns] + gate * part).astype(BF16)
            r.dmlp[rows, columns] = (gate * dy).astype(BF16)
            r.dmod[q, :, 5 * width + columns.start : 5 * width + columns.stop] = jnp.sum(
                dy * part, axis=0, keepdims=True
            )

        segments = (row_ref, column_ref)
        run_forward(stream, r, mod_ref, segments, total_rows // 8, finish_part, done)
        copies.start(r.out, decoded)
        r.mask[...] = jnp.zeros_like(r.mask)

        def finish(q, rows, grad):
            r.mask[...] += jnp.sum(grad * r.free[rows, :1], axis=0, keepdims=True)
            r.dbranch[rows, :] = grad.astype(BF16)

        def grad_of(rows):
            return r.dy[rows, :].astype(F32)

        def done_back(name):
            if name == "dbranch":
                copies.start(getattr(r, name), out_of[name]).wait()
                copies.pending.pop()
            else:
                done(name)

        run_backward(stream, 4, r, mod_ref, segments, total_rows // 8, grad_of, finish, done_back)
        for m in range(2):
            place = placed(kept_ref, m, slot)
            got[m] = dot_rows(place, r.dbranch[m * slot : (m + 1) * slot, :]).astype(BF16)
        copies.start(got, back)
        copies.start(r.mask, mask_out)
        copies.finish()

    when(lax.axis_index("section") == 1, work)


def encode_back_kernel(
    names, rights, saved, received, kept_ref, mod_ref, row_ref, column_ref, wq, wp, wu, wd, *rest
):
    kept_in = dict(zip(saved, rest[: len(saved)]))
    rest = rest[len(saved) + len(rights) + 1 :]
    right_outs = dict(zip(rights, rest[: len(rights)]))
    dmod_out, token_out = rest[len(rights) : len(rights) + 2]
    scratch = rest[len(rights) + 2 :]
    r = SimpleNamespace(**dict(zip(names, scratch[: len(names)])))
    ring, stream_sems, sems = scratch[len(names) :]
    width = r.x.shape[1]

    def work():
        stream = Stream(ring, stream_sems, width)
        backward_stages(stream, (wq, wp, wu, wd))
        copies = Copies(sems)
        first = [copies.start(received, r.dy)]
        for name in reversed(saved):
            first.append(copies.start(kept_in[name], getattr(r, name)))
        stream.begin(0)
        for copy in first[:2]:
            copy.wait()
        total_rows = r.x.shape[0]
        out_of = {**right_outs, "dmod": dmod_out, "slope": right_outs["dhid"]}

        def done(name):
            if name == "dmod":
                copies.start(getattr(r, name), out_of[name])
            else:
                copies.start(getattr(r, name), out_of[name].at[pl.ds(0, total_rows)])

        def start(q, rows):
            gate = piece_of(mod_ref, q, 5, width)
            dy = r.dy[rows, :].astype(F32)
            r.dmlp[rows, :] = (gate * dy).astype(BF16)
            r.dmod[q, :, 5 * width :] = jnp.sum(dy * r.mlp[rows, :].astype(F32), axis=0, keepdims=True)

        each_quarter(total_rows // 8, start)
        for copy in first[2:]:
            copy.wait()
        copies.pending = []

        def finish(q, rows, grad):
            r.mlp[rows, :] = grad.astype(BF16)

        def grad_of(rows):
            return r.dy[rows, :].astype(F32)

        segments = (row_ref, column_ref)
        run_backward(stream, 0, r, mod_ref, segments, total_rows // 8, grad_of, finish, done)
        kept = kept_ref.shape[2]
        slot = token_out.shape[1]
        for m in range(2):
            place = placed(kept_ref, m, slot)
            r.tokens[m] = dot(place, r.mlp[m * kept : (m + 1) * kept, :]).astype(BF16)
        copies.start(r.tokens, token_out)
        copies.finish()

    when(lax.axis_index("section") == 0, work)


VMEM_BYTES = 60 * 1024 * 1024
LEFTS = ("a1", "att", "a2", "act")
RIGHTS = ("dqkv", "dbranch", "dhid", "dmlp")
SAVED = ("x", "x2", "qkv", "branch", "slope", "mlp")


def buffer_shapes(rows, width, wide_width):
    full, broad = lambda t: ((rows, width), t), lambda n, t: ((rows, n), t)
    return dict(
        x=full(F32), x2=full(F32), dx2=full(F32), acc=full(F32), a1=full(BF16),
        att=full(BF16), a2=full(BF16), branch=full(BF16), mlp=full(BF16), out=full(BF16),
        dy=full(BF16), dmlp=full(BF16), dbranch=full(BF16), datt=full(BF16),
        qkv=broad(3 * width, BF16), dqkv=broad(3 * width, BF16), act=broad(wide_width, BF16),
        slope=broad(wide_width, BF16), dhid=broad(wide_width, BF16),
        dmod=((8, 1, 6 * width), F32), mask=((1, width), F32), free=((rows, 128), F32),
    )


def rings(width):
    dma = pltpu.SemaphoreType.DMA
    return [pltpu.VMEM((2, DEPTH, width, width), BF16), dma((2, DEPTH)), dma((24,))]


def encode(tokens, kept, modulation, segments, weights, rows, all_rows):
    width, wide_width = weights[0].shape[0], weights[2].shape[1]
    shapes = buffer_shapes(rows, width, wide_width)
    names = LEFTS + SAVED + ("out",)
    outs = [jax.ShapeDtypeStruct(((all_rows if n in LEFTS else rows), shapes[n][0][1]), shapes[n][1]) for n in names]
    results = pl.pallas_call(
        functools.partial(encode_kernel, names),
        out_shape=outs,
        in_specs=[anywhere] + [in_vmem] * 4 + [anywhere] * 4,
        out_specs=[anywhere] * len(names),
        scratch_shapes=[pltpu.VMEM(*shapes[n]) for n in names + ("acc",)]
        + [pltpu.VMEM(tokens.shape, BF16)]
        + rings(width),
        compiler_params=pltpu.CompilerParams(vmem_limit_bytes=VMEM_BYTES),
        name="encode",
    )(tokens, kept, modulation, *segments, *weights)
    return results[:4], results[4:-1], results[-1]


def decode(received, cotangent, kept, mask_token, modulation, segments, weights, lefts):
    width, wide_width = weights[0].shape[0], weights[2].shape[1]
    rows = cotangent.shape[0]
    shapes = buffer_shapes(rows, width, wide_width)
    names = LEFTS + (
        "x", "x2", "qkv", "branch", "slope", "out", "dy", "dmlp", "dbranch", "datt", "dqkv", "dmod",
        "mask", "free",
    )
    scratch = [pltpu.VMEM(*shapes[n]) for n in names]
    names += ("dx2", "acc")
    scratch += [pltpu.VMEM(*shapes["dx2"]), pltpu.VMEM(*shapes["acc"])]
    outs = [jax.ShapeDtypeStruct(*shapes[n]) for n in LEFTS + RIGHTS + ("dmod", "out")]
    outs += [jax.ShapeDtypeStruct(received.shape, BF16), jax.ShapeDtypeStruct((1, width), F32)]
    results = pl.pallas_call(
        functools.partial(decode_kernel, names, RIGHTS),
        out_shape=outs,
        in_specs=[anywhere] * 2 + [in_vmem] * 5 + [anywhere] * 8,
        out_specs=[anywhere] * len(outs),
        scratch_shapes=scratch + [pltpu.VMEM(received.shape, BF16)] + rings(width),
        input_output_aliases={11 + j: j for j in range(4)},
        compiler_params=pltpu.CompilerParams(vmem_limit_bytes=VMEM_BYTES),
        name="decode",
    )(received, cotangent, kept, mask_token, modulation, *segments, *weights, *lefts)
    return results[:4], results[4:8], results[8:]


def encode_back(received, kept, modulation, segments, weights, saved, rights, grad_mod, token_shape):
    width, wide_width = weights[0].shape[0], weights[2].shape[1]
    rows = received.shape[0]
    shapes = buffer_shapes(rows, width, wide_width)
    names = SAVED + ("dy", "dmlp", "dbranch", "datt", "dqkv", "dmod", "dx2", "acc", "tokens")
    shapes["tokens"] = (token_shape, BF16)
    outs = [jax.ShapeDtypeStruct(x.shape, x.dtype) for x in tuple(rights) + (grad_mod,)]
    outs.append(jax.ShapeDtypeStruct(token_shape, BF16))
    before = 9 + len(saved)
    results = pl.pallas_call(
        functools.partial(encode_back_kernel, names, RIGHTS, SAVED),
        out_shape=outs,
        in_specs=[anywhere] + [in_vmem] * 4 + [anywhere] * (4 + len(saved) + 5),
        out_specs=[anywhere] * len(outs),
        scratch_shapes=[pltpu.VMEM(*shapes[n]) for n in names] + rings(width),
        input_output_aliases={before + j: j for j in range(5)},
        compiler_params=pltpu.CompilerParams(vmem_limit_bytes=VMEM_BYTES),
        name="encode_back",
    )(received, kept, modulation, *segments, *weights, *saved, *rights, grad_mod)
    return results[:4], results[4], results[5]


def gather_encode_kernel(length, plan, names, *refs):
    sources, (partial, big_ref, tokens, kept_ref, row_ref, column_ref) = refs[:4], refs[4:10]
    outs, (mod_out, received) = refs[10:14], refs[14:16]
    saved_outs = refs[16 : 16 + len(names)]
    rest = refs[16 + len(names) :]
    r = SimpleNamespace(**dict(zip(names + ("out",), rest[: len(names) + 1])))
    (
        loaded, mod_ref, tiles, last_tile, part_held, part_core, part_pair, part_line,
    ) = rest[len(names) + 1 : len(names) + 9]
    sems = rest[len(names) + 9 : len(names) + 18]
    part_sems, line_sems, tile_sems, out_sems, copy_sems = rest[len(names) + 18 :]
    a, b, c = position()
    encoder = lax.axis_index("section") == 0
    other = {"section": 1 - lax.axis_index("section")}
    barrier = pltpu.get_barrier_semaphore()

    def tell(target):
        pl.semaphore_signal(barrier, inc=1, device_id=target, device_id_type=MESH)

    tell(at(a, 1 - b, c))
    tell(at(a, b, 1 - c))
    tell(other)
    for k in range(1, length):
        tell(at(lax.rem(a + k, length), b, c))
    pl.semaphore_wait(barrier, length + 2)

    n = len(plan)
    width = r.x.shape[1]
    total_rows = r.x.shape[0]
    quarter_rows = total_rows // 8
    issue, move, complete, drain = gather_moves(length, plan, sources, outs, sems, a, b, c)
    copies = Copies(copy_sems)
    out_of = dict(zip(names, saved_outs))

    part_load = pltpu.make_async_copy(partial.at[:, :, c], part_held, part_sems.at[0])
    part_to_core = remote(partial.at[:, :, 1 - c], part_core, part_sems.at[1], part_sems.at[2], at(a, b, 1 - c))
    part_across = remote(part_held.at[:, 1 - b], part_pair, part_sems.at[3], part_sems.at[4], at(a, 1 - b, c))

    def part_to_line(k):
        to = lax.rem(a + k, length)
        return remote(
            part_held.at[to, b], part_line.at[k - 1], line_sems.at[0, k - 1], line_sems.at[1, k - 1], at(to, b, c)
        )

    def add_part(where, got):
        part_held[where] = part_held[where] + got

    def part_first():
        part_to_core.wait_recv()
        part_load.wait()
        for s in range(2 * length):
            add_part((s // 2, s % 2), part_core[s // 2, s % 2])
        part_across.start()

    def part_second():
        part_across.wait()
        for aa in range(length):
            add_part((aa, b), part_pair[aa])
        for k in range(1, length):
            part_to_line(k).start()

    def part_last():
        total = part_held[a, b].astype(F32)
        for k in range(1, length):
            part_to_line(k).wait_recv()
            total = total + part_line[k - 1].astype(F32)
        for q in range(8):
            first = q // SMALL_PER * SMALL_PER
            mod_ref[q] = jnp.where(big_ref[q] > 0, total[first : first + 1], total[q : q + 1])
        copies.start(mod_ref, mod_out)

    def load_tile(w, low, t):
        src = outs[w].at[:, :, :, :, pl.ds(low + t * TILE, TILE)]
        return pltpu.make_async_copy(src, tiles.at[t % 2], tile_sems.at[t % 2])

    def products(w, low, left, put):
        count = width // TILE
        for t in range(min(2, count)):
            load_tile(w, low, t).start()
        for t in range(count):
            load_tile(w, low, t).wait()
            tile = tiles[t % 2].astype(F32).reshape(width, TILE).astype(BF16)
            result = dot(getattr(r, left)[...], tile)
            if t + 2 < count:
                load_tile(w, low, t + 2).start()
            put(columns_of(low // TILE + t), result)

    def done(name):
        copies.start(getattr(r, name), out_of[name].at[pl.ds(0, total_rows)])

    def start_encode():
        fetch = pltpu.make_async_copy(tokens, loaded, tile_sems.at[2])
        fetch.start()
        fetch.wait()
        kept, slot = kept_ref.shape[2], loaded.shape[1]
        for m in range(2):
            r.x[m * kept : (m + 1) * kept, :] = dot_rows(placed(kept_ref, m, slot), loaded[m])

    def put_qkv(columns, result):
        r.qkv[:, columns] = result.astype(BF16)

    def put_proj(columns, result):
        proj_tile(r, mod_ref, quarter_rows, columns, result)

    def put_up(columns, result):
        up_tile(r, columns, result)

    def send_out(t):
        columns = columns_of(t)
        return remote(
            r.out.at[:, columns], received.at[:, columns], out_sems.at[0, t], out_sems.at[1, t], other
        )

    def encode_chunk(i):
        w, low, _, _ = plan[i]
        if w == 0:
            if i == 0:
                modulate(r.x, mod_ref, r.a1, 0, quarter_rows)
            products(w, low, "a1", put_qkv)
        elif w == 1:
            rows, allowed = slice(0, total_rows), row_ref[...] == column_ref[0]
            attend(r.qkv, rows, allowed, r.att)
            products(w, low, "att", put_proj)
            modulate(r.x2, mod_ref, r.a2, 3, quarter_rows)
        elif w == 2:
            products(w, low, "a2", put_up)
        else:
            src = outs[w].at[:, :, :, :, pl.ds(low, TILE)]
            fetch = pltpu.make_async_copy(src, last_tile, tile_sems.at[2])
            fetch.start()
            fetch.wait()
            tile = last_tile[...].reshape(r.act.shape[1], TILE)
            out_tile(r, mod_ref, quarter_rows, columns_of(low // TILE), dot(r.act[...], tile))
            send_out(low // TILE).start()

    part_load.start()
    part_to_core.start()
    issue(0)
    when(encoder, start_encode)
    part_first()
    for i in range(1, AHEAD):
        issue(i)
    for t in range(n + length - 1):
        move(t, AHEAD)
        if t == 0:
            part_second()
        if t == 1:
            part_last()
        i = t - length + 1
        if i >= 0:
            complete(i)
            when(encoder, lambda: encode_chunk(i))
    for i in range(n):
        drain(i)
    part_to_core.wait_send()
    for k in range(1, length):
        part_to_line(k).wait_send()

    def close():
        for name in names:
            done(name)
        for copy in copies.pending[1:]:
            copy.wait()
        for t in range(width // TILE):
            send_out(t).wait_send()

    when(encoder, close)
    copies.pending[0].wait()

    def arrive():
        for t in range(width // TILE):
            send_out(t).wait_recv()

    when(jnp.logical_not(encoder), arrive)


AHEAD = 4


def gather_encode(shards, partial, big, tokens, kept, segments, plan, length, rows, all_rows):
    n = len(plan)
    width, wide_width = shards[1].shape[1], shards[2].shape[1]
    shapes = buffer_shapes(rows, width, wide_width)
    names = LEFTS + SAVED
    quarters = partial.shape[3]
    part_slab = partial.shape[3:]
    dma = pltpu.SemaphoreType.DMA
    outs = [jax.ShapeDtypeStruct((length, 2, 2) + s.shape, BF16) for s in shards]
    outs += [jax.ShapeDtypeStruct((quarters, 1, 6 * width), F32), jax.ShapeDtypeStruct((rows, width), BF16)]
    outs += [jax.ShapeDtypeStruct(((all_rows if m in LEFTS else rows), shapes[m][0][1]), shapes[m][1]) for m in names]
    results = pl.pallas_call(
        functools.partial(gather_encode_kernel, length, plan, names),
        out_shape=outs,
        in_specs=[anywhere] * 5 + [in_vmem, anywhere] + [in_vmem] * 3,
        out_specs=[anywhere] * len(outs),
        scratch_shapes=[pltpu.VMEM(*shapes[m]) for m in names + ("out",)]
        + [
            pltpu.VMEM(tokens.shape, BF16),
            pltpu.VMEM((quarters, 1, 6 * width), F32),
            pltpu.VMEM((2, length, 2, 2, shards[0].shape[0], TILE), BF16),
            pltpu.VMEM((length, 2, 2, shards[3].shape[0], TILE), BF16),
            pltpu.VMEM((length, 2) + part_slab, BF16),
            pltpu.VMEM((length, 2) + part_slab, BF16),
            pltpu.VMEM((length,) + part_slab, BF16),
            pltpu.VMEM((length - 1,) + part_slab, BF16),
        ]
        + [dma((n, length, 2))] * 4
        + [dma((n, length))] * 2
        + [dma((n, length, 2))] * 2
        + [dma((n,)), dma((5,)), dma((2, length - 1)), dma((3,)), dma((2, width // TILE)), dma((len(names) + 1,))],
        compiler_params=pltpu.CompilerParams(
            collective_id=0, has_side_effects=True, vmem_limit_bytes=VMEM_BYTES
        ),
        name="gather_encode",
    )(*shards, partial, big, tokens, kept, *segments)
    return results[:4], results[4], results[5], results[6:10], results[10:]


def plan_of(widths, lead, unit, line_first):
    plan = [(w, low, unit) for w, width in enumerate(widths) for low in range(0, width, unit)]
    plan += [(len(widths), j, 0) for j in range(lead)]
    return tuple(p + ("line" if i in line_first else "pair",) for i, p in enumerate(plan))


def swap_sections(x):
    return lax.ppermute(x, "section", [(0, 1), (1, 0)])


def on_device(
    tokens, kept_index, big_image, timesteps, labels, cotangent, mask_token, time_weight, class_table,
    ada_weight, ada_bias, qkv_weight, proj_weight, up_weight, down_weight,
):
    section = lax.axis_index("section")
    me = lax.axis_index("dp")
    devices = lax.axis_size("dp")
    micro, slot, width = tokens.shape
    kept_count = kept_index.shape[1]
    own_width = ada_weight.shape[1]
    images = micro * SMALL_PER
    quarters = micro * SMALL_PER
    ada = ada_weight[0]

    length = devices // 4
    ids = jnp.concatenate([timesteps.reshape(1, images), labels.reshape(1, images)])
    if length == 4:
        ids = small_gather(jnp.pad(ids, ((0, 6), (0, 128 - images))), devices, 2)
    else:
        ids = lax.all_gather(ids, "dp", axis=0)
    times = ids[:, 0, :images].reshape(devices * images)
    classes = ids[:, 1, :images].reshape(devices * images)
    half = time_weight.shape[0] // 2
    frequencies = jnp.exp(-math.log(10000.0) * jnp.arange(half, dtype=F32) / half)
    angles = times.astype(F32)[:, None] * frequencies[None, :]
    embedding = jnp.concatenate([jnp.cos(angles), jnp.sin(angles)], axis=-1).astype(BF16)
    onehot = (classes[:, None] == jnp.arange(class_table.shape[0])[None, :]).astype(BF16)
    cond = dot(embedding, time_weight) + dot(onehot, class_table)
    cond = lax.dynamic_slice_in_dim(cond, me * own_width, own_width, axis=1)
    lifted = jax.nn.silu(cond).astype(BF16)
    bias_width = ada_bias.shape[1]
    bias = lax.dynamic_update_slice_in_dim(
        jnp.zeros((1, 6 * width), F32), ada_bias.astype(F32), me * bias_width, axis=1
    )
    partial = (dot(lifted, ada) + bias).astype(BF16).reshape(devices, images, 6 * width)

    big = big_image[:, :1] > 0
    quarter_ids = jnp.arange(quarters, dtype=jnp.int32).reshape(micro, SMALL_PER)
    segment_of = jnp.where(big, quarter_ids[:, :1], quarter_ids).reshape(quarters)
    kept = kept_index.reshape(micro, 1, kept_count)

    def segments(quarter_rows):
        ids = jnp.repeat(segment_of, quarter_rows)
        return ids.reshape(-1, 1), ids.reshape(-1, 1, ATT_ROWS)

    enc_rows, dec_rows = micro * kept_count, micro * slot
    enc_segments = segments(enc_rows // quarters)
    dec_segments = segments(dec_rows // quarters)

    shards = (qkv_weight[0], proj_weight[0], up_weight[0])
    lead = down_weight.shape[1] // qkv_weight.shape[1]
    widths = [x.shape[1] for x in shards]
    if length == 4:
        plan = [(w, low, width, "line") for w in range(3) for low in range(0, widths[w], width)]
        plan += [(3, low, TILE, "line") for low in range(0, width, TILE)]
        plan = tuple(p[:3] + ("pair" if i in (1, 7) else "line",) for i, p in enumerate(plan))
        flags = jnp.repeat(big[:, 0], SMALL_PER).astype(jnp.int32).reshape(quarters, 1, 1)
        whole, modulation, received, lefts, saved = gather_encode(
            shards + (down_weight[0],), partial.reshape((length, 2, 2) + partial.shape[1:]), flags, tokens, kept,
            enc_segments, plan, length, enc_rows, dec_rows,
        )
        weights = tuple(w.reshape(-1, w.shape[-1]) for w in whole)
        received = received.reshape(micro, kept_count, width)
    else:
        whole = (lax.all_gather(x, "dp", axis=0, tiled=True) for x in shards + (down_weight[0],))
        weights = tuple(whole)
        modulation = lax.psum_scatter(partial, "dp", scatter_dimension=0, tiled=False).astype(F32)
        modulation = modulation.reshape(micro, SMALL_PER, 6 * width)
        modulation = jnp.where(big[:, :, None], modulation[:, :1], modulation).reshape(quarters, 1, 6 * width)
        lefts, saved, encoded = encode(tokens, kept, modulation, enc_segments, weights, enc_rows, dec_rows)
        received = swap_sections(encoded).reshape(micro, kept_count, width)

    lefts, rights, (grad_mod, decoded, back, mask_part) = decode(
        received, cotangent.reshape(dec_rows, width), kept, mask_token.reshape(1, width), modulation,
        dec_segments, weights, lefts,
    )
    received = swap_sections(back).reshape(enc_rows, width)
    rights, grad_mod, token_grad = encode_back(
        received, kept, modulation, enc_segments, weights, saved, rights, grad_mod, (micro, slot, width)
    )
    decoded = decoded.reshape(micro, slot, width)
    mask_part = jnp.where(section == 1, mask_part, 0.0).reshape(width)

    half_width = width // 2
    outgoing = jnp.where(section == 0, token_grad[:, :, half_width:], decoded[:, :, :half_width])

    grad_mod = grad_mod.reshape(micro, SMALL_PER, 6 * width)
    first_only = (jnp.arange(SMALL_PER) == 0)[None, :, None]
    grad_mod = jnp.where(
        big[:, :, None], jnp.where(first_only, jnp.sum(grad_mod, axis=1, keepdims=True), 0.0), grad_mod
    )
    grad_mod = grad_mod.reshape(images, 6 * width).astype(BF16)
    silu_slope = jax.vjp(jax.nn.silu, cond)[1](jnp.ones_like(cond))[0]
    shapes = tuple(x.shape for x in shards) + ((lead, own_width, width),)
    every_image = devices * images
    if length == 4:
        mask_rows = mask_part.reshape(-1, every_image)
        extras = (grad_mod, lifted.T, silu_slope.T, ada, mask_rows)
        plan = plan_of(widths, lead, width, (0, 6))
        *mine, ada_grad, bias_sum, shared, incoming = scatter_all(
            lefts, rights, extras, outgoing, shapes, plan, length
        )
        shared = shared.reshape(devices, -1, every_image)
        every_cond = shared[:, :own_width].reshape(width, every_image)
        mask_grad = jnp.sum(shared[:, own_width : own_width + mask_rows.shape[0]], axis=0).reshape(width)
        bias_grad = lax.dynamic_slice_in_dim(bias_sum, me * bias_width, bias_width, axis=1)
    else:
        incoming = swap_sections(outgoing)
        every_mod = lax.all_gather(grad_mod, "dp", axis=0, tiled=True)
        ada_grad = dot_rows(lifted, every_mod)
        bias_sum = jnp.sum(every_mod.astype(F32), axis=0, keepdims=True)
        bias_grad = lax.dynamic_slice_in_dim(bias_sum, me * bias_width, bias_width, axis=1)
        grad_cond = dot_back(every_mod, ada) * silu_slope
        every_cond = lax.psum(lax.all_gather(grad_cond.T, "dp", axis=0, tiled=True), "section")
        mask_grad = lax.psum(mask_part, ("section", "dp"))
        half_rows = jnp.arange(dec_rows)[:, None] < jnp.where(section == 0, enc_rows, dec_rows)
        lefts, rights = ([jnp.where(half_rows, x, jnp.zeros_like(x)) for x in xs] for xs in (lefts, rights))
        split = (dot_rows(x, y).astype(BF16).reshape((devices,) + s) for x, y, s in zip(lefts, rights, shapes))
        mine = tuple(lax.psum_scatter(g, "dp", scatter_dimension=0) for g in split)
    decoded_half = jnp.where(section == 0, incoming, decoded[:, :, half_width:])
    token_half = jnp.where(section == 0, token_grad[:, :, :half_width], incoming)
    every_cond = every_cond.astype(BF16)
    time_grad, table_grad = (
        lax.dot_general(x, every_cond, (((0,), (1,)), ((), ())), preferred_element_type=F32)
        for x in (embedding, onehot)
    )
    qkv_grad, proj_grad, up_grad, down_grad = (g.astype(F32) for g in mine)
    return (
        decoded_half,
        token_half,
        mask_grad,
        time_grad,
        table_grad,
        ada_grad[None],
        bias_grad,
        qkv_grad[None],
        proj_grad[None],
        up_grad[None],
        down_grad.reshape(down_weight.shape),
    )


def solution(mesh):
    rows = P(None, "dp", None)
    ids = P(None, "dp")
    weight = P("section", "dp", None)
    halves = P(None, "dp", "section")
    in_specs = (rows, ids, ids, ids, ids, rows, P(), P(), P(), weight, P("section", "dp")) + (weight,) * 4
    out_specs = (halves, halves, P(), P(), P(), weight, P("section", "dp")) + (weight,) * 4
    return jax.shard_map(
        on_device, mesh=mesh, in_specs=in_specs, out_specs=out_specs, check_vma=False
    )
```

```python
import functools
import math
from types import SimpleNamespace

import jax
import jax.numpy as jnp
from jax import lax
from jax.experimental import pallas as pl
from jax.experimental.pallas import tpu as pltpu
from jax.sharding import PartitionSpec as P

HEADS = 16
HD = 72
SMALL_PER = 4
ATT_ROWS = 256
EPS = 1e-6
MASKED = -1e30
MESH = pl.DeviceIdType.MESH
F32 = jnp.float32
BF16 = jnp.bfloat16


anywhere = pl.BlockSpec(memory_space=pl.ANY)
in_vmem = pl.BlockSpec(memory_space=pltpu.VMEM)


def remote(src, dst, send_sem, recv_sem, target):
    return pltpu.make_async_remote_copy(
        src_ref=src,
        dst_ref=dst,
        send_sem=send_sem,
        recv_sem=recv_sem,
        device_id=target,
        device_id_type=MESH,
    )


def when(condition, run):
    pl.when(condition)(run)


def position():
    me = lax.axis_index("dp")
    return me // 4, (me // 2) % 2, me % 2


def at(line, pair, core):
    return {"dp": (line * 2 + pair) * 2 + core}


def greet(length, a, b, c):
    has_up, has_down = a < length - 1, a > 0
    barrier = pltpu.get_barrier_semaphore()

    def tell(target):
        pl.semaphore_signal(barrier, inc=1, device_id=target, device_id_type=MESH)

    tell(at(a, 1 - b, c))
    tell(at(a, b, 1 - c))
    when(has_up, lambda: tell(at(a + 1, b, c)))
    when(has_down, lambda: tell(at(a - 1, b, c)))
    pl.semaphore_wait(barrier, 2 + has_up.astype(jnp.int32) + has_down.astype(jnp.int32))
    return has_up, has_down


def piece(ref, lead, plan_entry):
    _, low, size, _ = plan_entry
    if size == 0:
        return ref.at[lead + (low,)]
    return ref.at[lead + (slice(None), pl.ds(low, size))]


def gather_moves(length, plan, sources, outs, sems, a, b, c):
    up_s, up_r, down_s, down_r, pair_s, pair_r, core_s, core_r, own_sem = sems
    has_up, has_down = a < length - 1, a > 0
    chunks = range(len(plan))
    line_first = [plan[i][3] == "line" for i in chunks]

    def slot(i, aa, bb, cc):
        return piece(outs[plan[i][0]], (aa, bb, cc), plan[i])

    def own(i):
        return piece(sources[plan[i][0]], (), plan[i])

    def rows_of(i):
        return (b,) if line_first[i] else (b, 1 - b)

    def up(i, k, bb, src=None):
        s = slot(i, a - k, bb, c)
        return remote(s if src is None else src, s, up_s.at[i, k, bb], up_r.at[i, k, bb], at(a + 1, b, c))

    def up_arrival(i, k, bb):
        s = slot(i, a - 1 - k, bb, c)
        return remote(s, s, up_s.at[i, k, bb], up_r.at[i, k, bb], at(a + 1, b, c))

    def down(i, k, bb, src=None):
        s = slot(i, a + k, bb, c)
        return remote(s if src is None else src, s, down_s.at[i, k, bb], down_r.at[i, k, bb], at(a - 1, b, c))

    def down_arrival(i, k, bb):
        s = slot(i, a + 1 + k, bb, c)
        return remote(s, s, down_s.at[i, k, bb], down_r.at[i, k, bb], at(a - 1, b, c))

    def across(i, aa, src=None):
        s = slot(i, aa, b, c)
        return remote(s if src is None else src, s, pair_s.at[i, aa], pair_r.at[i, aa], at(a, 1 - b, c))

    def across_arrival(i, aa):
        s = slot(i, aa, 1 - b, c)
        return remote(s, s, pair_s.at[i, aa], pair_r.at[i, aa], at(a, 1 - b, c))

    def to_core(i, aa, bb, src=None):
        s = slot(i, aa, bb, c)
        return remote(s if src is None else src, s, core_s.at[i, aa, bb], core_r.at[i, aa, bb], at(a, b, 1 - c))

    def core_arrival(i, aa, bb):
        s = slot(i, aa, bb, 1 - c)
        return remote(s, s, core_s.at[i, aa, bb], core_r.at[i, aa, bb], at(a, b, 1 - c))

    def after_across(i, aa):
        across_arrival(i, aa).wait_recv()
        to_core(i, aa, 1 - b).start()

    def issue(i):
        src = own(i)
        pltpu.make_async_copy(src, slot(i, a, b, c), own_sem.at[i]).start()
        across(i, a, src).start()
        when(has_up, lambda: up(i, 0, b, src).start())
        when(has_down, lambda: down(i, 0, b, src).start())
        to_core(i, a, b, src).start()

    def pair_step(i):
        across_arrival(i, a).wait_recv()
        when(has_up, lambda: up(i, 0, 1 - b).start())
        when(has_down, lambda: down(i, 0, 1 - b).start())
        to_core(i, a, 1 - b).start()

    def line_step(i, k):
        for bb in rows_of(i):

            def from_below():
                up_arrival(i, k - 1, bb).wait_recv()
                when(has_up, lambda: up(i, k, bb).start())
                if line_first[i]:
                    across(i, a - k).start()
                to_core(i, a - k, bb).start()

            def from_above():
                down_arrival(i, k - 1, bb).wait_recv()
                when(has_down, lambda: down(i, k, bb).start())
                if line_first[i]:
                    across(i, a + k).start()
                to_core(i, a + k, bb).start()

            when(a - k >= 0, from_below)
            when(a + k <= length - 1, from_above)

    def across_step(i, k):
        if not line_first[i]:
            return
        if k == 0:
            after_across(i, a)
        else:
            when(a - k >= 0, lambda: after_across(i, a - k))
            when(a + k <= length - 1, lambda: after_across(i, a + k))

    def complete(i):
        pltpu.make_async_copy(own(i), slot(i, a, b, c), own_sem.at[i]).wait()
        for aa in range(length):
            for bb in range(2):
                core_arrival(i, aa, bb).wait_recv()

    def drain(i):
        for aa in range(length):
            for bb in range(2):
                to_core(i, aa, bb).wait_send()
            if line_first[i]:
                across(i, aa).wait_send()
        if not line_first[i]:
            across(i, a).wait_send()
        for k in range(length - 1):
            for bb in rows_of(i):
                when(jnp.logical_and(has_up, a - k >= 0), lambda: up(i, k, bb).wait_send())
                when(
                    jnp.logical_and(has_down, a + k <= length - 1),
                    lambda: down(i, k, bb).wait_send(),
                )

    def move(t, ahead):
        n = len(plan)
        if t + ahead < n:
            issue(t + ahead)
        if t < n and not line_first[t]:
            pair_step(t)
        for k in range(1, length):
            i = t - k + 1
            if 0 <= i < n:
                line_step(i, k)
        for k in range(length):
            i = t - k
            if 0 <= i < n:
                across_step(i, k)

    return issue, move, complete, drain


SIDE_TIMES = (2, 4, 5, 6, 8, 10)
LAG, LINE_LAG = 1, (0, 1, 2, 3)


def greet_all(length, a, b, c, between):
    barrier = pltpu.get_barrier_semaphore()

    def tell(target):
        pl.semaphore_signal(barrier, inc=1, device_id=target, device_id_type=MESH)

    tell(at(a, 1 - b, c))
    tell(at(a, b, 1 - c))
    tell({"section": 1 - lax.axis_index("section")})
    for k in range(1, length):
        tell(at(lax.rem(a + k, length), b, c))
    between()
    pl.semaphore_wait(barrier, length + 2)


def spread(length, buffer, sems, a, b, c):
    line_s, line_r, pair_core = sems

    def to_line(k):
        mine = buffer.at[a, b, c]
        return remote(mine, mine, line_s.at[k - 1], line_r.at[k - 1], at(lax.rem(a + k, length), b, c))

    def from_line(k):
        slab = buffer.at[lax.rem(a + length - k, length), b, c]
        return remote(slab, slab, line_s.at[k - 1], line_r.at[k - 1], at(a, 1 - b, c))

    def across(bb):
        part = buffer.at[:, bb, c]
        return remote(part, part, pair_core.at[0], pair_core.at[1], at(a, 1 - b, c))

    def to_core(cc):
        part = buffer.at[:, :, cc]
        return remote(part, part, pair_core.at[2], pair_core.at[3], at(a, b, 1 - c))

    def start():
        for k in range(1, length):
            to_line(k).start()

    def second():
        for k in range(1, length):
            from_line(k).wait_recv()
            to_line(k).wait_send()
        across(b).start()

    def third():
        across(1 - b).wait_recv()
        across(b).wait_send()
        to_core(c).start()

    def end():
        to_core(1 - c).wait_recv()
        to_core(c).wait_send()

    return start, second, third, end


def conditioning_steps(length, inputs, outputs, scratch, a, b, c):
    grad_mod, lifted_t, slope_t, ada, mask_rows = inputs
    ada_grad, bias_sum, shared = outputs
    every, stage, payload, other = scratch[:4]
    mod_sems, shared_sems, side_sems, stage_sems = scratch[4:7], scratch[7:10], scratch[10], scratch[11]
    mod_start, mod_second, mod_third, mod_end = spread(length, every, mod_sems, a, b, c)
    shared_start, shared_second, shared_third, shared_end = spread(length, shared, shared_sems, a, b, c)
    own_rows, images = lifted_t.shape
    mask_count = mask_rows.shape[0]
    width = stage.shape[2]
    count = grad_mod.shape[1] // width
    side = remote(payload, other, side_sems.at[0], side_sems.at[1], {"section": 1 - lax.axis_index("section")})

    def save(j):
        return pltpu.make_async_copy(
            stage.at[j % 2], ada_grad.at[:, pl.ds(j * width, width)], stage_sems.at[j % 2]
        )

    def begin():
        every[a, b, c] = grad_mod[...]
        mod_start()

    def compute():
        mod_end()
        total = None
        for j in range(count):
            columns = slice(j * width, (j + 1) * width)
            rows = every[:, :, :, :, columns].astype(F32).reshape(images, width)
            bias_sum[:, columns] = jnp.sum(rows, axis=0, keepdims=True)
            rows = rows.astype(BF16)
            if j >= 2:
                save(j - 2).wait()
            stage[j % 2] = dot(lifted_t[...], rows)
            save(j).start()
            part = dot_back(ada[:, columns], rows)
            total = part if total is None else total + part
        payload[...] = jnp.zeros_like(payload)
        payload[:own_rows, :] = total * slope_t[...]
        payload[own_rows : own_rows + mask_count, :] = mask_rows[...]
        side.start()

    def add():
        side.wait()
        shared[a, b, c] = payload[...] + other[...]
        shared_start()

    def end():
        shared_end()
        for j in range(count - 2, count):
            save(j).wait()

    return begin, mod_second, mod_third, compute, add, shared_second, shared_third, end


def scatter_kernel(length, plan, slots, pair_slots, *refs):
    lefts, rights = refs[:4], refs[4:8]
    extras, outgoing = refs[8:13], refs[13]
    outs = refs[14:18]
    extra_outs, incoming = refs[18:21], refs[21]
    (
        raw, right, left_t, held, sent, core_in, pair_in, pair_late, up_in, down_in,
    ) = refs[22:32]
    (
        raw_sem, right_sem, core_s, core_r, pair_s, pair_r, up_s, up_r, down_s, down_r, out_sem,
        core_credit, pair_credit,
    ) = refs[32:45]
    a, b, c = position()
    side_steps = conditioning_steps(length, extras, extra_outs, refs[45:-1], a, b, c)
    swap_sem = refs[-1]
    swap = remote(
        outgoing, incoming, swap_sem.at[0], swap_sem.at[1], {"section": 1 - lax.axis_index("section")}
    )
    n = len(plan)
    rows, width = held.shape[3:]
    total_rows = raw.shape[1]
    encoder = lax.axis_index("section") == 0
    used_rows = jnp.where(encoder, total_rows // 2, total_rows)
    pair_first = [p[3] == "pair" for p in plan]
    order = [sum(pair_first[:i]) if pair_first[i] else i - sum(pair_first[:i]) for i in range(n)]
    base, total = [], 0
    for i in range(n):
        base.append(total)
        total += (length - 1) * (1 if pair_first[i] else 2)
    groups = 2 * length

    def blocks_of(w):
        return lefts[w].shape[1] // width

    raw_jobs = []
    right_jobs = []
    for i, (w, low, size, _) in enumerate(plan):
        if i == 0 or plan[i - 1][0] != w:
            raw_jobs += [(w, k) for k in range(blocks_of(w))]
        if size != 0 or plan[i - 1][0] != w:
            right_jobs.append(i)

    def raw_load(x):
        w, k = raw_jobs[x]
        src = lefts[w].at[:, pl.ds(k * width, width)]
        return pltpu.make_async_copy(src, raw.at[x % 2], raw_sem.at[x])

    def right_load(x):
        w, low, size, _ = plan[right_jobs[x]]
        src = rights[w].at[:, pl.ds(low if size else 0, width)]
        return pltpu.make_async_copy(src, right.at[x % 2], right_sem.at[x])

    progress = {"raw": 0, "right": -1}

    def turn(w):
        count = blocks_of(w)
        for k in range(count):
            x = progress["raw"]
            progress["raw"] += 1
            raw_load(x).wait()
            slot = x % 2

            def body(r, carry):
                start = pl.multiple_of(r * 128, 128)
                block = raw[slot, pl.ds(start, 128), :].astype(F32).T
                if count == 1:
                    split = block.reshape(groups, 2, rows, 128)
                    for q in range(2):
                        part = split[:, q].reshape(groups * rows, 128)
                        left_t[q, :, pl.ds(start, 128)] = part.astype(BF16)
                else:
                    near = groups // count
                    split = block.reshape(near, 2, count, rows, 128)
                    for q in range(2):
                        for j in range(count):
                            part = split[:, q, j].reshape(near * rows, 128)
                            left_t[
                                q * count + j, pl.ds(k * near * rows, near * rows), pl.ds(start, 128)
                            ] = part.astype(BF16)
                return carry

            lax.fori_loop(0, used_rows // 128, body, 0)
            if x + 2 < len(raw_jobs):
                raw_load(x + 2).start()

    def product(i, q, put):
        w, low, size, _ = plan[i]
        count = blocks_of(w)
        row_set = q if count == 1 else q * count + low
        slot = progress["right"] % 2
        tile = width // 3

        def body(k, carry):
            columns = pl.ds(pl.multiple_of(k * tile, 128), tile)

            def multiply(depth):
                result = dot(left_t[row_set, :, :depth], right[slot, :depth, columns])
                for s in range(groups):
                    put(s, columns, result[s * rows : (s + 1) * rows].astype(BF16))

            when(encoder, lambda: multiply(total_rows // 2))
            when(jnp.logical_not(encoder), lambda: multiply(total_rows))
            return carry

        lax.fori_loop(0, 3, body, 0)

    def to_core(i):
        return remote(sent.at[i % slots], core_in.at[i % slots], core_s.at[i], core_r.at[i], at(a, b, 1 - c))

    def across(i):
        target = at(a, 1 - b, c)
        if pair_first[i]:
            return remote(
                held.at[i, :, 1 - b], pair_in.at[order[i] % pair_slots], pair_s.at[i], pair_r.at[i], target
            )
        return remote(held.at[i, a, 1 - b], pair_late.at[order[i]], pair_s.at[i], pair_r.at[i], target)

    def rows_of(i):
        return (b,) if pair_first[i] else (b, 1 - b)

    def flow_index(i, dest, bb):
        if pair_first[i]:
            return base[i] + dest
        return base[i] + dest * 2 + bb

    def up(i, line, dest, bb):
        x = flow_index(i, dest - 1, bb)
        return remote(held.at[i, dest, bb], up_in.at[x], up_s.at[x], up_r.at[x], at(line + 1, b, c))

    def down(i, line, dest, bb):
        x = flow_index(i, dest, bb)
        return remote(held.at[i, dest, bb], down_in.at[x], down_s.at[x], down_r.at[x], at(line - 1, b, c))

    def add(dst, src):
        dst[...] = dst[...] + src[...]

    def credit(sem, target):
        pl.semaphore_signal(sem, inc=1, device_id=target, device_id_type=MESH)

    def produce(i):
        w = plan[i][0]
        if i > 0 and plan[i - 1][0] != w:
            turn(w)
        if progress["right"] + 1 < len(right_jobs) and right_jobs[progress["right"] + 1] == i:
            progress["right"] += 1
            right_load(progress["right"]).wait()
            if progress["right"] + 1 < len(right_jobs):
                right_load(progress["right"] + 1).start()
        if i >= slots:
            to_core(i - slots).wait_send()

        def put_sent(s, columns, value):
            sent[i % slots, s // 2, s % 2, :, columns] = value

        def put_held(s, columns, value):
            held[i, s // 2, s % 2, :, columns] = value

        product(i, 1 - c, put_sent)
        if i >= slots:
            pl.semaphore_wait(core_credit, 1)
        to_core(i).start()
        product(i, c, put_held)

    def first_add(i):
        to_core(i).wait_recv()

        def body(s, carry):
            add(held.at[i, s // 2, s % 2], core_in.at[i % slots, s // 2, s % 2])
            return carry

        lax.fori_loop(0, groups, body, 0)
        if i + slots < n:
            credit(core_credit, at(a, b, 1 - c))
        if pair_first[i]:
            if order[i] >= pair_slots:
                pl.semaphore_wait(pair_credit, 1)
            across(i).start()

    def second_add(i):
        if not pair_first[i]:
            return
        across(i).wait_recv()

        def body(s, carry):
            add(held.at[i, s, b], pair_in.at[order[i] % pair_slots, s])
            return carry

        lax.fori_loop(0, length, body, 0)
        if order[i] + pair_slots < sum(pair_first):
            credit(pair_credit, at(a, 1 - b, c))

    def line_step(i, j):
        def going_up():
            for dest in range(length - 1, j - 1, -1):
                for bb in rows_of(i):
                    if j > 0:
                        up(i, j - 1, dest, bb).wait_recv()
                        add(held.at[i, dest, bb], up_in.at[flow_index(i, dest - 1, bb)])
                    if dest > j:
                        up(i, j, dest, bb).start()

        def going_down():
            here = length - 1 - j
            for dest in range(0, here + 1):
                for bb in rows_of(i):
                    if j > 0:
                        down(i, here + 1, dest, bb).wait_recv()
                        add(held.at[i, dest, bb], down_in.at[flow_index(i, dest, bb)])
                    if dest < here:
                        down(i, here, dest, bb).start()

        when(a == j, going_up)
        when(a == length - 1 - j, going_down)

    def result(i):
        w, low, size, _ = plan[i]
        dst = outs[w].at[low] if size == 0 else outs[w].at[:, pl.ds(low, size)]
        return pltpu.make_async_copy(held.at[i, a, b], dst, out_sem.at[i])

    def finish(i):
        if pair_first[i]:
            result(i).start()
        else:
            across(i).start()

    def finish_late(i):
        if not pair_first[i]:
            across(i).wait_recv()
            add(held.at[i, a, b], pair_late.at[order[i]])
            result(i).start()

    raw_load(0).start()
    right_load(0).start()
    raw_load(1).start()
    greet_all(length, a, b, c, lambda: turn(plan[0][0]))
    side_steps[0]()
    swap.start()
    produce(0)
    for t in range(n + LAG + LINE_LAG[-1] + 1):
        if t in SIDE_TIMES:
            side_steps[SIDE_TIMES.index(t) + 1]()
        if t < n:
            first_add(t)
        if t + 1 < n:
            produce(t + 1)
        if 0 <= t - LAG < n:
            second_add(t - LAG)
        for j in range(length):
            i = t - LAG - LINE_LAG[j]
            if 0 <= i < n:
                line_step(i, j)
        i = t - LAG - LINE_LAG[length - 1]
        if 0 <= i < n:
            finish(i)
        if 0 <= i - 1 < n:
            finish_late(i - 1)
    side_steps[-1]()
    swap.wait()
    for i in range(n):
        if i >= n - slots:
            to_core(i).wait_send()
        across(i).wait_send()
        result(i).wait()
        for bb in rows_of(i):
            for here in range(length):

                def gone():
                    for dest in range(here + 1, length):
                        up(i, here, dest, bb).wait_send()
                    for dest in range(0, here):
                        down(i, here, dest, bb).wait_send()

                when(a == here, gone)


def scatter_all(lefts, rights, extras, outgoing, shard_shapes, plan, length):
    n = len(plan)
    slots, pair_slots = 2, 4
    total_rows = lefts[0].shape[0]
    rows, width = shard_shapes[0][0], plan[0][2]
    late = sum(p[3] != "pair" for p in plan)
    flows = (length - 1) * (n + late)
    lead = shard_shapes[-1][0]
    dma = pltpu.SemaphoreType.DMA
    grad_mod, lifted_t, slope_t, ada, mask_rows = extras
    images = lifted_t.shape[1]
    payload = (-(-(rows + mask_rows.shape[0]) // 8) * 8, images)
    small = [dma((length - 1,)), dma((length - 1,)), dma((4,))]
    slab = (rows, width)
    return pl.pallas_call(
        functools.partial(scatter_kernel, length, plan, slots, pair_slots),
        out_shape=tuple(jax.ShapeDtypeStruct(s, BF16) for s in shard_shapes)
        + (
            jax.ShapeDtypeStruct(ada.shape, F32),
            jax.ShapeDtypeStruct((1, ada.shape[1]), F32),
            jax.ShapeDtypeStruct((length, 2, 2) + payload, F32),
            jax.ShapeDtypeStruct(outgoing.shape, BF16),
        ),
        in_specs=[anywhere] * 8 + [in_vmem] * 5 + [anywhere],
        out_specs=[anywhere] * 5 + [in_vmem] * 2 + [anywhere],
        scratch_shapes=[
            pltpu.VMEM((2, total_rows, width), BF16),
            pltpu.VMEM((2, total_rows, width), BF16),
            pltpu.VMEM((2 * lead, 2 * length * rows, total_rows), BF16),
            pltpu.VMEM((n, length, 2) + slab, BF16),
            pltpu.VMEM((slots, length, 2) + slab, BF16),
            pltpu.VMEM((slots, length, 2) + slab, BF16),
            pltpu.VMEM((pair_slots, length) + slab, BF16),
            pltpu.VMEM((late,) + slab, BF16),
            pltpu.VMEM((flows,) + slab, BF16),
            pltpu.VMEM((flows,) + slab, BF16),
            dma((lead + 3,)), dma((n,)), dma((n,)), dma((n,)), dma((n,)), dma((n,)),
            dma((flows,)), dma((flows,)), dma((flows,)), dma((flows,)), dma((n,)),
            pltpu.SemaphoreType.REGULAR, pltpu.SemaphoreType.REGULAR,
            pltpu.VMEM((length, 2, 2) + grad_mod.shape, BF16),
            pltpu.VMEM((2, rows, width), F32),
            pltpu.VMEM(payload, F32),
            pltpu.VMEM(payload, F32),
        ]
        + small
        + small
        + [dma((2,)), dma((2,)), dma((2,))],
        compiler_params=pltpu.CompilerParams(
            collective_id=1, has_side_effects=True, vmem_limit_bytes=62 * 1024 * 1024
        ),
        name="scatter_grads",
    )(*lefts, *rights, *extras, outgoing)


def small_gather_kernel(devices, own_ref, out_ref, send, recv):
    me = lax.axis_index("dp")
    barrier = pltpu.get_barrier_semaphore()
    ahead = [lax.rem(me + k, devices) for k in range(1, devices)]
    for target in ahead:
        pl.semaphore_signal(barrier, inc=1, device_id={"dp": target}, device_id_type=MESH)
    pl.semaphore_wait(barrier, devices - 1)
    out_ref[me] = own_ref[...]
    mine = out_ref.at[me]
    copies = [remote(mine, mine, send.at[k], recv.at[k], {"dp": to}) for k, to in enumerate(ahead)]
    for copy in copies:
        copy.start()
    for k, copy in enumerate(copies):
        slab = out_ref.at[lax.rem(me + devices - 1 - k, devices)]
        remote(slab, slab, send.at[k], recv.at[k], {"dp": ahead[k]}).wait_recv()
        copy.wait_send()


def small_gather(own, devices, collective_id):
    dma = pltpu.SemaphoreType.DMA
    return pl.pallas_call(
        functools.partial(small_gather_kernel, devices),
        out_shape=jax.ShapeDtypeStruct((devices,) + own.shape, own.dtype),
        in_specs=[in_vmem],
        out_specs=in_vmem,
        scratch_shapes=[dma((devices - 1,)), dma((devices - 1,))],
        compiler_params=pltpu.CompilerParams(collective_id=collective_id, has_side_effects=True),
        name="small_gather",
    )(own)


def head_window(h):
    low, high = h * HD, h * HD + HD
    start = low // 128 * 128
    return low, high, start, -(-high // 128) * 128


def contract(x, y, dims):
    return lax.dot_general(x, y, ((dims[0], dims[1]), ((), ())), preferred_element_type=F32)


def head_operands(qkv_ref, rows, h):
    width = qkv_ref.shape[1] // 3
    low, high, start, stop = head_window(h)
    lane = lax.broadcasted_iota(jnp.int32, (1, stop - start), 1) + start
    inside = jnp.logical_and(lane >= low, lane < high)
    parts = [qkv_ref[rows, j * width + start : j * width + stop] for j in range(3)]
    return inside, slice(start, stop), parts


def only(inside, x):
    return jnp.where(inside, x, jnp.zeros_like(x))


def softmax_of(query, key, allowed):
    scores = jnp.where(allowed, contract(query, key, ((1,), (1,))) * HD**-0.5, MASKED)
    weights = jnp.exp(scores - jnp.max(scores, axis=-1, keepdims=True))
    return weights * (1.0 / jnp.sum(weights, axis=-1, keepdims=True))


def place(out_ref, rows, start, inside, value):
    window = slice(start, start + value.shape[1])
    out_ref[rows, window] = jnp.where(inside, value.astype(BF16), out_ref[rows, window])


def attend(qkv_ref, rows, allowed, out_ref):
    for h in range(HEADS):
        inside, window, (query, key, value) = head_operands(qkv_ref, rows, h)
        probs = softmax_of(only(inside, query), key, allowed).astype(BF16)
        place(out_ref, rows, window.start, inside, contract(probs, value, ((1,), (0,))))


def attend_back(qkv_ref, grad_ref, rows, allowed, out_ref):
    width = grad_ref.shape[1]
    for h in range(HEADS):
        inside, window, (query, key, value) = head_operands(qkv_ref, rows, h)
        query, grad = only(inside, query), only(inside, grad_ref[rows, window])
        scores = jnp.where(allowed, contract(key, query, ((1,), (1,))) * HD**-0.5, MASKED)
        weights = jnp.exp(scores - jnp.max(scores, axis=0, keepdims=True))
        probs = weights * (1.0 / jnp.sum(weights, axis=0, keepdims=True))
        grad_probs = contract(value, grad, ((1,), (1,)))
        centre = jnp.sum(probs * grad_probs, axis=0, keepdims=True)
        grad_scores = (probs * (grad_probs - centre)).astype(BF16)
        start = window.start
        place(out_ref, rows, 2 * width + start, inside, contract(probs.astype(BF16), grad, ((1,), (0,))))
        place(out_ref, rows, width + start, inside, contract(grad_scores, query, ((1,), (0,))) * HD**-0.5)
        place(out_ref, rows, start, inside, contract(grad_scores, key, ((0,), (0,))) * HD**-0.5)


def dot(x, y):
    return jnp.dot(x, y, preferred_element_type=F32)


def dot_back(x, y):
    return lax.dot_general(x, y, (((1,), (1,)), ((), ())), preferred_element_type=F32)


def dot_rows(x, y):
    return lax.dot_general(x, y, (((0,), (0,)), ((), ())), preferred_element_type=F32)


def normal(x):
    centred = x - jnp.mean(x, axis=-1, keepdims=True)
    scale = lax.rsqrt(jnp.mean(centred * centred, axis=-1, keepdims=True) + EPS)
    return centred * scale, scale


TILE = 384
DEPTH = 2
GELU = math.sqrt(2.0 / math.pi)


def columns_of(t):
    if isinstance(t, int):
        return pl.ds(t * TILE, TILE)
    return pl.ds(pl.multiple_of(t * TILE, 128), TILE)


def unit_of(t, width):
    if isinstance(t, int):
        return pl.ds(t * width, width)
    return pl.ds(pl.multiple_of(t * width, 128), width)


class Stream:
    def __init__(self, ring, sems, width):
        self.ring, self.sems, self.width = ring, sems, width
        self.stages = []

    def add(self, weight, back, inner, outer):
        self.stages.append((weight, back, inner, outer))

    def tile(self, stage, n, k):
        weight, back, inner, _ = self.stages[stage]
        t = n * inner + k
        slot = t % DEPTH if isinstance(t, int) else lax.rem(t, DEPTH)
        deep, side = unit_of(k, self.width), unit_of(n, self.width)
        src = weight.at[side, deep] if back else weight.at[deep, side]
        buffer = self.ring.at[stage % 2, slot]
        return pltpu.make_async_copy(src, buffer, self.sems.at[stage % 2, slot]), buffer

    def begin(self, stage):
        if stage < len(self.stages):
            _, _, inner, outer = self.stages[stage]
            for t in range(min(DEPTH, inner * outer)):
                self.tile(stage, t // inner, t % inner)[0].start()

    def run(self, stage, use, ahead=True):
        _, _, inner, outer = self.stages[stage]
        if ahead:
            self.begin(stage + 1)
        count = inner * outer

        def group(n):
            def product(k, left, back):
                copy, buffer = self.tile(stage, n, k)
                copy.wait()
                result = (dot_back if back else dot)(left, buffer[...])
                t = n * inner + k + DEPTH

                def refill():
                    self.tile(stage, lax.div(t, inner), lax.rem(t, inner))[0].start()

                if not isinstance(t, int):
                    when(t < count, refill)
                elif t < count:
                    self.tile(stage, t // inner, t % inner)[0].start()
                return result

            use(n, product)

        def body(n, carry):
            group(n)
            return carry

        if outer == 1:
            group(0)
        else:
            lax.fori_loop(0, outer, body, 0)


def each_quarter(rows, run):
    def body(q, carry):
        run(q, pl.ds(pl.multiple_of(q * rows, rows), rows))
        return carry

    lax.fori_loop(0, 8, body, 0)


def piece_of(mod_ref, q, p, width, columns=None):
    if columns is None:
        return mod_ref[q, :, p * width : (p + 1) * width]
    return mod_ref[q, :, pl.ds(p * width + columns.start, TILE)]


def modulate(x_ref, mod_ref, out_ref, first, quarter_rows):
    width = x_ref.shape[1]

    def run(q, rows):
        hat = normal(x_ref[rows, :])[0]
        shift, scale = piece_of(mod_ref, q, first, width), piece_of(mod_ref, q, first + 1, width)
        out_ref[rows, :] = (hat * (1.0 + scale) + shift).astype(BF16)

    each_quarter(quarter_rows, run)


def modulate_back(grad, x, scale):
    hat, inverse = normal(x)
    inner = grad * (1.0 + scale)
    along = jnp.mean(inner * hat, axis=-1, keepdims=True)
    grad_x = inverse * (inner - jnp.mean(inner, axis=-1, keepdims=True) - hat * along)
    return grad_x, jnp.sum(grad, axis=0, keepdims=True), jnp.sum(grad * hat, axis=0, keepdims=True)


def split_quarters(quarter_rows, run):
    for q in range(8):
        run(q, slice(q * quarter_rows, (q + 1) * quarter_rows))


def allowed_of(row_ref, column_ref, block):
    rows = pl.ds(pl.multiple_of(block * ATT_ROWS, ATT_ROWS), ATT_ROWS)
    return rows, row_ref[rows, :] == column_ref[block]


def each_block(total_rows, run):
    def body(block, carry):
        run(block)
        return carry

    lax.fori_loop(0, total_rows // ATT_ROWS, body, 0)


def forward_stages(stream, weights):
    width = weights[0].shape[0]
    qkv, proj, up, down = weights
    stream.add(qkv, False, 1, qkv.shape[1] // width)
    stream.add(proj, False, 1, 1)
    stream.add(up, False, 1, up.shape[1] // width)
    stream.add(down, False, down.shape[0] // width, 1)


def backward_stages(stream, weights):
    width = weights[0].shape[0]
    qkv, proj, up, down = weights
    stream.add(down, True, 1, down.shape[0] // width)
    stream.add(up, True, up.shape[1] // width, 1)
    stream.add(proj, True, 1, 1)
    stream.add(qkv, True, qkv.shape[1] // width, 1)


def by_parts(quarter_rows, width, run):
    def one(q, rows):
        for t in range(width // TILE):
            run(q, rows, slice(t * TILE, (t + 1) * TILE))

    each_quarter(quarter_rows, one)


def proj_tile(r, mod_ref, quarter_rows, columns, branch):
    width = r.x.shape[1]
    r.branch[:, columns] = branch.astype(BF16)

    def gated(q, rows):
        gate = piece_of(mod_ref, q, 2, width, columns)
        r.x2[rows, columns] = r.x[rows, columns] + gate * branch[rows]

    split_quarters(quarter_rows, gated)


def gelu_parts(h):
    square = h * h
    t = jnp.tanh(h * (GELU + (GELU * 0.044715) * square))
    half = 0.5 + 0.5 * t
    return h * half, half + (0.5 * h) * (1.0 - t * t) * (GELU + (3.0 * GELU * 0.044715) * square)


def up_tile(r, columns, h):
    act, slope = gelu_parts(h)
    r.act[:, columns] = act.astype(BF16)
    r.slope[:, columns] = slope.astype(BF16)


def out_tile(r, mod_ref, quarter_rows, columns, mlp):
    width = r.x.shape[1]
    r.mlp[:, columns] = mlp.astype(BF16)

    def gated(q, rows):
        gate = piece_of(mod_ref, q, 5, width, columns)
        r.out[rows, columns] = (r.x2[rows, columns] + gate * mlp[rows]).astype(BF16)

    split_quarters(quarter_rows, gated)


def run_forward(stream, r, mod_ref, segments, quarter_rows, finish_part, done):
    width = r.x.shape[1]
    total_rows = r.x.shape[0]
    modulate(r.x, mod_ref, r.a1, 0, quarter_rows)

    def qkv(n, product):
        r.qkv[:, unit_of(n, width)] = product(0, r.a1[...], False).astype(BF16)

    stream.run(0, qkv)
    done("a1")

    def mix(block):
        rows, allowed = allowed_of(*segments, block)
        attend(r.qkv, rows, allowed, r.att)

    each_block(total_rows, mix)

    def proj(n, product):
        r.acc[...] = product(0, r.att[...], False)

    stream.run(1, proj)
    done("att")

    def gated(q, rows, columns):
        branch = r.acc[rows, columns]
        r.branch[rows, columns] = branch.astype(BF16)
        gate = piece_of(mod_ref, q, 2, width, columns)
        r.x2[rows, columns] = r.x[rows, columns] + gate * branch

    by_parts(quarter_rows, width, gated)
    modulate(r.x2, mod_ref, r.a2, 3, quarter_rows)

    def up(n, product):
        r.acc[...] = product(0, r.a2[...], False)

        def part(q, rows, columns):
            into = pl.ds(pl.multiple_of(n * width + columns.start, 128), TILE)
            act, slope = gelu_parts(r.acc[rows, columns])
            r.act[rows, into] = act.astype(BF16)
            r.slope[rows, into] = slope.astype(BF16)

        by_parts(quarter_rows, width, part)

    stream.run(2, up)
    done("a2")

    def down(n, product):
        for k in range(r.act.shape[1] // width):
            part = product(k, r.act[:, k * width : (k + 1) * width], False)
            if k == 0:
                r.acc[...] = part
            else:
                r.acc[...] += part

    stream.run(3, down)
    done("act")
    by_parts(quarter_rows, width, lambda q, rows, columns: finish_part(q, rows, columns, r.acc[rows, columns]))


def run_backward(stream, first, r, mod_ref, segments, quarter_rows, grad_of, finish, done):
    width = r.x.shape[1]
    total_rows = r.x.shape[0]

    def down(n, product):
        columns = unit_of(n, width)
        grad = product(0, r.dmlp[...], True)
        r.slope[:, columns] = (grad * r.slope[:, columns].astype(F32)).astype(BF16)

    stream.run(first, down)
    done("dmlp")
    done("slope")

    def up(n, product):
        for k in range(r.slope.shape[1] // width):
            part = product(k, r.slope[:, k * width : (k + 1) * width], True)
            if k == 0:
                r.dx2[...] = part
            else:
                r.dx2[...] += part

    stream.run(first + 1, up)

    def middle(q, rows):
        scale, gate = piece_of(mod_ref, q, 4, width), piece_of(mod_ref, q, 2, width)
        grad, shift_grad, scale_grad = modulate_back(r.dx2[rows, :], r.x2[rows, :], scale)
        grad = grad + grad_of(rows)
        r.dx2[rows, :] = grad
        r.dmod[q, :, 3 * width : 4 * width] = shift_grad
        r.dmod[q, :, 4 * width : 5 * width] = scale_grad
        r.dmod[q, :, 2 * width : 3 * width] = jnp.sum(
            grad * r.branch[rows, :].astype(F32), axis=0, keepdims=True
        )
        r.dbranch[rows, :] = (gate * grad).astype(BF16)

    each_quarter(quarter_rows, middle)

    def proj(n, product):
        r.datt[...] = product(0, r.dbranch[...], True).astype(BF16)

    stream.run(first + 2, proj)
    done("dbranch")

    def mix(block):
        rows, allowed = allowed_of(*segments, block)
        attend_back(r.qkv, r.datt, rows, allowed, r.dqkv)

    each_block(total_rows, mix)
    done("dqkv")

    def qkv(n, product):
        for k in range(3):
            part = product(k, r.dqkv[:, k * width : (k + 1) * width], True)
            if k == 0:
                r.acc[...] = part
            else:
                r.acc[...] += part

    stream.run(first + 3, qkv, ahead=False)

    def outer(q, rows):
        scale = piece_of(mod_ref, q, 1, width)
        grad, shift_grad, scale_grad = modulate_back(r.acc[rows, :], r.x[rows, :], scale)
        r.dmod[q, :, :width] = shift_grad
        r.dmod[q, :, width : 2 * width] = scale_grad
        finish(q, rows, grad + r.dx2[rows, :])

    each_quarter(quarter_rows, outer)
    done("dmod")


def placed(kept_ref, m, slot):
    kept = kept_ref[m]
    positions = lax.broadcasted_iota(jnp.int32, (slot, kept.shape[1]), 0)
    return jnp.where(positions == kept, 1.0, 0.0).astype(BF16)


class Copies:
    def __init__(self, sems):
        self.sems, self.count, self.pending = sems, 0, []

    def start(self, src, dst):
        copy = pltpu.make_async_copy(src, dst, self.sems.at[self.count])
        self.count += 1
        copy.start()
        self.pending.append(copy)
        return copy

    def finish(self):
        for copy in self.pending:
            copy.wait()
        self.pending = []


def encode_kernel(names, tokens, kept_ref, mod_ref, row_ref, column_ref, wq, wp, wu, wd, *rest):
    outs, scratch = rest[: len(names)], rest[len(names) :]
    r = SimpleNamespace(**dict(zip(names + ("acc",), scratch[: len(names) + 1])))
    loaded, ring, stream_sems, sems = scratch[len(names) + 1 :]
    width = loaded.shape[2]
    slot = loaded.shape[1]

    def work():
        stream = Stream(ring, stream_sems, width)
        forward_stages(stream, (wq, wp, wu, wd))
        copies = Copies(sems)
        copies.start(tokens, loaded)
        stream.begin(0)
        copies.finish()
        kept = kept_ref.shape[2]
        for m in range(2):
            r.x[m * kept : (m + 1) * kept, :] = dot_rows(placed(kept_ref, m, slot), loaded[m])
        total_rows = r.x.shape[0]
        out_of = dict(zip(names, outs))

        def done(name):
            copies.start(getattr(r, name), out_of[name].at[pl.ds(0, total_rows)])

        def finish_part(q, rows, columns, mlp):
            r.mlp[rows, columns] = mlp.astype(BF16)
            gate = piece_of(mod_ref, q, 5, width, columns)
            r.out[rows, columns] = (r.x2[rows, columns] + gate * mlp).astype(BF16)

        run_forward(stream, r, mod_ref, (row_ref, column_ref), total_rows // 8, finish_part, done)
        for name in ("x", "x2", "qkv", "branch", "slope", "mlp", "out"):
            done(name)
        copies.finish()

    when(lax.axis_index("section") == 0, work)


def decode_kernel(
    names, rights, received, cotangent, kept_ref, mask_ref, mod_ref, row_ref, column_ref, wq, wp, wu, wd,
    a1, att, a2, act, *rest,
):
    outs, scratch = rest[: 4 + len(rights) + 4], rest[4 + len(rights) + 4 :]
    lefts = dict(zip(("a1", "att", "a2", "act"), outs[:4]))
    right_outs = dict(zip(rights, outs[4 : 4 + len(rights)]))
    dmod_out, decoded, back, mask_out = outs[4 + len(rights) :]
    r = SimpleNamespace(**dict(zip(names, scratch[: len(names)])))
    got, ring, stream_sems, sems = scratch[len(names) :]
    width = got.shape[2]

    def work():
        stream = Stream(ring, stream_sems, width)
        forward_stages(stream, (wq, wp, wu, wd))
        backward_stages(stream, (wq, wp, wu, wd))
        copies = Copies(sems)
        copies.start(received, got)
        copies.start(cotangent, r.dy)
        stream.begin(0)
        copies.finish()
        total_rows = r.x.shape[0]
        slot, kept = total_rows // 2, kept_ref.shape[2]
        for m in range(2):
            place = placed(kept_ref, m, slot)
            flags = jnp.sum(place.astype(F32), axis=1, keepdims=True)
            r.free[m * slot : (m + 1) * slot, :] = jnp.broadcast_to(1.0 - flags, (slot, 128))
            filled = dot(place, got[m]) + (1.0 - flags) * mask_ref[...].astype(F32)
            r.x[m * slot : (m + 1) * slot, :] = filled
        out_of = {**lefts, **right_outs, "dmod": dmod_out, "slope": right_outs["dhid"]}

        def done(name):
            copies.start(getattr(r, name), out_of[name])

        def finish_part(q, rows, columns, part):
            gate = piece_of(mod_ref, q, 5, width, columns)
            dy = r.dy[rows, columns].astype(F32)
            r.out[rows, columns] = (r.x2[rows, columns] + gate * part).astype(BF16)
            r.dmlp[rows, columns] = (gate * dy).astype(BF16)
            r.dmod[q, :, 5 * width + columns.start : 5 * width + columns.stop] = jnp.sum(
                dy * part, axis=0, keepdims=True
            )

        segments = (row_ref, column_ref)
        run_forward(stream, r, mod_ref, segments, total_rows // 8, finish_part, done)
        copies.start(r.out, decoded)
        r.mask[...] = jnp.zeros_like(r.mask)

        def finish(q, rows, grad):
            r.mask[...] += jnp.sum(grad * r.free[rows, :1], axis=0, keepdims=True)
            r.dbranch[rows, :] = grad.astype(BF16)

        def grad_of(rows):
            return r.dy[rows, :].astype(F32)

        def done_back(name):
            if name == "dbranch":
                copies.start(getattr(r, name), out_of[name]).wait()
                copies.pending.pop()
            else:
                done(name)

        run_backward(stream, 4, r, mod_ref, segments, total_rows // 8, grad_of, finish, done_back)
        for m in range(2):
            place = placed(kept_ref, m, slot)
            got[m] = dot_rows(place, r.dbranch[m * slot : (m + 1) * slot, :]).astype(BF16)
        copies.start(got, back)
        copies.start(r.mask, mask_out)
        copies.finish()

    when(lax.axis_index("section") == 1, work)


def encode_back_kernel(
    names, rights, saved, received, kept_ref, mod_ref, row_ref, column_ref, wq, wp, wu, wd, *rest
):
    kept_in = dict(zip(saved, rest[: len(saved)]))
    rest = rest[len(saved) + len(rights) + 1 :]
    right_outs = dict(zip(rights, rest[: len(rights)]))
    dmod_out, token_out = rest[len(rights) : len(rights) + 2]
    scratch = rest[len(rights) + 2 :]
    r = SimpleNamespace(**dict(zip(names, scratch[: len(names)])))
    ring, stream_sems, sems = scratch[len(names) :]
    width = r.x.shape[1]

    def work():
        stream = Stream(ring, stream_sems, width)
        backward_stages(stream, (wq, wp, wu, wd))
        copies = Copies(sems)
        first = [copies.start(received, r.dy)]
        for name in reversed(saved):
            first.append(copies.start(kept_in[name], getattr(r, name)))
        stream.begin(0)
        for copy in first[:2]:
            copy.wait()
        total_rows = r.x.shape[0]
        out_of = {**right_outs, "dmod": dmod_out, "slope": right_outs["dhid"]}

        def done(name):
            if name == "dmod":
                copies.start(getattr(r, name), out_of[name])
            else:
                copies.start(getattr(r, name), out_of[name].at[pl.ds(0, total_rows)])

        def start(q, rows):
            gate = piece_of(mod_ref, q, 5, width)
            dy = r.dy[rows, :].astype(F32)
            r.dmlp[rows, :] = (gate * dy).astype(BF16)
            r.dmod[q, :, 5 * width :] = jnp.sum(dy * r.mlp[rows, :].astype(F32), axis=0, keepdims=True)

        each_quarter(total_rows // 8, start)
        for copy in first[2:]:
            copy.wait()
        copies.pending = []

        def finish(q, rows, grad):
            r.mlp[rows, :] = grad.astype(BF16)

        def grad_of(rows):
            return r.dy[rows, :].astype(F32)

        segments = (row_ref, column_ref)
        run_backward(stream, 0, r, mod_ref, segments, total_rows // 8, grad_of, finish, done)
        kept = kept_ref.shape[2]
        slot = token_out.shape[1]
        for m in range(2):
            place = placed(kept_ref, m, slot)
            r.tokens[m] = dot(place, r.mlp[m * kept : (m + 1) * kept, :]).astype(BF16)
        copies.start(r.tokens, token_out)
        copies.finish()

    when(lax.axis_index("section") == 0, work)


VMEM_BYTES = 60 * 1024 * 1024
LEFTS = ("a1", "att", "a2", "act")
RIGHTS = ("dqkv", "dbranch", "dhid", "dmlp")
SAVED = ("x", "x2", "qkv", "branch", "slope", "mlp")


def buffer_shapes(rows, width, wide_width):
    full, broad = lambda t: ((rows, width), t), lambda n, t: ((rows, n), t)
    return dict(
        x=full(F32), x2=full(F32), dx2=full(F32), acc=full(F32), a1=full(BF16),
        att=full(BF16), a2=full(BF16), branch=full(BF16), mlp=full(BF16), out=full(BF16),
        dy=full(BF16), dmlp=full(BF16), dbranch=full(BF16), datt=full(BF16),
        qkv=broad(3 * width, BF16), dqkv=broad(3 * width, BF16), act=broad(wide_width, BF16),
        slope=broad(wide_width, BF16), dhid=broad(wide_width, BF16),
        dmod=((8, 1, 6 * width), F32), mask=((1, width), F32), free=((rows, 128), F32),
    )


def rings(width):
    dma = pltpu.SemaphoreType.DMA
    return [pltpu.VMEM((2, DEPTH, width, width), BF16), dma((2, DEPTH)), dma((24,))]


def encode(tokens, kept, modulation, segments, weights, rows, all_rows):
    width, wide_width = weights[0].shape[0], weights[2].shape[1]
    shapes = buffer_shapes(rows, width, wide_width)
    names = LEFTS + SAVED + ("out",)
    outs = [jax.ShapeDtypeStruct(((all_rows if n in LEFTS else rows), shapes[n][0][1]), shapes[n][1]) for n in names]
    results = pl.pallas_call(
        functools.partial(encode_kernel, names),
        out_shape=outs,
        in_specs=[anywhere] + [in_vmem] * 4 + [anywhere] * 4,
        out_specs=[anywhere] * len(names),
        scratch_shapes=[pltpu.VMEM(*shapes[n]) for n in names + ("acc",)]
        + [pltpu.VMEM(tokens.shape, BF16)]
        + rings(width),
        compiler_params=pltpu.CompilerParams(vmem_limit_bytes=VMEM_BYTES),
        name="encode",
    )(tokens, kept, modulation, *segments, *weights)
    return results[:4], results[4:-1], results[-1]


def decode(received, cotangent, kept, mask_token, modulation, segments, weights, lefts):
    width, wide_width = weights[0].shape[0], weights[2].shape[1]
    rows = cotangent.shape[0]
    shapes = buffer_shapes(rows, width, wide_width)
    names = LEFTS + (
        "x", "x2", "qkv", "branch", "slope", "out", "dy", "dmlp", "dbranch", "datt", "dqkv", "dmod",
        "mask", "free",
    )
    scratch = [pltpu.VMEM(*shapes[n]) for n in names]
    names += ("dx2", "acc")
    scratch += [pltpu.VMEM(*shapes["dx2"]), pltpu.VMEM(*shapes["acc"])]
    outs = [jax.ShapeDtypeStruct(*shapes[n]) for n in LEFTS + RIGHTS + ("dmod", "out")]
    outs += [jax.ShapeDtypeStruct(received.shape, BF16), jax.ShapeDtypeStruct((1, width), F32)]
    results = pl.pallas_call(
        functools.partial(decode_kernel, names, RIGHTS),
        out_shape=outs,
        in_specs=[anywhere] * 2 + [in_vmem] * 5 + [anywhere] * 8,
        out_specs=[anywhere] * len(outs),
        scratch_shapes=scratch + [pltpu.VMEM(received.shape, BF16)] + rings(width),
        input_output_aliases={11 + j: j for j in range(4)},
        compiler_params=pltpu.CompilerParams(vmem_limit_bytes=VMEM_BYTES),
        name="decode",
    )(received, cotangent, kept, mask_token, modulation, *segments, *weights, *lefts)
    return results[:4], results[4:8], results[8:]


def encode_back(received, kept, modulation, segments, weights, saved, rights, grad_mod, token_shape):
    width, wide_width = weights[0].shape[0], weights[2].shape[1]
    rows = received.shape[0]
    shapes = buffer_shapes(rows, width, wide_width)
    names = SAVED + ("dy", "dmlp", "dbranch", "datt", "dqkv", "dmod", "dx2", "acc", "tokens")
    shapes["tokens"] = (token_shape, BF16)
    outs = [jax.ShapeDtypeStruct(x.shape, x.dtype) for x in tuple(rights) + (grad_mod,)]
    outs.append(jax.ShapeDtypeStruct(token_shape, BF16))
    before = 9 + len(saved)
    results = pl.pallas_call(
        functools.partial(encode_back_kernel, names, RIGHTS, SAVED),
        out_shape=outs,
        in_specs=[anywhere] + [in_vmem] * 4 + [anywhere] * (4 + len(saved) + 5),
        out_specs=[anywhere] * len(outs),
        scratch_shapes=[pltpu.VMEM(*shapes[n]) for n in names] + rings(width),
        input_output_aliases={before + j: j for j in range(5)},
        compiler_params=pltpu.CompilerParams(vmem_limit_bytes=VMEM_BYTES),
        name="encode_back",
    )(received, kept, modulation, *segments, *weights, *saved, *rights, grad_mod)
    return results[:4], results[4], results[5]


def gather_encode_kernel(length, plan, names, *refs):
    sources, (partial, big_ref, tokens, kept_ref, row_ref, column_ref) = refs[:4], refs[4:10]
    outs, (mod_out, received) = refs[10:14], refs[14:16]
    saved_outs = refs[16 : 16 + len(names)]
    rest = refs[16 + len(names) :]
    r = SimpleNamespace(**dict(zip(names + ("out",), rest[: len(names) + 1])))
    (
        loaded, mod_ref, tiles, last_tile, part_held, part_core, part_pair, part_line,
    ) = rest[len(names) + 1 : len(names) + 9]
    sems = rest[len(names) + 9 : len(names) + 18]
    part_sems, line_sems, tile_sems, out_sems, copy_sems = rest[len(names) + 18 :]
    a, b, c = position()
    encoder = lax.axis_index("section") == 0
    other = {"section": 1 - lax.axis_index("section")}
    barrier = pltpu.get_barrier_semaphore()

    def tell(target):
        pl.semaphore_signal(barrier, inc=1, device_id=target, device_id_type=MESH)

    tell(at(a, 1 - b, c))
    tell(at(a, b, 1 - c))
    tell(other)
    for k in range(1, length):
        tell(at(lax.rem(a + k, length), b, c))
    pl.semaphore_wait(barrier, length + 2)

    n = len(plan)
    width = r.x.shape[1]
    total_rows = r.x.shape[0]
    quarter_rows = total_rows // 8
    issue, move, complete, drain = gather_moves(length, plan, sources, outs, sems, a, b, c)
    copies = Copies(copy_sems)
    out_of = dict(zip(names, saved_outs))

    part_load = pltpu.make_async_copy(partial.at[:, :, c], part_held, part_sems.at[0])
    part_to_core = remote(partial.at[:, :, 1 - c], part_core, part_sems.at[1], part_sems.at[2], at(a, b, 1 - c))
    part_across = remote(part_held.at[:, 1 - b], part_pair, part_sems.at[3], part_sems.at[4], at(a, 1 - b, c))

    def part_to_line(k):
        to = lax.rem(a + k, length)
        return remote(
            part_held.at[to, b], part_line.at[k - 1], line_sems.at[0, k - 1], line_sems.at[1, k - 1], at(to, b, c)
        )

    def add_part(where, got):
        part_held[where] = part_held[where] + got

    def part_first():
        part_to_core.wait_recv()
        part_load.wait()
        for s in range(2 * length):
            add_part((s // 2, s % 2), part_core[s // 2, s % 2])
        part_across.start()

    def part_second():
        part_across.wait()
        for aa in range(length):
            add_part((aa, b), part_pair[aa])
        for k in range(1, length):
            part_to_line(k).start()

    def part_last():
        total = part_held[a, b].astype(F32)
        for k in range(1, length):
            part_to_line(k).wait_recv()
            total = total + part_line[k - 1].astype(F32)
        for q in range(8):
            first = q // SMALL_PER * SMALL_PER
            mod_ref[q] = jnp.where(big_ref[q] > 0, total[first : first + 1], total[q : q + 1])
        copies.start(mod_ref, mod_out)

    def load_tile(w, low, t):
        src = outs[w].at[:, :, :, :, pl.ds(low + t * TILE, TILE)]
        return pltpu.make_async_copy(src, tiles.at[t % 2], tile_sems.at[t % 2])

    def products(w, low, left, put):
        count = width // TILE
        for t in range(min(2, count)):
            load_tile(w, low, t).start()
        for t in range(count):
            load_tile(w, low, t).wait()
            tile = tiles[t % 2].astype(F32).reshape(width, TILE).astype(BF16)
            result = dot(getattr(r, left)[...], tile)
            if t + 2 < count:
                load_tile(w, low, t + 2).start()
            put(columns_of(low // TILE + t), result)

    def done(name):
        copies.start(getattr(r, name), out_of[name].at[pl.ds(0, total_rows)])

    def start_encode():
        fetch = pltpu.make_async_copy(tokens, loaded, tile_sems.at[2])
        fetch.start()
        fetch.wait()
        kept, slot = kept_ref.shape[2], loaded.shape[1]
        for m in range(2):
            r.x[m * kept : (m + 1) * kept, :] = dot_rows(placed(kept_ref, m, slot), loaded[m])

    def put_qkv(columns, result):
        r.qkv[:, columns] = result.astype(BF16)

    def put_proj(columns, result):
        proj_tile(r, mod_ref, quarter_rows, columns, result)

    def put_up(columns, result):
        up_tile(r, columns, result)

    def send_out(t):
        columns = columns_of(t)
        return remote(
            r.out.at[:, columns], received.at[:, columns], out_sems.at[0, t], out_sems.at[1, t], other
        )

    def encode_chunk(i):
        w, low, _, _ = plan[i]
        if w == 0:
            if i == 0:
                modulate(r.x, mod_ref, r.a1, 0, quarter_rows)
            products(w, low, "a1", put_qkv)
        elif w == 1:
            rows, allowed = slice(0, total_rows), row_ref[...] == column_ref[0]
            attend(r.qkv, rows, allowed, r.att)
            products(w, low, "att", put_proj)
            modulate(r.x2, mod_ref, r.a2, 3, quarter_rows)
        elif w == 2:
            products(w, low, "a2", put_up)
        else:
            src = outs[w].at[:, :, :, :, pl.ds(low, TILE)]
            fetch = pltpu.make_async_copy(src, last_tile, tile_sems.at[2])
            fetch.start()
            fetch.wait()
            tile = last_tile[...].reshape(r.act.shape[1], TILE)
            out_tile(r, mod_ref, quarter_rows, columns_of(low // TILE), dot(r.act[...], tile))
            send_out(low // TILE).start()

    part_load.start()
    part_to_core.start()
    issue(0)
    when(encoder, start_encode)
    part_first()
    for i in range(1, AHEAD):
        issue(i)
    for t in range(n + length - 1):
        move(t, AHEAD)
        if t == 0:
            part_second()
        if t == 1:
            part_last()
        i = t - length + 1
        if i >= 0:
            complete(i)
            when(encoder, lambda: encode_chunk(i))
    for i in range(n):
        drain(i)
    part_to_core.wait_send()
    for k in range(1, length):
        part_to_line(k).wait_send()

    def close():
        for name in names:
            done(name)
        for copy in copies.pending[1:]:
            copy.wait()
        for t in range(width // TILE):
            send_out(t).wait_send()

    when(encoder, close)
    copies.pending[0].wait()

    def arrive():
        for t in range(width // TILE):
            send_out(t).wait_recv()

    when(jnp.logical_not(encoder), arrive)


AHEAD = 4


def gather_encode(shards, partial, big, tokens, kept, segments, plan, length, rows, all_rows):
    n = len(plan)
    width, wide_width = shards[1].shape[1], shards[2].shape[1]
    shapes = buffer_shapes(rows, width, wide_width)
    names = LEFTS + SAVED
    quarters = partial.shape[3]
    part_slab = partial.shape[3:]
    dma = pltpu.SemaphoreType.DMA
    outs = [jax.ShapeDtypeStruct((length, 2, 2) + s.shape, BF16) for s in shards]
    outs += [jax.ShapeDtypeStruct((quarters, 1, 6 * width), F32), jax.ShapeDtypeStruct((rows, width), BF16)]
    outs += [jax.ShapeDtypeStruct(((all_rows if m in LEFTS else rows), shapes[m][0][1]), shapes[m][1]) for m in names]
    results = pl.pallas_call(
        functools.partial(gather_encode_kernel, length, plan, names),
        out_shape=outs,
        in_specs=[anywhere] * 5 + [in_vmem, anywhere] + [in_vmem] * 3,
        out_specs=[anywhere] * len(outs),
        scratch_shapes=[pltpu.VMEM(*shapes[m]) for m in names + ("out",)]
        + [
            pltpu.VMEM(tokens.shape, BF16),
            pltpu.VMEM((quarters, 1, 6 * width), F32),
            pltpu.VMEM((2, length, 2, 2, shards[0].shape[0], TILE), BF16),
            pltpu.VMEM((length, 2, 2, shards[3].shape[0], TILE), BF16),
            pltpu.VMEM((length, 2) + part_slab, BF16),
            pltpu.VMEM((length, 2) + part_slab, BF16),
            pltpu.VMEM((length,) + part_slab, BF16),
            pltpu.VMEM((length - 1,) + part_slab, BF16),
        ]
        + [dma((n, length, 2))] * 4
        + [dma((n, length))] * 2
        + [dma((n, length, 2))] * 2
        + [dma((n,)), dma((5,)), dma((2, length - 1)), dma((3,)), dma((2, width // TILE)), dma((len(names) + 1,))],
        compiler_params=pltpu.CompilerParams(
            collective_id=0, has_side_effects=True, vmem_limit_bytes=VMEM_BYTES
        ),
        name="gather_encode",
    )(*shards, partial, big, tokens, kept, *segments)
    return results[:4], results[4], results[5], results[6:10], results[10:]


def plan_of(widths, lead, unit, line_first):
    plan = [(w, low, unit) for w, width in enumerate(widths) for low in range(0, width, unit)]
    plan += [(len(widths), j, 0) for j in range(lead)]
    return tuple(p + ("line" if i in line_first else "pair",) for i, p in enumerate(plan))


def swap_sections(x):
    return lax.ppermute(x, "section", [(0, 1), (1, 0)])


def on_device(
    tokens, kept_index, big_image, timesteps, labels, cotangent, mask_token, time_weight, class_table,
    ada_weight, ada_bias, qkv_weight, proj_weight, up_weight, down_weight,
):
    section = lax.axis_index("section")
    me = lax.axis_index("dp")
    devices = lax.axis_size("dp")
    micro, slot, width = tokens.shape
    kept_count = kept_index.shape[1]
    own_width = ada_weight.shape[1]
    images = micro * SMALL_PER
    quarters = micro * SMALL_PER
    ada = ada_weight[0]

    length = devices // 4
    ids = jnp.concatenate([timesteps.reshape(1, images), labels.reshape(1, images)])
    if length == 4:
        ids = small_gather(jnp.pad(ids, ((0, 6), (0, 128 - images))), devices, 2)
    else:
        ids = lax.all_gather(ids, "dp", axis=0)
    times = ids[:, 0, :images].reshape(devices * images)
    classes = ids[:, 1, :images].reshape(devices * images)
    half = time_weight.shape[0] // 2
    frequencies = jnp.exp(-math.log(10000.0) * jnp.arange(half, dtype=F32) / half)
    angles = times.astype(F32)[:, None] * frequencies[None, :]
    embedding = jnp.concatenate([jnp.cos(angles), jnp.sin(angles)], axis=-1).astype(BF16)
    onehot = (classes[:, None] == jnp.arange(class_table.shape[0])[None, :]).astype(BF16)
    cond = dot(embedding, time_weight) + dot(onehot, class_table)
    cond = lax.dynamic_slice_in_dim(cond, me * own_width, own_width, axis=1)
    lifted = jax.nn.silu(cond).astype(BF16)
    bias_width = ada_bias.shape[1]
    bias = lax.dynamic_update_slice_in_dim(
        jnp.zeros((1, 6 * width), F32), ada_bias.astype(F32), me * bias_width, axis=1
    )
    partial = (dot(lifted, ada) + bias).astype(BF16).reshape(devices, images, 6 * width)

    big = big_image[:, :1] > 0
    quarter_ids = jnp.arange(quarters, dtype=jnp.int32).reshape(micro, SMALL_PER)
    segment_of = jnp.where(big, quarter_ids[:, :1], quarter_ids).reshape(quarters)
    kept = kept_index.reshape(micro, 1, kept_count)

    def segments(quarter_rows):
        ids = jnp.repeat(segment_of, quarter_rows)
        return ids.reshape(-1, 1), ids.reshape(-1, 1, ATT_ROWS)

    enc_rows, dec_rows = micro * kept_count, micro * slot
    enc_segments = segments(enc_rows // quarters)
    dec_segments = segments(dec_rows // quarters)

    shards = (qkv_weight[0], proj_weight[0], up_weight[0])
    lead = down_weight.shape[1] // qkv_weight.shape[1]
    widths = [x.shape[1] for x in shards]
    if length == 4:
        plan = [(w, low, width, "line") for w in range(3) for low in range(0, widths[w], width)]
        plan += [(3, low, TILE, "line") for low in range(0, width, TILE)]
        plan = tuple(p[:3] + ("pair" if i in (1, 7) else "line",) for i, p in enumerate(plan))
        flags = jnp.repeat(big[:, 0], SMALL_PER).astype(jnp.int32).reshape(quarters, 1, 1)
        whole, modulation, received, lefts, saved = gather_encode(
            shards + (down_weight[0],), partial.reshape((length, 2, 2) + partial.shape[1:]), flags, tokens, kept,
            enc_segments, plan, length, enc_rows, dec_rows,
        )
        weights = tuple(w.reshape(-1, w.shape[-1]) for w in whole)
        received = received.reshape(micro, kept_count, width)
    else:
        whole = (lax.all_gather(x, "dp", axis=0, tiled=True) for x in shards + (down_weight[0],))
        weights = tuple(whole)
        modulation = lax.psum_scatter(partial, "dp", scatter_dimension=0, tiled=False).astype(F32)
        modulation = modulation.reshape(micro, SMALL_PER, 6 * width)
        modulation = jnp.where(big[:, :, None], modulation[:, :1], modulation).reshape(quarters, 1, 6 * width)
        lefts, saved, encoded = encode(tokens, kept, modulation, enc_segments, weights, enc_rows, dec_rows)
        received = swap_sections(encoded).reshape(micro, kept_count, width)

    lefts, rights, (grad_mod, decoded, back, mask_part) = decode(
        received, cotangent.reshape(dec_rows, width), kept, mask_token.reshape(1, width), modulation,
        dec_segments, weights, lefts,
    )
    received = swap_sections(back).reshape(enc_rows, width)
    rights, grad_mod, token_grad = encode_back(
        received, kept, modulation, enc_segments, weights, saved, rights, grad_mod, (micro, slot, width)
    )
    decoded = decoded.reshape(micro, slot, width)
    mask_part = jnp.where(section == 1, mask_part, 0.0).reshape(width)

    half_width = width // 2
    outgoing = jnp.where(section == 0, token_grad[:, :, half_width:], decoded[:, :, :half_width])

    grad_mod = grad_mod.reshape(micro, SMALL_PER, 6 * width)
    first_only = (jnp.arange(SMALL_PER) == 0)[None, :, None]
    grad_mod = jnp.where(
        big[:, :, None], jnp.where(first_only, jnp.sum(grad_mod, axis=1, keepdims=True), 0.0), grad_mod
    )
    grad_mod = grad_mod.reshape(images, 6 * width).astype(BF16)
    silu_slope = jax.vjp(jax.nn.silu, cond)[1](jnp.ones_like(cond))[0]
    shapes = tuple(x.shape for x in shards) + ((lead, own_width, width),)
    every_image = devices * images
    if length == 4:
        mask_rows = mask_part.reshape(-1, every_image)
        extras = (grad_mod, lifted.T, silu_slope.T, ada, mask_rows)
        plan = plan_of(widths, lead, width, (0, 6))
        *mine, ada_grad, bias_sum, shared, incoming = scatter_all(
            lefts, rights, extras, outgoing, shapes, plan, length
        )
        shared = shared.reshape(devices, -1, every_image)
        every_cond = shared[:, :own_width].reshape(width, every_image)
        mask_grad = jnp.sum(shared[:, own_width : own_width + mask_rows.shape[0]], axis=0).reshape(width)
        bias_grad = lax.dynamic_slice_in_dim(bias_sum, me * bias_width, bias_width, axis=1)
    else:
        incoming = swap_sections(outgoing)
        every_mod = lax.all_gather(grad_mod, "dp", axis=0, tiled=True)
        ada_grad = dot_rows(lifted, every_mod)
        bias_sum = jnp.sum(every_mod.astype(F32), axis=0, keepdims=True)
        bias_grad = lax.dynamic_slice_in_dim(bias_sum, me * bias_width, bias_width, axis=1)
        grad_cond = dot_back(every_mod, ada) * silu_slope
        every_cond = lax.psum(lax.all_gather(grad_cond.T, "dp", axis=0, tiled=True), "section")
        mask_grad = lax.psum(mask_part, ("section", "dp"))
        half_rows = jnp.arange(dec_rows)[:, None] < jnp.where(section == 0, enc_rows, dec_rows)
        lefts, rights = ([jnp.where(half_rows, x, jnp.zeros_like(x)) for x in xs] for xs in (lefts, rights))
        split = (dot_rows(x, y).astype(BF16).reshape((devices,) + s) for x, y, s in zip(lefts, rights, shapes))
        mine = tuple(lax.psum_scatter(g, "dp", scatter_dimension=0) for g in split)
    decoded_half = jnp.where(section == 0, incoming, decoded[:, :, half_width:])
    token_half = jnp.where(section == 0, token_grad[:, :, :half_width], incoming)
    every_cond = every_cond.astype(BF16)
    time_grad, table_grad = (
        lax.dot_general(x, every_cond, (((0,), (1,)), ((), ())), preferred_element_type=F32)
        for x in (embedding, onehot)
    )
    qkv_grad, proj_grad, up_grad, down_grad = (g.astype(F32) for g in mine)
    return (
        decoded_half,
        token_half,
        mask_grad,
        time_grad,
        table_grad,
        ada_grad[None],
        bias_grad,
        qkv_grad[None],
        proj_grad[None],
        up_grad[None],
        down_grad.reshape(down_weight.shape),
    )


def solution(mesh):
    rows = P(None, "dp", None)
    ids = P(None, "dp")
    weight = P("section", "dp", None)
    halves = P(None, "dp", "section")
    in_specs = (rows, ids, ids, ids, ids, rows, P(), P(), P(), weight, P("section", "dp")) + (weight,) * 4
    out_specs = (halves, halves, P(), P(), P(), weight, P("section", "dp")) + (weight,) * 4
    return jax.shard_map(
        on_device, mesh=mesh, in_specs=in_specs, out_specs=out_specs, check_vma=False
    )
```
